32 devices in a mesh: section: 2 (over core), seq: 4 (over y, x), heads: 4 (over z).
Axes of the slice: x: 2, y: 2, z: 4, core: 2. Of those that a mesh axis runs over, the one named last changes fastest.
Arguments:
- frames: bfloat16 [2, 704, 1024], P(None, 'seq', 'heads'), may hold values from -6 to 6
- cotangent: bfloat16 [2, 704, 1024], P(None, 'seq', 'heads'), may hold values from -6 to 6
- utt_lengths: int32 [2, 3], replicated, may hold values from 1 to 702, as said below
- time_ids: int32 [2, 3], replicated, may hold values from 0 to 999
- w_time_in: bfloat16 [256, 1024], replicated, may hold values from -0.375 to 0.375
- w_time_out: bfloat16 [1024, 1024], replicated, may hold values from -0.1875 to 0.1875
- w_mod: bfloat16 [2, 1024, 6, 1024], P('section', None, None, 'heads'), may hold values from -0.375 to 0.375
- w_qkv: bfloat16 [2, 1024, 3, 1024], P('section', None, None, 'heads'), may hold values from -0.1875 to 0.1875
- w_out: bfloat16 [2, 1024, 1024], P('section', 'heads'), may hold values from -3 to 3
- w_up: bfloat16 [2, 1024, 2048], P('section', None, 'heads'), may hold values from -0.1875 to 0.1875
- w_down: bfloat16 [2, 2048, 1024], P('section', 'heads'), may hold values from -0.125 to 0.125
Outputs:
- acts: bfloat16 [2, 2, 704, 1024], P('section', None, 'seq', 'heads')
- grads: float32 [2, 2, 704, 1024], P('section', None, 'seq', 'heads')
- g_time_in: float32 [256, 1024], replicated
- g_time_out: float32 [1024, 1024], replicated
- g_mod: float32 [2, 1024, 6, 1024], P('section', None, None, 'heads')
- g_qkv: float32 [2, 1024, 3, 1024], P('section', None, None, 'heads')
- g_out: float32 [2, 1024, 1024], P('section', 'heads')
- g_up: float32 [2, 1024, 2048], P('section', None, 'heads')
- g_down: float32 [2, 2048, 1024], P('section', 'heads')
The draws below stay inside these ranges and needn't reach their ends.
Inputs may be any that keep to these rules, and one draw needn't show every extreme that they name: `utt_lengths`: each micro-batch packs three utterances in order: the first and the last have 1 to 88 frames each, the middle one has the rest, so that the three sum to 704.
All inputs are finite; a program needn't handle non-finite values.
Results may differ from the reference program's by a relative error of at most 0.025.
Values may be sent and summed in bfloat16 or wider, within the bound.
No kernel may reach another device: no remote copies, remote signals or barrier semaphores. Data moves between devices by JAX's collectives and lax.ppermute only.
A program may use at most 128 MiB of HBM per device.

```python
import math
import jax
import jax.numpy as jnp
from jax import lax

D = 1024
HEADS = 16
HEAD_DIM = 64
FF = 2048
FREQ = 256
TIME_STEPS = 1000
TOK_DEV = 176
MICRO = 2
LAYERS = 2
FRAMES = 704


def draw_utt_lengths(key, part):
    key = jax.random.fold_in(key, 11)
    first_key, last_key = jax.random.split(key)
    head_len = jax.random.randint(first_key, (MICRO,), 1, TOK_DEV // 2 + 1)
    tail_len = jax.random.randint(last_key, (MICRO,), 1, TOK_DEV // 2 + 1)
    middle_len = FRAMES - head_len - tail_len
    return jnp.stack([head_len, middle_len, tail_len], axis=1).astype(jnp.int32)


def set_ends(entries, stream_key, smallest, high):
    index_at = [jax.random.randint(jax.random.fold_in(stream_key, axis), (), 0, length) for axis, length in enumerate(entries.shape)]
    widest = entries.shape.index(max(entries.shape))
    neighbour = index_at[:widest] + [(index_at[widest] + 1) % entries.shape[widest]] + index_at[widest + 1:]
    return entries.at[tuple(index_at)].set(smallest).at[tuple(neighbour)].set(high)


def block_scale(key, shape, cuts, least, top_value):
    def one(dim, parts):
        heights = jax.random.uniform(jax.random.fold_in(jax.random.fold_in(key, 6), dim), (parts,), jnp.float32, least / len(cuts), top_value / len(cuts))
        return jnp.repeat(jnp.exp(heights), shape[dim] // parts).reshape((-1,) + (1,) * (len(shape) - dim - 1))

    factor_of = one(*cuts[0])
    for cut in cuts[1:]:
        factor_of = factor_of * one(*cut)
    return factor_of


def gaussian(rng, dims, spread, limit, shards=(), kind=jnp.bfloat16):
    entries = spread * jax.random.normal(rng, dims, jnp.float32)
    if shards:
        entries = entries * block_scale(rng, dims, shards, -0.22, 0.18)
    return jnp.clip(entries, -limit, limit).astype(kind)


def setup_inputs(seed: int = 0) -> dict:
    seeds = jax.random.split(jax.random.key(seed), 12)
    frames = gaussian(seeds[0], (MICRO, FRAMES, D), 1.0, 6.0, ((1, 4), (2, 4)))
    cotangent = gaussian(seeds[1], (MICRO, FRAMES, D), 1.0, 6.0, ((1, 4), (2, 4)))
    utt_lengths = draw_utt_lengths(jax.random.fold_in(seeds[11], 71), 0)
    time_ids = set_ends(jax.random.randint(seeds[3], (MICRO, 3), 0, TIME_STEPS), jax.random.fold_in(seeds[3], 1), 0, TIME_STEPS - 1).astype(jnp.int32)
    w_time_in = gaussian(seeds[4], (FREQ, D), FREQ ** -0.5, 0.375)
    w_time_out = gaussian(seeds[5], (D, D), D ** -0.5, 0.1875)
    w_mod = gaussian(seeds[6], (LAYERS, D, 6, D), (D // 4) ** -0.5, 0.375, ((0, 2), (3, 4)))
    w_qkv = gaussian(seeds[7], (LAYERS, D, 3, D), D ** -0.5, 0.1875, ((0, 2), (3, 4)))
    w_out = gaussian(seeds[8], (LAYERS, D, D), (max(D // 256, 1)) ** -0.5, 3.0, ((0, 2), (1, 4)))
    w_up = gaussian(seeds[9], (LAYERS, D, FF), D ** -0.5, 0.1875, ((0, 2), (2, 4)))
    w_down = gaussian(seeds[10], (LAYERS, FF, D), FF ** -0.5, 0.125, ((0, 2), (1, 4)))
    return {"frames": frames, "cotangent": cotangent, "utt_lengths": utt_lengths, "time_ids": time_ids, "w_time_in": w_time_in, "w_time_out": w_time_out, "w_mod": w_mod, "w_qkv": w_qkv, "w_out": w_out, "w_up": w_up, "w_down": w_down}


@jax.custom_vjp
def low(v):
    return lax.optimization_barrier(v.astype(jnp.bfloat16)).astype(jnp.float32)

@jax.custom_vjp
def low_back(v):
    return v

def low_keep(v):
    return (low(v), None)

def low_pass(kept, grad):
    return (grad,)

def back_keep(v):
    return (v, None)

def back_low(kept, grad):
    return (low(grad),)
low.defvjp(low_keep, low_pass)
low_back.defvjp(back_keep, back_low)

def matmul(left, right):
    return jnp.dot(left, right, precision=lax.Precision.HIGHEST)

def sinusoid(time_ids):
    half_width = FREQ // 2
    frequency = jnp.exp(jnp.arange(half_width, dtype=jnp.float32) * (-math.log(10000.0) / (half_width - 1)))
    angle_t = time_ids.astype(jnp.float32)[..., None] * frequency
    return jnp.concatenate([jnp.sin(angle_t), jnp.cos(angle_t)], axis=-1)

def frame_layout(lengths, first_row, row_count):
    index_row = first_row + jnp.arange(row_count, dtype=jnp.int32)
    end_first = lengths[0]
    end_second = lengths[0] + lengths[1]
    segment = (index_row >= end_first).astype(jnp.int32) + (index_row >= end_second).astype(jnp.int32)
    begin_row = jnp.where(segment == 0, 0, jnp.where(segment == 1, end_first, end_second))
    position = (index_row - begin_row).astype(jnp.float32)
    one_hot_mask = (segment[:, None] == jnp.arange(3, dtype=jnp.int32)[None, :]).astype(jnp.float32)
    return (segment, position, one_hot_mask)

def rotation(position):
    half_width = HEAD_DIM // 2
    rate_table = jnp.exp(jnp.arange(half_width, dtype=jnp.float32) * (-2.0 * math.log(10000.0) / HEAD_DIM))
    angle_t = position[:, None] * rate_table[None, :]
    return (jnp.cos(angle_t)[:, None, :], jnp.sin(angle_t)[:, None, :])

def rotate(values_in, cosine_table, sine_timestep, sign_factor):
    paired = values_in.reshape(values_in.shape[:-1] + (HEAD_DIM // 2, 2))
    even_part = paired[..., 0]
    odd_part = paired[..., 1]
    turned_even = even_part * cosine_table - sign_factor * odd_part * sine_timestep
    turned_odd = sign_factor * even_part * sine_timestep + odd_part * cosine_table
    return jnp.stack([turned_even, turned_odd], axis=-1).reshape(values_in.shape)

def normalize(values_in):
    row_mean = lax.optimization_barrier(jnp.mean(values_in, axis=-1, keepdims=True))
    centred = values_in - row_mean
    return centred * lax.rsqrt(lax.optimization_barrier(jnp.mean(centred * centred, axis=-1, keepdims=True)) + 1e-06)

def head_attention(queries, key_block, value_block, same_utterance_mask):
    scores = low_back(matmul(queries, key_block.T) / math.sqrt(HEAD_DIM))
    scores = jnp.where(same_utterance_mask, scores, -1e+30)
    run_peak = lax.optimization_barrier(jnp.max(scores, axis=1, keepdims=True))
    weights = jnp.exp(scores - run_peak)
    weights = weights / lax.optimization_barrier(jnp.sum(weights, axis=1, keepdims=True))
    return matmul(low(weights), value_block)

def diffusion_layer_step(residual_input, modulation_vector, one_hot_mask, cosine_table, sine_timestep, same_utterance_mask, projection_matrix, output_matrix, up_matrix, down_matrix):
    frame_count = residual_input.shape[0]
    modulators = [matmul(one_hot_mask, modulation_vector[:, which, :]) for which in range(6)]
    xa_norm = low(normalize(residual_input) * (1.0 + modulators[1]) + modulators[0])
    q_pre = low_back(matmul(xa_norm, projection_matrix[:, 0, :]))
    k_pre = low_back(matmul(xa_norm, projection_matrix[:, 1, :]))
    v_pre = low_back(matmul(xa_norm, projection_matrix[:, 2, :]))
    shape_heads = (frame_count, HEADS, HEAD_DIM)
    queries = low(rotate(q_pre.reshape(shape_heads), cosine_table, sine_timestep, 1.0))
    key_block = low(rotate(k_pre.reshape(shape_heads), cosine_table, sine_timestep, 1.0))
    value_block = low(v_pre.reshape(shape_heads))

    def per_head(triple):
        return head_attention(triple[0], triple[1], triple[2], same_utterance_mask)
    mixed_heads = lax.map(jax.checkpoint(per_head), (queries.transpose(1, 0, 2), key_block.transpose(1, 0, 2), value_block.transpose(1, 0, 2)))
    attended = low(low_back(mixed_heads.transpose(1, 0, 2).reshape(frame_count, D)))
    resid_mid = residual_input + modulators[2] * low_back(matmul(attended, output_matrix))
    xf_norm = low(normalize(resid_mid) * (1.0 + modulators[4]) + modulators[3])
    hidden = low(jax.nn.gelu(low_back(matmul(xf_norm, up_matrix)), approximate=True))
    return resid_mid + modulators[5] * low_back(matmul(hidden, down_matrix))

def time_activation(stamps, time_in, time_out):
    inner = matmul(sinusoid(stamps), time_in)
    return jax.nn.silu(matmul(jax.nn.silu(inner), time_out))

def reference(frames, cotangent, utt_lengths, time_ids, w_time_in, w_time_out, w_mod, w_qkv, w_out, w_up, w_down):
    float_weights = tuple((weight.astype(jnp.float32) for weight in (w_time_in, w_time_out, w_mod, w_qkv, w_out, w_up, w_down)))

    def one_batch(grad_sums, items):
        frame_in, tangent, lengths, stamps = items
        segment, position, one_hot_mask = frame_layout(lengths, 0, FRAMES)
        cosine_table, sine_timestep = rotation(position)
        same_utterance_mask = segment[:, None] == segment[None, :]

        def forward(initial_input, spacer, time_in, time_out, mod_weight, projection_matrix, output_matrix, up_matrix, down_matrix):
            temb_act = time_activation(stamps, time_in, time_out)
            modulation_terms = jnp.einsum('ud,ldce->luce', temb_act, mod_weight, precision=lax.Precision.HIGHEST)
            middle_activation = diffusion_layer_step(initial_input, modulation_terms[0], one_hot_mask, cosine_table, sine_timestep, same_utterance_mask, projection_matrix[0], output_matrix[0], up_matrix[0], down_matrix[0])
            relayed_state = low(low_back(middle_activation)) + spacer
            last_output = diffusion_layer_step(relayed_state, modulation_terms[1], one_hot_mask, cosine_table, sine_timestep, same_utterance_mask, projection_matrix[1], output_matrix[1], up_matrix[1], down_matrix[1])
            return (relayed_state, last_output)
        initial_input = frame_in.astype(jnp.float32)
        spacer = jnp.zeros_like(initial_input)
        (relayed_state, last_output), pull_back = jax.vjp(forward, initial_input, spacer, *float_weights)
        grad_list = pull_back((jnp.zeros_like(relayed_state), tangent.astype(jnp.float32)))
        grad_sums = tuple((total_now + part for total_now, part in zip(grad_sums, grad_list[2:])))
        return (grad_sums, (relayed_state.astype(jnp.bfloat16), last_output.astype(jnp.bfloat16), grad_list[0], grad_list[1]))
    zero_sums = tuple((jnp.zeros_like(weight) for weight in float_weights))
    grad_sums, (passed_all, final_all, first_grad, middle_grad) = lax.scan(one_batch, zero_sums, (frames, cotangent, utt_lengths, time_ids))
    acts = jnp.stack([passed_all, final_all])
    grads = jnp.stack([first_grad, middle_grad])
    return (acts, grads, grad_sums[0], grad_sums[1], grad_sums[2], grad_sums[3], grad_sums[4], grad_sums[5], grad_sums[6])
```

```python
import functools
import math

import jax
import jax.numpy as jnp
import numpy as np
from jax import lax
from jax.experimental import pallas as pl
from jax.experimental.pallas import tpu as pltpu
from jax.sharding import PartitionSpec as P

HEAD_DIM = 64
FREQ = 256
EPS = 1e-06
BF = jnp.bfloat16
F32 = jnp.float32
MIB = 1024 * 1024


def shifted(value, axis, by):
    length = lax.axis_size(axis)
    if by % length == 0:
        return value
    return lax.ppermute(value, axis, [(i, (i + by) % length) for i in range(length)])


def gather(value, axis):
    return [shifted(value, axis, k) for k in range(lax.axis_size(axis))]


def exchange(chunks, axis):
    return [shifted(chunk, axis, k) for k, chunk in enumerate(chunks)]


def pair_shift(value, axis, by):
    length = lax.axis_size(axis)
    pairs = [
        (c * length + i, (1 - c) * length + (i + by) % length)
        for c in range(2)
        for i in range(length)
    ]
    return lax.ppermute(value, ("section", axis), pairs)


def pair_gather(value, axis):
    return [pair_shift(value, axis, k) for k in range(lax.axis_size(axis))]


def swap(value):
    return lax.ppermute(value, "section", [(0, 1), (1, 0)])


def owner_shift(value, layer, by):
    length = lax.axis_size("seq")
    if by % length == 0:
        return value
    base = layer * length
    pairs = [(base + i, base + (i + by) % length) for i in range(length)]
    return lax.ppermute(value, ("section", "seq"), pairs)


def add_chunks(chunks):
    total = chunks[0].astype(F32)
    for chunk in chunks[1:]:
        total = total + chunk.astype(F32)
    return total.astype(BF)


def dot(left, right, contract=((1,), (0,))):
    return lax.dot_general(left, right, (contract, ((), ())), preferred_element_type=F32)


def split3(value):
    high = value.astype(BF)
    rest = value - high.astype(F32)
    middle = rest.astype(BF)
    low = (rest - middle.astype(F32)).astype(BF)
    return high, middle, low


def exact_dot(left, right, contract=((1,), (0,))):
    rows = left.shape[0]
    stacked = jnp.concatenate(split3(left), axis=0)
    out = dot(stacked, right, contract)
    return out[:rows] + (out[rows : 2 * rows] + out[2 * rows :])


def exact_outer(left, right):
    a = split3(left)
    b = split3(right)
    order = ((0, 0), (0, 1), (1, 0), (1, 1), (0, 2), (2, 0))
    tall = jnp.concatenate([a[i] for i, _ in order], axis=0)
    wide = jnp.concatenate([b[j] for _, j in order], axis=0)
    return dot(tall, wide, ((0,), (0,)))


def segments(sc, shape, axis, first):
    index = lax.broadcasted_iota(jnp.int32, shape, axis) + first
    return (index >= sc[3]).astype(jnp.int32) + (index >= sc[4]).astype(jnp.int32)


def spread(mod, sc, layer, which, seg):
    base = sc[2] * 4
    rows = [mod[layer, which, pl.ds(base + u, 1), :] for u in range(3)]
    return jnp.where(seg == 0, rows[0], jnp.where(seg == 1, rows[1], rows[2]))


def spread_narrow(mod, sc, layer, which, seg, columns):
    block = mod[layer, which, :, columns]
    index = lax.broadcasted_iota(jnp.int32, block.shape, 0) - sc[2] * 4
    rows = [
        jnp.sum(jnp.where(index == u, block, 0.0), axis=0, keepdims=True) for u in range(3)
    ]
    return jnp.where(seg == 0, rows[0], jnp.where(seg == 1, rows[1], rows[2]))


def utterance_sums(value, seg):
    rows = [
        jnp.sum(jnp.where(seg == u, value, 0.0), axis=0, keepdims=True) for u in range(3)
    ]
    return jnp.concatenate(rows + [jnp.zeros_like(rows[0])], axis=0)


def norm_of(value):
    mean = jnp.mean(value, axis=1, keepdims=True)
    centred = value - mean
    inv = lax.rsqrt(jnp.mean(centred * centred, axis=1, keepdims=True) + EPS)
    return centred * inv, inv


def norm_pull(grad, normed, inv):
    return inv * (
        grad
        - jnp.mean(grad, axis=1, keepdims=True)
        - normed * jnp.mean(grad * normed, axis=1, keepdims=True)
    )


def lanes_of(index, count, width):
    return pl.ds(pl.multiple_of(lax.rem(index, count) * width, width), width)


def place(buffer, chunks, own, width):
    count = len(chunks)
    for k, chunk in enumerate(chunks):
        buffer[:, lanes_of(own - k + count, count, width)] = chunk[...].astype(buffer.dtype)


def hand_out(outs, buffer, own, width):
    count = len(outs)
    for k, out in enumerate(outs):
        out[...] = buffer[:, lanes_of(own + k, count, width)].astype(out.dtype)


class Fetch:
    def __init__(self, sc, layer, own, other, buffer, sem):
        self.copy = pltpu.make_async_copy(own, buffer, sem)
        other_copy = pltpu.make_async_copy(other, buffer, sem)

        @pl.when(sc[2] == layer)
        def _():
            self.copy.start()

        @pl.when(sc[2] != layer)
        def _():
            other_copy.start()

    def wait(self):
        self.copy.wait()


def turn(value, cosine, sine):
    width = value.shape[1]
    even = lax.broadcasted_iota(jnp.int32, value.shape, 1) % 2 == 0
    swapped = jnp.where(even, pltpu.roll(value, width - 1, 1), pltpu.roll(value, 1, 1))
    return value * cosine + swapped * sine


def widen_table(table, width):
    copies = width // table.shape[1]
    return jnp.concatenate([table] * copies, axis=1) if copies > 1 else table[:, :width]


VM = pl.BlockSpec(memory_space=pltpu.VMEM)
SM = pl.BlockSpec(memory_space=pltpu.SMEM)
HB = pl.BlockSpec(memory_space=pl.ANY)


def sds(shape, dtype):
    return jax.ShapeDtypeStruct(tuple(shape), dtype)


def call(body, ins, specs, outs, scratch=(), flops=0, limit=24, name=None):
    moved = sum(math.prod(a.shape) * a.dtype.itemsize for a in list(ins) + list(outs))
    return pl.pallas_call(
        body,
        out_shape=list(outs),
        in_specs=list(specs),
        out_specs=[VM] * len(outs),
        scratch_shapes=list(scratch),
        compiler_params=pltpu.CompilerParams(vmem_limit_bytes=limit * MIB),
        cost_estimate=pl.CostEstimate(
            flops=int(flops), bytes_accessed=int(moved), transcendentals=0
        ),
        name=name,
    )(*ins)


def cut(refs, *counts):
    out = []
    at = 0
    for n in counts:
        if n == 1:
            out.append(refs[at])
        else:
            out.append(refs[at : at + n])
        at += n
    assert at == len(refs)
    return out


class Group(list):
    pass


def time_forward(sinus, time_in, time_out, mod_weight):
    rows, width = sinus.shape[0], time_in.shape[1]
    kinds, _, narrow = mod_weight.shape

    def body(sinus, time_in, time_out, mod_weight, inner_out, outer_out, act_out, modul):
        inner = exact_dot(sinus[...], time_in[...])
        inner_out[...] = inner
        hidden = inner / (1.0 + jnp.exp(-inner))
        outer = exact_dot(hidden, time_out[...])
        outer_out[...] = outer
        act = outer / (1.0 + jnp.exp(-outer))
        act_out[...] = act
        for which in range(kinds):
            modul[which] = exact_dot(act, mod_weight[which])

    return call(
        body,
        [sinus, time_in, time_out, mod_weight],
        [VM] * 4,
        [sds((rows, width), F32)] * 3 + [sds((kinds, rows, narrow), F32)],
        flops=2 * 256 * 4_000_000,
        name="time_forward",
    )


def collect_modulation(sc, own, other):
    count = len(own)
    kinds, rows, narrow = own[0].shape

    def body(sc, *refs):
        own, other, out = refs[:count], refs[count : 2 * count], refs[2 * count]
        for k in range(count):
            columns = lanes_of(sc[0] - k + count, count, narrow)
            for layer in range(2):
                out[layer, :, :, columns] = jnp.where(
                    sc[2] == layer, own[k][...], other[k][...]
                )

    return call(
        body,
        [sc] + own + other,
        [SM] + [VM] * (2 * count),
        [sds((2, kinds, rows, narrow * count), F32)],
        name="collect_modulation",
    )[0]


def project(dims, layer, sc, pieces, mod, w_own, w_other, cosine, sine):
    first = layer == 0
    rows, width, narrow, local = dims.rows, dims.width, dims.narrow, dims.local
    count, n_seq, n_out = dims.n_heads, dims.n_seq, dims.n_chunks
    n_in = len(pieces)

    def body(sc, *refs):
        pieces = refs[:n_in]
        mod, w_own, w_other, cosine, sine = refs[n_in : n_in + 5]
        outs = refs[n_in + 5 :]
        x_out, narrow_out, xa_out = outs[:3]
        chunks = outs[3 : 3 + n_out]
        buffer, weight, ready, sem = outs[3 + n_out :]
        fetch = Fetch(sc, layer, w_own, w_other, weight, sem)
        own_row = sc[1] * rows
        seg = segments(sc, (rows, 1), 0, own_row)
        if first:
            place(buffer, pieces, sc[0], narrow)
            x = buffer[...]
            x_out[...] = x.astype(BF)
            narrow_out[...] = pieces[0][...]
        else:
            place(buffer, pieces[1:], sc[0], narrow)
            x = pieces[0][...] + spread(mod, sc, 0, 5, seg) * buffer[...]
            low = x.astype(BF)
            x_out[...] = low
            x = low.astype(F32)
            buffer[...] = x
            narrow_out[...] = buffer[:, lanes_of(sc[0], count, narrow)].astype(BF)
        normed, _ = norm_of(x)
        xa = (normed * (1.0 + spread(mod, sc, layer, 1, seg)) + spread(mod, sc, layer, 0, seg)).astype(BF)
        xa_out[...] = xa
        here = pl.ds(pl.multiple_of(own_row, 8), rows)
        cos = widen_table(cosine[here, :], local)
        sin = widen_table(sine[here, :], local)
        fetch.wait()
        q = turn(dot(xa, weight[0]), cos, sin).astype(BF)
        k = turn(dot(xa, weight[1]), cos, sin).astype(BF)
        v = dot(xa, weight[2]).astype(BF)
        if dims.spread_heads:
            wide = local // n_seq
            for j in range(n_seq):
                part = slice(j * wide, (j + 1) * wide)
                ready[j] = jnp.concatenate([q[:, part], k[:, part], v[:, part]], axis=1)
            for j in range(n_seq):
                chunks[j][...] = ready[lax.rem(sc[1] + j, n_seq)]
        else:
            chunks[0][...] = q
            chunks[1][...] = jnp.concatenate([k, v], axis=1)

    if dims.spread_heads:
        outs = [sds((rows, 3 * local // n_seq), BF)] * n_seq
        ready = pltpu.VMEM((n_seq, rows, 3 * local // n_seq), BF)
    else:
        outs = [sds((rows, local), BF), sds((rows, 2 * local), BF)]
        ready = pltpu.VMEM((8, 128), BF)
    return call(
        body,
        [sc] + pieces + [mod, w_own, w_other, cosine, sine],
        [SM] + [VM] * n_in + [VM, HB, HB, VM, VM],
        [sds((rows, width), BF), sds((rows, narrow), BF), sds((rows, width), BF)] + outs,
        [
            pltpu.VMEM((rows, width), F32),
            pltpu.VMEM(w_own.shape, BF),
            ready,
            pltpu.SemaphoreType.DMA,
        ],
        flops=6 * rows * width * local,
        name=f"project_{layer}",
    )


def attend(dims, sc, chunks, queries):
    rows, n_seq, frames = dims.rows, dims.n_seq, dims.frames
    heads = dims.heads_here
    wide = heads * HEAD_DIM
    shared = dims.spread_heads
    blocks = n_seq if shared else 1
    n_chunks = len(chunks)
    parts = 3 if shared else 2

    def body(sc, *refs):
        chunks = refs[:n_chunks]
        rest = refs[n_chunks:]
        if not shared:
            queries, rest = rest[0], rest[1:]
        kept, probs = rest[:2]
        outs = rest[2 : 2 + blocks]
        (mixed,) = rest[2 + blocks :]
        for k in range(n_chunks):
            at = pl.multiple_of(lax.rem(sc[1] - k + n_seq, n_seq) * rows, rows)
            kept[pl.ds(at, rows), :] = chunks[k][...]
        key_seg = segments(sc, (1, frames), 1, 0)
        for block in range(blocks):
            if shared:
                here = slice(block * rows, (block + 1) * rows)
                seg = segments(sc, (rows, 1), 0, block * rows)
            else:
                here = slice(0, rows)
                seg = segments(sc, (rows, 1), 0, sc[1] * rows)
            same = seg == key_seg
            for head in range(heads):
                cols = slice(head * HEAD_DIM, (head + 1) * HEAD_DIM)
                base = (parts - 2) * wide
                key = kept[:, base + head * HEAD_DIM : base + (head + 1) * HEAD_DIM]
                base = (parts - 1) * wide
                val = kept[:, base + head * HEAD_DIM : base + (head + 1) * HEAD_DIM]
                q = kept[here, cols] if shared else queries[:, cols]
                scores = dot(q, key, ((1,), (1,))) * (1.0 / math.sqrt(HEAD_DIM))
                scores = jnp.where(same, scores, -1e30)
                weight = jnp.exp(scores - jnp.max(scores, axis=1, keepdims=True))
                weight = weight * (1.0 / jnp.sum(weight, axis=1, keepdims=True))
                low = weight.astype(BF)
                probs[head, here, :] = low
                mixed[block, :, cols] = dot(low, val).astype(BF)
        if shared:
            for k in range(n_seq):
                outs[k][...] = mixed[lax.rem(sc[1] + k, n_seq)]
        else:
            outs[0][...] = mixed[0]

    q_rows = blocks * rows
    ins = [sc] + chunks + ([] if shared else [queries])
    return call(
        body,
        ins,
        [SM] + [VM] * (len(ins) - 1),
        [sds((frames, parts * wide), BF), sds((heads, q_rows, frames), BF)]
        + [sds((rows, wide), BF)] * blocks,
        [pltpu.VMEM((blocks, rows, wide), BF)],
        flops=4 * heads * q_rows * frames * HEAD_DIM,
        name="attend",
    )


def put_heads(dims, sc, chunks, ready):
    n_seq = dims.n_seq
    if not dims.spread_heads:
        return chunks[0][...]
    for k in range(n_seq):
        ready[lax.rem(sc[1] - k + n_seq, n_seq)] = chunks[k][...]
    return jnp.concatenate([ready[j] for j in range(n_seq)], axis=1)


def project_out(dims, layer, sc, chunks, w_own, w_other):
    rows, width, narrow, local, count = (
        dims.rows, dims.width, dims.narrow, dims.local, dims.n_heads,
    )
    n_in = len(chunks)

    def body(sc, *refs):
        chunks = refs[:n_in]
        w_own, w_other, att_out = refs[n_in : n_in + 3]
        outs = refs[n_in + 3 : n_in + 3 + count]
        weight, ready, buffer, sem = refs[n_in + 3 + count :]
        fetch = Fetch(sc, layer, w_own, w_other, weight, sem)
        att = put_heads(dims, sc, chunks, ready)
        att_out[...] = att
        fetch.wait()
        buffer[...] = dot(att, weight[...]).astype(BF)
        hand_out(outs, buffer, sc[0], narrow)

    return call(
        body,
        [sc] + chunks + [w_own, w_other],
        [SM] + [VM] * n_in + [HB, HB],
        [sds((rows, local), BF)] + [sds((rows, narrow), BF)] * count,
        [
            pltpu.VMEM(w_own.shape, BF),
            pltpu.VMEM((n_in,) + chunks[0].shape, BF),
            pltpu.VMEM((rows, width), BF),
            pltpu.SemaphoreType.DMA,
        ],
        flops=2 * rows * width * local,
        name=f"project_out_{layer}",
    )


def feed_forward(dims, layer, sc, x, branch, mod, up, down):
    rows, width, narrow, count, hidden = (
        dims.rows, dims.width, dims.narrow, dims.n_heads, dims.hidden,
    )

    def body(sc, x, *refs):
        branch = refs[:count]
        mod, up_own, up_other, down_own, down_other = refs[count : count + 5]
        x1_out, xf_out, h_out, slope_out = refs[count + 5 : count + 9]
        outs = refs[count + 9 : 2 * count + 9]
        up, down, buffer, low, sem_up, sem_down = refs[2 * count + 9 :]
        fetch_up = Fetch(sc, layer, up_own, up_other, up, sem_up)
        fetch_down = Fetch(sc, layer, down_own, down_other, down, sem_down)
        seg = segments(sc, (rows, 1), 0, sc[1] * rows)
        place(buffer, branch, sc[0], narrow)
        x1 = x[...].astype(F32) + spread(mod, sc, layer, 2, seg) * buffer[...]
        x1_out[...] = x1
        normed, _ = norm_of(x1)
        xf = (normed * (1.0 + spread(mod, sc, layer, 4, seg)) + spread(mod, sc, layer, 3, seg)).astype(BF)
        xf_out[...] = xf
        fetch_up.wait()
        a = dot(xf, up[...])
        c0 = math.sqrt(2.0 / math.pi)
        square = a * a
        t = jnp.tanh(c0 * (a + 0.044715 * (a * square)))
        h = (0.5 * a * (1.0 + t)).astype(BF)
        h_out[...] = h
        slope_out[...] = 0.5 * (1.0 + t) + 0.5 * a * (1.0 - t * t) * (
            c0 * (1.0 + 3.0 * 0.044715 * square)
        )
        fetch_down.wait()
        low[...] = dot(h, down[...]).astype(BF)
        hand_out(outs, low, sc[0], narrow)

    return call(
        body,
        [sc, x] + branch + [mod, up[0], up[1], down[0], down[1]],
        [SM, VM] + [VM] * count + [VM, HB, HB, HB, HB],
        [
            sds((rows, width), F32),
            sds((rows, width), BF),
            sds((rows, hidden), BF),
            sds((rows, hidden), F32),
        ]
        + [sds((rows, narrow), BF)] * count,
        [
            pltpu.VMEM(up[0].shape, BF),
            pltpu.VMEM(down[0].shape, BF),
            pltpu.VMEM((rows, width), F32),
            pltpu.VMEM((rows, width), BF),
            pltpu.SemaphoreType.DMA,
            pltpu.SemaphoreType.DMA,
        ],
        flops=4 * rows * width * hidden,
        name=f"feed_forward_{layer}",
    )


def feed_backward(dims, layer, sc, pieces, slope, mod, up, down):
    rows, width, narrow, count, hidden = (
        dims.rows, dims.width, dims.narrow, dims.n_heads, dims.hidden,
    )
    last = layer == 1
    n_in = len(pieces)
    n_extra = 0 if last else 2

    def body(sc, *refs):
        pieces = refs[:n_in]
        slope, mod, up_own, up_other, down_own, down_other = refs[n_in : n_in + 6]
        rest = refs[n_in + 6 :]
        g_out, dz_out, da_out = rest[:3]
        outs = rest[3 : 3 + count]
        extra = rest[3 + count : 3 + count + n_extra]
        up, down, buffer, low, other_buffer, sem_up, sem_down = rest[3 + count + n_extra :]
        fetch_down = Fetch(sc, layer, down_own, down_other, down, sem_down)
        fetch_up = Fetch(sc, layer, up_own, up_other, up, sem_up)
        seg = segments(sc, (rows, 1), 0, sc[1] * rows)
        place(buffer, pieces[:count], sc[0], narrow)
        if last:
            g = buffer[...]
            g_out[...] = g.astype(BF)
        else:
            x, d_mid = pieces[count:]
            grad_out, sums_out = extra
            dxa = buffer[...]
            normed, inv = norm_of(x[...].astype(F32))
            other_buffer[...] = dxa * normed
            mine = lanes_of(sc[0], count, narrow)
            sums_out[0] = utterance_sums(buffer[:, mine], seg)
            sums_out[1] = utterance_sums(other_buffer[:, mine], seg)
            dx = d_mid[...] + norm_pull(
                dxa * (1.0 + spread(mod, sc, 1, 1, seg)), normed, inv
            )
            other_buffer[...] = dx
            grad_out[...] = other_buffer[:, mine]
            g = dx.astype(BF)
            g_out[...] = g
            g = g.astype(F32)
        dz = (g * spread(mod, sc, layer, 5, seg)).astype(BF)
        dz_out[...] = dz
        fetch_down.wait()
        da = (dot(dz, down[...], ((1,), (1,))) * slope[...]).astype(BF)
        da_out[...] = da
        fetch_up.wait()
        low[...] = dot(da, up[...], ((1,), (1,))).astype(BF)
        hand_out(outs, low, sc[0], narrow)

    extra = [] if last else [sds((rows, narrow), F32), sds((2, 4, narrow), F32)]
    return call(
        body,
        [sc] + pieces + [slope, mod, up[0], up[1], down[0], down[1]],
        [SM] + [VM] * n_in + [VM, VM, HB, HB, HB, HB],
        [sds((rows, width), BF), sds((rows, width), BF), sds((rows, hidden), BF)]
        + [sds((rows, narrow), BF)] * count
        + extra,
        [
            pltpu.VMEM(up[0].shape, BF),
            pltpu.VMEM(down[0].shape, BF),
            pltpu.VMEM((rows, width), F32),
            pltpu.VMEM((rows, width), BF),
            pltpu.VMEM((rows, width), F32),
            pltpu.SemaphoreType.DMA,
            pltpu.SemaphoreType.DMA,
        ],
        flops=4 * rows * width * hidden,
        name=f"feed_backward_{layer}",
    )


def middle_backward(dims, layer, sc, g, x1, sums, branch, mod, w_own, w_other):
    rows, width, narrow, local, count = (
        dims.rows, dims.width, dims.narrow, dims.local, dims.n_heads,
    )
    n_seq = dims.n_seq
    n_out = n_seq if dims.spread_heads else 1

    def body(sc, g, x1, *refs):
        sums = refs[:count]
        branch, mod, w_own, w_other = refs[count : count + 4]
        d_mid_out, dy_out, small = refs[count + 4 : count + 7]
        outs = refs[count + 7 : count + 7 + n_out]
        weight, buffer, other, ready, sem = refs[count + 7 + n_out :]
        fetch = Fetch(sc, layer, w_own, w_other, weight, sem)
        seg = segments(sc, (rows, 1), 0, sc[1] * rows)
        mine = lanes_of(sc[0], count, narrow)
        place(buffer, sums, sc[0], narrow)
        dxf = buffer[...]
        normed, inv = norm_of(x1[...])
        other[...] = dxf * normed
        small[1] = utterance_sums(buffer[:, mine], seg)
        small[2] = utterance_sums(other[:, mine], seg)
        d_mid = g[...].astype(F32) + norm_pull(
            dxf * (1.0 + spread(mod, sc, layer, 4, seg)), normed, inv
        )
        d_mid_out[...] = d_mid
        other[...] = d_mid
        small[0] = utterance_sums(other[:, mine] * branch[...].astype(F32), seg)
        dy = (d_mid * spread(mod, sc, layer, 2, seg)).astype(BF)
        dy_out[...] = dy
        fetch.wait()
        datt = dot(dy, weight[...], ((1,), (1,))).astype(BF)
        if dims.spread_heads:
            wide = local // n_seq
            for j in range(n_seq):
                ready[j] = datt[:, j * wide : (j + 1) * wide]
            for k in range(n_seq):
                outs[k][...] = ready[lax.rem(sc[1] + k, n_seq)]
        else:
            outs[0][...] = datt

    wide = local // n_out
    return call(
        body,
        [sc, g, x1] + sums + [branch, mod, w_own, w_other],
        [SM, VM, VM] + [VM] * count + [VM, VM, HB, HB],
        [sds((rows, width), F32), sds((rows, width), BF), sds((3, 4, narrow), F32)]
        + [sds((rows, wide), BF)] * n_out,
        [
            pltpu.VMEM(w_own.shape, BF),
            pltpu.VMEM((rows, width), F32),
            pltpu.VMEM((rows, width), F32),
            pltpu.VMEM((n_out, rows, wide), BF),
            pltpu.SemaphoreType.DMA,
        ],
        flops=2 * rows * width * local,
        name=f"middle_backward_{layer}",
    )


def attend_backward(dims, sc, chunks, queries, kept, probs, cosine, sine):
    rows, n_seq, frames = dims.rows, dims.n_seq, dims.frames
    heads = dims.heads_here
    wide = heads * HEAD_DIM
    shared = dims.spread_heads
    n_in = len(chunks)
    q_rows = frames if shared else rows
    parts = 3 if shared else 2
    scale = 1.0 / math.sqrt(HEAD_DIM)

    def body(sc, *refs):
        chunks = refs[:n_in]
        rest = refs[n_in:]
        if not shared:
            queries, rest = rest[0], rest[1:]
        kept, probs, cosine, sine = rest[:4]
        rest = rest[4:]
        if not shared:
            q_out, rest = rest[0], rest[1:]
        outs = rest[:n_seq]
        grad, done, d_score = rest[n_seq:]
        if shared:
            for k in range(n_in):
                at = pl.multiple_of(lax.rem(sc[1] - k + n_seq, n_seq) * rows, rows)
                grad[pl.ds(at, rows), :] = chunks[k][...]
            cos = cosine[:, :HEAD_DIM]
            sin = -sine[:, :HEAD_DIM]
            cos_q, sin_q = cos, sin
        else:
            grad[...] = chunks[0][...]
            cos = cosine[:, :HEAD_DIM]
            sin = -sine[:, :HEAD_DIM]
            here = pl.ds(pl.multiple_of(sc[1] * rows, 8), rows)
            cos_q = cosine[here, :HEAD_DIM]
            sin_q = -sine[here, :HEAD_DIM]
        for head in range(heads):
            cols = slice(head * HEAD_DIM, (head + 1) * HEAD_DIM)
            base = (parts - 2) * wide + head * HEAD_DIM
            key = kept[:, base : base + HEAD_DIM]
            base = (parts - 1) * wide + head * HEAD_DIM
            val = kept[:, base : base + HEAD_DIM]
            q = kept[:, cols] if shared else queries[:, cols]
            for at in range(0, q_rows, rows):
                here = slice(at, at + rows)
                prob = probs[head, here, :].astype(F32)
                d_prob = dot(grad[here, cols], val, ((1,), (1,)))
                delta = jnp.sum(d_prob * prob, axis=1, keepdims=True)
                d_score[here, :] = (prob * (d_prob - delta)).astype(BF)
            dq = dot(d_score[...], key) * scale
            dk = dot(d_score[...], q, ((0,), (0,))) * scale
            dv = dot(probs[head], grad[:, cols], ((0,), (0,)))
            dq = turn(dq, cos_q, sin_q).astype(BF)
            dk = turn(dk, cos, sin).astype(BF)
            base = 0
            if shared:
                done[:, cols] = dq
                base = wide
            else:
                q_out[:, cols] = dq
            done[:, base + head * HEAD_DIM : base + (head + 1) * HEAD_DIM] = dk
            base += wide
            done[:, base + head * HEAD_DIM : base + (head + 1) * HEAD_DIM] = dv.astype(BF)
        for k in range(n_seq):
            at = pl.multiple_of(lax.rem(sc[1] + k, n_seq) * rows, rows)
            outs[k][...] = done[pl.ds(at, rows), :]

    ins = [sc] + chunks + ([] if shared else [queries]) + [kept, probs, cosine, sine]
    outs = [sds((rows, parts * wide), BF)] * n_seq
    if not shared:
        outs = [sds((rows, wide), BF)] + outs
    return call(
        body,
        ins,
        [SM] + [VM] * (len(ins) - 1),
        outs,
        [
            pltpu.VMEM((q_rows, wide), BF),
            pltpu.VMEM((frames, parts * wide), BF),
            pltpu.VMEM((q_rows, frames), BF),
        ],
        flops=8 * heads * q_rows * frames * HEAD_DIM,
        name="attend_backward",
    )


def project_backward(dims, layer, sc, chunks, w_own, w_other):
    rows, width, narrow, local, count = (
        dims.rows, dims.width, dims.narrow, dims.local, dims.n_heads,
    )
    n_seq = dims.n_seq
    n_in = len(chunks)

    def body(sc, *refs):
        chunks = refs[:n_in]
        w_own, w_other, d_out = refs[n_in : n_in + 3]
        outs = refs[n_in + 3 : n_in + 3 + count]
        weight, ready, buffer, sem = refs[n_in + 3 + count :]
        fetch = Fetch(sc, layer, w_own, w_other, weight, sem)
        if dims.spread_heads:
            wide = local // n_seq
            for k in range(n_seq):
                ready[lax.rem(sc[1] - k + n_seq, n_seq)] = chunks[k][...]
            grads = [
                jnp.concatenate(
                    [ready[j][:, p * wide : (p + 1) * wide] for j in range(n_seq)], axis=1
                )
                for p in range(3)
            ]
        else:
            total = chunks[1][...].astype(F32)
            for k in range(2, n_in):
                total = total + chunks[k][...].astype(F32)
            total = total.astype(BF)
            grads = [chunks[0][...], total[:, :local], total[:, local:]]
        for p in range(3):
            d_out[p] = grads[p]
        fetch.wait()
        total = dot(grads[0], weight[0], ((1,), (1,)))
        total = total + dot(grads[1], weight[1], ((1,), (1,)))
        total = total + dot(grads[2], weight[2], ((1,), (1,)))
        buffer[...] = total.astype(BF)
        hand_out(outs, buffer, sc[0], narrow)

    ready = (n_seq, rows, 3 * local // n_seq) if dims.spread_heads else (1, 8, 128)
    return call(
        body,
        [sc] + chunks + [w_own, w_other],
        [SM] + [VM] * n_in + [HB, HB],
        [sds((3, rows, local), BF)] + [sds((rows, narrow), BF)] * count,
        [
            pltpu.VMEM(w_own.shape, BF),
            pltpu.VMEM(ready, BF),
            pltpu.VMEM((rows, width), BF),
            pltpu.SemaphoreType.DMA,
        ],
        flops=6 * rows * width * local,
        name=f"project_backward_{layer}",
    )


def weight_grads(pairs, name):
    n = len(pairs)
    ins = [a for pair in pairs for a in pair]
    outs = []
    flops = 0
    for left, right in pairs:
        if right.ndim == 3:
            outs.append(sds((right.shape[0], left.shape[1], right.shape[2]), BF))
        else:
            outs.append(sds((left.shape[1], right.shape[1]), BF))
        flops += 2 * left.shape[0] * math.prod(outs[-1].shape)

    def body(*refs):
        for i in range(n):
            left, right, out = refs[2 * i], refs[2 * i + 1], refs[2 * n + i]
            if len(right.shape) == 3:
                for p in range(right.shape[0]):
                    out[p] = dot(left[...], right[p], ((0,), (0,))).astype(BF)
            else:
                out[...] = dot(left[...], right[...], ((0,), (0,))).astype(BF)

    return call(body, ins, [VM] * (2 * n), outs, flops=flops, name=name)


def split_sum(sc, tensors, others, n_seq):
    n = len(tensors)

    def rows_of(tensor):
        return tensor.shape[-2] // n_seq

    outs = []
    for tensor in tensors:
        shape = list(tensor.shape)
        shape[-2] = rows_of(tensor)
        outs += [sds(shape, BF)] * n_seq

    def body(sc, *refs):
        tensors, others, outs = refs[:n], refs[n : 2 * n], refs[2 * n :]
        for i in range(n):
            share = tensors[i].shape[-2] // n_seq
            for k in range(n_seq):
                at = pl.ds(pl.multiple_of(lax.rem(sc[1] + k, n_seq) * share, share), share)
                if len(tensors[i].shape) == 3:
                    total = tensors[i][:, at, :].astype(F32) + others[i][:, at, :].astype(F32)
                else:
                    total = tensors[i][at, :].astype(F32) + others[i][at, :].astype(F32)
                outs[i * n_seq + k][...] = total.astype(BF)

    flat = call(body, [sc] + tensors + others, [SM] + [VM] * (2 * n), outs, name="split_sum")
    return [flat[i * n_seq : (i + 1) * n_seq] for i in range(n)]


def assemble(sc, shares, shapes, n_seq):
    n = len(shapes)
    flat = [share for layer in shares for tensor in layer for share in tensor]

    def body(sc, *refs):
        outs = refs[2 * n * n_seq :]
        for layer in range(2):

            @pl.when(sc[2] == layer)
            def _(layer=layer):
                for i in range(n):
                    for k in range(n_seq):
                        share = refs[(layer * n + i) * n_seq + k]
                        size = share.shape[-2]
                        at = pl.ds(
                            pl.multiple_of(lax.rem(sc[1] - k + n_seq, n_seq) * size, size), size
                        )
                        if len(share.shape) == 3:
                            outs[i][:, at, :] = share[...].astype(F32)
                        else:
                            outs[i][at, :] = share[...].astype(F32)

    return call(
        body,
        [sc] + flat,
        [SM] + [VM] * len(flat),
        [sds(shape, F32) for shape in shapes],
        limit=40,
        name="assemble",
    )


def gate_sums(dims, layer, sc, g, x1, z, mod):
    rows, narrow, count = dims.rows, dims.narrow, dims.n_heads

    def body(sc, g, x1, z, mod, small, *shown):
        seg = segments(sc, (rows, 1), 0, sc[1] * rows)
        mine = lanes_of(sc[0], count, narrow)
        value = z[...].astype(F32)
        small[...] = utterance_sums(g[:, mine].astype(F32) * value, seg)
        if shown:
            gate = spread_narrow(mod, sc, layer, 5, seg, mine)
            shown[0][...] = (x1[:, mine] + gate * value).astype(BF)

    outs = [sds((4, narrow), F32)]
    if layer == 1:
        outs.append(sds((rows, narrow), BF))
    return call(body, [sc, g, x1, z, mod], [SM] + [VM] * 4, outs, name=f"gate_sums_{layer}")


def last_norm(dims, sc, terms, x, mod):
    rows, narrow, count = dims.rows, dims.narrow, dims.n_heads

    def body(sc, *refs):
        terms = refs[:count]
        x, mod, total_out, normed_out, inv_out, small, rows_out, buffer = refs[count:]
        seg = segments(sc, (rows, 1), 0, sc[1] * rows)
        mine = lanes_of(sc[0], count, narrow)
        total = terms[0][...].astype(F32)
        for term in terms[1:]:
            total = total + term[...].astype(F32)
        normed, inv = norm_of(x[...].astype(F32))
        buffer[...] = normed
        normed = buffer[:, mine]
        small[0] = utterance_sums(total, seg)
        small[1] = utterance_sums(total * normed, seg)
        scale = spread_narrow(mod, sc, 0, 1, seg, mine)
        grad = total * (1.0 + scale)
        total_out[...] = grad
        normed_out[...] = normed
        inv_out[...] = inv
        rows_out[...] = jnp.concatenate(
            [jnp.sum(grad, axis=1, keepdims=True), jnp.sum(grad * normed, axis=1, keepdims=True)],
            axis=1,
        )

    return call(
        body,
        [sc] + terms + [x, mod],
        [SM] + [VM] * (count + 2),
        [
            sds((rows, narrow), F32),
            sds((rows, narrow), F32),
            sds((rows, 1), F32),
            sds((2, 4, narrow), F32),
            sds((rows, 2), F32),
        ],
        [pltpu.VMEM((rows, dims.width), F32)],
        name="last_norm",
    )


def last_pull(dims, sc, d_mid, grad, normed, inv, sums):
    rows, narrow, count, width = dims.rows, dims.narrow, dims.n_heads, dims.width

    def body(sc, d_mid, grad, normed, inv, *refs):
        sums, out = refs[:count], refs[count]
        total = sums[0][...]
        for term in sums[1:]:
            total = total + term[...]
        total = total * (1.0 / width)
        mine = lanes_of(sc[0], count, narrow)
        out[...] = d_mid[:, mine] + inv[...] * (
            grad[...] - total[:, 0:1] - normed[...] * total[:, 1:2]
        )

    return call(
        body,
        [sc, d_mid, grad, normed, inv] + sums,
        [SM] + [VM] * (4 + count),
        [sds((rows, narrow), F32)],
        name="last_pull",
    )[0]


def modulation_grads(sc, act, mod_weight, own, other, n_seq):
    kinds, width, narrow = mod_weight.shape

    def body(sc, act, mod_weight, *refs):
        own, other = refs[:n_seq], refs[n_seq : 2 * n_seq]
        g_mod, part, box = refs[2 * n_seq :]
        for k in range(n_seq):
            at = lax.rem(sc[1] - k + n_seq, n_seq)
            box[at, sc[2]] = own[k][...]
            box[at, 1 - sc[2]] = other[k][...]
        total = box[0]
        for j in range(1, n_seq):
            total = total + box[j]
        act_now = act[...]
        result = jnp.zeros((8, width), F32)
        for which in range(kinds):
            rows = jnp.concatenate([total[0, which], total[1, which]], axis=0)
            g_mod[which] = exact_outer(act_now, rows)
            result = result + exact_dot(rows, mod_weight[which], ((1,), (1,)))
        part[...] = result

    return call(
        body,
        [sc, act, mod_weight] + own + other,
        [SM] + [VM] * (2 + 2 * n_seq),
        [sds((kinds, width, narrow), F32), sds((8, width), F32)],
        [pltpu.VMEM((n_seq, 2, kinds, 4, narrow), F32)],
        limit=40,
        flops=2 * 64 * 3_000_000,
        name="modulation_grads",
    )


def time_backward(sc, sinus, inner, outer, time_out, own, other):
    count = len(own)
    rows, width = inner.shape

    def body(sc, sinus, inner, outer, time_out, *refs):
        own, other = refs[:count], refs[count : 2 * count]
        g_in, g_out, box = refs[2 * count :]
        for k in range(count):
            at = lax.rem(sc[0] - k + count, count)
            box[at, sc[2]] = own[k][...]
            box[at, 1 - sc[2]] = other[k][...]
        total = jnp.zeros((rows, width), F32)
        for j in range(count):
            for c in range(2):
                total = total + box[j, c]

        def slope(value):
            gate = 1.0 / (1.0 + jnp.exp(-value))
            return gate * (1.0 + value * (1.0 - gate))

        pre = inner[...]
        hidden = pre / (1.0 + jnp.exp(-pre))
        d_outer = total * slope(outer[...])
        g_out[...] = exact_outer(hidden, d_outer)
        d_inner = exact_dot(d_outer, time_out[...], ((1,), (1,))) * slope(pre)
        g_in[...] = exact_outer(sinus[...], d_inner)

    return call(
        body,
        [sc, sinus, inner, outer, time_out] + own + other,
        [SM] + [VM] * (4 + 2 * count),
        [sds((sinus.shape[1], width), F32), sds((width, width), F32)],
        [pltpu.VMEM((count, 2, rows, width), F32)],
        flops=2 * 64 * 1_500_000,
        name="time_backward",
    )


class Dims:
    pass


def local_program(
    frames,
    cotangent,
    utt_lengths,
    time_ids,
    w_time_in,
    w_time_out,
    w_mod,
    w_qkv,
    w_out,
    w_up,
    w_down,
):
    micro_count, rows, narrow = frames.shape
    dims = Dims()
    dims.n_heads = lax.axis_size("heads")
    dims.n_seq = n_seq = lax.axis_size("seq")
    dims.rows, dims.narrow = rows, narrow
    dims.width = narrow * dims.n_heads
    dims.local = w_qkv.shape[3]
    dims.hidden = w_up.shape[2]
    dims.frames = rows * n_seq
    heads_local = dims.local // HEAD_DIM
    dims.spread_heads = heads_local % n_seq == 0
    dims.heads_here = heads_local // n_seq if dims.spread_heads else heads_local
    dims.n_chunks = n_seq if dims.spread_heads else 2
    at_heads = lax.axis_index("heads")
    at_seq = lax.axis_index("seq")
    section = lax.axis_index("section")

    lengths = lax.dynamic_index_in_dim(utt_lengths, section, 0, keepdims=False)
    sc = jnp.stack(
        [at_heads, at_seq, section, lengths[0], lengths[0] + lengths[1]]
    ).astype(jnp.int32)

    qkv = jnp.transpose(w_qkv[0], (1, 0, 2))
    mod_weight = jnp.transpose(w_mod[0], (1, 0, 2))
    own_weights = (qkv, w_out[0], w_up[0], w_down[0])
    wide_frames = gather(
        lax.dynamic_index_in_dim(frames, section, 0, keepdims=False), "heads"
    )
    qkv_w, out_w, up_w, down_w = [(w, swap(w)) for w in own_weights]
    wide_cotangent = gather(
        lax.dynamic_index_in_dim(cotangent, section, 0, keepdims=False), "heads"
    )

    index = jnp.arange(dims.frames, dtype=jnp.int32)
    begin = jnp.where(index >= sc[4], sc[4], jnp.where(index >= sc[3], sc[3], 0))
    position = (index - begin).astype(F32)
    lane = np.arange(2 * HEAD_DIM)
    rate = np.exp(
        np.arange(HEAD_DIM // 2, dtype=np.float32)
        * np.float32(-2.0 * math.log(10000.0) / HEAD_DIM)
    ).astype(np.float32)[(lane % HEAD_DIM) // 2]
    angle = position[:, None] * jnp.asarray(rate)[None, :]
    cosine = jnp.cos(angle)
    sine = jnp.sin(angle) * jnp.asarray(np.where(lane % 2 == 0, -1.0, 1.0), F32)[None, :]

    half = FREQ // 2
    frequency = jnp.exp(jnp.arange(half, dtype=F32) * (-math.log(10000.0) / (half - 1)))
    angle_t = time_ids.astype(F32)[..., None] * frequency
    sinus = jnp.concatenate([jnp.sin(angle_t), jnp.cos(angle_t)], axis=-1)
    sinus = jnp.pad(sinus, ((0, 0), (0, 1), (0, 0))).reshape(micro_count * 4, FREQ)
    inner, outer, act, modul = time_forward(sinus, w_time_in, w_time_out, mod_weight)
    mod = collect_modulation(sc, gather(modul, "heads"), pair_gather(modul, "heads"))

    saved = []
    pieces = wide_frames
    for layer in range(2):
        x, x_narrow, xa, *sent = project(
            dims, layer, sc, pieces, mod, *qkv_w, cosine, sine
        )
        if dims.spread_heads:
            queries = None
            kept, probs, *mixed = attend(dims, sc, exchange(sent, "seq"), None)
            mixed = exchange(mixed, "seq")
        else:
            queries = sent[0]
            kept, probs, *mixed = attend(dims, sc, gather(sent[1], "seq"), queries)
        att, *terms = project_out(dims, layer, sc, mixed, *out_w)
        branch = gather(add_chunks(exchange(terms, "heads")), "heads")
        x1, xf, h, slope, *terms = feed_forward(dims, layer, sc, x, branch, mod, up_w, down_w)
        if layer == 0:
            z = gather(add_chunks(exchange(terms, "heads")), "heads")
            pieces = [x1] + z
        else:
            z = [terms]
        saved.append(
            dict(x=x, x_narrow=x_narrow, xa=xa, kept=kept, probs=probs, queries=queries, att=att,
                 branch=branch[0], x1=x1, xf=xf, h=h, slope=slope, z=z[0])
        )

    shares = [None, None]
    small = [None, None]
    pieces = wide_cotangent
    for layer in (1, 0):
        now = saved[layer]
        g, dz, da, *rest = feed_backward(
            dims, layer, sc, pieces, now["slope"], mod, up_w, down_w
        )
        terms, rest = rest[: dims.n_heads], rest[dims.n_heads :]
        if layer == 0:
            middle_grad, small_a1 = rest
        sums = gather(add_chunks(exchange(terms, "heads")), "heads")
        if layer == 1:
            z_terms = now["z"]
            z_now = add_chunks(exchange(z_terms, "heads"))
        else:
            z_now = now["z"]
        gate_small, *shown_last = gate_sums(dims, layer, sc, g, now["x1"], z_now, mod)
        if layer == 1:
            shown = shown_last[0]
        g_down, g_up = weight_grads([(now["h"], dz), (now["xf"], da)], f"feed_grads_{layer}")
        d_mid, dy, small_f, *sent = middle_backward(
            dims, layer, sc, g, now["x1"], sums, now["branch"], mod, *out_w
        )
        (g_out,) = weight_grads([(now["att"], dy)], f"out_grad_{layer}")
        if dims.spread_heads:
            sent = exchange(sent, "seq")
        sent = attend_backward(
            dims, sc, sent, now["queries"], now["kept"], now["probs"], cosine, sine
        )
        if dims.spread_heads:
            sent = exchange(sent, "seq")
        else:
            sent = [sent[0]] + exchange(sent[1:], "seq")
        d_qkv, *terms = project_backward(dims, layer, sc, sent, *qkv_w)
        (g_qkv,) = weight_grads([(now["xa"], d_qkv)], f"qkv_grad_{layer}")
        if layer == 1:
            pieces = gather(add_chunks(exchange(terms, "heads")), "heads") + [now["x"], d_mid]
        else:
            terms = exchange(terms, "heads")
        small[layer] = (gate_small, small_f)
        done = []
        for group in ([g_down, g_up], [g_out], [g_qkv]):
            parts = split_sum(sc, group, [swap(g) for g in group], n_seq)
            for part in parts:
                total = add_chunks([owner_shift(p, layer, k) for k, p in enumerate(part)])
                done.append([owner_shift(total, layer, k) for k in range(n_seq)])
        shares[layer] = done

    grad, normed, inv, small_a0, row_sums = last_norm(dims, sc, terms, saved[0]["x"], mod)
    first_grad = last_pull(dims, sc, d_mid, grad, normed, inv, gather(row_sums, "heads"))

    def stack(layer, small_a):
        gate, mid = small[layer]
        return jnp.concatenate([small_a, mid, gate[None]], axis=0)

    by_layer = jnp.stack([stack(0, small_a0), stack(1, small_a1)])
    own_layer = lax.dynamic_index_in_dim(by_layer, section, 0, keepdims=False)
    other_layer = lax.dynamic_index_in_dim(by_layer, 1 - section, 0, keepdims=False)
    g_mod, part = modulation_grads(
        sc, act, mod_weight, gather(own_layer, "seq"), pair_gather(other_layer, "seq"), n_seq
    )
    g_first, g_second = time_backward(
        sc, sinus, inner, outer, w_time_out, gather(part, "heads"), pair_gather(part, "heads")
    )

    shapes = [w_down.shape[1:], w_up.shape[1:], w_out.shape[1:], qkv.shape]
    outs = []
    for picked in ((0, 1), (2,), (3,)):
        outs += assemble(
            sc,
            [[shares[layer][i] for i in picked] for layer in range(2)],
            [shapes[i] for i in picked],
            n_seq,
        )
    g_reduce, g_expand, g_out, g_qkv = outs

    def relaid(layer_0, layer_1):
        own = jnp.where(section == 0, layer_0, layer_1)
        other = swap(jnp.where(section == 0, layer_1, layer_0))
        return jnp.where(section == 0, jnp.stack([own, other]), jnp.stack([other, own]))[None]

    acts = relaid(saved[1]["x_narrow"], shown)
    grads = relaid(first_grad, middle_grad)
    return (
        acts,
        grads,
        g_first,
        g_second,
        jnp.transpose(g_mod, (1, 0, 2))[None],
        jnp.transpose(g_qkv, (1, 0, 2))[None],
        g_out[None],
        g_expand[None],
        g_reduce[None],
    )


def solution(mesh):
    placed = (
        P(None, "seq", "heads"),
        P(None, "seq", "heads"),
        P(),
        P(),
        P(),
        P(),
        P("section", None, None, "heads"),
        P("section", None, None, "heads"),
        P("section", "heads", None),
        P("section", None, "heads"),
        P("section", "heads", None),
    )
    return jax.shard_map(
        local_program,
        mesh=mesh,
        in_specs=placed,
        out_specs=(
            P("section", None, "seq", "heads"),
            P("section", None, "seq", "heads"),
            P(),
            P(),
            P("section", None, None, "heads"),
            P("section", None, None, "heads"),
            P("section", "heads", None),
            P("section", None, "heads"),
            P("section", "heads", None),
        ),
        check_vma=False,
    )
```

```python
import functools
import math

import jax
import jax.numpy as jnp
import numpy as np
from jax import lax
from jax.experimental import pallas as pl
from jax.experimental.pallas import tpu as pltpu
from jax.sharding import PartitionSpec as P

HEAD_DIM = 64
FREQ = 256
EPS = 1e-06
BF = jnp.bfloat16
F32 = jnp.float32
MIB = 1024 * 1024


def partner(value, axis, by):
    if by == 0:
        return value
    return lax.ppermute(value, axis, [(i, i ^ by) for i in range(lax.axis_size(axis))])


def order_of(count):
    return (3, 1, 2) if count == 4 else tuple(range(count - 1, 0, -1))


def gather(value, axis):
    count = lax.axis_size(axis)
    out = [value] * count
    for k in order_of(count):
        out[k] = partner(value, axis, k)
    return out


def exchange(chunks, axis):
    out = list(chunks)
    for k in order_of(len(chunks)):
        out[k] = partner(chunks[k], axis, k)
    return out


def swap(value):
    return lax.ppermute(value, "section", [(0, 1), (1, 0)])


def to_owner(value, layer):
    return lax.ppermute(value, "section", [(1 - layer, layer)])


def owner_partner(value, layer, by):
    if by == 0:
        return value
    length = lax.axis_size("seq")
    base = layer * length
    return lax.ppermute(
        value, ("section", "seq"), [(base + i, base + (i ^ by)) for i in range(length)]
    )


def owner_exchange(chunks, layer):
    out = list(chunks)
    for k in order_of(len(chunks)):
        out[k] = owner_partner(chunks[k], layer, k)
    return out


def after(value, *done):
    return lax.optimization_barrier((value, done))[0]


def add_chunks(chunks):
    total = chunks[0].astype(F32)
    for chunk in chunks[1:]:
        total = total + chunk.astype(F32)
    return total.astype(BF)


def dot(left, right, contract=((1,), (0,))):
    return lax.dot_general(left, right, (contract, ((), ())), preferred_element_type=F32)


def split3(value):
    high = value.astype(BF)
    rest = value - high.astype(F32)
    middle = rest.astype(BF)
    low = (rest - middle.astype(F32)).astype(BF)
    return high, middle, low


def exact_dot(left, right, contract=((1,), (0,))):
    rows = left.shape[0]
    stacked = jnp.concatenate(split3(left), axis=0)
    out = dot(stacked, right, contract)
    return out[:rows] + (out[rows : 2 * rows] + out[2 * rows :])


def exact_outer(left, right):
    a = split3(left)
    b = split3(right)
    order = ((0, 0), (0, 1), (1, 0), (1, 1), (0, 2), (2, 0))
    tall = jnp.concatenate([a[i] for i, _ in order], axis=0)
    wide = jnp.concatenate([b[j] for _, j in order], axis=0)
    return dot(tall, wide, ((0,), (0,)))


def segments(sc, shape, axis, first):
    index = lax.broadcasted_iota(jnp.int32, shape, axis) + first
    return (index >= sc[3]).astype(jnp.int32) + (index >= sc[4]).astype(jnp.int32)


def spread(mod, layer, which, seg, columns=slice(None)):
    block = mod[layer * 6 + which, :, columns]
    rows = [block[u : u + 1] for u in range(3)]
    return jnp.where(seg == 0, rows[0], jnp.where(seg == 1, rows[1], rows[2]))


def utterance_sums(value, seg):
    rows = [
        jnp.sum(jnp.where(seg == u, value, 0.0), axis=0, keepdims=True) for u in range(3)
    ]
    return jnp.concatenate(rows + [jnp.zeros_like(rows[0])], axis=0)


def norm_of(value):
    mean = jnp.mean(value, axis=1, keepdims=True)
    centred = value - mean
    inv = lax.rsqrt(jnp.mean(centred * centred, axis=1, keepdims=True) + EPS)
    return centred * inv, inv


def norm_pull(grad, normed, inv):
    return inv * (
        grad
        - jnp.mean(grad, axis=1, keepdims=True)
        - normed * jnp.mean(grad * normed, axis=1, keepdims=True)
    )


def lanes_of(index, count, width):
    return pl.ds(pl.multiple_of(lax.rem(index, count) * width, width), width)


def place(buffer, chunks, own, width):
    for k, chunk in enumerate(chunks):
        at = pl.multiple_of(jnp.bitwise_xor(own, k) * width, width)
        buffer[:, pl.ds(at, width)] = chunk[...].astype(buffer.dtype)


def hand_out(outs, buffer, own, width):
    for k, out in enumerate(outs):
        at = pl.multiple_of(jnp.bitwise_xor(own, k) * width, width)
        out[...] = buffer[:, pl.ds(at, width)].astype(out.dtype)


class Fetch:
    def __init__(self, sc, layer, own, other, buffer, sem):
        self.copy = pltpu.make_async_copy(own, buffer, sem)
        other_copy = pltpu.make_async_copy(other, buffer, sem)

        @pl.when(sc[2] == layer)
        def _():
            self.copy.start()

        @pl.when(sc[2] != layer)
        def _():
            other_copy.start()

    def wait(self):
        self.copy.wait()


def turn(value, cosine, sine):
    width = value.shape[1]
    even = lax.broadcasted_iota(jnp.int32, value.shape, 1) % 2 == 0
    swapped = jnp.where(even, pltpu.roll(value, width - 1, 1), pltpu.roll(value, 1, 1))
    return value * cosine + swapped * sine


def widen_table(table, width):
    copies = width // table.shape[1]
    return jnp.concatenate([table] * copies, axis=1) if copies > 1 else table[:, :width]


VM = pl.BlockSpec(memory_space=pltpu.VMEM)
SM = pl.BlockSpec(memory_space=pltpu.SMEM)
HB = pl.BlockSpec(memory_space=pl.ANY)


def sds(shape, dtype):
    return jax.ShapeDtypeStruct(tuple(shape), dtype)


def call(body, ins, specs, outs, scratch=(), flops=0, limit=20, name=None):
    moved = sum(math.prod(a.shape) * a.dtype.itemsize for a in list(ins) + list(outs))
    return pl.pallas_call(
        body,
        out_shape=list(outs),
        in_specs=list(specs),
        out_specs=[VM] * len(outs),
        scratch_shapes=list(scratch),
        compiler_params=pltpu.CompilerParams(vmem_limit_bytes=limit * MIB),
        cost_estimate=pl.CostEstimate(
            flops=int(flops), bytes_accessed=int(moved), transcendentals=0
        ),
        name=name,
    )(*ins)


def cut(refs, *counts):
    out = []
    at = 0
    for n in counts:
        if n == 1:
            out.append(refs[at])
        else:
            out.append(refs[at : at + n])
        at += n
    assert at == len(refs)
    return out


class Group(list):
    pass


def start(sc, time_ids, time_in, time_out, mod_weight, rows):
    width = time_in.shape[1]
    kinds, _, narrow = mod_weight.shape
    half = FREQ // 2

    def body(sc, ids, time_in, time_out, mod_weight, *refs):
        sinus_out, inner_out, outer_out, act_out, mine_out, theirs_out, cosine, sine = refs[:8]
        w_in, w_out, w_mod, sems = refs[8:]
        copies = [
            pltpu.make_async_copy(time_in, w_in, sems.at[0]),
            pltpu.make_async_copy(time_out, w_out, sems.at[1]),
            pltpu.make_async_copy(mod_weight, w_mod, sems.at[2]),
        ]
        for copy in copies:
            copy.start()
        row = lax.broadcasted_iota(jnp.int32, (8, half), 0)
        lane = lax.broadcasted_iota(jnp.int32, (8, half), 1).astype(F32)
        stamp = jnp.zeros((8, half), F32)
        for m in range(2):
            for u in range(3):
                stamp = jnp.where(row == m * 4 + u, ids[m, u].astype(F32), stamp)
        angle_t = stamp * jnp.exp(lane * (-math.log(10000.0) / (half - 1)))
        sinus = jnp.concatenate([jnp.sin(angle_t), jnp.cos(angle_t)], axis=1)
        sinus_out[...] = sinus

        index = lax.broadcasted_iota(jnp.int32, (rows, 2 * HEAD_DIM), 0) + sc[1] * rows
        begin = jnp.where(index >= sc[4], sc[4], jnp.where(index >= sc[3], sc[3], 0))
        lane = lax.broadcasted_iota(jnp.int32, (rows, 2 * HEAD_DIM), 1)
        pair = lax.broadcasted_iota(jnp.int32, (1, 2 * HEAD_DIM), 1)
        rate = jnp.exp(
            ((pair % HEAD_DIM) // 2).astype(F32) * (-2.0 * math.log(10000.0) / HEAD_DIM)
        )
        angle = (index - begin).astype(F32) * rate
        cosine[...] = jnp.cos(angle)
        sine[...] = jnp.sin(angle) * jnp.where(lane % 2 == 0, -1.0, 1.0)

        copies[0].wait()
        inner = exact_dot(sinus, w_in[...])
        inner_out[...] = inner
        hidden = inner / (1.0 + jnp.exp(-inner))
        copies[1].wait()
        outer = exact_dot(hidden, w_out[...])
        outer_out[...] = outer
        act = outer / (1.0 + jnp.exp(-outer))
        act_out[...] = act
        copies[2].wait()
        for which in range(kinds):
            modul = exact_dot(act, w_mod[which])
            mine_out[which] = jnp.where(sc[2] == 0, modul[:4], modul[4:])
            theirs_out[which] = jnp.where(sc[2] == 0, modul[4:], modul[:4])

    return call(
        body,
        [sc, time_ids, time_in, time_out, mod_weight],
        [SM, SM, HB, HB, HB],
        [sds((8, FREQ), F32)]
        + [sds((8, width), F32)] * 3
        + [sds((kinds, 4, narrow), F32)] * 2
        + [sds((rows, 2 * HEAD_DIM), F32)] * 2,
        [
            pltpu.VMEM(time_in.shape, BF),
            pltpu.VMEM(time_out.shape, BF),
            pltpu.VMEM(mod_weight.shape, BF),
            pltpu.SemaphoreType.DMA((3,)),
        ],
        flops=2 * 256 * 4_000_000,
        name="start",
    )


def project(dims, layer, sc, pieces, mods, weights, cosine, sine):
    first = layer == 0
    rows, width, narrow, local = dims.rows, dims.width, dims.narrow, dims.local
    count = dims.n_heads
    n_in, n_mod = len(pieces), len(mods)

    def body(sc, *refs):
        pieces, mods = refs[:n_in], refs[n_in : n_in + n_mod]
        w_own, w_other, cosine, sine = refs[n_in + n_mod : n_in + n_mod + 4]
        outs = refs[n_in + n_mod + 4 :]
        x_out, narrow_out, xa_out, q_out, kv_out = outs[:5]
        if first:
            mod = outs[5]
        else:
            mod = mods[0]
        buffer, weight, sem = outs[-3:]
        fetch = Fetch(sc, layer, w_own, w_other, weight, sem)
        seg = segments(sc, (rows, 1), 0, sc[1] * rows)
        if first:
            for k in range(count):
                at = pl.multiple_of(jnp.bitwise_xor(sc[0], k) * narrow, narrow)
                block = mods[k][...]
                for l in range(2):
                    mod[l * 6 : l * 6 + 6, :, pl.ds(at, narrow)] = jnp.where(
                        sc[2] == l, block[:6], block[6:]
                    )
            place(buffer, pieces, sc[0], narrow)
            x = buffer[...]
            x_out[...] = x.astype(BF)
            narrow_out[...] = pieces[0][...]
        else:
            place(buffer, pieces[1:], sc[0], narrow)
            x = pieces[0][...] + spread(mod, 0, 5, seg) * buffer[...]
            low = x.astype(BF)
            x_out[...] = low
            x = low.astype(F32)
            buffer[...] = x
            at = pl.multiple_of(sc[0] * narrow, narrow)
            narrow_out[...] = buffer[:, pl.ds(at, narrow)].astype(BF)
        normed, _ = norm_of(x)
        xa = (normed * (1.0 + spread(mod, layer, 1, seg)) + spread(mod, layer, 0, seg)).astype(BF)
        xa_out[...] = xa
        cos = widen_table(cosine[...], local)
        sin = widen_table(sine[...], local)
        fetch.wait()
        q_out[...] = turn(dot(xa, weight[0]), cos, sin).astype(BF)
        kv_out[:, :local] = turn(dot(xa, weight[1]), cos, sin).astype(BF)
        kv_out[:, local:] = dot(xa, weight[2]).astype(BF)

    return call(
        body,
        [sc] + pieces + mods + [weights[0], weights[1], cosine, sine],
        [SM] + [VM] * (n_in + n_mod) + [HB, HB, VM, VM],
        [
            sds((rows, width), BF),
            sds((rows, narrow), BF),
            sds((rows, width), BF),
            sds((rows, local), BF),
            sds((rows, 2 * local), BF),
        ]
        + ([sds((12, 4, width), F32)] if first else []),
        [
            pltpu.VMEM((rows, width), F32),
            pltpu.VMEM(weights[0].shape, BF),
            pltpu.SemaphoreType.DMA,
        ],
        flops=6 * rows * width * local,
        name=f"project_{layer}",
    )


def attend(dims, layer, sc, chunks, queries, weights):
    rows, n_seq, frames = dims.rows, dims.n_seq, dims.frames
    width, narrow, local, count = dims.width, dims.narrow, dims.local, dims.n_heads
    heads = local // HEAD_DIM

    def body(sc, *refs):
        chunks = refs[:n_seq]
        queries, w_own, w_other = refs[n_seq : n_seq + 3]
        kept, probs, mixed = refs[n_seq + 3 : n_seq + 6]
        outs = refs[n_seq + 6 : n_seq + 6 + count]
        weight, buffer, sem = refs[n_seq + 6 + count :]
        fetch = Fetch(sc, layer, w_own, w_other, weight, sem)
        for k in range(n_seq):
            at = pl.multiple_of(jnp.bitwise_xor(sc[1], k) * rows, rows)
            kept[pl.ds(at, rows), :] = chunks[k][...]
        same = segments(sc, (rows, 1), 0, sc[1] * rows) == segments(sc, (1, frames), 1, 0)
        for head in range(heads):
            cols = slice(head * HEAD_DIM, (head + 1) * HEAD_DIM)
            scores = dot(queries[:, cols], kept[:, cols], ((1,), (1,)))
            scores = jnp.where(same, scores * (1.0 / math.sqrt(HEAD_DIM)), -1e30)
            prob = jnp.exp(scores - jnp.max(scores, axis=1, keepdims=True))
            prob = prob * (1.0 / jnp.sum(prob, axis=1, keepdims=True))
            low = prob.astype(BF)
            probs[head] = low
            value = kept[:, local + head * HEAD_DIM : local + (head + 1) * HEAD_DIM]
            mixed[:, cols] = dot(low, value).astype(BF)
        fetch.wait()
        buffer[...] = dot(mixed[...], weight[...]).astype(BF)
        hand_out(outs, buffer, sc[0], narrow)

    return call(
        body,
        [sc] + chunks + [queries, weights[0], weights[1]],
        [SM] + [VM] * (n_seq + 1) + [HB, HB],
        [
            sds((frames, 2 * local), BF),
            sds((heads, rows, frames), BF),
            sds((rows, local), BF),
        ]
        + [sds((rows, narrow), BF)] * count,
        [
            pltpu.VMEM(weights[0].shape, BF),
            pltpu.VMEM((rows, width), BF),
            pltpu.SemaphoreType.DMA,
        ],
        flops=4 * rows * frames * local + 2 * rows * width * local,
        name=f"attend_{layer}",
    )


def feed_forward(dims, layer, sc, x, branch, mod, up, down):
    rows, width, narrow, count, hidden = (
        dims.rows, dims.width, dims.narrow, dims.n_heads, dims.hidden,
    )

    def body(sc, x, *refs):
        branch = refs[:count]
        mod, up_own, up_other, down_own, down_other = refs[count : count + 5]
        x1_out, xf_out, h_out, slope_out = refs[count + 5 : count + 9]
        outs = refs[count + 9 : 2 * count + 9]
        up, down, buffer, low, sem_up, sem_down = refs[2 * count + 9 :]
        fetch_up = Fetch(sc, layer, up_own, up_other, up, sem_up)
        fetch_down = Fetch(sc, layer, down_own, down_other, down, sem_down)
        seg = segments(sc, (rows, 1), 0, sc[1] * rows)
        place(buffer, branch, sc[0], narrow)
        x1 = x[...].astype(F32) + spread(mod, layer, 2, seg) * buffer[...]
        x1_out[...] = x1
        normed, _ = norm_of(x1)
        xf = (normed * (1.0 + spread(mod, layer, 4, seg)) + spread(mod, layer, 3, seg)).astype(BF)
        xf_out[...] = xf
        fetch_up.wait()
        a = dot(xf, up[...])
        c0 = math.sqrt(2.0 / math.pi)
        square = a * a
        t = jnp.tanh(c0 * (a + 0.044715 * (a * square)))
        h = (0.5 * a * (1.0 + t)).astype(BF)
        h_out[...] = h
        slope_out[...] = 0.5 * (1.0 + t) + 0.5 * a * (1.0 - t * t) * (
            c0 * (1.0 + 3.0 * 0.044715 * square)
        )
        fetch_down.wait()
        low[...] = dot(h, down[...]).astype(BF)
        hand_out(outs, low, sc[0], narrow)

    return call(
        body,
        [sc, x] + branch + [mod, up[0], up[1], down[0], down[1]],
        [SM, VM] + [VM] * count + [VM, HB, HB, HB, HB],
        [
            sds((rows, width), F32),
            sds((rows, width), BF),
            sds((rows, hidden), BF),
            sds((rows, hidden), F32),
        ]
        + [sds((rows, narrow), BF)] * count,
        [
            pltpu.VMEM(up[0].shape, BF),
            pltpu.VMEM(down[0].shape, BF),
            pltpu.VMEM((rows, width), F32),
            pltpu.VMEM((rows, width), BF),
            pltpu.SemaphoreType.DMA,
            pltpu.SemaphoreType.DMA,
        ],
        flops=4 * rows * width * hidden,
        name=f"feed_forward_{layer}",
    )


def feed_backward(dims, layer, sc, pieces, slope, mod, up, down):
    rows, width, narrow, count, hidden = (
        dims.rows, dims.width, dims.narrow, dims.n_heads, dims.hidden,
    )
    last = layer == 1
    n_in = len(pieces)
    n_extra = 0 if last else 2

    def body(sc, *refs):
        pieces = refs[:n_in]
        slope, mod, up_own, up_other, down_own, down_other = refs[n_in : n_in + 6]
        rest = refs[n_in + 6 :]
        g_out, dz_out, da_out = rest[:3]
        outs = rest[3 : 3 + count]
        extra = rest[3 + count : 3 + count + n_extra]
        up, down, buffer, low, other_buffer, sem_up, sem_down = rest[3 + count + n_extra :]
        fetch_down = Fetch(sc, layer, down_own, down_other, down, sem_down)
        fetch_up = Fetch(sc, layer, up_own, up_other, up, sem_up)
        seg = segments(sc, (rows, 1), 0, sc[1] * rows)
        place(buffer, pieces[:count], sc[0], narrow)
        if last:
            g = buffer[...]
            g_out[...] = g.astype(BF)
        else:
            x, d_mid = pieces[count:]
            grad_out, sums_out = extra
            dxa = buffer[...]
            normed, inv = norm_of(x[...].astype(F32))
            other_buffer[...] = dxa * normed
            mine = pl.ds(pl.multiple_of(sc[0] * narrow, narrow), narrow)
            sums_out[0] = utterance_sums(buffer[:, mine], seg)
            sums_out[1] = utterance_sums(other_buffer[:, mine], seg)
            dx = d_mid[...] + norm_pull(dxa * (1.0 + spread(mod, 1, 1, seg)), normed, inv)
            other_buffer[...] = dx
            grad_out[...] = other_buffer[:, mine]
            g = dx.astype(BF)
            g_out[...] = g
            g = g.astype(F32)
        dz = (g * spread(mod, layer, 5, seg)).astype(BF)
        dz_out[...] = dz
        fetch_down.wait()
        da = (dot(dz, down[...], ((1,), (1,))) * slope[...]).astype(BF)
        da_out[...] = da
        fetch_up.wait()
        low[...] = dot(da, up[...], ((1,), (1,))).astype(BF)
        hand_out(outs, low, sc[0], narrow)

    extra = [] if last else [sds((rows, narrow), F32), sds((2, 4, narrow), F32)]
    return call(
        body,
        [sc] + pieces + [slope, mod, up[0], up[1], down[0], down[1]],
        [SM] + [VM] * n_in + [VM, VM, HB, HB, HB, HB],
        [sds((rows, width), BF), sds((rows, width), BF), sds((rows, hidden), BF)]
        + [sds((rows, narrow), BF)] * count
        + extra,
        [
            pltpu.VMEM(up[0].shape, BF),
            pltpu.VMEM(down[0].shape, BF),
            pltpu.VMEM((rows, width), F32),
            pltpu.VMEM((rows, width), BF),
            pltpu.VMEM((rows, width), F32),
            pltpu.SemaphoreType.DMA,
            pltpu.SemaphoreType.DMA,
        ],
        flops=4 * rows * width * hidden,
        name=f"feed_backward_{layer}",
    )


def middle_backward(dims, layer, sc, g, x1, sums, branch, mod, weights, queries, kept, probs, cosine, sine):
    rows, width, narrow, local, count = (
        dims.rows, dims.width, dims.narrow, dims.local, dims.n_heads,
    )
    n_seq, frames = dims.n_seq, dims.frames
    heads = local // HEAD_DIM
    scale = 1.0 / math.sqrt(HEAD_DIM)

    def body(sc, g, x1, *refs):
        sums = refs[:count]
        branch, mod, w_own, w_other, queries, kept, probs, cosine, sine = refs[count : count + 9]
        d_mid_out, dy_out, small, q_out = refs[count + 9 : count + 13]
        outs = refs[count + 13 : count + 13 + n_seq]
        weight, buffer, other, done, sem = refs[count + 13 + n_seq :]
        fetch = Fetch(sc, layer, w_own, w_other, weight, sem)
        seg = segments(sc, (rows, 1), 0, sc[1] * rows)
        mine = pl.ds(pl.multiple_of(sc[0] * narrow, narrow), narrow)
        place(buffer, sums, sc[0], narrow)
        dxf = buffer[...]
        normed, inv = norm_of(x1[...])
        other[...] = dxf * normed
        small[1] = utterance_sums(buffer[:, mine], seg)
        small[2] = utterance_sums(other[:, mine], seg)
        d_mid = g[...].astype(F32) + norm_pull(
            dxf * (1.0 + spread(mod, layer, 4, seg)), normed, inv
        )
        d_mid_out[...] = d_mid
        other[...] = d_mid
        small[0] = utterance_sums(other[:, mine] * branch[...].astype(F32), seg)
        dy = (d_mid * spread(mod, layer, 2, seg)).astype(BF)
        dy_out[...] = dy
        fetch.wait()
        d_att = dot(dy, weight[...], ((1,), (1,))).astype(BF)
        cos = cosine[:, :HEAD_DIM]
        sin = -sine[:, :HEAD_DIM]
        for head in range(heads):
            cols = slice(head * HEAD_DIM, (head + 1) * HEAD_DIM)
            vals = slice(local + head * HEAD_DIM, local + (head + 1) * HEAD_DIM)
            low = probs[head]
            prob = low.astype(F32)
            grad = d_att[:, cols]
            d_prob = dot(grad, kept[:, vals], ((1,), (1,)))
            delta = jnp.sum(d_prob * prob, axis=1, keepdims=True)
            d_score = (prob * (d_prob - delta)).astype(BF)
            dq = dot(d_score, kept[:, cols]) * scale
            q_out[:, cols] = turn(dq, cos, sin).astype(BF)
            done[:, cols] = (dot(d_score, queries[:, cols], ((0,), (0,))) * scale).astype(BF)
            done[:, vals] = dot(low, grad, ((0,), (0,))).astype(BF)
        for k in range(n_seq):
            at = pl.multiple_of(jnp.bitwise_xor(sc[1], k) * rows, rows)
            outs[k][...] = done[pl.ds(at, rows), :]

    return call(
        body,
        [sc, g, x1] + sums + [branch, mod, weights[0], weights[1], queries, kept, probs, cosine, sine],
        [SM, VM, VM] + [VM] * count + [VM, VM, HB, HB] + [VM] * 5,
        [
            sds((rows, width), F32),
            sds((rows, width), BF),
            sds((3, 4, narrow), F32),
            sds((rows, local), BF),
        ]
        + [sds((rows, 2 * local), BF)] * n_seq,
        [
            pltpu.VMEM(weights[0].shape, BF),
            pltpu.VMEM((rows, width), F32),
            pltpu.VMEM((rows, width), F32),
            pltpu.VMEM((frames, 2 * local), BF),
            pltpu.SemaphoreType.DMA,
        ],
        flops=2 * rows * width * local + 8 * rows * frames * local,
        name=f"middle_backward_{layer}",
    )


def project_backward(dims, layer, sc, d_query, chunks, weights, cosine, sine):
    rows, width, narrow, local, count = (
        dims.rows, dims.width, dims.narrow, dims.local, dims.n_heads,
    )
    n_in = len(chunks)

    def body(sc, d_query, *refs):
        chunks = refs[:n_in]
        w_own, w_other, cosine, sine, d_out = refs[n_in : n_in + 5]
        outs = refs[n_in + 5 : n_in + 5 + count]
        weight, buffer, sem = refs[n_in + 5 + count :]
        fetch = Fetch(sc, layer, w_own, w_other, weight, sem)
        total = chunks[0][...].astype(F32)
        for chunk in chunks[1:]:
            total = total + chunk[...].astype(F32)
        cos = widen_table(cosine[...], local)
        sin = -widen_table(sine[...], local)
        dk = turn(total[:, :local], cos, sin).astype(BF)
        dv = total[:, local:].astype(BF)
        d_out[0] = d_query[...]
        d_out[1] = dk
        d_out[2] = dv
        fetch.wait()
        total = dot(d_query[...], weight[0], ((1,), (1,)))
        total = total + dot(dk, weight[1], ((1,), (1,)))
        total = total + dot(dv, weight[2], ((1,), (1,)))
        buffer[...] = total.astype(BF)
        hand_out(outs, buffer, sc[0], narrow)

    return call(
        body,
        [sc, d_query] + chunks + [weights[0], weights[1], cosine, sine],
        [SM, VM] + [VM] * n_in + [HB, HB, VM, VM],
        [sds((3, rows, local), BF)] + [sds((rows, narrow), BF)] * count,
        [
            pltpu.VMEM(weights[0].shape, BF),
            pltpu.VMEM((rows, width), BF),
            pltpu.SemaphoreType.DMA,
        ],
        flops=6 * rows * width * local,
        name=f"project_backward_{layer}",
    )


def weight_grads(tall, wide, n_seq, name):
    width = tall[0][1].shape[1]
    local = tall[0][0].shape[1]
    n = len(tall) + len(wide)
    share = local // n_seq
    ins = [a for pair in list(tall) + list(wide) for a in pair]

    def body(*refs):
        out = refs[2 * n]
        for i in range(n):
            left, right = refs[2 * i], refs[2 * i + 1]
            grad = dot(left[...], right[...], ((0,), (0,))).astype(BF)
            for j in range(n_seq):
                if i < len(tall):
                    out[j, i] = grad[j * share : (j + 1) * share]
                    continue
                for group in range(width // local):
                    at = j * (width // n_seq) + group * share
                    out[j, i, :, group * local : (group + 1) * local] = grad[at : at + share]

    return call(
        body,
        ins,
        [VM] * (2 * n),
        [sds((n_seq, n, share, width), BF)],
        flops=2 * n * tall[0][0].shape[0] * width * local,
        name=name,
    )[0]


def add_shares(sc, pack, other):
    n_seq = pack.shape[0]

    def body(sc, pack, other, *outs):
        for k in range(n_seq):
            at = jnp.bitwise_xor(sc[1], k)
            outs[k][...] = (pack[at].astype(F32) + other[at].astype(F32)).astype(BF)

    return call(
        body,
        [sc, pack, other],
        [SM, VM, VM],
        [sds(pack.shape[1:], BF)] * n_seq,
        name="add_shares",
    )


def assemble(sc, shares, tall, wide, local, width, n_seq, name):
    flat = list(shares[0]) + list(shares[1])
    share = local // n_seq

    def body(sc, *refs):
        outs = refs[2 * n_seq :]
        for layer in range(2):

            @pl.when(sc[2] == layer)
            def _(layer=layer):
                for k in range(n_seq):
                    part = refs[layer * n_seq + k]
                    at = jnp.bitwise_xor(sc[1], k)
                    for i in range(tall):
                        outs[i][pl.ds(pl.multiple_of(at * share, share), share), :] = part[
                            i
                        ].astype(F32)
                    for i in range(wide):
                        for group in range(width // local):
                            row = at * (width // n_seq) + group * share
                            outs[tall + i][pl.ds(pl.multiple_of(row, share), share), :] = part[
                                tall + i, :, group * local : (group + 1) * local
                            ].astype(F32)

    return call(
        body,
        [sc] + flat,
        [SM] + [VM] * len(flat),
        [sds((local, width), F32)] * tall + [sds((width, local), F32)] * wide,
        name=name,
    )


def gate_sums(dims, layer, sc, g, x1, z, mod):
    rows, narrow = dims.rows, dims.narrow

    def body(sc, g, x1, z, mod, small, *shown):
        seg = segments(sc, (rows, 1), 0, sc[1] * rows)
        mine = pl.ds(pl.multiple_of(sc[0] * narrow, narrow), narrow)
        value = z[...].astype(F32)
        small[...] = utterance_sums(g[:, mine].astype(F32) * value, seg)
        if shown:
            gate = spread(mod, layer, 5, seg, mine)
            shown[0][...] = (x1[:, mine] + gate * value).astype(BF)

    outs = [sds((4, narrow), F32)]
    if layer == 1:
        outs.append(sds((rows, narrow), BF))
    return call(body, [sc, g, x1, z, mod], [SM] + [VM] * 4, outs, name=f"gate_sums_{layer}")


def last_norm(dims, sc, terms, x, mod):
    rows, narrow, count = dims.rows, dims.narrow, dims.n_heads

    def body(sc, *refs):
        terms = refs[:count]
        x, mod, total_out, normed_out, inv_out, small, rows_out, buffer = refs[count:]
        seg = segments(sc, (rows, 1), 0, sc[1] * rows)
        mine = pl.ds(pl.multiple_of(sc[0] * narrow, narrow), narrow)
        total = terms[0][...].astype(F32)
        for term in terms[1:]:
            total = total + term[...].astype(F32)
        normed, inv = norm_of(x[...].astype(F32))
        buffer[...] = normed
        normed = buffer[:, mine]
        small[0] = utterance_sums(total, seg)
        small[1] = utterance_sums(total * normed, seg)
        grad = total * (1.0 + spread(mod, 0, 1, seg, mine))
        total_out[...] = grad
        normed_out[...] = normed
        inv_out[...] = inv
        rows_out[...] = jnp.concatenate(
            [jnp.sum(grad, axis=1, keepdims=True), jnp.sum(grad * normed, axis=1, keepdims=True)],
            axis=1,
        )

    return call(
        body,
        [sc] + terms + [x, mod],
        [SM] + [VM] * (count + 2),
        [
            sds((rows, narrow), F32),
            sds((rows, narrow), F32),
            sds((rows, 1), F32),
            sds((2, 4, narrow), F32),
            sds((rows, 2), F32),
        ],
        [pltpu.VMEM((rows, dims.width), F32)],
        name="last_norm",
    )


def last_pull(dims, sc, d_mid, grad, normed, inv, sums):
    rows, narrow, count, width = dims.rows, dims.narrow, dims.n_heads, dims.width

    def body(sc, d_mid, grad, normed, inv, *refs):
        sums, out = refs[:count], refs[count]
        total = sums[0][...]
        for term in sums[1:]:
            total = total + term[...]
        total = total * (1.0 / width)
        mine = pl.ds(pl.multiple_of(sc[0] * narrow, narrow), narrow)
        out[...] = d_mid[:, mine] + inv[...] * (
            grad[...] - total[:, 0:1] - normed[...] * total[:, 1:2]
        )

    return call(
        body,
        [sc, d_mid, grad, normed, inv] + sums,
        [SM] + [VM] * (4 + count),
        [sds((rows, narrow), F32)],
        name="last_pull",
    )[0]


def modulation_grads(sc, act, mod_weight, own, n_seq):
    kinds, width, narrow = mod_weight.shape

    def body(sc, act, mod_weight, *refs):
        own = refs[:n_seq]
        g_mod, part, box, weight, sem = refs[n_seq:]
        copy = pltpu.make_async_copy(mod_weight, weight, sem)
        copy.start()
        for k in range(n_seq):
            box[jnp.bitwise_xor(sc[1], k)] = own[k][...]
        total = box[0]
        for j in range(1, n_seq):
            total = total + box[j]
        act_now = act[...]
        grads = []
        for which in range(kinds):
            mine, theirs = total[which], total[kinds + which]
            grads.append(
                jnp.concatenate(
                    [jnp.where(sc[2] == 0, mine, theirs), jnp.where(sc[2] == 0, theirs, mine)],
                    axis=0,
                )
            )
        copy.wait()
        result = jnp.zeros((8, width), F32)
        for which in range(kinds):
            result = result + exact_dot(grads[which], weight[which], ((1,), (1,)))
        part[...] = result
        for which in range(kinds):
            g_mod[which] = exact_outer(act_now, grads[which])

    return call(
        body,
        [sc, act, mod_weight] + own,
        [SM, VM, HB] + [VM] * n_seq,
        [sds((kinds, width, narrow), F32), sds((8, width), F32)],
        [
            pltpu.VMEM((n_seq, 2 * kinds, 4, narrow), F32),
            pltpu.VMEM(mod_weight.shape, BF),
            pltpu.SemaphoreType.DMA,
        ],
        flops=2 * 64 * 3_000_000,
        name="modulation_grads",
    )


def time_backward(sc, sinus, inner, outer, time_out, own):
    count = len(own)
    rows, width = inner.shape

    def body(sc, sinus, inner, outer, time_out, *refs):
        own = refs[:count]
        g_in, g_out, box, weight, sem = refs[count:]
        copy = pltpu.make_async_copy(time_out, weight, sem)
        copy.start()
        for k in range(count):
            at = jnp.bitwise_xor(sc[0], k)
            box[at, sc[2]] = own[k][0]
            box[at, 1 - sc[2]] = own[k][1]
        total = jnp.zeros((rows, width), F32)
        for j in range(count):
            for c in range(2):
                total = total + box[j, c]

        def slope(value):
            gate = 1.0 / (1.0 + jnp.exp(-value))
            return gate * (1.0 + value * (1.0 - gate))

        pre = inner[...]
        hidden = pre / (1.0 + jnp.exp(-pre))
        d_outer = total * slope(outer[...])
        g_out[...] = exact_outer(hidden, d_outer)
        copy.wait()
        d_inner = exact_dot(d_outer, weight[...], ((1,), (1,))) * slope(pre)
        g_in[...] = exact_outer(sinus[...], d_inner)

    return call(
        body,
        [sc, sinus, inner, outer, time_out] + own,
        [SM, VM, VM, VM, HB] + [VM] * count,
        [sds((sinus.shape[1], width), F32), sds((width, width), F32)],
        [
            pltpu.VMEM((count, 2, rows, width), F32),
            pltpu.VMEM(time_out.shape, BF),
            pltpu.SemaphoreType.DMA,
        ],
        flops=2 * 64 * 1_500_000,
        name="time_backward",
    )


class Dims:
    pass


def local_program(
    frames,
    cotangent,
    utt_lengths,
    time_ids,
    w_time_in,
    w_time_out,
    w_mod,
    w_qkv,
    w_out,
    w_up,
    w_down,
):
    dims = Dims()
    dims.n_heads = lax.axis_size("heads")
    dims.n_seq = n_seq = lax.axis_size("seq")
    _, dims.rows, dims.narrow = frames.shape
    dims.width = dims.narrow * dims.n_heads
    dims.local = w_qkv.shape[3]
    dims.hidden = w_up.shape[2]
    dims.frames = dims.rows * n_seq
    section = lax.axis_index("section")

    def here(both):
        return lax.dynamic_index_in_dim(both, section, 0, keepdims=False)

    lengths = here(utt_lengths)
    sc = jnp.stack(
        [
            lax.axis_index("heads"),
            lax.axis_index("seq"),
            section,
            lengths[0],
            lengths[0] + lengths[1],
        ]
    ).astype(jnp.int32)

    qkv = jnp.transpose(w_qkv[0], (1, 0, 2))
    mod_weight = jnp.transpose(w_mod[0], (1, 0, 2))
    wide_frames = gather(here(frames), "heads")
    qkv_w = (qkv, swap(qkv))
    sinus, inner, outer, act, mod_mine, mod_theirs, cosine, sine = start(
        sc, time_ids, w_time_in, w_time_out, mod_weight, dims.rows
    )
    mods = gather(jnp.concatenate([mod_mine, swap(mod_theirs)], axis=0), "heads")

    saved = []
    mod = None
    pieces = wide_frames
    for layer in range(2):
        x, x_narrow, xa, q, kv, *rest = project(
            dims, layer, sc, pieces, mods if layer == 0 else [mod], qkv_w, cosine, sine
        )
        if layer == 0:
            mod = rest[0]
            out_w, up_w, down_w = [
                (w[0], swap(after(w[0], kv))) for w in (w_out, w_up, w_down)
            ]
        chunks = gather(kv, "seq")
        kept, probs, att, *terms = attend(dims, layer, sc, chunks, q, out_w)
        branch = gather(add_chunks(exchange(terms, "heads")), "heads")
        if layer == 0:
            wide_cotangent = gather(after(here(cotangent), branch[0]), "heads")
        x1, xf, h, slope, *terms = feed_forward(dims, layer, sc, x, branch, mod, up_w, down_w)
        z = None
        if layer == 0:
            z = gather(add_chunks(exchange(terms, "heads")), "heads")
            pieces = [x1] + z
        saved.append(
            dict(x=x, x_narrow=x_narrow, xa=xa, kept=kept, probs=probs, q=q, att=att,
                 branch=branch[0], x1=x1, xf=xf, h=h, slope=slope, z=z)
        )
    z_terms = terms

    small = [None, None]
    shares = [[None, None], [None, None]]
    pieces = wide_cotangent
    pending = None
    for layer in (1, 0):
        now = saved[layer]
        g, dz, da, *rest = feed_backward(
            dims, layer, sc, pieces, now["slope"], mod, up_w, down_w
        )
        terms, rest = rest[: dims.n_heads], rest[dims.n_heads :]
        if layer == 0:
            middle_grad, small_a1 = rest
        total = add_chunks(exchange(terms, "heads"))
        pack = weight_grads([(now["h"], dz)], [(now["xf"], da)], n_seq, f"feed_grads_{layer}")
        moved = to_owner(pack, layer)
        total = after(total, moved)
        sums = gather(total, "heads")
        feed_shares = add_shares(sc, pack, moved)
        sums[0] = after(sums[0], feed_shares)
        feed_shares = owner_exchange(feed_shares, layer)
        if pending is not None:
            sums[0] = after(sums[0], *pending[0])
        d_mid, dy, small_f, dq, *sent = middle_backward(
            dims, layer, sc, g, now["x1"], sums, now["branch"], mod, out_w,
            now["q"], now["kept"], now["probs"], cosine, sine,
        )
        sent[0] = after(sent[0], *feed_shares)
        got = exchange(sent, "seq")
        if layer == 1:
            z_now = add_chunks(exchange([after(t, sent[0]) for t in z_terms], "heads"))
        else:
            z_now = now["z"][0]
        gate_small, *shown_last = gate_sums(dims, layer, sc, g, now["x1"], z_now, mod)
        if layer == 1:
            shown = shown_last[0]
        feed_total = add_chunks(feed_shares)
        d_qkv, *terms = project_backward(
            dims, layer, sc, dq, got, qkv_w, cosine, sine
        )
        terms[0] = after(terms[0], feed_total)
        feed_done = owner_exchange([feed_total] * n_seq, layer)
        shares[0][layer] = feed_done
        got = exchange(terms, "heads")
        pack = weight_grads(
            [(now["att"], dy)],
            [(now["xa"], d_qkv[p]) for p in range(3)],
            n_seq,
            f"attend_grads_{layer}",
        )
        moved = to_owner(pack, layer)
        parts = add_shares(sc, pack, moved)
        got_shares = owner_exchange(parts, layer)
        if layer == 1:
            total = after(add_chunks(got), moved)
            pieces = gather(total, "heads")
            pieces[0] = after(pieces[0], *feed_done)
            pieces = pieces + [now["x"], d_mid]
        attend_done = owner_exchange([add_chunks(got_shares)] * n_seq, layer)
        shares[1][layer] = attend_done
        pending = (got_shares, attend_done)
        small[layer] = (gate_small, small_f)

    grad, normed, inv, small_a0, row_sums = last_norm(dims, sc, got, saved[0]["x"], mod)
    first_grad = last_pull(dims, sc, d_mid, grad, normed, inv, gather(row_sums, "heads"))

    def stack(layer, small_a):
        gate, mid = small[layer]
        return jnp.concatenate([small_a, mid, gate[None]], axis=0)

    by_layer = jnp.stack([stack(0, small_a0), stack(1, small_a1)])
    both = jnp.concatenate(
        [here(by_layer), swap(here(by_layer[::-1]))], axis=0
    )
    g_mod, part = modulation_grads(sc, act, mod_weight, gather(both, "seq"), n_seq)
    both = jnp.stack([part, swap(part)])
    g_first, g_second = time_backward(
        sc, sinus, inner, outer, w_time_out, gather(both, "heads")
    )

    g_reduce, g_expand = assemble(
        sc, shares[0], 1, 1, dims.hidden, dims.width, n_seq, "assemble_feed"
    )
    g_out, *g_qkv = assemble(
        sc, shares[1], 1, 3, dims.local, dims.width, n_seq, "assemble_attend"
    )
    g_qkv = jnp.stack(g_qkv, axis=1)

    def relaid(layer_0, layer_1):
        own = jnp.where(section == 0, layer_0, layer_1)
        other = swap(jnp.where(section == 0, layer_1, layer_0))
        return jnp.where(section == 0, jnp.stack([own, other]), jnp.stack([other, own]))[None]

    acts = relaid(saved[1]["x_narrow"], shown)
    grads = relaid(first_grad, middle_grad)
    return (
        acts,
        grads,
        g_first,
        g_second,
        jnp.transpose(g_mod, (1, 0, 2))[None],
        g_qkv[None],
        g_out[None],
        g_expand[None],
        g_reduce[None],
    )


def solution(mesh):
    placed = (
        P(None, "seq", "heads"),
        P(None, "seq", "heads"),
        P(),
        P(),
        P(),
        P(),
        P("section", None, None, "heads"),
        P("section", None, None, "heads"),
        P("section", "heads", None),
        P("section", None, "heads"),
        P("section", "heads", None),
    )
    return jax.shard_map(
        local_program,
        mesh=mesh,
        in_specs=placed,
        out_specs=(
            P("section", None, "seq", "heads"),
            P("section", None, "seq", "heads"),
            P(),
            P(),
            P("section", None, None, "heads"),
            P("section", None, None, "heads"),
            P("section", "heads", None),
            P("section", None, "heads"),
            P("section", "heads", None),
        ),
        check_vma=False,
    )
```

```python
import functools
import math

import jax
import jax.numpy as jnp
import numpy as np
from jax import lax
from jax.experimental import pallas as pl
from jax.experimental.pallas import tpu as pltpu
from jax.sharding import PartitionSpec as P

HEAD_DIM = 64
FREQ = 256
EPS = 1e-06
BF = jnp.bfloat16
F32 = jnp.float32
MIB = 1024 * 1024


def partner(value, axis, by):
    if by == 0:
        return value
    return lax.ppermute(value, axis, [(i, i ^ by) for i in range(lax.axis_size(axis))])


def order_of(count):
    return (3, 1, 2) if count == 4 else tuple(range(count - 1, 0, -1))


def gather(value, axis):
    count = lax.axis_size(axis)
    out = [value] * count
    for k in order_of(count):
        out[k] = partner(value, axis, k)
    return out


def exchange(chunks, axis):
    out = list(chunks)
    for k in order_of(len(chunks)):
        out[k] = partner(chunks[k], axis, k)
    return out


def swap(value):
    return lax.ppermute(value, "section", [(0, 1), (1, 0)])


def to_owner(value, layer):
    return lax.ppermute(value, "section", [(1 - layer, layer)])


def crossed(value, step):
    length = lax.axis_size("seq")
    last = length.bit_length() - 2
    pairs = []
    for c in range(2):
        by = 1 << (step if c == 0 else last - step)
        pairs += [(c * length + i, c * length + (i ^ by)) for i in range(length)]
    return lax.ppermute(value, ("section", "seq"), pairs)


def after(value, *done):
    value = lax.optimization_barrier((value, done))[0]
    return list(value) if isinstance(value, (list, tuple)) else value


def add_chunks(chunks):
    total = chunks[0].astype(F32)
    for chunk in chunks[1:]:
        total = total + chunk.astype(F32)
    return total.astype(BF)


def dot(left, right, contract=((1,), (0,))):
    return lax.dot_general(left, right, (contract, ((), ())), preferred_element_type=F32)


def split3(value):
    high = value.astype(BF)
    rest = value - high.astype(F32)
    middle = rest.astype(BF)
    low = (rest - middle.astype(F32)).astype(BF)
    return high, middle, low


def exact_dot(left, right, contract=((1,), (0,))):
    rows = left.shape[0]
    stacked = jnp.concatenate(split3(left), axis=0)
    out = dot(stacked, right, contract)
    return out[:rows] + (out[rows : 2 * rows] + out[2 * rows :])


def exact_outer(left, right):
    a = split3(left)
    b = split3(right)
    order = ((0, 0), (0, 1), (1, 0), (1, 1), (0, 2), (2, 0))
    tall = jnp.concatenate([a[i] for i, _ in order], axis=0)
    wide = jnp.concatenate([b[j] for _, j in order], axis=0)
    return dot(tall, wide, ((0,), (0,)))


def segments(sc, shape, axis, first):
    index = lax.broadcasted_iota(jnp.int32, shape, axis) + first
    return (index >= sc[3]).astype(jnp.int32) + (index >= sc[4]).astype(jnp.int32)


def spread(mod, layer, which, seg, columns=slice(None)):
    block = mod[layer * 6 + which, :, columns]
    rows = [block[u : u + 1] for u in range(3)]
    return jnp.where(seg == 0, rows[0], jnp.where(seg == 1, rows[1], rows[2]))


def utterance_sums(value, seg):
    rows = [
        jnp.sum(jnp.where(seg == u, value, 0.0), axis=0, keepdims=True) for u in range(3)
    ]
    return jnp.concatenate(rows + [jnp.zeros_like(rows[0])], axis=0)


def norm_of(value):
    mean = jnp.mean(value, axis=1, keepdims=True)
    centred = value - mean
    inv = lax.rsqrt(jnp.mean(centred * centred, axis=1, keepdims=True) + EPS)
    return centred * inv, inv


def norm_pull(grad, normed, inv):
    return inv * (
        grad
        - jnp.mean(grad, axis=1, keepdims=True)
        - normed * jnp.mean(grad * normed, axis=1, keepdims=True)
    )


def lanes_of(index, count, width):
    return pl.ds(pl.multiple_of(lax.rem(index, count) * width, width), width)


def place(buffer, chunks, own, width):
    for k, chunk in enumerate(chunks):
        at = pl.multiple_of(jnp.bitwise_xor(own, k) * width, width)
        buffer[:, pl.ds(at, width)] = chunk[...].astype(buffer.dtype)


def hand_out(outs, buffer, own, width):
    for k, out in enumerate(outs):
        at = pl.multiple_of(jnp.bitwise_xor(own, k) * width, width)
        out[...] = buffer[:, pl.ds(at, width)].astype(out.dtype)


class Fetch:
    def __init__(self, sc, layer, own, other, buffer, sem):
        self.copy = pltpu.make_async_copy(own, buffer, sem)
        other_copy = pltpu.make_async_copy(other, buffer, sem)

        @pl.when(sc[2] == layer)
        def _():
            self.copy.start()

        @pl.when(sc[2] != layer)
        def _():
            other_copy.start()

    def wait(self):
        self.copy.wait()


def turn(value, cosine, sine):
    width = value.shape[1]
    even = lax.broadcasted_iota(jnp.int32, value.shape, 1) % 2 == 0
    swapped = jnp.where(even, pltpu.roll(value, width - 1, 1), pltpu.roll(value, 1, 1))
    return value * cosine + swapped * sine


def widen_table(table, width):
    copies = width // table.shape[1]
    return jnp.concatenate([table] * copies, axis=1) if copies > 1 else table[:, :width]


VM = pl.BlockSpec(memory_space=pltpu.VMEM)
SM = pl.BlockSpec(memory_space=pltpu.SMEM)
HB = pl.BlockSpec(memory_space=pltpu.HBM)


def sds(shape, dtype):
    return jax.ShapeDtypeStruct(tuple(shape), dtype)


def call(body, ins, specs, outs, scratch=(), limit=12, name=None):
    return pl.pallas_call(
        body,
        out_shape=list(outs),
        in_specs=list(specs),
        out_specs=[VM] * len(outs),
        scratch_shapes=list(scratch),
        compiler_params=pltpu.CompilerParams(vmem_limit_bytes=limit * MIB),
        cost_estimate=pl.CostEstimate(flops=1, bytes_accessed=1, transcendentals=0),
        name=name,
    )(*ins)


def start(lengths, time_ids, time_in, time_out, mod_weight, rows):
    width = time_in.shape[1]
    kinds, _, narrow = mod_weight.shape
    half = FREQ // 2

    def body(lengths, ids, time_in, time_out, mod_weight, *refs):
        section = lax.axis_index("section")
        first_end = lengths[section, 0]
        second_end = first_end + lengths[section, 1]
        sinus_out, inner_out, outer_out, act_out, mine_out, theirs_out, cosine, sine = refs[:8]
        w_in, w_out, w_mod, sems = refs[8:]
        copies = [
            pltpu.make_async_copy(time_in, w_in, sems.at[0]),
            pltpu.make_async_copy(time_out, w_out, sems.at[1]),
            pltpu.make_async_copy(mod_weight, w_mod, sems.at[2]),
        ]
        for copy in copies:
            copy.start()
        row = lax.broadcasted_iota(jnp.int32, (8, half), 0)
        lane = lax.broadcasted_iota(jnp.int32, (8, half), 1).astype(F32)
        stamp = jnp.zeros((8, half), F32)
        for m in range(2):
            for u in range(3):
                stamp = jnp.where(row == m * 4 + u, ids[m, u].astype(F32), stamp)
        angle_t = stamp * jnp.exp(lane * (-math.log(10000.0) / (half - 1)))
        sinus = jnp.concatenate([jnp.sin(angle_t), jnp.cos(angle_t)], axis=1)
        sinus_out[...] = sinus

        index = lax.broadcasted_iota(jnp.int32, (rows, 2 * HEAD_DIM), 0)
        index = index + lax.axis_index("seq") * rows
        begin = jnp.where(
            index >= second_end, second_end, jnp.where(index >= first_end, first_end, 0)
        )
        lane = lax.broadcasted_iota(jnp.int32, (rows, 2 * HEAD_DIM), 1)
        pair = lax.broadcasted_iota(jnp.int32, (1, 2 * HEAD_DIM), 1)
        rate = jnp.exp(
            ((pair % HEAD_DIM) // 2).astype(F32) * (-2.0 * math.log(10000.0) / HEAD_DIM)
        )
        angle = (index - begin).astype(F32) * rate
        cosine[...] = jnp.cos(angle)
        sine[...] = jnp.sin(angle) * jnp.where(lane % 2 == 0, -1.0, 1.0)

        copies[0].wait()
        inner = exact_dot(sinus, w_in[...])
        inner_out[...] = inner
        hidden = inner / (1.0 + jnp.exp(-inner))
        copies[1].wait()
        outer = exact_dot(hidden, w_out[...])
        outer_out[...] = outer
        act = outer / (1.0 + jnp.exp(-outer))
        act_out[...] = act
        copies[2].wait()
        for which in range(kinds):
            modul = exact_dot(act, w_mod[which])
            mine_out[which] = jnp.where(section == 0, modul[:4], modul[4:])
            theirs_out[which] = jnp.where(section == 0, modul[4:], modul[:4])

    return call(
        body,
        [lengths, time_ids, time_in, time_out, mod_weight],
        [SM, SM, HB, HB, HB],
        [sds((8, FREQ), F32)]
        + [sds((8, width), F32)] * 3
        + [sds((kinds, 4, narrow), F32)] * 2
        + [sds((rows, 2 * HEAD_DIM), F32)] * 2,
        [
            pltpu.VMEM(time_in.shape, BF),
            pltpu.VMEM(time_out.shape, BF),
            pltpu.VMEM(mod_weight.shape, BF),
            pltpu.SemaphoreType.DMA((3,)),
        ],
        limit=56,
        name="start",
    )


def project(dims, layer, sc, pieces, mods, weights, cosine, sine):
    first = layer == 0
    rows, width, narrow, local = dims.rows, dims.width, dims.narrow, dims.local
    count = dims.n_heads
    n_in, n_mod = len(pieces), len(mods)

    def body(sc, *refs):
        pieces, mods = refs[:n_in], refs[n_in : n_in + n_mod]
        w_own, w_other, cosine, sine = refs[n_in + n_mod : n_in + n_mod + 4]
        outs = refs[n_in + n_mod + 4 :]
        x_out, narrow_out, xa_out, q_out, kv_out = outs[:5]
        if first:
            mod = outs[5]
        else:
            mod = mods[0]
        buffer, weight, sem = outs[-3:]
        fetch = Fetch(sc, layer, w_own, w_other, weight, sem)
        seg = segments(sc, (rows, 1), 0, sc[1] * rows)
        if first:
            for k in range(count):
                at = pl.multiple_of(jnp.bitwise_xor(sc[0], k) * narrow, narrow)
                block = mods[k][...]
                for l in range(2):
                    mod[l * 6 : l * 6 + 6, :, pl.ds(at, narrow)] = jnp.where(
                        sc[2] == l, block[:6], block[6:]
                    )
            place(buffer, pieces, sc[0], narrow)
            x = buffer[...]
            x_out[...] = x.astype(BF)
            narrow_out[...] = pieces[0][...]
        else:
            place(buffer, pieces[1:], sc[0], narrow)
            x = pieces[0][...] + spread(mod, 0, 5, seg) * buffer[...]
            low = x.astype(BF)
            x_out[...] = low
            x = low.astype(F32)
            buffer[...] = x
            at = pl.multiple_of(sc[0] * narrow, narrow)
            narrow_out[...] = buffer[:, pl.ds(at, narrow)].astype(BF)
        normed, _ = norm_of(x)
        xa = (normed * (1.0 + spread(mod, layer, 1, seg)) + spread(mod, layer, 0, seg)).astype(BF)
        xa_out[...] = xa
        cos = widen_table(cosine[...], local)
        sin = widen_table(sine[...], local)
        fetch.wait()
        q_out[...] = turn(dot(xa, weight[0]), cos, sin).astype(BF)
        kv_out[:, :local] = turn(dot(xa, weight[1]), cos, sin).astype(BF)
        kv_out[:, local:] = dot(xa, weight[2]).astype(BF)

    return call(
        body,
        [sc] + pieces + mods + [weights[0], weights[1], cosine, sine],
        [SM] + [VM] * (n_in + n_mod) + [HB, HB, VM, VM],
        [
            sds((rows, width), BF),
            sds((rows, narrow), BF),
            sds((rows, width), BF),
            sds((rows, local), BF),
            sds((rows, 2 * local), BF),
        ]
        + ([sds((12, 4, width), F32)] if first else []),
        [
            pltpu.VMEM((rows, width), F32),
            pltpu.VMEM(weights[0].shape, BF),
            pltpu.SemaphoreType.DMA,
        ],
        name=f"project_{layer}",
    )


def attend(dims, layer, sc, chunks, queries, weights):
    rows, n_seq, frames = dims.rows, dims.n_seq, dims.frames
    width, narrow, local, count = dims.width, dims.narrow, dims.local, dims.n_heads
    heads = local // HEAD_DIM

    def body(sc, *refs):
        chunks = refs[:n_seq]
        queries, w_own, w_other = refs[n_seq : n_seq + 3]
        kept, probs, mixed = refs[n_seq + 3 : n_seq + 6]
        outs = refs[n_seq + 6 : n_seq + 6 + count]
        weight, buffer, sem = refs[n_seq + 6 + count :]
        fetch = Fetch(sc, layer, w_own, w_other, weight, sem)
        for k in range(n_seq):
            at = pl.multiple_of(jnp.bitwise_xor(sc[1], k) * rows, rows)
            kept[pl.ds(at, rows), :] = chunks[k][...]
        same = segments(sc, (rows, 1), 0, sc[1] * rows) == segments(sc, (1, frames), 1, 0)
        for head in range(heads):
            cols = slice(head * HEAD_DIM, (head + 1) * HEAD_DIM)
            scores = dot(queries[:, cols], kept[:, cols], ((1,), (1,)))
            scores = jnp.where(same, scores * (1.0 / math.sqrt(HEAD_DIM)), -1e30)
            prob = jnp.exp(scores - jnp.max(scores, axis=1, keepdims=True))
            prob = prob * (1.0 / jnp.sum(prob, axis=1, keepdims=True))
            low = prob.astype(BF)
            probs[head] = low
            value = kept[:, local + head * HEAD_DIM : local + (head + 1) * HEAD_DIM]
            mixed[:, cols] = dot(low, value).astype(BF)
        fetch.wait()
        buffer[...] = dot(mixed[...], weight[...]).astype(BF)
        hand_out(outs, buffer, sc[0], narrow)

    return call(
        body,
        [sc] + chunks + [queries, weights[0], weights[1]],
        [SM] + [VM] * (n_seq + 1) + [HB, HB],
        [
            sds((frames, 2 * local), BF),
            sds((heads, rows, frames), BF),
            sds((rows, local), BF),
        ]
        + [sds((rows, narrow), BF)] * count,
        [
            pltpu.VMEM(weights[0].shape, BF),
            pltpu.VMEM((rows, width), BF),
            pltpu.SemaphoreType.DMA,
        ],
        name=f"attend_{layer}",
    )


def feed_forward(dims, layer, sc, x, branch, mod, up, down):
    rows, width, narrow, count, hidden = (
        dims.rows, dims.width, dims.narrow, dims.n_heads, dims.hidden,
    )

    def body(sc, x, *refs):
        branch = refs[:count]
        mod, up_own, up_other, down_own, down_other = refs[count : count + 5]
        x1_out, xf_out, h_out, slope_out = refs[count + 5 : count + 9]
        outs = refs[count + 9 : 2 * count + 9]
        up, down, buffer, low, sem_up, sem_down = refs[2 * count + 9 :]
        fetch_up = Fetch(sc, layer, up_own, up_other, up, sem_up)
        fetch_down = Fetch(sc, layer, down_own, down_other, down, sem_down)
        seg = segments(sc, (rows, 1), 0, sc[1] * rows)
        place(buffer, branch, sc[0], narrow)
        x1 = x[...].astype(F32) + spread(mod, layer, 2, seg) * buffer[...]
        x1_out[...] = x1
        normed, _ = norm_of(x1)
        xf = (normed * (1.0 + spread(mod, layer, 4, seg)) + spread(mod, layer, 3, seg)).astype(BF)
        xf_out[...] = xf
        fetch_up.wait()
        a = dot(xf, up[...])
        c0 = math.sqrt(2.0 / math.pi)
        square = a * a
        t = jnp.tanh(c0 * (a + 0.044715 * (a * square)))
        h = (0.5 * a * (1.0 + t)).astype(BF)
        h_out[...] = h
        slope_out[...] = 0.5 * (1.0 + t) + 0.5 * a * (1.0 - t * t) * (
            c0 * (1.0 + 3.0 * 0.044715 * square)
        )
        fetch_down.wait()
        low[...] = dot(h, down[...]).astype(BF)
        hand_out(outs, low, sc[0], narrow)

    return call(
        body,
        [sc, x] + branch + [mod, up[0], up[1], down[0], down[1]],
        [SM, VM] + [VM] * count + [VM, HB, HB, HB, HB],
        [
            sds((rows, width), F32),
            sds((rows, width), BF),
            sds((rows, hidden), BF),
            sds((rows, hidden), F32),
        ]
        + [sds((rows, narrow), BF)] * count,
        [
            pltpu.VMEM(up[0].shape, BF),
            pltpu.VMEM(down[0].shape, BF),
            pltpu.VMEM((rows, width), F32),
            pltpu.VMEM((rows, width), BF),
            pltpu.SemaphoreType.DMA,
            pltpu.SemaphoreType.DMA,
        ],
        name=f"feed_forward_{layer}",
    )


def feed_backward(dims, layer, sc, pieces, slope, mod, up, down):
    rows, width, narrow, count, hidden = (
        dims.rows, dims.width, dims.narrow, dims.n_heads, dims.hidden,
    )
    last = layer == 1
    n_in = len(pieces)
    n_extra = 0 if last else 2

    def body(sc, *refs):
        pieces = refs[:n_in]
        slope, mod, up_own, up_other, down_own, down_other = refs[n_in : n_in + 6]
        rest = refs[n_in + 6 :]
        g_out, dz_out, da_out = rest[:3]
        outs = rest[3 : 3 + count]
        extra = rest[3 + count : 3 + count + n_extra]
        up, down, buffer, low, other_buffer, sem_up, sem_down = rest[3 + count + n_extra :]
        fetch_down = Fetch(sc, layer, down_own, down_other, down, sem_down)
        fetch_up = Fetch(sc, layer, up_own, up_other, up, sem_up)
        seg = segments(sc, (rows, 1), 0, sc[1] * rows)
        place(buffer, pieces[:count], sc[0], narrow)
        if last:
            g = buffer[...]
            g_out[...] = g.astype(BF)
        else:
            x, d_mid = pieces[count:]
            grad_out, sums_out = extra
            dxa = buffer[...]
            normed, inv = norm_of(x[...].astype(F32))
            other_buffer[...] = dxa * normed
            mine = pl.ds(pl.multiple_of(sc[0] * narrow, narrow), narrow)
            sums_out[0] = utterance_sums(buffer[:, mine], seg)
            sums_out[1] = utterance_sums(other_buffer[:, mine], seg)
            dx = d_mid[...] + norm_pull(dxa * (1.0 + spread(mod, 1, 1, seg)), normed, inv)
            other_buffer[...] = dx
            grad_out[...] = other_buffer[:, mine]
            g = dx.astype(BF)
            g_out[...] = g
            g = g.astype(F32)
        dz = (g * spread(mod, layer, 5, seg)).astype(BF)
        dz_out[...] = dz
        fetch_down.wait()
        da = (dot(dz, down[...], ((1,), (1,))) * slope[...]).astype(BF)
        da_out[...] = da
        fetch_up.wait()
        low[...] = dot(da, up[...], ((1,), (1,))).astype(BF)
        hand_out(outs, low, sc[0], narrow)

    extra = [] if last else [sds((rows, narrow), F32), sds((2, 4, narrow), F32)]
    return call(
        body,
        [sc] + pieces + [slope, mod, up[0], up[1], down[0], down[1]],
        [SM] + [VM] * n_in + [VM, VM, HB, HB, HB, HB],
        [sds((rows, width), BF), sds((rows, width), BF), sds((rows, hidden), BF)]
        + [sds((rows, narrow), BF)] * count
        + extra,
        [
            pltpu.VMEM(up[0].shape, BF),
            pltpu.VMEM(down[0].shape, BF),
            pltpu.VMEM((rows, width), F32),
            pltpu.VMEM((rows, width), BF),
            pltpu.VMEM((rows, width), F32),
            pltpu.SemaphoreType.DMA,
            pltpu.SemaphoreType.DMA,
        ],
        name=f"feed_backward_{layer}",
    )


def middle_backward(dims, layer, sc, g, x1, sums, branch, mod, weights, queries, kept, probs, cosine, sine):
    rows, width, narrow, local, count = (
        dims.rows, dims.width, dims.narrow, dims.local, dims.n_heads,
    )
    n_seq, frames = dims.n_seq, dims.frames
    heads = local // HEAD_DIM
    scale = 1.0 / math.sqrt(HEAD_DIM)

    def body(sc, g, x1, *refs):
        sums = refs[:count]
        branch, mod, w_own, w_other, queries, kept, probs, cosine, sine = refs[count : count + 9]
        d_mid_out, dy_out, small, q_out = refs[count + 9 : count + 13]
        outs = refs[count + 13 : count + 13 + n_seq]
        weight, buffer, other, done, sem = refs[count + 13 + n_seq :]
        fetch = Fetch(sc, layer, w_own, w_other, weight, sem)
        seg = segments(sc, (rows, 1), 0, sc[1] * rows)
        mine = pl.ds(pl.multiple_of(sc[0] * narrow, narrow), narrow)
        place(buffer, sums, sc[0], narrow)
        dxf = buffer[...]
        normed, inv = norm_of(x1[...])
        other[...] = dxf * normed
        small[1] = utterance_sums(buffer[:, mine], seg)
        small[2] = utterance_sums(other[:, mine], seg)
        d_mid = g[...].astype(F32) + norm_pull(
            dxf * (1.0 + spread(mod, layer, 4, seg)), normed, inv
        )
        d_mid_out[...] = d_mid
        other[...] = d_mid
        small[0] = utterance_sums(other[:, mine] * branch[...].astype(F32), seg)
        dy = (d_mid * spread(mod, layer, 2, seg)).astype(BF)
        dy_out[...] = dy
        fetch.wait()
        d_att = dot(dy, weight[...], ((1,), (1,))).astype(BF)
        cos = cosine[:, :HEAD_DIM]
        sin = -sine[:, :HEAD_DIM]
        for head in range(heads):
            cols = slice(head * HEAD_DIM, (head + 1) * HEAD_DIM)
            vals = slice(local + head * HEAD_DIM, local + (head + 1) * HEAD_DIM)
            low = probs[head]
            prob = low.astype(F32)
            grad = d_att[:, cols]
            d_prob = dot(grad, kept[:, vals], ((1,), (1,)))
            delta = jnp.sum(d_prob * prob, axis=1, keepdims=True)
            d_score = (prob * (d_prob - delta)).astype(BF)
            dq = dot(d_score, kept[:, cols]) * scale
            q_out[:, cols] = turn(dq, cos, sin).astype(BF)
            done[:, cols] = (dot(d_score, queries[:, cols], ((0,), (0,))) * scale).astype(BF)
            done[:, vals] = dot(low, grad, ((0,), (0,))).astype(BF)
        for k in range(n_seq):
            at = pl.multiple_of(jnp.bitwise_xor(sc[1], k) * rows, rows)
            outs[k][...] = done[pl.ds(at, rows), :]

    return call(
        body,
        [sc, g, x1] + sums + [branch, mod, weights[0], weights[1], queries, kept, probs, cosine, sine],
        [SM, VM, VM] + [VM] * count + [VM, VM, HB, HB] + [VM] * 5,
        [
            sds((rows, width), F32),
            sds((rows, width), BF),
            sds((3, 4, narrow), F32),
            sds((rows, local), BF),
        ]
        + [sds((rows, 2 * local), BF)] * n_seq,
        [
            pltpu.VMEM(weights[0].shape, BF),
            pltpu.VMEM((rows, width), F32),
            pltpu.VMEM((rows, width), F32),
            pltpu.VMEM((frames, 2 * local), BF),
            pltpu.SemaphoreType.DMA,
        ],
        name=f"middle_backward_{layer}",
    )


def project_backward(dims, layer, sc, d_query, chunks, weights, cosine, sine):
    rows, width, narrow, local, count = (
        dims.rows, dims.width, dims.narrow, dims.local, dims.n_heads,
    )
    n_in = len(chunks)

    def body(sc, d_query, *refs):
        chunks = refs[:n_in]
        w_own, w_other, cosine, sine, d_out = refs[n_in : n_in + 5]
        outs = refs[n_in + 5 : n_in + 5 + count]
        weight, buffer, sem = refs[n_in + 5 + count :]
        fetch = Fetch(sc, layer, w_own, w_other, weight, sem)
        total = chunks[0][...].astype(F32)
        for chunk in chunks[1:]:
            total = total + chunk[...].astype(F32)
        cos = widen_table(cosine[...], local)
        sin = -widen_table(sine[...], local)
        dk = turn(total[:, :local], cos, sin).astype(BF)
        dv = total[:, local:].astype(BF)
        d_out[:, :local] = d_query[...]
        d_out[:, local : 2 * local] = dk
        d_out[:, 2 * local :] = dv
        fetch.wait()
        total = dot(d_query[...], weight[0], ((1,), (1,)))
        total = total + dot(dk, weight[1], ((1,), (1,)))
        total = total + dot(dv, weight[2], ((1,), (1,)))
        buffer[...] = total.astype(BF)
        hand_out(outs, buffer, sc[0], narrow)

    return call(
        body,
        [sc, d_query] + chunks + [weights[0], weights[1], cosine, sine],
        [SM, VM] + [VM] * n_in + [HB, HB, VM, VM],
        [sds((rows, 3 * local), BF)] + [sds((rows, narrow), BF)] * count,
        [
            pltpu.VMEM(weights[0].shape, BF),
            pltpu.VMEM((rows, width), BF),
            pltpu.SemaphoreType.DMA,
        ],
        name=f"project_backward_{layer}",
    )


def weight_grads(sc, tall, wide, name):
    width = tall[1].shape[1]
    local = tall[0].shape[1]
    n = 1 + wide[1].shape[1] // local

    def body(sc, left, right, wide_left, wide_right, *outs):
        first = dot(left[...], right[...], ((0,), (0,))).astype(BF)
        rest = dot(wide_left[...], wide_right[...], ((0,), (0,))).astype(BF)

        def put(out, half):
            for i in range(n // 2):
                index = half * (n // 2) + i
                at = slice(i * local, (i + 1) * local)
                if index == 0:
                    out[at, :] = first
                    continue
                columns = slice((index - 1) * local, index * local)
                for group in range(width // local):
                    rows = slice(group * local, (group + 1) * local)
                    out[at, rows] = rest[rows, columns]

        for half in range(2):

            @pl.when(sc[2] == half)
            def _(half=half):
                put(outs[0], half)
                put(outs[1], 1 - half)

    return call(
        body,
        [sc, *tall, *wide],
        [SM] + [VM] * 4,
        [sds((n // 2 * local, width), BF)] * 2,
        name=name,
    )


def add_split(sc, left, right, step):
    rows, width = left.shape
    half = rows // 2

    def body(sc, left, right, keep, send):
        bit = sc[5 + step]
        mine = pl.ds(pl.multiple_of(bit * half, half), half)
        other = pl.ds(pl.multiple_of((1 - bit) * half, half), half)
        keep[...] = (left[mine, :].astype(F32) + right[mine, :].astype(F32)).astype(BF)
        send[...] = (left[other, :].astype(F32) + right[other, :].astype(F32)).astype(BF)

    return call(
        body, [sc, left, right], [SM, VM, VM], [sds((half, width), BF)] * 2, name="add_split"
    )


def join(sc, mine, other, step):
    half, width = mine.shape

    def body(sc, mine, other, out):
        bit = sc[5 + step]
        out[pl.ds(pl.multiple_of(bit * half, half), half), :] = mine[...]
        out[pl.ds(pl.multiple_of((1 - bit) * half, half), half), :] = other[...]

    return call(
        body, [sc, mine, other], [SM, VM, VM], [sds((2 * half, width), BF)], name="join"
    )[0]


class HalfSum:
    def __init__(self, sc, layer, tall, wide, name):
        self.sc, self.layer = sc, layer
        self.mine, self.ready = weight_grads(sc, tall, wide, name)
        self.bits = lax.axis_size("seq").bit_length() - 1
        self.at = 0

    def send(self, *begin):
        value, bits = after(self.ready, *begin), self.bits
        if self.at == 0:
            self.came = swap(value)
        elif self.at <= bits:
            self.came = crossed(value, self.at - 1)
        elif self.at <= 2 * bits:
            self.came = crossed(value, 2 * bits - self.at)
        else:
            self.came = to_owner(value, self.layer)
        self.at += 1
        return self.came

    def take(self):
        sc, bits = self.sc, self.bits
        if self.at <= bits:
            self.mine, self.ready = add_split(sc, self.mine, self.came, self.at - 1)
        elif self.at == bits + 1:
            self.mine = self.ready = add_chunks([self.mine, self.came])
        else:
            self.mine = self.ready = join(sc, self.mine, self.came, 2 * bits + 1 - self.at)
        return self.ready

    def finish(self):
        while self.at < 2 * self.bits + 2:
            if self.at:
                self.take()
            self.send()
        return self.mine, self.came


def assemble(sc, halves, tall, wide, local, name):
    rows, width = halves[0][0].shape
    count = rows // local

    def body(sc, *refs):
        outs = refs[4:]

        def put(part, i, index):
            at = slice(i * local, (i + 1) * local)
            if index < tall:
                outs[index][...] = part[at, :].astype(F32)
                return
            for group in range(width // local):
                columns = slice(group * local, (group + 1) * local)
                outs[tall][index - tall, columns, :] = part[at, columns].astype(F32)

        for layer in range(2):
            own, other = refs[2 * layer], refs[2 * layer + 1]

            @pl.when(sc[2] == layer)
            def _(layer=layer, own=own, other=other):
                for i in range(count):
                    put(own, i, layer * count + i)
                    put(other, i, (1 - layer) * count + i)

    return call(
        body,
        [sc] + [half for layer in halves for half in layer],
        [SM] + [VM] * 4,
        [sds((local, width), F32)] * tall + [sds((wide, width, local), F32)],
        limit=16,
        name=name,
    )


def by_section(sc, mine, theirs, layer_0, layer_1):
    mine[...] = jnp.where(sc[2] == 0, layer_0, layer_1)
    theirs[...] = jnp.where(sc[2] == 0, layer_1, layer_0)


def gate_sums(dims, layer, sc, g, x1, z, mod, passed):
    rows, narrow = dims.rows, dims.narrow

    def body(sc, g, x1, z, mod, passed, small, *shown):
        seg = segments(sc, (rows, 1), 0, sc[1] * rows)
        mine = pl.ds(pl.multiple_of(sc[0] * narrow, narrow), narrow)
        value = z[...].astype(F32)
        small[...] = utterance_sums(g[:, mine].astype(F32) * value, seg)
        if shown:
            gate = spread(mod, layer, 5, seg, mine)
            result = (x1[:, mine] + gate * value).astype(BF)
            by_section(sc, *shown, passed[...], result)

    outs = [sds((4, narrow), F32)]
    if layer == 1:
        outs += [sds((rows, narrow), BF)] * 2
    return call(
        body, [sc, g, x1, z, mod, passed], [SM] + [VM] * 5, outs, name=f"gate_sums_{layer}"
    )


def last_norm(dims, sc, terms, x, mod, small_0, small_1):
    rows, narrow, count = dims.rows, dims.narrow, dims.n_heads

    def body(sc, *refs):
        terms = refs[:count]
        x, mod, mid_0, gate_0, in_1, mid_1, gate_1 = refs[count : count + 7]
        total_out, normed_out, inv_out, mine_out, theirs_out, rows_out, buffer = refs[count + 7 :]
        seg = segments(sc, (rows, 1), 0, sc[1] * rows)
        mine = pl.ds(pl.multiple_of(sc[0] * narrow, narrow), narrow)
        total = terms[0][...].astype(F32)
        for term in terms[1:]:
            total = total + term[...].astype(F32)
        normed, inv = norm_of(x[...].astype(F32))
        buffer[...] = normed
        normed = buffer[:, mine]
        first = (
            [utterance_sums(total, seg), utterance_sums(total * normed, seg)]
            + [mid_0[i] for i in range(3)]
            + [gate_0[...]]
        )
        second = [in_1[0], in_1[1]] + [mid_1[i] for i in range(3)] + [gate_1[...]]
        for i in range(6):
            by_section(sc, mine_out.at[i], theirs_out.at[i], first[i], second[i])
        grad = total * (1.0 + spread(mod, 0, 1, seg, mine))
        total_out[...] = grad
        normed_out[...] = normed
        inv_out[...] = inv
        rows_out[...] = jnp.concatenate(
            [jnp.sum(grad, axis=1, keepdims=True), jnp.sum(grad * normed, axis=1, keepdims=True)],
            axis=1,
        )

    return call(
        body,
        [sc] + terms + [x, mod] + small_0 + small_1,
        [SM] + [VM] * (count + 7),
        [
            sds((rows, narrow), F32),
            sds((rows, narrow), F32),
            sds((rows, 1), F32),
            sds((6, 4, narrow), F32),
            sds((6, 4, narrow), F32),
            sds((rows, 2), F32),
        ],
        [pltpu.VMEM((rows, dims.width), F32)],
        name="last_norm",
    )


def last_pull(dims, sc, d_mid, grad, normed, inv, sums, middle_grad):
    rows, narrow, count, width = dims.rows, dims.narrow, dims.n_heads, dims.width

    def body(sc, d_mid, grad, normed, inv, middle, *refs):
        sums, outs = refs[:count], refs[count:]
        total = sums[0][...]
        for term in sums[1:]:
            total = total + term[...]
        total = total * (1.0 / width)
        mine = pl.ds(pl.multiple_of(sc[0] * narrow, narrow), narrow)
        first = d_mid[:, mine] + inv[...] * (
            grad[...] - total[:, 0:1] - normed[...] * total[:, 1:2]
        )
        by_section(sc, *outs, first, middle[...])

    return call(
        body,
        [sc, d_mid, grad, normed, inv, middle_grad] + sums,
        [SM] + [VM] * (5 + count),
        [sds((rows, narrow), F32)] * 2,
        name="last_pull",
    )


def modulation_grads(sc, act, mod_weight, own, n_seq):
    kinds, width, narrow = mod_weight.shape

    def body(sc, act, mod_weight, *refs):
        own = refs[:n_seq]
        g_mod, part, box, weight, sem = refs[n_seq:]
        copy = pltpu.make_async_copy(mod_weight, weight, sem)
        copy.start()
        for k in range(n_seq):
            box[jnp.bitwise_xor(sc[1], k)] = own[k][...]
        total = box[0]
        for j in range(1, n_seq):
            total = total + box[j]
        act_now = act[...]
        grads = []
        for which in range(kinds):
            mine, theirs = total[which], total[kinds + which]
            grads.append(
                jnp.concatenate(
                    [jnp.where(sc[2] == 0, mine, theirs), jnp.where(sc[2] == 0, theirs, mine)],
                    axis=0,
                )
            )
        copy.wait()
        result = jnp.zeros((8, width), F32)
        for which in range(kinds):
            result = result + exact_dot(grads[which], weight[which], ((1,), (1,)))
        part[...] = result
        for which in range(kinds):
            g_mod[which] = exact_outer(act_now, grads[which])

    return call(
        body,
        [sc, act, mod_weight] + own,
        [SM, VM, HB] + [VM] * n_seq,
        [sds((kinds, width, narrow), F32), sds((8, width), F32)],
        [
            pltpu.VMEM((n_seq, 2 * kinds, 4, narrow), F32),
            pltpu.VMEM(mod_weight.shape, BF),
            pltpu.SemaphoreType.DMA,
        ],
        name="modulation_grads",
    )


def time_backward(sc, sinus, inner, outer, time_out, own):
    count = len(own)
    rows, width = inner.shape

    def body(sc, sinus, inner, outer, time_out, *refs):
        own = refs[:count]
        g_in, g_out, box, weight, sem = refs[count:]
        copy = pltpu.make_async_copy(time_out, weight, sem)
        copy.start()
        for k in range(count):
            at = jnp.bitwise_xor(sc[0], k)
            box[at, sc[2]] = own[k][0]
            box[at, 1 - sc[2]] = own[k][1]
        total = jnp.zeros((rows, width), F32)
        for j in range(count):
            for c in range(2):
                total = total + box[j, c]

        def slope(value):
            gate = 1.0 / (1.0 + jnp.exp(-value))
            return gate * (1.0 + value * (1.0 - gate))

        pre = inner[...]
        hidden = pre / (1.0 + jnp.exp(-pre))
        d_outer = total * slope(outer[...])
        g_out[...] = exact_outer(hidden, d_outer)
        copy.wait()
        d_inner = exact_dot(d_outer, weight[...], ((1,), (1,))) * slope(pre)
        g_in[...] = exact_outer(sinus[...], d_inner)

    return call(
        body,
        [sc, sinus, inner, outer, time_out] + own,
        [SM, VM, VM, VM, HB] + [VM] * count,
        [sds((sinus.shape[1], width), F32), sds((width, width), F32)],
        [
            pltpu.VMEM((count, 2, rows, width), F32),
            pltpu.VMEM(time_out.shape, BF),
            pltpu.SemaphoreType.DMA,
        ],
        name="time_backward",
    )


class Dims:
    pass


def local_program(
    frames,
    cotangent,
    utt_lengths,
    time_ids,
    w_time_in,
    w_time_out,
    w_mod,
    w_qkv,
    w_out,
    w_up,
    w_down,
):
    dims = Dims()
    dims.n_heads = lax.axis_size("heads")
    dims.n_seq = n_seq = lax.axis_size("seq")
    _, dims.rows, dims.narrow = frames.shape
    dims.width = dims.narrow * dims.n_heads
    dims.local = w_qkv.shape[3]
    dims.hidden = w_up.shape[2]
    dims.frames = dims.rows * n_seq
    section = lax.axis_index("section")
    at_seq = lax.axis_index("seq")
    bits = n_seq.bit_length() - 1

    def here(both):
        return lax.dynamic_index_in_dim(both, section, 0, keepdims=False)

    lengths = here(utt_lengths)
    sc = jnp.stack(
        [
            lax.axis_index("heads"),
            at_seq,
            section,
            lengths[0],
            lengths[0] + lengths[1],
        ]
        + [
            jnp.where(section == 0, at_seq >> bit, at_seq >> (bits - 1 - bit)) & 1
            for bit in range(bits)
        ]
    ).astype(jnp.int32)

    qkv = jnp.transpose(w_qkv[0], (1, 0, 2))
    mod_weight = jnp.transpose(w_mod[0], (1, 0, 2))
    wide_frames = gather(here(frames), "heads")
    qkv_w = (qkv, swap(qkv))
    sinus, inner, outer, act, mod_mine, mod_theirs, cosine, sine = start(
        utt_lengths, time_ids, w_time_in, w_time_out, mod_weight, dims.rows
    )
    mod_theirs = swap(after(mod_theirs, *wide_frames))
    mods = gather(jnp.concatenate([mod_mine, mod_theirs], axis=0), "heads")

    saved = []
    mod = None
    pieces = wide_frames
    for layer in range(2):
        x, x_narrow, xa, q, kv, *rest = project(
            dims, layer, sc, pieces, mods if layer == 0 else [mod], qkv_w, cosine, sine
        )
        chunks = gather(kv, "seq")
        if layer == 0:
            mod = rest[0]
            out_w = (w_out[0], swap(after(w_out[0], kv)))
        else:
            wide_cotangent = gather(after(here(cotangent), chunks[1]), "heads")
        kept, probs, att, *terms = attend(dims, layer, sc, chunks, q, out_w)
        if layer == 0:
            up_w, down_w = [(w[0], swap(after(w[0], att))) for w in (w_up, w_down)]
        else:
            terms[0] = after(terms[0], *wide_cotangent)
        branch = gather(add_chunks(exchange(terms, "heads")), "heads")
        x1, xf, h, slope, *terms = feed_forward(dims, layer, sc, x, branch, mod, up_w, down_w)
        z = None
        if layer == 0:
            z = gather(add_chunks(exchange(terms, "heads")), "heads")
            pieces = [x1] + z
        saved.append(
            dict(x=x, x_narrow=x_narrow, xa=xa, kept=kept, probs=probs, q=q, att=att,
                 branch=branch[0], x1=x1, xf=xf, h=h, slope=slope, z=z)
        )
    z_terms = terms

    small = [None, None]
    pieces = wide_cotangent

    def feed_pairs(now, dz, da):
        return (now["h"], dz), (now["xf"], da)

    def attention_pairs(now, dy, d_qkv):
        return (now["att"], dy), (now["xa"], d_qkv)

    now = saved[1]
    g, dz, da, *terms = feed_backward(dims, 1, sc, pieces, now["slope"], mod, up_w, down_w)
    got = exchange(terms, "heads")
    feed_1 = HalfSum(sc, 1, *feed_pairs(now, dz, da), "feed_grads_1")
    total = after(add_chunks(got), feed_1.mine, feed_1.ready)

    feed_1.send(total)
    sums = after(gather(total, "heads"), feed_1.came)
    d_mid_1, dy, small_f, dq, *sent = middle_backward(
        dims, 1, sc, g, now["x1"], sums, now["branch"], mod, out_w,
        now["q"], now["kept"], now["probs"], cosine, sine,
    )

    got = exchange(sent, "seq")
    feed_1.take()
    z_now = add_chunks(exchange(after(z_terms, sent[0]), "heads"))
    gate_small, *acts = gate_sums(dims, 1, sc, g, now["x1"], z_now, mod, now["x_narrow"])
    got = after(got, feed_1.mine, feed_1.ready, *acts)
    acts[1] = swap(after(acts[1], got[0]))
    d_qkv, *terms = project_backward(dims, 1, sc, dq, got, qkv_w, cosine, sine)
    small[1] = [small_f, gate_small]

    got = exchange(terms, "heads")
    feed_1.send(terms[0])
    attention_1 = HalfSum(sc, 1, *attention_pairs(now, dy, d_qkv), "attend_grads_1")
    total = after(add_chunks(got), feed_1.came, attention_1.mine, attention_1.ready)

    feed_1.take()
    feed_1.send(total)
    attention_1.send(total)
    pieces = after(gather(total, "heads"), feed_1.came, attention_1.came)

    now = saved[0]
    g, dz, da, *rest = feed_backward(
        dims, 0, sc, pieces + [saved[1]["x"], d_mid_1], now["slope"], mod, up_w, down_w
    )
    terms, (middle_grad, small_a1) = rest[: dims.n_heads], rest[dims.n_heads :]
    got = exchange(terms, "heads")
    feed_1.take()
    feed_1.send(terms[0])
    attention_1.take()
    attention_1.send(terms[0])
    feed_0 = HalfSum(sc, 0, *feed_pairs(now, dz, da), "feed_grads_0")
    total = after(
        add_chunks(got), feed_1.came, attention_1.came, feed_0.mine, feed_0.ready
    )

    feed_1.take()
    feed_1.send(total)
    attention_1.take()
    attention_1.send(total)
    sums = after(gather(total, "heads"), feed_1.came, attention_1.came)
    d_mid, dy, small_f, dq, *sent = middle_backward(
        dims, 0, sc, g, now["x1"], sums, now["branch"], mod, out_w,
        now["q"], now["kept"], now["probs"], cosine, sine,
    )

    got = exchange(sent, "seq")
    feed_0.send(sent[0])
    attention_1.take()
    gate_small, *_ = gate_sums(dims, 0, sc, g, now["x1"], now["z"][0], mod, now["x_narrow"])
    got = after(got, feed_0.came, attention_1.ready, gate_small)
    d_qkv, *terms = project_backward(dims, 0, sc, dq, got, qkv_w, cosine, sine)
    small[0] = [small_f, gate_small]

    got = exchange(terms, "heads")
    feed_0.take()
    feed_0.send(terms[0])
    attention_1.send(terms[0])
    attention_0 = HalfSum(sc, 0, *attention_pairs(now, dy, d_qkv), "attend_grads_0")
    got = after(got, feed_0.came, attention_1.came, attention_0.ready, attention_0.mine)

    grad, normed, inv, mine, theirs, row_sums = last_norm(
        dims, sc, got, saved[0]["x"], mod, small[0], [small_a1] + small[1]
    )
    attention_0.send(row_sums)
    theirs = after(swap(theirs), attention_0.came)
    both = jnp.concatenate([mine, theirs], axis=0)
    attention_0.take()
    attention_0.send(theirs)
    feed_0.take()
    feed_0.send(theirs)
    both = after(gather(both, "seq"), attention_0.came, feed_0.came)
    attention_0.take()
    attention_0.send(both[0])
    feed_0.take()
    feed_0.send(both[0])
    row_sums = gather(after(row_sums, both[0]), "heads")
    g_mod, part = modulation_grads(sc, act, mod_weight, both, n_seq)
    part = after(part, attention_0.came, feed_0.came, *row_sums)
    grads = last_pull(dims, sc, d_mid, grad, normed, inv, row_sums, middle_grad)
    both = jnp.stack([part, swap(part)])
    attention_0.take()
    attention_0.send(part)
    feed_0.take()
    feed_0.send(part)
    both = after(gather(both, "heads"), attention_0.came, feed_0.came, *grads)
    attention_0.take()
    attention_0.send(both[0])
    attention_1.take()
    attention_1.send(both[0])
    feed_0.take()
    feed_0.send(both[0])
    grads = [grads[0], swap(grads[1])]
    g_first, g_second = time_backward(sc, sinus, inner, outer, w_time_out, both)
    attention_0.take()
    g_second = after(g_second, attention_0.ready, attention_1.came, feed_0.came, grads[1])
    attention_0.send(g_second)
    g_reduce, g_expand = assemble(
        sc, [feed_0.finish(), feed_1.finish()], 1, 1, dims.hidden, "assemble_feed"
    )
    attention_0.came = after(attention_0.came, g_reduce)
    g_out, g_qkv = assemble(
        sc, [attention_0.finish(), attention_1.finish()], 1, 3, dims.local, "assemble_attend"
    )

    def relaid(own, other):
        return jnp.where(section == 0, jnp.stack([own, other]), jnp.stack([other, own]))[None]

    return (
        relaid(*acts),
        relaid(*grads),
        g_first,
        g_second,
        jnp.transpose(g_mod, (1, 0, 2))[None],
        jnp.transpose(g_qkv, (1, 0, 2))[None],
        g_out[None],
        g_expand,
        g_reduce[None],
    )


def solution(mesh):
    placed = (
        P(None, "seq", "heads"),
        P(None, "seq", "heads"),
        P(),
        P(),
        P(),
        P(),
        P("section", None, None, "heads"),
        P("section", None, None, "heads"),
        P("section", "heads", None),
        P("section", None, "heads"),
        P("section", "heads", None),
    )
    return jax.shard_map(
        local_program,
        mesh=mesh,
        in_specs=placed,
        out_specs=(
            P("section", None, "seq", "heads"),
            P("section", None, "seq", "heads"),
            P(),
            P(),
            P("section", None, None, "heads"),
            P("section", None, None, "heads"),
            P("section", "heads", None),
            P("section", None, "heads"),
            P("section", "heads", None),
        ),
        check_vma=False,
    )
```

```python
import functools
import math

import jax
import jax.numpy as jnp
import numpy as np
from jax import lax
from jax.experimental import pallas as pl
from jax.experimental.pallas import tpu as pltpu
from jax.sharding import PartitionSpec as P

HEAD_DIM = 64
FREQ = 256
EPS = 1e-06
BF = jnp.bfloat16
F32 = jnp.float32
MIB = 1024 * 1024


def partner(value, axis, by):
    if by == 0:
        return value
    return lax.ppermute(value, axis, [(i, i ^ by) for i in range(lax.axis_size(axis))])


def order_of(count):
    return (3, 1, 2) if count == 4 else tuple(range(count - 1, 0, -1))


def gather(value, axis):
    count = lax.axis_size(axis)
    out = [value] * count
    for k in order_of(count):
        out[k] = partner(value, axis, k)
    return out


def exchange(chunks, axis):
    out = list(chunks)
    for k in order_of(len(chunks)):
        out[k] = partner(chunks[k], axis, k)
    return out


def swap(value):
    return lax.ppermute(value, "section", [(0, 1), (1, 0)])


def to_owner(value, layer):
    return lax.ppermute(value, "section", [(1 - layer, layer)])


def crossed(value, step):
    length = lax.axis_size("seq")
    last = length.bit_length() - 2
    pairs = []
    for c in range(2):
        by = 1 << (step if c == 0 else last - step)
        pairs += [(c * length + i, c * length + (i ^ by)) for i in range(length)]
    return lax.ppermute(value, ("section", "seq"), pairs)


def after(value, *done):
    value = lax.optimization_barrier((value, done))[0]
    return list(value) if isinstance(value, (list, tuple)) else value


def add_chunks(chunks):
    total = chunks[0].astype(F32)
    for chunk in chunks[1:]:
        total = total + chunk.astype(F32)
    return total.astype(BF)


def dot(left, right, contract=((1,), (0,))):
    return lax.dot_general(left, right, (contract, ((), ())), preferred_element_type=F32)


def split3(value):
    high = value.astype(BF)
    rest = value - high.astype(F32)
    middle = rest.astype(BF)
    low = (rest - middle.astype(F32)).astype(BF)
    return high, middle, low


def diagonal(rows, columns):
    row = lax.broadcasted_iota(jnp.int32, (rows, columns), 0)
    return (row == lax.broadcasted_iota(jnp.int32, (rows, columns), 1)).astype(BF)


def exact_dot(left, right, contract=((1,), (0,))):
    rows = left.shape[0]
    stacked = jnp.concatenate(split3(left), axis=0)
    out = dot(stacked, right, contract)
    return out[:rows] + (out[rows : 2 * rows] + out[2 * rows :])


def exact_outer(left, right):
    tall, wide = outer_parts(left, right)
    return dot(tall, wide, ((0,), (0,)))


def outer_parts(left, right):
    a, b = split3(left), split3(right)
    tall = jnp.concatenate([a[0], a[0], a[1]], axis=0)
    wide = jnp.concatenate([b[0], b[1], b[0]], axis=0)
    return tall, wide


def segments(sc, shape, axis, first):
    index = lax.broadcasted_iota(jnp.int32, shape, axis) + first
    return (index >= sc[3]).astype(jnp.int32) + (index >= sc[4]).astype(jnp.int32)


def spread(mod, layer, which, seg, columns=slice(None)):
    block = mod[layer * 6 + which, :, columns]
    rows = [block[u : u + 1] for u in range(3)]
    return jnp.where(seg == 0, rows[0], jnp.where(seg == 1, rows[1], rows[2]))


def utterance_sums(value, seg):
    rows = [
        jnp.sum(jnp.where(seg == u, value, 0.0), axis=0, keepdims=True) for u in range(3)
    ]
    return jnp.concatenate(rows + [jnp.zeros_like(rows[0])], axis=0)


def norm_of(value):
    mean = jnp.mean(value, axis=1, keepdims=True)
    centred = value - mean
    inv = lax.rsqrt(jnp.mean(centred * centred, axis=1, keepdims=True) + EPS)
    return centred * inv, inv


def norm_pull(grad, normed, inv):
    return inv * (
        grad
        - jnp.mean(grad, axis=1, keepdims=True)
        - normed * jnp.mean(grad * normed, axis=1, keepdims=True)
    )


def lanes_of(index, count, width):
    return pl.ds(pl.multiple_of(lax.rem(index, count) * width, width), width)


def place(buffer, chunks, own, width):
    for k, chunk in enumerate(chunks):
        at = pl.multiple_of(jnp.bitwise_xor(own, k) * width, width)
        buffer[:, pl.ds(at, width)] = chunk[...].astype(buffer.dtype)


def hand_out(outs, buffer, own, width):
    for k, out in enumerate(outs):
        at = pl.multiple_of(jnp.bitwise_xor(own, k) * width, width)
        out[...] = buffer[:, pl.ds(at, width)].astype(out.dtype)


class Fetch:
    def __init__(self, sc, layer, own, other, buffer, sem):
        self.copy = pltpu.make_async_copy(own, buffer, sem)
        other_copy = pltpu.make_async_copy(other, buffer, sem)

        @pl.when(sc[2] == layer)
        def _():
            self.copy.start()

        @pl.when(sc[2] != layer)
        def _():
            other_copy.start()

    def wait(self):
        self.copy.wait()


def turn(value, cosine, sine):
    width = value.shape[1]
    even = lax.broadcasted_iota(jnp.int32, value.shape, 1) % 2 == 0
    swapped = jnp.where(even, pltpu.roll(value, width - 1, 1), pltpu.roll(value, 1, 1))
    return value * cosine + swapped * sine


def widen_table(table, width):
    copies = width // table.shape[1]
    return jnp.concatenate([table] * copies, axis=1) if copies > 1 else table[:, :width]


VM = pl.BlockSpec(memory_space=pltpu.VMEM)
SM = pl.BlockSpec(memory_space=pltpu.SMEM)
HB = pl.BlockSpec(memory_space=pltpu.HBM)


def sds(shape, dtype):
    return jax.ShapeDtypeStruct(tuple(shape), dtype)


class Place:
    def __init__(self, lengths):
        self.lengths = lengths
        self.known = {}
        for index in range(5):
            self[index]

    def __getitem__(self, index):
        if index not in self.known:
            self.known[index] = self.find(index)
        return self.known[index]

    def find(self, index):
        if index < 3:
            return lax.axis_index(("heads", "seq", "section")[index])
        if index == 3:
            return self.lengths[self[2], 0]
        if index == 4:
            return self[3] + self.lengths[self[2], 1]
        low = index - 5
        high = lax.axis_size("seq").bit_length() - 2 - low
        return jnp.where(self[2] == 0, self[1] >> low, self[1] >> high) & 1


def call(body, ins, specs, outs, scratch=(), limit=12, name=None, out_space=None):
    def placed(lengths, *refs):
        body(Place(lengths), *refs)

    return pl.pallas_call(
        placed,
        out_shape=list(outs),
        in_specs=list(specs),
        out_specs=[out_space or VM] * len(outs),
        scratch_shapes=list(scratch),
        compiler_params=pltpu.CompilerParams(vmem_limit_bytes=limit * MIB),
        cost_estimate=pl.CostEstimate(flops=1, bytes_accessed=1, transcendentals=0),
        name=name,
    )(*ins)


def start(sc, time_ids, time_in, time_out, mod_weight):
    width = time_in.shape[1]
    kinds, _, narrow = mod_weight.shape
    half = FREQ // 2

    def body(sc, ids, time_in, time_out, mod_weight, *refs):
        sinus_out, inner_out, outer_out, act_out, mine_out, theirs_out = refs[:6]
        w_in, w_out, w_mod, sems = refs[6:]
        copies = [
            pltpu.make_async_copy(time_in, w_in, sems.at[0]),
            pltpu.make_async_copy(time_out, w_out, sems.at[1]),
            pltpu.make_async_copy(mod_weight, w_mod, sems.at[2]),
        ]
        for copy in copies:
            copy.start()
        row = lax.broadcasted_iota(jnp.int32, (8, half), 0)
        lane = lax.broadcasted_iota(jnp.int32, (8, half), 1).astype(F32)
        stamp = jnp.zeros((8, half), F32)
        for m in range(2):
            for u in range(3):
                stamp = jnp.where(row == m * 4 + u, ids[m, u].astype(F32), stamp)
        angle_t = stamp * jnp.exp(lane * (-math.log(10000.0) / (half - 1)))
        sinus = jnp.concatenate([jnp.sin(angle_t), jnp.cos(angle_t)], axis=1)
        sinus_out[...] = sinus

        copies[0].wait()
        inner = exact_dot(sinus, w_in[...])
        inner_out[...] = inner
        hidden = inner / (1.0 + jnp.exp(-inner))
        copies[1].wait()
        outer = exact_dot(hidden, w_out[...])
        outer_out[...] = outer
        act = outer / (1.0 + jnp.exp(-outer))
        act_out[...] = act
        copies[2].wait()
        for which in range(kinds):
            modul = exact_dot(act, w_mod[which])
            mine_out[which] = jnp.where(sc[2] == 0, modul[:4], modul[4:])
            theirs_out[which] = jnp.where(sc[2] == 0, modul[4:], modul[:4])

    return call(
        body,
        [sc, time_ids, time_in, time_out, mod_weight],
        [SM, SM, HB, HB, HB],
        [sds((8, FREQ), F32)]
        + [sds((8, width), F32)] * 3
        + [sds((kinds, 4, narrow), F32)] * 2,
        [
            pltpu.VMEM(time_in.shape, BF),
            pltpu.VMEM(time_out.shape, BF),
            pltpu.VMEM(mod_weight.shape, BF),
            pltpu.SemaphoreType.DMA((3,)),
        ],
        limit=56,
        name="start",
    )


def tables(sc, rows):
    def body(sc, cosine, sine):
        index = lax.broadcasted_iota(jnp.int32, (rows, 2 * HEAD_DIM), 0) + sc[1] * rows
        begin = jnp.where(index >= sc[4], sc[4], jnp.where(index >= sc[3], sc[3], 0))
        lane = lax.broadcasted_iota(jnp.int32, (rows, 2 * HEAD_DIM), 1)
        pair = lax.broadcasted_iota(jnp.int32, (1, 2 * HEAD_DIM), 1)
        rate = jnp.exp(
            ((pair % HEAD_DIM) // 2).astype(F32) * (-2.0 * math.log(10000.0) / HEAD_DIM)
        )
        angle = (index - begin).astype(F32) * rate
        cosine[...] = jnp.cos(angle)
        sine[...] = jnp.sin(angle) * jnp.where(lane % 2 == 0, -1.0, 1.0)

    return call(body, [sc], [SM], [sds((rows, 2 * HEAD_DIM), F32)] * 2, name="tables")


def project(dims, layer, sc, pieces, mods, weights, cosine, sine):
    first = layer == 0
    rows, width, narrow, local = dims.rows, dims.width, dims.narrow, dims.local
    count = dims.n_heads
    n_in, n_mod = len(pieces), len(mods)

    def body(sc, *refs):
        pieces, mods = refs[:n_in], refs[n_in : n_in + n_mod]
        w_own, w_other, cosine, sine = refs[n_in + n_mod : n_in + n_mod + 4]
        outs = refs[n_in + n_mod + 4 :]
        x_out, narrow_out, xa_out, q_out, kv_out = outs[:5]
        if first:
            mod = outs[5]
        else:
            mod = mods[0]
        buffer, weight, sem = outs[-3:]
        fetch = Fetch(sc, layer, w_own, w_other, weight, sem)
        seg = segments(sc, (rows, 1), 0, sc[1] * rows)
        if first:
            for k in range(count):
                at = pl.multiple_of(jnp.bitwise_xor(sc[0], k) * narrow, narrow)
                block = mods[k][...]
                for l in range(2):
                    mod[l * 6 : l * 6 + 6, :, pl.ds(at, narrow)] = jnp.where(
                        sc[2] == l, block[:6], block[6:]
                    )
            place(buffer, pieces, sc[0], narrow)
            x = buffer[...]
            x_out[...] = x.astype(BF)
            narrow_out[...] = pieces[0][...]
        else:
            place(buffer, pieces[1:], sc[0], narrow)
            x = pieces[0][...] + spread(mod, 0, 5, seg) * buffer[...]
            low = x.astype(BF)
            x_out[...] = low
            x = low.astype(F32)
            buffer[...] = x
            at = pl.multiple_of(sc[0] * narrow, narrow)
            narrow_out[...] = buffer[:, pl.ds(at, narrow)].astype(BF)
        normed, _ = norm_of(x)
        xa = (normed * (1.0 + spread(mod, layer, 1, seg)) + spread(mod, layer, 0, seg)).astype(BF)
        xa_out[...] = xa
        cos = widen_table(cosine[...], local)
        sin = widen_table(sine[...], local)
        fetch.wait()
        q_out[...] = turn(dot(xa, weight[0]), cos, sin).astype(BF)
        kv_out[:, :local] = turn(dot(xa, weight[1]), cos, sin).astype(BF)
        kv_out[:, local:] = dot(xa, weight[2]).astype(BF)

    return call(
        body,
        [sc] + pieces + mods + [weights[0], weights[1], cosine, sine],
        [SM] + [VM] * (n_in + n_mod) + [HB, HB, VM, VM],
        [
            sds((rows, width), BF),
            sds((rows, narrow), BF),
            sds((rows, width), BF),
            sds((rows, local), BF),
            sds((rows, 2 * local), BF),
        ]
        + ([sds((12, 4, width), F32)] if first else []),
        [
            pltpu.VMEM((rows, width), F32),
            pltpu.VMEM(weights[0].shape, BF),
            pltpu.SemaphoreType.DMA,
        ],
        name=f"project_{layer}",
    )


def attend(dims, layer, sc, chunks, queries, xa, weights):
    rows, n_seq, frames = dims.rows, dims.n_seq, dims.frames
    width, narrow, local, count = dims.width, dims.narrow, dims.local, dims.n_heads
    heads = local // HEAD_DIM

    def body(sc, *refs):
        chunks = refs[:n_seq]
        queries, xa, w_own, w_other = refs[n_seq : n_seq + 4]
        kept, probs, for_grads, exact = refs[n_seq + 4 : n_seq + 8]
        outs = refs[n_seq + 8 : n_seq + 8 + count]
        weight, buffer, sem = refs[n_seq + 8 + count :]
        fetch = Fetch(sc, layer, w_own, w_other, weight, sem)
        for k in range(n_seq):
            at = pl.multiple_of(jnp.bitwise_xor(sc[1], k) * rows, rows)
            kept[pl.ds(at, rows), :] = chunks[k][...]
        same = segments(sc, (rows, 1), 0, sc[1] * rows) == segments(sc, (1, frames), 1, 0)
        for head in range(heads):
            cols = slice(head * HEAD_DIM, (head + 1) * HEAD_DIM)
            scores = dot(queries[:, cols], kept[:, cols], ((1,), (1,)))
            scores = jnp.where(same, scores * (1.0 / math.sqrt(HEAD_DIM)), -1e30)
            prob = jnp.exp(scores - jnp.max(scores, axis=1, keepdims=True))
            prob = prob * (1.0 / jnp.sum(prob, axis=1, keepdims=True))
            low = prob.astype(BF)
            probs[head] = low
            value = kept[:, local + head * HEAD_DIM : local + (head + 1) * HEAD_DIM]
            exact[:, cols] = dot(low, value)
        mixed = exact[...].astype(BF)
        for_grads[:, :local] = mixed
        for_grads[:, local:] = xa[...]
        fetch.wait()
        buffer[...] = dot(mixed, weight[...]).astype(BF)
        hand_out(outs, buffer, sc[0], narrow)

    return call(
        body,
        [sc] + chunks + [queries, xa, weights[0], weights[1]],
        [SM] + [VM] * (n_seq + 2) + [HB, HB],
        [
            sds((frames, 2 * local), BF),
            sds((heads, rows, frames), BF),
            sds((rows, local + width), BF),
            sds((rows, local), F32),
        ]
        + [sds((rows, narrow), BF)] * count,
        [
            pltpu.VMEM(weights[0].shape, BF),
            pltpu.VMEM((rows, width), BF),
            pltpu.SemaphoreType.DMA,
        ],
        name=f"attend_{layer}",
    )


def feed_forward(dims, layer, sc, x, branch, mod, up, down):
    rows, width, narrow, count, hidden = (
        dims.rows, dims.width, dims.narrow, dims.n_heads, dims.hidden,
    )

    def body(sc, x, *refs):
        branch = refs[:count]
        mod, up_own, up_other, down_own, down_other = refs[count : count + 5]
        x1_out, for_grads, slope_out = refs[count + 5 : count + 8]
        outs = refs[count + 8 : 2 * count + 8]
        up, down, buffer, low, sem_up, sem_down = refs[2 * count + 8 :]
        fetch_up = Fetch(sc, layer, up_own, up_other, up, sem_up)
        fetch_down = Fetch(sc, layer, down_own, down_other, down, sem_down)
        seg = segments(sc, (rows, 1), 0, sc[1] * rows)
        place(buffer, branch, sc[0], narrow)
        x1 = x[...].astype(F32) + spread(mod, layer, 2, seg) * buffer[...]
        x1_out[...] = x1
        normed, _ = norm_of(x1)
        xf = (normed * (1.0 + spread(mod, layer, 4, seg)) + spread(mod, layer, 3, seg)).astype(BF)
        for_grads[:, hidden:] = xf
        fetch_up.wait()
        a = dot(xf, up[...])
        c0 = math.sqrt(2.0 / math.pi)
        square = a * a
        t = jnp.tanh(c0 * (a + 0.044715 * (a * square)))
        h = (0.5 * a * (1.0 + t)).astype(BF)
        for_grads[:, :hidden] = h
        slope_out[...] = 0.5 * (1.0 + t) + 0.5 * a * (1.0 - t * t) * (
            c0 * (1.0 + 3.0 * 0.044715 * square)
        )
        fetch_down.wait()
        low[...] = dot(h, down[...]).astype(BF)
        hand_out(outs, low, sc[0], narrow)

    return call(
        body,
        [sc, x] + branch + [mod, up[0], up[1], down[0], down[1]],
        [SM, VM] + [VM] * count + [VM, HB, HB, HB, HB],
        [
            sds((rows, width), F32),
            sds((rows, hidden + width), BF),
            sds((rows, hidden), F32),
        ]
        + [sds((rows, narrow), BF)] * count,
        [
            pltpu.VMEM(up[0].shape, BF),
            pltpu.VMEM(down[0].shape, BF),
            pltpu.VMEM((rows, width), F32),
            pltpu.VMEM((rows, width), BF),
            pltpu.SemaphoreType.DMA,
            pltpu.SemaphoreType.DMA,
        ],
        name=f"feed_forward_{layer}",
    )


def feed_backward(dims, layer, sc, pieces, slope, mod, up, down):
    rows, width, narrow, count, hidden = (
        dims.rows, dims.width, dims.narrow, dims.n_heads, dims.hidden,
    )
    last = layer == 1
    n_in = len(pieces)
    n_extra = 0 if last else 2

    def body(sc, *refs):
        pieces = refs[:n_in]
        slope, mod, up_own, up_other, down_own, down_other = refs[n_in : n_in + 6]
        rest = refs[n_in + 6 :]
        g_out, for_grads = rest[:2]
        outs = rest[2 : 2 + count]
        extra = rest[2 + count : 2 + count + n_extra]
        up, down, buffer, low, other_buffer, sem_up, sem_down = rest[2 + count + n_extra :]
        fetch_down = Fetch(sc, layer, down_own, down_other, down, sem_down)
        fetch_up = Fetch(sc, layer, up_own, up_other, up, sem_up)
        seg = segments(sc, (rows, 1), 0, sc[1] * rows)
        place(buffer, pieces[:count], sc[0], narrow)
        if last:
            g = buffer[...]
            g_out[...] = g.astype(BF)
        else:
            x, d_mid = pieces[count:]
            grad_out, sums_out = extra
            dxa = buffer[...]
            normed, inv = norm_of(x[...].astype(F32))
            other_buffer[...] = dxa * normed
            mine = pl.ds(pl.multiple_of(sc[0] * narrow, narrow), narrow)
            sums_out[0] = utterance_sums(buffer[:, mine], seg)
            sums_out[1] = utterance_sums(other_buffer[:, mine], seg)
            dx = d_mid[...] + norm_pull(dxa * (1.0 + spread(mod, 1, 1, seg)), normed, inv)
            other_buffer[...] = dx
            grad_out[...] = other_buffer[:, mine]
            g = dx.astype(BF)
            g_out[...] = g
            g = g.astype(F32)
        dz = (g * spread(mod, layer, 5, seg)).astype(BF)
        for_grads[:, :width] = dz
        fetch_down.wait()
        da = (dot(dz, down[...], ((1,), (1,))) * slope[...]).astype(BF)
        for_grads[:, width:] = da
        fetch_up.wait()
        low[...] = dot(da, up[...], ((1,), (1,))).astype(BF)
        hand_out(outs, low, sc[0], narrow)

    extra = [] if last else [sds((rows, narrow), F32), sds((2, 4, narrow), F32)]
    return call(
        body,
        [sc] + pieces + [slope, mod, up[0], up[1], down[0], down[1]],
        [SM] + [VM] * n_in + [VM, VM, HB, HB, HB, HB],
        [sds((rows, width), BF), sds((rows, width + hidden), BF)]
        + [sds((rows, narrow), BF)] * count
        + extra,
        [
            pltpu.VMEM(up[0].shape, BF),
            pltpu.VMEM(down[0].shape, BF),
            pltpu.VMEM((rows, width), F32),
            pltpu.VMEM((rows, width), BF),
            pltpu.VMEM((rows, width), F32),
            pltpu.SemaphoreType.DMA,
            pltpu.SemaphoreType.DMA,
        ],
        name=f"feed_backward_{layer}",
    )


def middle_backward(
    dims, layer, sc, g, x1, sums, branch, mod, weights, queries, kept, probs, exact, cosine, sine
):
    rows, width, narrow, local, count = (
        dims.rows, dims.width, dims.narrow, dims.local, dims.n_heads,
    )
    n_seq, frames = dims.n_seq, dims.frames
    heads = local // HEAD_DIM
    scale = 1.0 / math.sqrt(HEAD_DIM)

    def body(sc, g, x1, *refs):
        sums = refs[:count]
        branch, mod, w_own, w_other, queries, kept, probs, exact, cosine, sine = refs[
            count : count + 10
        ]
        d_mid_out, dy_out, small, q_out = refs[count + 10 : count + 14]
        outs = refs[count + 14 : count + 14 + n_seq]
        weight, buffer, other, done, sem = refs[count + 14 + n_seq :]
        fetch = Fetch(sc, layer, w_own, w_other, weight, sem)
        seg = segments(sc, (rows, 1), 0, sc[1] * rows)
        mine = pl.ds(pl.multiple_of(sc[0] * narrow, narrow), narrow)
        place(buffer, sums, sc[0], narrow)
        dxf = buffer[...]
        normed, inv = norm_of(x1[...])
        other[...] = dxf * normed
        small[1] = utterance_sums(buffer[:, mine], seg)
        small[2] = utterance_sums(other[:, mine], seg)
        d_mid = g[...].astype(F32) + norm_pull(
            dxf * (1.0 + spread(mod, layer, 4, seg)), normed, inv
        )
        d_mid_out[...] = d_mid
        other[...] = d_mid
        small[0] = utterance_sums(other[:, mine] * branch[...].astype(F32), seg)
        dy = (d_mid * spread(mod, layer, 2, seg)).astype(BF)
        dy_out[...] = dy
        fetch.wait()
        d_att = dot(dy, weight[...], ((1,), (1,))).astype(BF)
        shared = d_att.astype(F32) * exact[...]
        cos = cosine[:, :HEAD_DIM]
        sin = -sine[:, :HEAD_DIM]
        for head in range(heads):
            cols = slice(head * HEAD_DIM, (head + 1) * HEAD_DIM)
            vals = slice(local + head * HEAD_DIM, local + (head + 1) * HEAD_DIM)
            low = probs[head]
            prob = low.astype(F32)
            grad = d_att[:, cols]
            d_prob = dot(grad, kept[:, vals], ((1,), (1,)))
            delta = jnp.sum(shared[:, cols], axis=1, keepdims=True)
            d_score = (prob * (d_prob - delta)).astype(BF)
            dq = dot(d_score, kept[:, cols]) * scale
            q_out[:, cols] = turn(dq, cos, sin).astype(BF)
            done[:, cols] = (dot(d_score, queries[:, cols], ((0,), (0,))) * scale).astype(BF)
            done[:, vals] = dot(low, grad, ((0,), (0,))).astype(BF)
        for k in range(n_seq):
            at = pl.multiple_of(jnp.bitwise_xor(sc[1], k) * rows, rows)
            outs[k][...] = done[pl.ds(at, rows), :]

    return call(
        body,
        [sc, g, x1]
        + sums
        + [branch, mod, weights[0], weights[1], queries, kept, probs, exact, cosine, sine],
        [SM, VM, VM] + [VM] * count + [VM, VM, HB, HB] + [VM] * 6,
        [
            sds((rows, width), F32),
            sds((rows, width), BF),
            sds((3, 4, narrow), F32),
            sds((rows, local), BF),
        ]
        + [sds((rows, 2 * local), BF)] * n_seq,
        [
            pltpu.VMEM(weights[0].shape, BF),
            pltpu.VMEM((rows, width), F32),
            pltpu.VMEM((rows, width), F32),
            pltpu.VMEM((frames, 2 * local), BF),
            pltpu.SemaphoreType.DMA,
        ],
        name=f"middle_backward_{layer}",
    )


def project_backward(dims, layer, sc, dy, d_query, chunks, weights, cosine, sine):
    rows, width, narrow, local, count = (
        dims.rows, dims.width, dims.narrow, dims.local, dims.n_heads,
    )
    n_in = len(chunks)

    def body(sc, dy, d_query, *refs):
        chunks = refs[:n_in]
        w_own, w_other, cosine, sine, d_out = refs[n_in : n_in + 5]
        outs = refs[n_in + 5 : n_in + 5 + count]
        weight, buffer, sem = refs[n_in + 5 + count :]
        fetch = Fetch(sc, layer, w_own, w_other, weight, sem)
        total = chunks[0][...].astype(F32)
        for chunk in chunks[1:]:
            total = total + chunk[...].astype(F32)
        cos = widen_table(cosine[...], local)
        sin = -widen_table(sine[...], local)
        dk = turn(total[:, :local], cos, sin).astype(BF)
        dv = total[:, local:].astype(BF)
        d_out[:, :width] = dy[...]
        for i, part in enumerate((d_query[...], dk, dv)):
            d_out[:, width + i * local : width + (i + 1) * local] = part
        fetch.wait()
        total = dot(d_query[...], weight[0], ((1,), (1,)))
        total = total + dot(dk, weight[1], ((1,), (1,)))
        total = total + dot(dv, weight[2], ((1,), (1,)))
        buffer[...] = total.astype(BF)
        hand_out(outs, buffer, sc[0], narrow)

    return call(
        body,
        [sc, dy, d_query] + chunks + [weights[0], weights[1], cosine, sine],
        [SM, VM, VM] + [VM] * n_in + [HB, HB, VM, VM],
        [sds((rows, width + 3 * local), BF)] + [sds((rows, narrow), BF)] * count,
        [
            pltpu.VMEM(weights[0].shape, BF),
            pltpu.VMEM((rows, width), BF),
            pltpu.SemaphoreType.DMA,
        ],
        name=f"project_backward_{layer}",
    )


def products(left, right, local, width):
    first = dot(left[:, :local], right[:, :width], ((0,), (0,))).astype(BF)
    rest = dot(left[:, local:], right[:, width:], ((0,), (0,))).astype(BF)
    out = [[(slice(None), first)]]
    for i in range(rest.shape[1] // local):
        columns = slice(i * local, (i + 1) * local)
        lines = [slice(group * local, (group + 1) * local) for group in range(width // local)]
        out.append([(line, rest[line, columns]) for line in lines])
    return out


def half_grads(sc, left, right, local, name):
    width = left.shape[1] - local
    count = (1 + (right.shape[1] - width) // local) // 2

    def body(sc, left, right, mine, theirs):
        grads = products(left[...], right[...], local, width)
        for section in range(2):

            @pl.when(sc[2] == section)
            def _(section=section):
                for out, first in ((mine, section * count), (theirs, (1 - section) * count)):
                    for i in range(count):
                        for columns, value in grads[first + i]:
                            out[i * local : (i + 1) * local, columns] = value

    return call(
        body,
        [sc, left, right],
        [SM, VM, VM],
        [sds((count * local, width), BF)] * 2,
        name=name,
    )


def whole_grads(sc, left, right, local, name):
    count = len(left)
    rows, wide = left[0].shape
    width = wide - local
    tensors = 1 + (right[0].shape[1] - width) // local

    def body(sc, *refs):
        left, right = refs[:count], refs[count : 2 * count]
        out, all_left, all_right = refs[2 * count :]
        for k in range(count):
            all_left[k * rows : (k + 1) * rows, :] = left[k][...]
            all_right[k * rows : (k + 1) * rows, :] = right[k][...]
        grads = products(all_left[...], all_right[...], local, width)
        for i, grad in enumerate(grads):
            for columns, value in grad:
                out[i * local : (i + 1) * local, columns] = value

    return call(
        body,
        [sc] + list(left) + list(right),
        [SM] + [VM] * (2 * count),
        [sds((tensors * local, width), BF)],
        [
            pltpu.VMEM((count * rows, wide), BF),
            pltpu.VMEM((count * rows, right[0].shape[1]), BF),
        ],
        limit=24,
        name=name,
    )[0]


def add_split(sc, left, right, step):
    rows, width = left.shape
    half = rows // 2

    def body(sc, left, right, keep, send):
        bit = sc[5 + step]
        mine = pl.ds(pl.multiple_of(bit * half, half), half)
        other = pl.ds(pl.multiple_of((1 - bit) * half, half), half)
        keep[...] = (left[mine, :].astype(F32) + right[mine, :].astype(F32)).astype(BF)
        send[...] = (left[other, :].astype(F32) + right[other, :].astype(F32)).astype(BF)

    return call(
        body, [sc, left, right], [SM, VM, VM], [sds((half, width), BF)] * 2, name="add_split"
    )


def join(sc, mine, other, step):
    half, width = mine.shape

    def body(sc, mine, other, out):
        bit = sc[5 + step]
        out[pl.ds(pl.multiple_of(bit * half, half), half), :] = mine[...]
        out[pl.ds(pl.multiple_of((1 - bit) * half, half), half), :] = other[...]

    return call(
        body, [sc, mine, other], [SM, VM, VM], [sds((2 * half, width), BF)], name="join"
    )[0]


class HalfSum:
    def __init__(self, sc, layer, left, right, local, name):
        self.sc, self.layer = sc, layer
        self.mine, self.ready = half_grads(sc, left, right, local, name)
        self.bits = lax.axis_size("seq").bit_length() - 1
        self.at = 0
        self.taken = True
        self.pieces = []

    def send(self, *begin):
        value, bits = after(self.ready, *begin), self.bits
        if self.at == 0:
            self.came = swap(value)
        elif self.at <= bits:
            self.came = crossed(value, self.at - 1)
        else:
            if self.at == 2 * bits:
                self.hand_over(value)
            self.came = crossed(value, 2 * bits - self.at)
        self.at += 1
        self.taken = False
        return self.came

    def hand_over(self, value):
        self.pieces.append((value, to_owner(value, self.layer)))

    def take(self):
        sc, bits = self.sc, self.bits
        self.taken = True
        if self.at <= bits:
            self.mine, self.ready = add_split(sc, self.mine, self.came, self.at - 1)
        elif self.at == bits + 1:
            self.mine = self.ready = add_chunks([self.mine, self.came])
        else:
            self.mine = self.ready = join(sc, self.mine, self.came, 2 * bits + 1 - self.at)
        return self.ready

    def last(self, *begin):
        while self.at <= 2 * self.bits:
            if not self.taken:
                self.take()
            self.send()
        self.hand_over(after(self.came, *begin))
        (own_0, other_0), (own_1, other_1) = self.pieces
        return [own_0, own_1, other_0, other_1]


class Spread:
    def __init__(self, value):
        self.parts = [value]
        self.bits = lax.axis_size("seq").bit_length() - 1
        self.early = None

    def one(self, *begin):
        self.parts.append(crossed(after(self.parts[0], *begin), 0))
        return self.parts[1]

    def two(self, *begin):
        self.early = crossed(after(self.parts[0], *begin), 1)
        return self.early

    def rest(self, *begin):
        for bit in range(1, self.bits):
            more = [] if bit > 1 else [self.early]
            start = 0 if bit > 1 else 1
            for part in self.parts[start:]:
                more.append(crossed(after(part, *begin), bit))
            self.parts = self.parts + more
        return self.parts[3:]


def assemble(sc, added, pieces, local, outs, name):
    width = added[0].shape[1]
    count = outs // 2
    size = pieces[0].shape[0]

    def body(sc, *refs):
        added, pieces = refs[:2], refs[2:6]
        first_out, rest_out, first, rest, held, sems, out_sems = refs[6:]

        def store(index):
            if index == 0:
                return pltpu.make_async_copy(first, first_out, out_sems.at[0])
            return pltpu.make_async_copy(
                rest.at[index - 1], rest_out.at[index - 1], out_sems.at[index]
            )

        def put(index, value, line):
            lines = value.shape[0]
            if index == 0:
                first[line : line + lines, :] = value
                return
            for group in range(width // local):
                columns = slice(group * local, (group + 1) * local)
                at = group * local + line
                rest[index - 1, at : at + lines, :] = value[:, columns]

        @pl.when(sc[2] == 0)
        def _():
            copies = []
            for i in range(outs):
                at = pl.ds(i * local, local)
                for j in range(2):
                    copies.append(
                        pltpu.make_async_copy(
                            added[j].at[at, :], held.at[j, at, :], sems.at[i, j]
                        )
                    )
                    copies[-1].start()
            for i in range(outs):
                copies[2 * i].wait()
                copies[2 * i + 1].wait()
                at = slice(i * local, (i + 1) * local)
                put(i, held[0, at, :].astype(F32) + held[1, at, :].astype(F32), 0)
                store(i).start()

        bits = lax.axis_size("seq").bit_length() - 1
        low, high = sc[1] & 1, (sc[1] >> (bits - 1)) & 1

        @pl.when(sc[2] == 1)
        def _():
            copies = []
            for p in range(4):
                copies.append(
                    pltpu.make_async_copy(
                        pieces[p], held.at[0, pl.ds(p * size, size), :], sems.at[p // 2, p % 2]
                    )
                )
                copies[-1].start()
            for copy in copies:
                copy.wait()
            for section, at, bit in ((1, 0, high), (0, 2, low)):
                for turn in range(2):

                    @pl.when(bit == turn)
                    def _(section=section, at=at, turn=turn):
                        for place in range(2):
                            base = (at + (place ^ turn)) * size
                            for i in range(count):
                                begin = max(i * local, place * size)
                                end = min((i + 1) * local, (place + 1) * size)
                                if begin < end:
                                    row = base + begin - place * size
                                    value = held[0, row : row + end - begin, :].astype(F32)
                                    put(section * count + i, value, begin - i * local)

            for i in range(outs):
                store(i).start()

        for i in range(outs):
            store(i).wait()

    return call(
        body,
        [sc] + list(added) + list(pieces),
        [SM] + [HB] * 6,
        [sds((local, width), F32), sds((outs - 1, width, local), F32)],
        [
            pltpu.VMEM((local, width), F32),
            pltpu.VMEM((outs - 1, width, local), F32),
            pltpu.VMEM((2, outs * local, width), BF),
            pltpu.SemaphoreType.DMA((outs, 2)),
            pltpu.SemaphoreType.DMA((outs,)),
        ],
        limit=16,
        out_space=HB,
        name=name,
    )


def lay_out(sc, pairs, name):
    def body(sc, *refs):
        outs = refs[2 * len(pairs) :]
        for i in range(len(pairs)):
            outs[i][sc[2]] = refs[2 * i][...]
            outs[i][1 - sc[2]] = refs[2 * i + 1][...]

    return call(
        body,
        [sc] + [value for pair in pairs for value in pair],
        [SM] + [VM] * (2 * len(pairs)),
        [sds((2,) + pair[0].shape, pair[0].dtype) for pair in pairs],
        name=name,
    )


def by_section(sc, mine, theirs, layer_0, layer_1):
    mine[...] = jnp.where(sc[2] == 0, layer_0, layer_1)
    theirs[...] = jnp.where(sc[2] == 0, layer_1, layer_0)


def gate_sums(dims, layer, sc, g, x1, z, mod, passed):
    rows, narrow = dims.rows, dims.narrow

    def body(sc, g, x1, z, mod, passed, small, *shown):
        seg = segments(sc, (rows, 1), 0, sc[1] * rows)
        mine = pl.ds(pl.multiple_of(sc[0] * narrow, narrow), narrow)
        value = z[...].astype(F32)
        small[...] = utterance_sums(g[:, mine].astype(F32) * value, seg)
        if shown:
            gate = spread(mod, layer, 5, seg, mine)
            result = (x1[:, mine] + gate * value).astype(BF)
            by_section(sc, *shown, passed[...], result)

    outs = [sds((4, narrow), F32)]
    if layer == 1:
        outs += [sds((rows, narrow), BF)] * 2
    return call(
        body, [sc, g, x1, z, mod, passed], [SM] + [VM] * 5, outs, name=f"gate_sums_{layer}"
    )


def last_norm(dims, sc, terms, x, mod, small_0, small_1):
    rows, narrow, count = dims.rows, dims.narrow, dims.n_heads

    def body(sc, *refs):
        terms = refs[:count]
        x, mod, mid_0, gate_0, in_1, mid_1, gate_1 = refs[count : count + 7]
        total_out, normed_out, inv_out, mine_out, theirs_out, rows_out, buffer = refs[count + 7 :]
        seg = segments(sc, (rows, 1), 0, sc[1] * rows)
        mine = pl.ds(pl.multiple_of(sc[0] * narrow, narrow), narrow)
        total = terms[0][...].astype(F32)
        for term in terms[1:]:
            total = total + term[...].astype(F32)
        normed, inv = norm_of(x[...].astype(F32))
        buffer[...] = normed
        normed = buffer[:, mine]
        first = (
            [utterance_sums(total, seg), utterance_sums(total * normed, seg)]
            + [mid_0[i] for i in range(3)]
            + [gate_0[...]]
        )
        second = [in_1[0], in_1[1]] + [mid_1[i] for i in range(3)] + [gate_1[...]]
        for i in range(6):
            by_section(sc, mine_out.at[i], theirs_out.at[i], first[i], second[i])
        grad = total * (1.0 + spread(mod, 0, 1, seg, mine))
        total_out[...] = grad
        normed_out[...] = normed
        inv_out[...] = inv
        lane = lax.broadcasted_iota(jnp.int32, (rows, 128), 1)
        sums = jnp.where(lane == 0, jnp.sum(grad, axis=1, keepdims=True), 0.0)
        sums = jnp.where(lane == 1, jnp.sum(grad * normed, axis=1, keepdims=True), sums)
        pick = diagonal(8, 128)
        rows_out[...] = sum(dot(pick, part, ((1,), (1,))) for part in split3(sums))

    return call(
        body,
        [sc] + terms + [x, mod] + small_0 + small_1,
        [SM] + [VM] * (count + 7),
        [
            sds((rows, narrow), F32),
            sds((rows, narrow), F32),
            sds((rows, 1), F32),
            sds((6, 4, narrow), F32),
            sds((6, 4, narrow), F32),
            sds((8, rows), F32),
        ],
        [pltpu.VMEM((rows, dims.width), F32)],
        name="last_norm",
    )


def last_pull(dims, sc, d_mid, grad, normed, inv, sums, middle_grad):
    rows, narrow, count, width = dims.rows, dims.narrow, dims.n_heads, dims.width

    def body(sc, d_mid, grad, normed, inv, middle, *refs):
        sums, outs = refs[:count], refs[count:]
        total = sums[0][...]
        for term in sums[1:]:
            total = total + term[...]
        pick = diagonal(8, 128)
        total = sum(dot(part, pick, ((0,), (0,))) for part in split3(total * (1.0 / width)))
        mine = pl.ds(pl.multiple_of(sc[0] * narrow, narrow), narrow)
        first = d_mid[:, mine] + inv[...] * (
            grad[...] - total[:, 0:1] - normed[...] * total[:, 1:2]
        )
        by_section(sc, *outs, first, middle[...])

    return call(
        body,
        [sc, d_mid, grad, normed, inv, middle_grad] + sums,
        [SM] + [VM] * (5 + count),
        [sds((rows, narrow), F32)] * 2,
        name="last_pull",
    )


def modulation_part(sc, mod_weight, own, n_seq):
    kinds, width, narrow = mod_weight.shape

    def body(sc, mod_weight, *refs):
        own = refs[:n_seq]
        grads_out, part, box = refs[n_seq:]
        for k in range(n_seq):
            box[jnp.bitwise_xor(sc[1], k)] = own[k][...]
        total = box[0]
        for j in range(1, n_seq):
            total = total + box[j]
        result = jnp.zeros((8, width), F32)
        for which in range(kinds):
            mine, theirs = total[which], total[kinds + which]
            grad = jnp.concatenate(
                [jnp.where(sc[2] == 0, mine, theirs), jnp.where(sc[2] == 0, theirs, mine)],
                axis=0,
            )
            grads_out[which] = grad
            result = result + exact_dot(grad, mod_weight[which], ((1,), (1,)))
        part[...] = result

    return call(
        body,
        [sc, mod_weight] + own,
        [SM, VM] + [VM] * n_seq,
        [sds((kinds, 8, narrow), F32), sds((8, width), F32)],
        [pltpu.VMEM((n_seq, 2 * kinds, 4, narrow), F32)],
        name="modulation_part",
    )


def modulation_weight(sc, act, grads):
    kinds, rows, narrow = grads.shape
    width = act.shape[1]

    def body(sc, act, grads, out, held, sems):
        tall = outer_parts(act[...], act[...])[0].astype(F32).T.astype(BF)
        for which in range(kinds):
            wide = outer_parts(grads[which], grads[which])[1]
            held[which] = dot(tall, wide)
            pltpu.make_async_copy(held.at[which], out.at[which], sems.at[which]).start()
        for which in range(kinds):
            pltpu.make_async_copy(held.at[which], out.at[which], sems.at[which]).wait()

    return call(
        body,
        [sc, act, grads],
        [SM, VM, VM],
        [sds((kinds, width, narrow), F32)],
        [pltpu.VMEM((kinds, width, narrow), F32), pltpu.SemaphoreType.DMA((kinds,))],
        limit=16,
        out_space=HB,
        name="modulation_weight",
    )[0]


def time_backward(sc, sinus, inner, outer, time_out, own):
    count = len(own)
    rows, width = inner.shape
    block = width // 4

    def body(sc, sinus, inner, outer, time_out, *refs):
        own = refs[:count]
        g_in, g_out, box, held_in, held_out, sems = refs[count:]
        for k in range(count):
            at = jnp.bitwise_xor(sc[0], k)
            box[at, sc[2]] = own[k][0]
            box[at, 1 - sc[2]] = own[k][1]
        total = jnp.zeros((rows, width), F32)
        for j in range(count):
            for c in range(2):
                total = total + box[j, c]

        def slope(value):
            gate = 1.0 / (1.0 + jnp.exp(-value))
            return gate * (1.0 + value * (1.0 - gate))

        pre = inner[...]
        hidden = pre / (1.0 + jnp.exp(-pre))
        d_outer = total * slope(outer[...])
        tall, wide = outer_parts(hidden, d_outer)
        tall = tall.astype(F32).T.astype(BF)
        copies = []
        for i in range(4):
            at = slice(i * block, (i + 1) * block)
            held_out[at, :] = dot(tall[at], wide)
            copies.append(
                pltpu.make_async_copy(held_out.at[at, :], g_out.at[at, :], sems.at[i])
            )
            copies[-1].start()
        d_inner = exact_dot(d_outer, time_out[...], ((1,), (1,))) * slope(pre)
        held_in[...] = exact_outer(sinus[...], d_inner)
        copies.append(pltpu.make_async_copy(held_in, g_in, sems.at[4]))
        copies[-1].start()
        for copy in copies:
            copy.wait()

    return call(
        body,
        [sc, sinus, inner, outer, time_out] + own,
        [SM, VM, VM, VM, VM] + [VM] * count,
        [sds((sinus.shape[1], width), F32), sds((width, width), F32)],
        [
            pltpu.VMEM((count, 2, rows, width), F32),
            pltpu.VMEM((sinus.shape[1], width), F32),
            pltpu.VMEM((width, width), F32),
            pltpu.SemaphoreType.DMA((5,)),
        ],
        limit=16,
        out_space=HB,
        name="time_backward",
    )


class Dims:
    pass


def local_program(
    frames,
    cotangent,
    utt_lengths,
    time_ids,
    w_time_in,
    w_time_out,
    w_mod,
    w_qkv,
    w_out,
    w_up,
    w_down,
):
    dims = Dims()
    dims.n_heads = lax.axis_size("heads")
    dims.n_seq = n_seq = lax.axis_size("seq")
    _, dims.rows, dims.narrow = frames.shape
    dims.width = dims.narrow * dims.n_heads
    dims.local = w_qkv.shape[3]
    dims.hidden = w_up.shape[2]
    dims.frames = dims.rows * n_seq
    section = lax.axis_index("section")

    def here(both):
        return lax.dynamic_index_in_dim(both, section, 0, keepdims=False)

    sc = utt_lengths
    qkv = jnp.transpose(w_qkv[0], (1, 0, 2))
    mod_weight = jnp.transpose(w_mod[0], (1, 0, 2))
    wide_frames = gather(here(frames), "heads")
    qkv_w = (qkv, swap(qkv))
    sinus, inner, outer, act, mod_mine, mod_theirs = start(
        sc, time_ids, w_time_in, w_time_out, mod_weight
    )
    mod_theirs = swap(after(mod_theirs, *wide_frames))
    mods = gather(jnp.concatenate([mod_mine, mod_theirs], axis=0), "heads")
    cosine, sine = tables(sc, dims.rows)
    mods = after(mods, cosine, sine)

    x_0, _, xa, q_0, kv, mod = project(dims, 0, sc, wide_frames, mods, qkv_w, cosine, sine)
    chunks = gather(kv, "seq")
    out_w = (w_out[0], swap(after(w_out[0], kv)))
    kept_0, probs_0, for_attention, exact_0, *terms = attend(
        dims, 0, sc, chunks, q_0, xa, out_w
    )
    fwd_a = Spread(for_attention)

    up_w, down_w = [(w[0], swap(after(w[0], terms[0]))) for w in (w_up, w_down)]
    total = after(add_chunks(exchange(terms, "heads")), up_w[1], down_w[1])

    branch_0 = gather(total, "heads")
    fwd_a.one(total)
    fwd_a.two(total)
    x1_0, for_feed, slope_0, *terms = feed_forward(
        dims, 0, sc, x_0, branch_0, mod, up_w, down_w
    )
    fwd_f = Spread(for_feed)

    total = after(add_chunks(exchange(terms, "heads")), fwd_a.parts[1], fwd_a.early)

    z_0 = gather(total, "heads")
    fwd_a.rest(total)
    fwd_f.one(total)

    x_2, passed, xa, q_1, kv = project(
        dims, 1, sc, [x1_0] + z_0, [mod], qkv_w, cosine, sine
    )
    kv = after(kv, fwd_f.parts[1], *fwd_a.parts[3:])
    chunks = gather(kv, "seq")
    wide_cotangent = gather(after(here(cotangent), chunks[1]), "heads")
    kept_1, probs_1, for_attention_1, exact_1, *terms = attend(
        dims, 1, sc, chunks, q_1, xa, out_w
    )

    terms[0] = after(terms[0], *wide_cotangent)
    total = add_chunks(exchange(terms, "heads"))
    fwd_f.two(terms[0])

    branch_1 = gather(total, "heads")
    x1_1, for_feed, slope_1, *z_terms = feed_forward(
        dims, 1, sc, x_2, branch_1, mod, up_w, down_w
    )
    g_1, late, *terms = feed_backward(
        dims, 1, sc, wide_cotangent, slope_1, mod, up_w, down_w
    )
    terms = after(terms, fwd_f.early)
    feed_1 = HalfSum(sc, 1, for_feed, late, dims.hidden, "feed_grads_1")
    feed_1.send()
    got = exchange(terms, "heads")
    total = after(add_chunks(got), feed_1.came, *fwd_f.rest(terms[0]))

    feed_1.take()
    feed_1.send(total)
    sums = after(gather(total, "heads"), feed_1.came)

    feed_1.take()
    feed_1.send(sums[0])
    d_mid_1, dy, small_f1, dq, *sent = middle_backward(
        dims, 1, sc, g_1, x1_1, after(sums, feed_1.ready), branch_1[0], mod, out_w,
        q_1, kept_1, probs_1, exact_1, cosine, sine,
    )
    sent = after(sent, feed_1.came)

    got = exchange(sent, "seq")
    feed_1.take()
    z_1 = add_chunks(exchange(after(z_terms, sent[0]), "heads"))
    gate_1, *acts = gate_sums(dims, 1, sc, g_1, x1_1, z_1, mod, passed)
    got = after(got, feed_1.ready, *acts)
    late, *terms = project_backward(dims, 1, sc, dy, dq, got, qkv_w, cosine, sine)

    got = exchange(terms, "heads")
    feed_1.send(terms[0])
    attention_1 = HalfSum(sc, 1, for_attention_1, late, dims.local, "attend_grads_1")
    acts = [acts[0], swap(after(acts[1], terms[0]))]
    total = after(
        add_chunks(got), feed_1.came, attention_1.mine, attention_1.ready, acts
    )

    feed_1.take()
    feed_1.send(total)
    attention_1.send(total)
    pieces = after(gather(total, "heads"), feed_1.came, attention_1.came)

    g_0, late, *rest = feed_backward(
        dims, 0, sc, pieces + [x_2, d_mid_1], slope_0, mod, up_w, down_w
    )
    terms, (middle_grad, small_a1) = rest[: dims.n_heads], rest[dims.n_heads :]
    late_f = Spread(late)
    got = exchange(terms, "heads")
    attention_1.take()
    attention_1.send(terms[0])
    total = after(add_chunks(got), attention_1.came, late_f.one(terms[0]))

    attention_1.take()
    attention_1.send(total)
    sums = after(gather(total, "heads"), attention_1.came, late_f.two(total))

    attention_1.take()
    attention_1.send(sums[0])
    d_mid_0, dy, small_f0, dq, *sent = middle_backward(
        dims, 0, sc, g_0, x1_0, after(sums, attention_1.ready), branch_0[0], mod, out_w,
        q_0, kept_0, probs_0, exact_0, cosine, sine,
    )
    sent = after(sent, attention_1.came)

    got = exchange(sent, "seq")
    attention_1.take()
    feed_1 = feed_1.last(sent[0])
    gate_0, *_ = gate_sums(dims, 0, sc, g_0, x1_0, z_0[0], mod, passed)
    got = after(got, attention_1.ready, gate_0, feed_1)
    late, *terms = project_backward(dims, 0, sc, dy, dq, got, qkv_w, cosine, sine)
    late_a = Spread(late)

    got = exchange(terms, "heads")
    got = after(got, late_a.one(terms[0]), *late_f.rest(terms[0]))

    grad, normed, inv, mine, theirs, row_sums = last_norm(
        dims, sc, got, x_0, mod, [small_f0, gate_0], [small_a1, small_f1, gate_1]
    )
    late_a.two(row_sums)
    theirs = swap(theirs)

    both = jnp.concatenate([mine, theirs], axis=0)
    both = gather(both, "seq")
    feed_0 = whole_grads(
        sc, after(fwd_f.parts, theirs), late_f.parts, dims.hidden, "feed_grads_0"
    )
    both = after(both, feed_0, late_a.early)

    mod_grads, part = modulation_part(sc, mod_weight, both, n_seq)
    late_a.rest(both[0])
    row_sums = gather(after(row_sums, both[0]), "heads")
    feed_0 = [feed_0, to_owner(after(feed_0, both[0]), 0)]
    both = jnp.stack([part, swap(part)])
    both = after(both, row_sums, feed_0, *late_a.parts[3:])

    attention_1.send(both)
    grads = last_pull(dims, sc, d_mid_0, grad, normed, inv, row_sums, middle_grad)
    attention_0 = whole_grads(
        sc, after(fwd_a.parts, both), late_a.parts, dims.local, "attend_grads_0"
    )
    g_mod = modulation_weight(sc, act, mod_grads)
    both = after(gather(both, "heads"), g_mod, attention_0, attention_1.came, *grads)

    attention_0 = [attention_0, to_owner(after(attention_0, both[0]), 0)]
    g_first, g_second = time_backward(sc, sinus, inner, outer, w_time_out, both)
    attention_1 = attention_1.last(g_second)
    grads = [grads[0], swap(after(grads[1], g_second))]
    g_reduce, g_expand = assemble(
        sc, after(feed_0, g_second), feed_1, dims.hidden, 2, "assemble_feed"
    )
    acts, grads = lay_out(sc, [acts, after(grads, g_reduce)], "lay_out")
    g_out, g_qkv = assemble(
        sc, after(attention_0, grads), attention_1, dims.local, 4, "assemble_attend"
    )

    return (
        acts[None],
        grads[None],
        g_first,
        g_second,
        jnp.transpose(g_mod, (1, 0, 2))[None],
        jnp.transpose(g_qkv, (1, 0, 2))[None],
        g_out[None],
        g_expand,
        g_reduce[None],
    )


def solution(mesh):
    placed = (
        P(None, "seq", "heads"),
        P(None, "seq", "heads"),
        P(),
        P(),
        P(),
        P(),
        P("section", None, None, "heads"),
        P("section", None, None, "heads"),
        P("section", "heads", None),
        P("section", None, "heads"),
        P("section", "heads", None),
    )
    return jax.shard_map(
        local_program,
        mesh=mesh,
        in_specs=placed,
        out_specs=(
            P("section", None, "seq", "heads"),
            P("section", None, "seq", "heads"),
            P(),
            P(),
            P("section", None, None, "heads"),
            P("section", None, None, "heads"),
            P("section", "heads", None),
            P("section", None, "heads"),
            P("section", "heads", None),
        ),
        check_vma=False,
    )
```

```python
import functools
import math

import jax
import jax.numpy as jnp
import numpy as np
from jax import lax
from jax.experimental import pallas as pl
from jax.experimental.pallas import tpu as pltpu
from jax.sharding import PartitionSpec as P

HEAD_DIM = 64
FREQ = 256
EPS = 1e-06
BF = jnp.bfloat16
F32 = jnp.float32
MIB = 1024 * 1024


def partner(value, axis, by):
    if by == 0:
        return value
    return lax.ppermute(value, axis, [(i, i ^ by) for i in range(lax.axis_size(axis))])


def order_of(count):
    return (3, 1, 2) if count == 4 else tuple(range(count - 1, 0, -1))


def gather(value, axis):
    count = lax.axis_size(axis)
    out = [value] * count
    for k in order_of(count):
        out[k] = partner(value, axis, k)
    return out


def exchange(chunks, axis):
    out = list(chunks)
    for k in order_of(len(chunks)):
        out[k] = partner(chunks[k], axis, k)
    return out


def swap(value):
    return lax.ppermute(value, "section", [(0, 1), (1, 0)])


def to_owner(value, layer):
    return lax.ppermute(value, "section", [(1 - layer, layer)])


def crossed(value, step):
    length = lax.axis_size("seq")
    last = length.bit_length() - 2
    pairs = []
    for c in range(2):
        by = 1 << (step if c == 0 else last - step)
        pairs += [(c * length + i, c * length + (i ^ by)) for i in range(length)]
    return lax.ppermute(value, ("section", "seq"), pairs)


def after(value, *done):
    value = lax.optimization_barrier((value, done))[0]
    return list(value) if isinstance(value, (list, tuple)) else value


def add_chunks(chunks):
    total = chunks[0].astype(F32)
    for chunk in chunks[1:]:
        total = total + chunk.astype(F32)
    return total.astype(BF)


def dot(left, right, contract=((1,), (0,))):
    return lax.dot_general(left, right, (contract, ((), ())), preferred_element_type=F32)


def split3(value):
    high = value.astype(BF)
    rest = value - high.astype(F32)
    middle = rest.astype(BF)
    low = (rest - middle.astype(F32)).astype(BF)
    return high, middle, low


def diagonal(rows, columns):
    row = lax.broadcasted_iota(jnp.int32, (rows, columns), 0)
    return (row == lax.broadcasted_iota(jnp.int32, (rows, columns), 1)).astype(BF)


def exact_dot(left, right, contract=((1,), (0,))):
    rows = left.shape[0]
    stacked = jnp.concatenate(split3(left), axis=0)
    out = dot(stacked, right, contract)
    return out[:rows] + (out[rows : 2 * rows] + out[2 * rows :])


def exact_outer(left, right):
    tall, wide = outer_parts(left, right)
    return dot(tall, wide, ((0,), (0,)))


def outer_parts(left, right):
    a, b = split3(left), split3(right)
    tall = jnp.concatenate([a[0], a[0], a[1]], axis=0)
    wide = jnp.concatenate([b[0], b[1], b[0]], axis=0)
    return tall, wide


def segments(sc, shape, axis, first):
    index = lax.broadcasted_iota(jnp.int32, shape, axis) + first
    return (index >= sc[3]).astype(jnp.int32) + (index >= sc[4]).astype(jnp.int32)


def spread(mod, layer, which, seg, columns=slice(None)):
    block = mod[layer * 6 + which, :, columns]
    rows = [block[u : u + 1] for u in range(3)]
    return jnp.where(seg == 0, rows[0], jnp.where(seg == 1, rows[1], rows[2]))


def utterance_sums(value, seg):
    rows = [
        jnp.sum(jnp.where(seg == u, value, 0.0), axis=0, keepdims=True) for u in range(3)
    ]
    return jnp.concatenate(rows + [jnp.zeros_like(rows[0])], axis=0)


def norm_of(value):
    mean = jnp.mean(value, axis=1, keepdims=True)
    centred = value - mean
    inv = lax.rsqrt(jnp.mean(centred * centred, axis=1, keepdims=True) + EPS)
    return centred * inv, inv


def norm_pull(grad, normed, inv):
    return inv * (
        grad
        - jnp.mean(grad, axis=1, keepdims=True)
        - normed * jnp.mean(grad * normed, axis=1, keepdims=True)
    )


def lanes_of(index, count, width):
    return pl.ds(pl.multiple_of(lax.rem(index, count) * width, width), width)


def place(buffer, chunks, own, width):
    for k, chunk in enumerate(chunks):
        at = pl.multiple_of(jnp.bitwise_xor(own, k) * width, width)
        buffer[:, pl.ds(at, width)] = chunk[...].astype(buffer.dtype)


def hand_out(outs, buffer, own, width):
    for k, out in enumerate(outs):
        at = pl.multiple_of(jnp.bitwise_xor(own, k) * width, width)
        out[...] = buffer[:, pl.ds(at, width)].astype(out.dtype)


class Fetch:
    def __init__(self, sc, layer, own, other, buffer, sem):
        self.copy = pltpu.make_async_copy(own, buffer, sem)
        other_copy = pltpu.make_async_copy(other, buffer, sem)

        @pl.when(sc[2] == layer)
        def _():
            self.copy.start()

        @pl.when(sc[2] != layer)
        def _():
            other_copy.start()

    def wait(self):
        self.copy.wait()


def turn(value, cosine, sine):
    width = value.shape[1]
    even = lax.broadcasted_iota(jnp.int32, value.shape, 1) % 2 == 0
    swapped = jnp.where(even, pltpu.roll(value, width - 1, 1), pltpu.roll(value, 1, 1))
    return value * cosine + swapped * sine


def widen_table(table, width):
    copies = width // table.shape[1]
    return jnp.concatenate([table] * copies, axis=1) if copies > 1 else table[:, :width]


VM = pl.BlockSpec(memory_space=pltpu.VMEM)
SM = pl.BlockSpec(memory_space=pltpu.SMEM)
HB = pl.BlockSpec(memory_space=pltpu.HBM)


def sds(shape, dtype):
    return jax.ShapeDtypeStruct(tuple(shape), dtype)


class Place:
    def __init__(self, lengths):
        self.lengths = lengths
        self.known = {}
        for index in range(5):
            self[index]

    def __getitem__(self, index):
        if index not in self.known:
            self.known[index] = self.find(index)
        return self.known[index]

    def find(self, index):
        if index < 3:
            return lax.axis_index(("heads", "seq", "section")[index])
        if index == 3:
            return self.lengths[self[2], 0]
        if index == 4:
            return self[3] + self.lengths[self[2], 1]
        low = index - 5
        high = lax.axis_size("seq").bit_length() - 2 - low
        return jnp.where(self[2] == 0, self[1] >> low, self[1] >> high) & 1


def call(body, ins, specs, outs, scratch=(), limit=12, name=None):
    return pl_call(body, ins, specs, outs, [VM] * len(outs), scratch, limit, name)


def pl_call(body, ins, specs, outs, out_specs, scratch, limit, name):
    def placed(lengths, *refs):
        body(Place(lengths), *refs)

    return pl.pallas_call(
        placed,
        out_shape=list(outs),
        in_specs=list(specs),
        out_specs=list(out_specs),
        scratch_shapes=list(scratch),
        compiler_params=pltpu.CompilerParams(vmem_limit_bytes=limit * MIB),
        cost_estimate=pl.CostEstimate(flops=1, bytes_accessed=1, transcendentals=0),
        name=name,
    )(*ins)


def start(sc, time_ids, time_in, time_out, mod_weight):
    width = time_in.shape[1]
    kinds, _, narrow = mod_weight.shape
    half = FREQ // 2

    def body(sc, ids, time_in, time_out, mod_weight, *refs):
        sinus_out, inner_out, outer_out, act_out, mine_out, theirs_out = refs[:6]
        w_in, w_out, w_mod, sems = refs[6:]
        copies = [
            pltpu.make_async_copy(time_in, w_in, sems.at[0]),
            pltpu.make_async_copy(time_out, w_out, sems.at[1]),
            pltpu.make_async_copy(mod_weight, w_mod, sems.at[2]),
        ]
        for copy in copies:
            copy.start()
        row = lax.broadcasted_iota(jnp.int32, (8, half), 0)
        lane = lax.broadcasted_iota(jnp.int32, (8, half), 1).astype(F32)
        stamp = jnp.zeros((8, half), F32)
        for m in range(2):
            for u in range(3):
                stamp = jnp.where(row == m * 4 + u, ids[m, u].astype(F32), stamp)
        angle_t = stamp * jnp.exp(lane * (-math.log(10000.0) / (half - 1)))
        sinus = jnp.concatenate([jnp.sin(angle_t), jnp.cos(angle_t)], axis=1)
        sinus_out[...] = sinus

        copies[0].wait()
        inner = exact_dot(sinus, w_in[...])
        inner_out[...] = inner
        hidden = inner / (1.0 + jnp.exp(-inner))
        copies[1].wait()
        outer = exact_dot(hidden, w_out[...])
        outer_out[...] = outer
        act = outer / (1.0 + jnp.exp(-outer))
        act_out[...] = act
        copies[2].wait()
        for which in range(kinds):
            modul = exact_dot(act, w_mod[which])
            mine_out[which] = jnp.where(sc[2] == 0, modul[:4], modul[4:])
            theirs_out[which] = jnp.where(sc[2] == 0, modul[4:], modul[:4])

    return call(
        body,
        [sc, time_ids, time_in, time_out, mod_weight],
        [SM, SM, HB, HB, HB],
        [sds((8, FREQ), F32)]
        + [sds((8, width), F32)] * 3
        + [sds((kinds, 4, narrow), F32)] * 2,
        [
            pltpu.VMEM(time_in.shape, BF),
            pltpu.VMEM(time_out.shape, BF),
            pltpu.VMEM(mod_weight.shape, BF),
            pltpu.SemaphoreType.DMA((3,)),
        ],
        limit=56,
        name="start",
    )


def tables(sc, rows):
    def body(sc, cosine, sine):
        index = lax.broadcasted_iota(jnp.int32, (rows, 2 * HEAD_DIM), 0) + sc[1] * rows
        begin = jnp.where(index >= sc[4], sc[4], jnp.where(index >= sc[3], sc[3], 0))
        lane = lax.broadcasted_iota(jnp.int32, (rows, 2 * HEAD_DIM), 1)
        pair = lax.broadcasted_iota(jnp.int32, (1, 2 * HEAD_DIM), 1)
        rate = jnp.exp(
            ((pair % HEAD_DIM) // 2).astype(F32) * (-2.0 * math.log(10000.0) / HEAD_DIM)
        )
        angle = (index - begin).astype(F32) * rate
        cosine[...] = jnp.cos(angle)
        sine[...] = jnp.sin(angle) * jnp.where(lane % 2 == 0, -1.0, 1.0)

    return call(body, [sc], [SM], [sds((rows, 2 * HEAD_DIM), F32)] * 2, name="tables")


def project(dims, layer, sc, pieces, mods, weights, cosine, sine):
    first = layer == 0
    rows, width, narrow, local = dims.rows, dims.width, dims.narrow, dims.local
    count = dims.n_heads
    n_in, n_mod = len(pieces), len(mods)

    def body(sc, *refs):
        pieces, mods = refs[:n_in], refs[n_in : n_in + n_mod]
        w_own, w_other, cosine, sine = refs[n_in + n_mod : n_in + n_mod + 4]
        outs = refs[n_in + n_mod + 4 :]
        x_out, narrow_out, xa_out, q_out, kv_out = outs[:5]
        if first:
            mod = outs[5]
        else:
            mod = mods[0]
        buffer, weight, sem = outs[-3:]
        fetch = Fetch(sc, layer, w_own, w_other, weight, sem)
        seg = segments(sc, (rows, 1), 0, sc[1] * rows)
        if first:
            for k in range(count):
                at = pl.multiple_of(jnp.bitwise_xor(sc[0], k) * narrow, narrow)
                block = mods[k][...]
                for l in range(2):
                    mod[l * 6 : l * 6 + 6, :, pl.ds(at, narrow)] = jnp.where(
                        sc[2] == l, block[:6], block[6:]
                    )
            place(buffer, pieces, sc[0], narrow)
            x = buffer[...]
            x_out[...] = x.astype(BF)
            narrow_out[...] = pieces[0][...]
        else:
            place(buffer, pieces[1:], sc[0], narrow)
            x = pieces[0][...] + spread(mod, 0, 5, seg) * buffer[...]
            low = x.astype(BF)
            x_out[...] = low
            x = low.astype(F32)
            buffer[...] = x
            at = pl.multiple_of(sc[0] * narrow, narrow)
            narrow_out[...] = buffer[:, pl.ds(at, narrow)].astype(BF)
        normed, _ = norm_of(x)
        xa = (normed * (1.0 + spread(mod, layer, 1, seg)) + spread(mod, layer, 0, seg)).astype(BF)
        xa_out[...] = xa
        cos = widen_table(cosine[...], local)
        sin = widen_table(sine[...], local)
        fetch.wait()
        q_out[...] = turn(dot(xa, weight[0]), cos, sin).astype(BF)
        kv_out[:, :local] = turn(dot(xa, weight[1]), cos, sin).astype(BF)
        kv_out[:, local:] = dot(xa, weight[2]).astype(BF)

    return call(
        body,
        [sc] + pieces + mods + [weights[0], weights[1], cosine, sine],
        [SM] + [VM] * (n_in + n_mod) + [HB, HB, VM, VM],
        [
            sds((rows, width), BF),
            sds((rows, narrow), BF),
            sds((rows, width), BF),
            sds((rows, local), BF),
            sds((rows, 2 * local), BF),
        ]
        + ([sds((12, 4, width), F32)] if first else []),
        [
            pltpu.VMEM((rows, width), F32),
            pltpu.VMEM(weights[0].shape, BF),
            pltpu.SemaphoreType.DMA,
        ],
        name=f"project_{layer}",
    )


def attend(dims, layer, sc, chunks, queries, xa, weights):
    rows, n_seq, frames = dims.rows, dims.n_seq, dims.frames
    width, narrow, local, count = dims.width, dims.narrow, dims.local, dims.n_heads
    heads = local // HEAD_DIM

    def body(sc, *refs):
        chunks = refs[:n_seq]
        queries, xa, w_own, w_other = refs[n_seq : n_seq + 4]
        kept, probs, for_grads, exact = refs[n_seq + 4 : n_seq + 8]
        outs = refs[n_seq + 8 : n_seq + 8 + count]
        weight, buffer, sem = refs[n_seq + 8 + count :]
        fetch = Fetch(sc, layer, w_own, w_other, weight, sem)
        for k in range(n_seq):
            at = pl.multiple_of(jnp.bitwise_xor(sc[1], k) * rows, rows)
            kept[pl.ds(at, rows), :] = chunks[k][...]
        same = segments(sc, (rows, 1), 0, sc[1] * rows) == segments(sc, (1, frames), 1, 0)
        for head in range(heads):
            cols = slice(head * HEAD_DIM, (head + 1) * HEAD_DIM)
            scores = dot(queries[:, cols], kept[:, cols], ((1,), (1,)))
            scores = jnp.where(same, scores * (1.0 / math.sqrt(HEAD_DIM)), -1e30)
            prob = jnp.exp(scores - jnp.max(scores, axis=1, keepdims=True))
            prob = prob * (1.0 / jnp.sum(prob, axis=1, keepdims=True))
            low = prob.astype(BF)
            probs[head] = low
            value = kept[:, local + head * HEAD_DIM : local + (head + 1) * HEAD_DIM]
            exact[:, cols] = dot(low, value)
        mixed = exact[...].astype(BF)
        for_grads[:, :local] = mixed
        for_grads[:, local:] = xa[...]
        fetch.wait()
        buffer[...] = dot(mixed, weight[...]).astype(BF)
        hand_out(outs, buffer, sc[0], narrow)

    return call(
        body,
        [sc] + chunks + [queries, xa, weights[0], weights[1]],
        [SM] + [VM] * (n_seq + 2) + [HB, HB],
        [
            sds((frames, 2 * local), BF),
            sds((heads, rows, frames), BF),
            sds((rows, local + width), BF),
            sds((rows, local), F32),
        ]
        + [sds((rows, narrow), BF)] * count,
        [
            pltpu.VMEM(weights[0].shape, BF),
            pltpu.VMEM((rows, width), BF),
            pltpu.SemaphoreType.DMA,
        ],
        name=f"attend_{layer}",
    )


def feed_forward(dims, layer, sc, x, branch, mod, up, down):
    rows, width, narrow, count, hidden = (
        dims.rows, dims.width, dims.narrow, dims.n_heads, dims.hidden,
    )

    def body(sc, x, *refs):
        branch = refs[:count]
        mod, up_own, up_other, down_own, down_other = refs[count : count + 5]
        x1_out, for_grads, slope_out = refs[count + 5 : count + 8]
        outs = refs[count + 8 : 2 * count + 8]
        up, down, buffer, low, sem_up, sem_down = refs[2 * count + 8 :]
        fetch_up = Fetch(sc, layer, up_own, up_other, up, sem_up)
        fetch_down = Fetch(sc, layer, down_own, down_other, down, sem_down)
        seg = segments(sc, (rows, 1), 0, sc[1] * rows)
        place(buffer, branch, sc[0], narrow)
        x1 = x[...].astype(F32) + spread(mod, layer, 2, seg) * buffer[...]
        x1_out[...] = x1
        normed, _ = norm_of(x1)
        xf = (normed * (1.0 + spread(mod, layer, 4, seg)) + spread(mod, layer, 3, seg)).astype(BF)
        for_grads[:, hidden:] = xf
        fetch_up.wait()
        a = dot(xf, up[...])
        c0 = math.sqrt(2.0 / math.pi)
        square = a * a
        t = jnp.tanh(c0 * (a + 0.044715 * (a * square)))
        h = (0.5 * a * (1.0 + t)).astype(BF)
        for_grads[:, :hidden] = h
        slope_out[...] = 0.5 * (1.0 + t) + 0.5 * a * (1.0 - t * t) * (
            c0 * (1.0 + 3.0 * 0.044715 * square)
        )
        fetch_down.wait()
        low[...] = dot(h, down[...]).astype(BF)
        hand_out(outs, low, sc[0], narrow)

    return call(
        body,
        [sc, x] + branch + [mod, up[0], up[1], down[0], down[1]],
        [SM, VM] + [VM] * count + [VM, HB, HB, HB, HB],
        [
            sds((rows, width), F32),
            sds((rows, hidden + width), BF),
            sds((rows, hidden), F32),
        ]
        + [sds((rows, narrow), BF)] * count,
        [
            pltpu.VMEM(up[0].shape, BF),
            pltpu.VMEM(down[0].shape, BF),
            pltpu.VMEM((rows, width), F32),
            pltpu.VMEM((rows, width), BF),
            pltpu.SemaphoreType.DMA,
            pltpu.SemaphoreType.DMA,
        ],
        name=f"feed_forward_{layer}",
    )


def feed_backward(dims, layer, sc, pieces, slope, mod, up, down):
    rows, width, narrow, count, hidden = (
        dims.rows, dims.width, dims.narrow, dims.n_heads, dims.hidden,
    )
    last = layer == 1
    n_in = len(pieces)
    n_extra = 0 if last else 2

    def body(sc, *refs):
        pieces = refs[:n_in]
        slope, mod, up_own, up_other, down_own, down_other = refs[n_in : n_in + 6]
        rest = refs[n_in + 6 :]
        g_out, for_grads = rest[:2]
        outs = rest[2 : 2 + count]
        extra = rest[2 + count : 2 + count + n_extra]
        up, down, buffer, low, other_buffer, sem_up, sem_down = rest[2 + count + n_extra :]
        fetch_down = Fetch(sc, layer, down_own, down_other, down, sem_down)
        fetch_up = Fetch(sc, layer, up_own, up_other, up, sem_up)
        seg = segments(sc, (rows, 1), 0, sc[1] * rows)
        place(buffer, pieces[:count], sc[0], narrow)
        if last:
            g = buffer[...]
            g_out[...] = g.astype(BF)
        else:
            x, d_mid = pieces[count:]
            grad_out, sums_out = extra
            dxa = buffer[...]
            normed, inv = norm_of(x[...].astype(F32))
            other_buffer[...] = dxa * normed
            mine = pl.ds(pl.multiple_of(sc[0] * narrow, narrow), narrow)
            sums_out[0] = utterance_sums(buffer[:, mine], seg)
            sums_out[1] = utterance_sums(other_buffer[:, mine], seg)
            dx = d_mid[...] + norm_pull(dxa * (1.0 + spread(mod, 1, 1, seg)), normed, inv)
            other_buffer[...] = dx
            grad_out[...] = other_buffer[:, mine]
            g = dx.astype(BF)
            g_out[...] = g
            g = g.astype(F32)
        dz = (g * spread(mod, layer, 5, seg)).astype(BF)
        for_grads[:, :width] = dz
        fetch_down.wait()
        da = (dot(dz, down[...], ((1,), (1,))) * slope[...]).astype(BF)
        for_grads[:, width:] = da
        fetch_up.wait()
        low[...] = dot(da, up[...], ((1,), (1,))).astype(BF)
        hand_out(outs, low, sc[0], narrow)

    extra = [] if last else [sds((rows, narrow), F32), sds((2, 4, narrow), F32)]
    return call(
        body,
        [sc] + pieces + [slope, mod, up[0], up[1], down[0], down[1]],
        [SM] + [VM] * n_in + [VM, VM, HB, HB, HB, HB],
        [sds((rows, width), BF), sds((rows, width + hidden), BF)]
        + [sds((rows, narrow), BF)] * count
        + extra,
        [
            pltpu.VMEM(up[0].shape, BF),
            pltpu.VMEM(down[0].shape, BF),
            pltpu.VMEM((rows, width), F32),
            pltpu.VMEM((rows, width), BF),
            pltpu.VMEM((rows, width), F32),
            pltpu.SemaphoreType.DMA,
            pltpu.SemaphoreType.DMA,
        ],
        name=f"feed_backward_{layer}",
    )


def middle_backward(
    dims, layer, sc, g, x1, sums, branch, mod, weights, queries, kept, probs, exact, cosine, sine
):
    rows, width, narrow, local, count = (
        dims.rows, dims.width, dims.narrow, dims.local, dims.n_heads,
    )
    n_seq, frames = dims.n_seq, dims.frames
    heads = local // HEAD_DIM
    scale = 1.0 / math.sqrt(HEAD_DIM)

    def body(sc, g, x1, *refs):
        sums = refs[:count]
        branch, mod, w_own, w_other, queries, kept, probs, exact, cosine, sine = refs[
            count : count + 10
        ]
        d_mid_out, dy_out, small, q_out = refs[count + 10 : count + 14]
        outs = refs[count + 14 : count + 14 + n_seq]
        weight, buffer, other, done, sem = refs[count + 14 + n_seq :]
        fetch = Fetch(sc, layer, w_own, w_other, weight, sem)
        seg = segments(sc, (rows, 1), 0, sc[1] * rows)
        mine = pl.ds(pl.multiple_of(sc[0] * narrow, narrow), narrow)
        place(buffer, sums, sc[0], narrow)
        dxf = buffer[...]
        normed, inv = norm_of(x1[...])
        other[...] = dxf * normed
        small[1] = utterance_sums(buffer[:, mine], seg)
        small[2] = utterance_sums(other[:, mine], seg)
        d_mid = g[...].astype(F32) + norm_pull(
            dxf * (1.0 + spread(mod, layer, 4, seg)), normed, inv
        )
        d_mid_out[...] = d_mid
        other[...] = d_mid
        small[0] = utterance_sums(other[:, mine] * branch[...].astype(F32), seg)
        dy = (d_mid * spread(mod, layer, 2, seg)).astype(BF)
        dy_out[...] = dy
        fetch.wait()
        d_att = dot(dy, weight[...], ((1,), (1,))).astype(BF)
        shared = d_att.astype(F32) * exact[...]
        d_keys, d_vals = [], []
        cos = cosine[:, :HEAD_DIM]
        sin = -sine[:, :HEAD_DIM]
        for head in range(heads):
            cols = slice(head * HEAD_DIM, (head + 1) * HEAD_DIM)
            vals = slice(local + head * HEAD_DIM, local + (head + 1) * HEAD_DIM)
            low = probs[head]
            prob = low.astype(F32)
            grad = d_att[:, cols]
            d_prob = dot(grad, kept[:, vals], ((1,), (1,)))
            delta = jnp.sum(shared[:, cols], axis=1, keepdims=True)
            d_score = (prob * (d_prob - delta)).astype(BF)
            dq = dot(d_score, kept[:, cols]) * scale
            q_out[:, cols] = turn(dq, cos, sin).astype(BF)
            d_keys.append((dot(queries[:, cols], d_score, ((0,), (0,))) * scale).astype(BF))
            d_vals.append(dot(grad, low, ((0,), (0,))).astype(BF))
        for first, parts in ((0, d_keys), (local, d_vals)):
            for head in range(0, heads, 2):
                at = first + head * HEAD_DIM
                both = jnp.concatenate(parts[head : head + 2], axis=0)
                done[:, at : at + 2 * HEAD_DIM] = both.T
        for k in range(n_seq):
            at = pl.multiple_of(jnp.bitwise_xor(sc[1], k) * rows, rows)
            outs[k][...] = done[pl.ds(at, rows), :]

    return call(
        body,
        [sc, g, x1]
        + sums
        + [branch, mod, weights[0], weights[1], queries, kept, probs, exact, cosine, sine],
        [SM, VM, VM] + [VM] * count + [VM, VM, HB, HB] + [VM] * 6,
        [
            sds((rows, width), F32),
            sds((rows, width), BF),
            sds((3, 4, narrow), F32),
            sds((rows, local), BF),
        ]
        + [sds((rows, 2 * local), BF)] * n_seq,
        [
            pltpu.VMEM(weights[0].shape, BF),
            pltpu.VMEM((rows, width), F32),
            pltpu.VMEM((rows, width), F32),
            pltpu.VMEM((frames, 2 * local), BF),
            pltpu.SemaphoreType.DMA,
        ],
        name=f"middle_backward_{layer}",
    )


def project_backward(dims, layer, sc, dy, d_query, chunks, weights, cosine, sine):
    rows, width, narrow, local, count = (
        dims.rows, dims.width, dims.narrow, dims.local, dims.n_heads,
    )
    n_in = len(chunks)

    def body(sc, dy, d_query, *refs):
        chunks = refs[:n_in]
        w_own, w_other, cosine, sine, d_out = refs[n_in : n_in + 5]
        outs = refs[n_in + 5 : n_in + 5 + count]
        weight, buffer, sem = refs[n_in + 5 + count :]
        fetch = Fetch(sc, layer, w_own, w_other, weight, sem)
        total = chunks[0][...].astype(F32)
        for chunk in chunks[1:]:
            total = total + chunk[...].astype(F32)
        cos = widen_table(cosine[...], local)
        sin = -widen_table(sine[...], local)
        dk = turn(total[:, :local], cos, sin).astype(BF)
        dv = total[:, local:].astype(BF)
        d_out[:, :width] = dy[...]
        for i, part in enumerate((d_query[...], dk, dv)):
            d_out[:, width + i * local : width + (i + 1) * local] = part
        fetch.wait()
        total = dot(d_query[...], weight[0], ((1,), (1,)))
        total = total + dot(dk, weight[1], ((1,), (1,)))
        total = total + dot(dv, weight[2], ((1,), (1,)))
        buffer[...] = total.astype(BF)
        hand_out(outs, buffer, sc[0], narrow)

    return call(
        body,
        [sc, dy, d_query] + chunks + [weights[0], weights[1], cosine, sine],
        [SM, VM, VM] + [VM] * n_in + [HB, HB, VM, VM],
        [sds((rows, width + 3 * local), BF)] + [sds((rows, narrow), BF)] * count,
        [
            pltpu.VMEM(weights[0].shape, BF),
            pltpu.VMEM((rows, width), BF),
            pltpu.SemaphoreType.DMA,
        ],
        name=f"project_backward_{layer}",
    )


def products(left, right, local, width):
    first = dot(left[:, :local], right[:, :width], ((0,), (0,))).astype(BF)
    rest = dot(left[:, local:], right[:, width:], ((0,), (0,))).astype(BF)
    out = [[(slice(None), first)]]
    for i in range(rest.shape[1] // local):
        columns = slice(i * local, (i + 1) * local)
        lines = [slice(group * local, (group + 1) * local) for group in range(width // local)]
        out.append([(line, rest[line, columns]) for line in lines])
    return out


def half_grads(sc, left, right, local, name):
    width = left.shape[1] - local
    count = (1 + (right.shape[1] - width) // local) // 2

    def body(sc, left, right, mine, theirs):
        grads = products(left[...], right[...], local, width)
        for section in range(2):

            @pl.when(sc[2] == section)
            def _(section=section):
                for out, first in ((mine, section * count), (theirs, (1 - section) * count)):
                    for i in range(count):
                        for columns, value in grads[first + i]:
                            out[i * local : (i + 1) * local, columns] = value

    return call(
        body,
        [sc, left, right],
        [SM, VM, VM],
        [sds((count * local, width), BF)] * 2,
        name=name,
    )


def whole_grads(sc, left, right, local, name):
    count = len(left)
    rows, wide = left[0].shape
    width = wide - local
    tensors = 1 + (right[0].shape[1] - width) // local

    def body(sc, *refs):
        left, right = refs[:count], refs[count : 2 * count]
        out, all_left, all_right = refs[2 * count :]
        for k in range(count):
            all_left[k * rows : (k + 1) * rows, :] = left[k][...]
            all_right[k * rows : (k + 1) * rows, :] = right[k][...]
        grads = products(all_left[...], all_right[...], local, width)
        for i, grad in enumerate(grads):
            for columns, value in grad:
                out[i * local : (i + 1) * local, columns] = value

    return call(
        body,
        [sc] + list(left) + list(right),
        [SM] + [VM] * (2 * count),
        [sds((tensors * local, width), BF)],
        [
            pltpu.VMEM((count * rows, wide), BF),
            pltpu.VMEM((count * rows, right[0].shape[1]), BF),
        ],
        limit=24,
        name=name,
    )[0]


def add_split(sc, left, right, step):
    rows, width = left.shape
    half = rows // 2

    def body(sc, left, right, keep, send):
        bit = sc[5 + step]
        mine = pl.ds(pl.multiple_of(bit * half, half), half)
        other = pl.ds(pl.multiple_of((1 - bit) * half, half), half)
        keep[...] = (left[mine, :].astype(F32) + right[mine, :].astype(F32)).astype(BF)
        send[...] = (left[other, :].astype(F32) + right[other, :].astype(F32)).astype(BF)

    return call(
        body, [sc, left, right], [SM, VM, VM], [sds((half, width), BF)] * 2, name="add_split"
    )


def join(sc, mine, other, step):
    half, width = mine.shape

    def body(sc, mine, other, out):
        bit = sc[5 + step]
        out[pl.ds(pl.multiple_of(bit * half, half), half), :] = mine[...]
        out[pl.ds(pl.multiple_of((1 - bit) * half, half), half), :] = other[...]

    return call(
        body, [sc, mine, other], [SM, VM, VM], [sds((2 * half, width), BF)], name="join"
    )[0]


class HalfSum:
    def __init__(self, sc, layer, left, right, local, name):
        self.sc, self.layer = sc, layer
        self.mine, self.ready = half_grads(sc, left, right, local, name)
        self.bits = lax.axis_size("seq").bit_length() - 1
        self.at = 0
        self.taken = True
        self.pieces = []

    def send(self, *begin):
        value, bits = after(self.ready, *begin), self.bits
        if self.at == 0:
            self.came = swap(value)
        elif self.at <= bits:
            self.came = crossed(value, self.at - 1)
        else:
            if self.at == 2 * bits and not self.pieces:
                self.hand_over(value)
            self.came = crossed(value, 2 * bits - self.at)
        self.at += 1
        self.taken = False
        return self.came

    def hand_over(self, value):
        self.pieces.append((value, to_owner(value, self.layer)))

    def take(self):
        sc, bits = self.sc, self.bits
        self.taken = True
        if self.at <= bits:
            self.mine, self.ready = add_split(sc, self.mine, self.came, self.at - 1)
        elif self.at == bits + 1:
            self.mine = self.ready = add_chunks([self.mine, self.came])
        else:
            self.mine = self.ready = join(sc, self.mine, self.came, 2 * bits + 1 - self.at)
        return self.ready

    def last(self, *begin):
        while self.at <= 2 * self.bits:
            if not self.taken:
                self.take()
            self.send()
        self.hand_over(after(self.came, *begin))
        (own_0, other_0), (own_1, other_1) = self.pieces
        return [own_0, own_1, other_0, other_1]


class Spread:
    def __init__(self, value):
        self.parts = [value]
        self.bits = lax.axis_size("seq").bit_length() - 1
        self.early = None

    def one(self, *begin):
        self.parts.append(crossed(after(self.parts[0], *begin), 0))
        return self.parts[1]

    def two(self, *begin):
        self.early = crossed(after(self.parts[0], *begin), 1)
        return self.early

    def rest(self, *begin):
        for bit in range(1, self.bits):
            more = [] if bit > 1 else [self.early]
            start = 0 if bit > 1 else 1
            for part in self.parts[start:]:
                more.append(crossed(after(part, *begin), bit))
            self.parts = self.parts + more
        return self.parts[3:]


class Assembly:
    SCRATCH = 5

    @staticmethod
    def scratch(added, local, outs):
        width = added[0].shape[1]
        return [
            pltpu.VMEM((local, width), F32),
            pltpu.VMEM((outs - 1, width, local), F32),
            pltpu.VMEM((2, outs * local, width), BF),
            pltpu.SemaphoreType.DMA((outs, 2)),
            pltpu.SemaphoreType.DMA((outs,)),
        ]

    def __init__(self, sc, added, pieces, outs, scratch):
        self.sc, self.added, self.pieces = sc, added, pieces
        self.first_out, self.rest_out = outs
        self.first, self.rest, self.held, self.sems, self.out_sems = scratch
        self.outs = 1 + self.rest.shape[0]
        self.local, self.width = self.first.shape
        self.size = pieces[0].shape[0]

    def fetches_added(self):
        copies = []
        for i in range(self.outs):
            at = pl.ds(i * self.local, self.local)
            for j in range(2):
                copies.append(
                    pltpu.make_async_copy(
                        self.added[j].at[at, :], self.held.at[j, at, :], self.sems.at[i, j]
                    )
                )
        return copies

    def fetches_pieces(self):
        return [
            pltpu.make_async_copy(
                self.pieces[p],
                self.held.at[0, pl.ds(p * self.size, self.size), :],
                self.sems.at[p // 2, p % 2],
            )
            for p in range(4)
        ]

    def start(self):
        @pl.when(self.sc[2] == 0)
        def _():
            for copy in self.fetches_added():
                copy.start()

        @pl.when(self.sc[2] == 1)
        def _():
            for copy in self.fetches_pieces():
                copy.start()

    def store(self, index):
        if index == 0:
            return pltpu.make_async_copy(self.first, self.first_out, self.out_sems.at[0])
        return pltpu.make_async_copy(
            self.rest.at[index - 1], self.rest_out.at[index - 1], self.out_sems.at[index]
        )

    def put(self, index, value, line):
        lines = value.shape[0]
        if index == 0:
            self.first[line : line + lines, :] = value
            return
        for group in range(self.width // self.local):
            columns = slice(group * self.local, (group + 1) * self.local)
            at = group * self.local + line
            self.rest[index - 1, at : at + lines, :] = value[:, columns]

    def run(self):
        sc, local, size, held = self.sc, self.local, self.size, self.held
        count = self.outs // 2

        @pl.when(sc[2] == 0)
        def _():
            copies = self.fetches_added()
            for i in range(self.outs):
                copies[2 * i].wait()
                copies[2 * i + 1].wait()
                at = slice(i * local, (i + 1) * local)
                self.put(i, held[0, at, :].astype(F32) + held[1, at, :].astype(F32), 0)
                self.store(i).start()

        bits = lax.axis_size("seq").bit_length() - 1
        low, high = sc[1] & 1, (sc[1] >> (bits - 1)) & 1

        @pl.when(sc[2] == 1)
        def _():
            for copy in self.fetches_pieces():
                copy.wait()
            for section, at, bit in ((1, 0, high), (0, 2, low)):
                for turn in range(2):

                    @pl.when(bit == turn)
                    def _(section=section, at=at, turn=turn):
                        for place in range(2):
                            base = (at + (place ^ turn)) * size
                            for i in range(count):
                                begin = max(i * local, place * size)
                                end = min((i + 1) * local, (place + 1) * size)
                                if begin < end:
                                    row = base + begin - place * size
                                    value = held[0, row : row + end - begin, :].astype(F32)
                                    self.put(section * count + i, value, begin - i * local)

            for i in range(self.outs):
                self.store(i).start()

    def wait(self):
        for i in range(self.outs):
            self.store(i).wait()


def by_section(sc, mine, theirs, layer_0, layer_1):
    mine[...] = jnp.where(sc[2] == 0, layer_0, layer_1)
    theirs[...] = jnp.where(sc[2] == 0, layer_1, layer_0)


def gate_sums(dims, layer, sc, g, x1, z, mod, passed):
    rows, narrow = dims.rows, dims.narrow

    def body(sc, g, x1, z, mod, passed, small, *shown):
        seg = segments(sc, (rows, 1), 0, sc[1] * rows)
        mine = pl.ds(pl.multiple_of(sc[0] * narrow, narrow), narrow)
        value = z[...].astype(F32)
        small[...] = utterance_sums(g[:, mine].astype(F32) * value, seg)
        if shown:
            gate = spread(mod, layer, 5, seg, mine)
            result = (x1[:, mine] + gate * value).astype(BF)
            by_section(sc, *shown, passed[...], result)

    outs = [sds((4, narrow), F32)]
    if layer == 1:
        outs += [sds((rows, narrow), BF)] * 2
    return call(
        body, [sc, g, x1, z, mod, passed], [SM] + [VM] * 5, outs, name=f"gate_sums_{layer}"
    )


def last_norm(dims, sc, terms, x, mod, small_0, small_1):
    rows, narrow, count = dims.rows, dims.narrow, dims.n_heads

    def body(sc, *refs):
        terms = refs[:count]
        x, mod, mid_0, gate_0, in_1, mid_1, gate_1 = refs[count : count + 7]
        total_out, normed_out, inv_out, mine_out, theirs_out, rows_out, buffer = refs[count + 7 :]
        seg = segments(sc, (rows, 1), 0, sc[1] * rows)
        mine = pl.ds(pl.multiple_of(sc[0] * narrow, narrow), narrow)
        total = terms[0][...].astype(F32)
        for term in terms[1:]:
            total = total + term[...].astype(F32)
        normed, inv = norm_of(x[...].astype(F32))
        buffer[...] = normed
        normed = buffer[:, mine]
        first = (
            [utterance_sums(total, seg), utterance_sums(total * normed, seg)]
            + [mid_0[i] for i in range(3)]
            + [gate_0[...]]
        )
        second = [in_1[0], in_1[1]] + [mid_1[i] for i in range(3)] + [gate_1[...]]
        for i in range(6):
            by_section(sc, mine_out.at[i], theirs_out.at[i], first[i], second[i])
        grad = total * (1.0 + spread(mod, 0, 1, seg, mine))
        total_out[...] = grad
        normed_out[...] = normed
        inv_out[...] = inv
        lane = lax.broadcasted_iota(jnp.int32, (rows, 128), 1)
        sums = jnp.where(lane == 0, jnp.sum(grad, axis=1, keepdims=True), 0.0)
        sums = jnp.where(lane == 1, jnp.sum(grad * normed, axis=1, keepdims=True), sums)
        pick = diagonal(8, 128)
        rows_out[...] = sum(dot(pick, part, ((1,), (1,))) for part in split3(sums))

    return call(
        body,
        [sc] + terms + [x, mod] + small_0 + small_1,
        [SM] + [VM] * (count + 7),
        [
            sds((rows, narrow), F32),
            sds((rows, narrow), F32),
            sds((rows, 1), F32),
            sds((6, 4, narrow), F32),
            sds((6, 4, narrow), F32),
            sds((8, rows), F32),
        ],
        [pltpu.VMEM((rows, dims.width), F32)],
        name="last_norm",
    )


def last_pull(dims, sc, d_mid, grad, normed, inv, sums, middle_grad):
    rows, narrow, count, width = dims.rows, dims.narrow, dims.n_heads, dims.width

    def body(sc, d_mid, grad, normed, inv, middle, *refs):
        sums, outs = refs[:count], refs[count:]
        total = sums[0][:8, :rows]
        for term in sums[1:]:
            total = total + term[:8, :rows]
        row = lax.broadcasted_iota(jnp.int32, (8, 128), 0)
        lane = lax.broadcasted_iota(jnp.int32, (8, 128), 1)
        pick = (row == 4 * lane + 3).astype(BF)
        total = sum(dot(part, pick, ((0,), (0,))) for part in split3(total * (1.0 / width)))
        mine = pl.ds(pl.multiple_of(sc[0] * narrow, narrow), narrow)
        first = d_mid[:, mine] + inv[...] * (
            grad[...] - total[:, 0:1] - normed[...] * total[:, 1:2]
        )
        by_section(sc, *outs, first, middle[...])

    return call(
        body,
        [sc, d_mid, grad, normed, inv, middle_grad] + sums,
        [SM] + [VM] * (5 + count),
        [sds((rows, narrow), F32)] * 2,
        name="last_pull",
    )


def modulation_part(sc, mod_weight, row_sums, own, n_seq):
    kinds, width, narrow = mod_weight.shape

    def body(sc, mod_weight, row_sums, *refs):
        own = refs[:n_seq]
        grads_out, part, box = refs[n_seq:]
        for k in range(n_seq):
            box[jnp.bitwise_xor(sc[1], k)] = own[k][...]
        total = box[0]
        for j in range(1, n_seq):
            total = total + box[j]
        result = jnp.zeros((8, width), F32)
        for which in range(kinds):
            mine, theirs = total[which], total[kinds + which]
            grad = jnp.concatenate(
                [jnp.where(sc[2] == 0, mine, theirs), jnp.where(sc[2] == 0, theirs, mine)],
                axis=0,
            )
            grads_out[which] = grad
            result = result + exact_dot(grad, mod_weight[which], ((1,), (1,)))
        part[...] = result
        for row in range(2):
            part[4 * row + 3 : 4 * row + 4, : row_sums.shape[1]] = row_sums[row : row + 1, :]

    return call(
        body,
        [sc, mod_weight, row_sums] + own,
        [SM, VM, VM] + [VM] * n_seq,
        [sds((kinds, 8, narrow), F32), sds((8, width), F32)],
        [pltpu.VMEM((n_seq, 2 * kinds, 4, narrow), F32)],
        name="modulation_part",
    )


def finish(dims, sc, act, grads, sinus, inner, outer, time_out, own, feed, acts):
    kinds, _, narrow = grads.shape
    count = len(own)
    rows, width = inner.shape
    freq = sinus.shape[1]
    block = width // 4
    sources = list(feed[0]) + list(feed[1])
    slots = 3

    def body(sc, act, grads, sinus, inner, outer, time_out, act_own, act_other, *refs):
        own, sources, refs = refs[:count], refs[count : count + 6], refs[count + 6 :]
        g_mod, g_in, g_out, feed_first, feed_rest, shown = refs[:6]
        box, held_mod, held_in, held_out, mod_sems, time_sems = refs[6:12]
        feed = Assembly(sc, sources[:2], sources[2:], (feed_first, feed_rest), refs[12:])
        feed.start()
        shown[sc[2]] = act_own[...]
        shown[1 - sc[2]] = act_other[...]

        for k in range(count):
            at = jnp.bitwise_xor(sc[0], k)
            box[at, sc[2]] = own[k][:rows]
            box[at, 1 - sc[2]] = own[k][rows : 2 * rows]
        total = jnp.zeros((rows, width), F32)
        for j in range(count):
            for c in range(2):
                total = total + box[j, c]
        row = lax.broadcasted_iota(jnp.int32, (rows, width), 0)
        total = jnp.where(row % 4 == 3, 0.0, total)

        def slope(value):
            gate = 1.0 / (1.0 + jnp.exp(-value))
            return gate * (1.0 + value * (1.0 - gate))

        pre = inner[...]
        hidden = pre / (1.0 + jnp.exp(-pre))
        d_outer = total * slope(outer[...])
        tall, wide = outer_parts(hidden, d_outer)
        tall = tall.astype(F32).T.astype(BF)
        copies = []
        for i in range(4):
            at = slice(i * block, (i + 1) * block)
            held_out[at, :] = dot(tall[at], wide)
            copies.append(
                pltpu.make_async_copy(held_out.at[at, :], g_out.at[at, :], time_sems.at[i])
            )
            copies[-1].start()
        d_inner = exact_dot(d_outer, time_out[...], ((1,), (1,))) * slope(pre)
        held_in[...] = exact_outer(sinus[...], d_inner)
        copies.append(pltpu.make_async_copy(held_in, g_in, time_sems.at[4]))
        copies[-1].start()

        tall = outer_parts(act[...], act[...])[0].astype(F32).T.astype(BF)

        def store(which):
            return pltpu.make_async_copy(
                held_mod.at[which % slots], g_mod.at[which], mod_sems.at[which % slots]
            )

        for which in range(kinds):
            if which >= slots:
                store(which - slots).wait()
            wide = outer_parts(grads[which], grads[which])[1]
            held_mod[which % slots] = dot(tall, wide)
            store(which).start()

        feed.run()
        for which in range(kinds - slots, kinds):
            store(which).wait()
        for copy in copies:
            copy.wait()
        feed.wait()

    return pl_call(
        body,
        [sc, act, grads, sinus, inner, outer, time_out] + list(acts) + list(own) + sources,
        [SM] + [VM] * (8 + count) + [HB] * 6,
        [
            sds((kinds, width, narrow), F32),
            sds((freq, width), F32),
            sds((width, width), F32),
            sds((dims.hidden, width), F32),
            sds((1, width, dims.hidden), F32),
            sds((2,) + acts[0].shape, BF),
        ],
        [HB] * 5 + [VM],
        [
            pltpu.VMEM((count, 2, rows, width), F32),
            pltpu.VMEM((slots, width, narrow), F32),
            pltpu.VMEM((freq, width), F32),
            pltpu.VMEM((width, width), F32),
            pltpu.SemaphoreType.DMA((slots,)),
            pltpu.SemaphoreType.DMA((5,)),
        ]
        + Assembly.scratch(feed[0], dims.hidden, 2),
        limit=24,
        name="finish",
    )


def finish_attention(dims, sc, attention, grads):
    def body(sc, own, other, *refs):
        attention = Assembly(sc, refs[:2], refs[2:6], refs[6:8], refs[9:])
        attention.start()
        refs[8][sc[2]] = own[...]
        refs[8][1 - sc[2]] = other[...]
        attention.run()
        attention.wait()

    width = dims.width
    return pl_call(
        body,
        [sc] + list(grads) + list(attention[0]) + list(attention[1]),
        [SM] + [VM] * 2 + [HB] * 6,
        [
            sds((dims.local, width), F32),
            sds((3, width, dims.local), F32),
            sds((2,) + grads[0].shape, F32),
        ],
        [HB] * 2 + [VM],
        Assembly.scratch(attention[0], dims.local, 4),
        limit=16,
        name="finish_attention",
    )


class Dims:
    pass


def local_program(
    frames,
    cotangent,
    utt_lengths,
    time_ids,
    w_time_in,
    w_time_out,
    w_mod,
    w_qkv,
    w_out,
    w_up,
    w_down,
):
    dims = Dims()
    dims.n_heads = lax.axis_size("heads")
    dims.n_seq = n_seq = lax.axis_size("seq")
    _, dims.rows, dims.narrow = frames.shape
    dims.width = dims.narrow * dims.n_heads
    dims.local = w_qkv.shape[3]
    dims.hidden = w_up.shape[2]
    dims.frames = dims.rows * n_seq
    section = lax.axis_index("section")

    def here(both):
        return lax.dynamic_index_in_dim(both, section, 0, keepdims=False)

    sc = utt_lengths
    qkv = jnp.transpose(w_qkv[0], (1, 0, 2))
    mod_weight = jnp.transpose(w_mod[0], (1, 0, 2))
    wide_frames = gather(here(frames), "heads")
    qkv_w = (qkv, swap(qkv))
    sinus, inner, outer, act, mod_mine, mod_theirs = start(
        sc, time_ids, w_time_in, w_time_out, mod_weight
    )
    mod_theirs = swap(after(mod_theirs, *wide_frames))
    mods = gather(jnp.concatenate([mod_mine, mod_theirs], axis=0), "heads")
    cosine, sine = tables(sc, dims.rows)
    mods = after(mods, cosine, sine)

    x_0, _, xa, q_0, kv, mod = project(dims, 0, sc, wide_frames, mods, qkv_w, cosine, sine)
    chunks = gather(kv, "seq")
    out_w = (w_out[0], swap(after(w_out[0], mods[0])))
    kept_0, probs_0, for_attention, exact_0, *terms = attend(
        dims, 0, sc, chunks, q_0, xa, out_w
    )
    fwd_a = Spread(for_attention)

    up_w, down_w = [(w[0], swap(after(w[0], terms[0]))) for w in (w_up, w_down)]
    total = after(add_chunks(exchange(terms, "heads")), up_w[1], down_w[1])

    branch_0 = gather(total, "heads")
    fwd_a.one(total)
    fwd_a.two(total)
    x1_0, for_feed, slope_0, *terms = feed_forward(
        dims, 0, sc, x_0, branch_0, mod, up_w, down_w
    )
    fwd_f = Spread(for_feed)

    total = after(add_chunks(exchange(terms, "heads")), fwd_a.parts[1], fwd_a.early)

    z_0 = gather(total, "heads")
    fwd_a.rest(total)
    fwd_f.one(total)

    x_2, passed, xa, q_1, kv = project(
        dims, 1, sc, [x1_0] + z_0, [mod], qkv_w, cosine, sine
    )
    kv = after(kv, fwd_f.parts[1], *fwd_a.parts[3:])
    chunks = gather(kv, "seq")
    wide_cotangent = gather(after(here(cotangent), chunks[1]), "heads")
    kept_1, probs_1, for_attention_1, exact_1, *terms = attend(
        dims, 1, sc, chunks, q_1, xa, out_w
    )

    terms[0] = after(terms[0], *wide_cotangent)
    total = add_chunks(exchange(terms, "heads"))
    fwd_f.two(terms[0])

    branch_1 = gather(total, "heads")
    x1_1, for_feed, slope_1, *z_terms = feed_forward(
        dims, 1, sc, x_2, branch_1, mod, up_w, down_w
    )
    g_1, late, *terms = feed_backward(
        dims, 1, sc, wide_cotangent, slope_1, mod, up_w, down_w
    )
    terms = after(terms, fwd_f.early)
    feed_1 = HalfSum(sc, 1, for_feed, late, dims.hidden, "feed_grads_1")
    feed_1.send()
    got = exchange(terms, "heads")
    total = after(add_chunks(got), feed_1.came, *fwd_f.rest(terms[0]))

    feed_1.take()
    feed_1.send(total)
    sums = after(gather(total, "heads"), feed_1.came)

    feed_1.take()
    feed_1.send(sums[0])
    d_mid_1, dy, small_f1, dq, *sent = middle_backward(
        dims, 1, sc, g_1, x1_1, after(sums, feed_1.ready), branch_1[0], mod, out_w,
        q_1, kept_1, probs_1, exact_1, cosine, sine,
    )
    sent = after(sent, feed_1.came)

    got = exchange(sent, "seq")
    feed_1.take()
    z_1 = add_chunks(exchange(after(z_terms, sent[0]), "heads"))
    gate_1, *acts = gate_sums(dims, 1, sc, g_1, x1_1, z_1, mod, passed)
    got = after(got, feed_1.ready, *acts)
    late, *terms = project_backward(dims, 1, sc, dy, dq, got, qkv_w, cosine, sine)

    got = exchange(terms, "heads")
    feed_1.send(terms[0])
    attention_1 = HalfSum(sc, 1, for_attention_1, late, dims.local, "attend_grads_1")
    acts = [acts[0], swap(after(acts[1], terms[0]))]
    total = after(
        add_chunks(got), feed_1.came, attention_1.mine, attention_1.ready, acts
    )

    feed_1.take()
    feed_1.send(total)
    attention_1.send(total)
    pieces = after(gather(total, "heads"), feed_1.came, attention_1.came)

    g_0, late, *rest = feed_backward(
        dims, 0, sc, pieces + [x_2, d_mid_1], slope_0, mod, up_w, down_w
    )
    terms, (middle_grad, small_a1) = rest[: dims.n_heads], rest[dims.n_heads :]
    late_f = Spread(late)
    got = exchange(terms, "heads")
    attention_1.take()
    attention_1.send(terms[0])
    total = after(add_chunks(got), attention_1.came, late_f.one(terms[0]))

    attention_1.take()
    attention_1.send(total)
    sums = after(gather(total, "heads"), attention_1.came, late_f.two(total))

    attention_1.take()
    attention_1.send(sums[0])
    d_mid_0, dy, small_f0, dq, *sent = middle_backward(
        dims, 0, sc, g_0, x1_0, after(sums, attention_1.ready), branch_0[0], mod, out_w,
        q_0, kept_0, probs_0, exact_0, cosine, sine,
    )
    sent = after(sent, attention_1.came)

    got = exchange(sent, "seq")
    attention_1.take()
    if attention_1.at == 2 * attention_1.bits:
        attention_1.hand_over(after(attention_1.ready, got[0]))
    feed_1 = feed_1.last(sent[0])
    gate_0, *_ = gate_sums(dims, 0, sc, g_0, x1_0, z_0[0], mod, passed)
    got = after(got, attention_1.ready, gate_0, feed_1)
    late, *terms = project_backward(dims, 0, sc, dy, dq, got, qkv_w, cosine, sine)
    late_a = Spread(late)

    got = exchange(terms, "heads")
    got = after(got, late_a.one(terms[0]), *late_f.rest(terms[0]))

    grad, normed, inv, mine, theirs, row_sums = last_norm(
        dims, sc, got, x_0, mod, [small_f0, gate_0], [small_a1, small_f1, gate_1]
    )
    attention_1.send(row_sums)
    theirs = swap(theirs)
    both = jnp.concatenate([mine, theirs], axis=0)
    both = gather(both, "seq")
    feed_0 = whole_grads(
        sc, after(fwd_f.parts, theirs), late_f.parts, dims.hidden, "feed_grads_0"
    )
    both = after(both, feed_0, attention_1.came)
    mod_grads, part = modulation_part(sc, mod_weight, row_sums, both, n_seq)

    late_a.two(part)
    late_a.rest(part)
    feed_0 = [feed_0, to_owner(after(feed_0, both[0]), 0)]
    attention_1 = attention_1.last(both[0])
    ends = jnp.concatenate([part, swap(part)], axis=0)
    ends = after(ends, feed_0, attention_1)
    ends = after(gather(ends, "heads"), late_a.early, *late_a.parts[3:])

    attention_0 = whole_grads(
        sc, after(fwd_a.parts, *ends), late_a.parts, dims.local, "attend_grads_0"
    )
    attention_0 = [attention_0, to_owner(attention_0, 0)]
    grads = last_pull(dims, sc, d_mid_0, grad, normed, inv, ends, middle_grad)
    g_mod, g_first, g_second, g_reduce, g_expand, acts = finish(
        dims, sc, act, mod_grads, sinus, inner, outer, w_time_out,
        after(ends, grads[0], attention_0[0]), (feed_0, feed_1), acts,
    )
    grads = [grads[0], swap(after(grads[1], g_second))]
    g_out, g_qkv, grads = finish_attention(
        dims, sc, (after(attention_0, g_second), attention_1), grads
    )

    return (
        acts[None],
        grads[None],
        g_first,
        g_second,
        jnp.transpose(g_mod, (1, 0, 2))[None],
        jnp.transpose(g_qkv, (1, 0, 2))[None],
        g_out[None],
        g_expand,
        g_reduce[None],
    )


def solution(mesh):
    placed = (
        P(None, "seq", "heads"),
        P(None, "seq", "heads"),
        P(),
        P(),
        P(),
        P(),
        P("section", None, None, "heads"),
        P("section", None, None, "heads"),
        P("section", "heads", None),
        P("section", None, "heads"),
        P("section", "heads", None),
    )
    return jax.shard_map(
        local_program,
        mesh=mesh,
        in_specs=placed,
        out_specs=(
            P("section", None, "seq", "heads"),
            P("section", None, "seq", "heads"),
            P(),
            P(),
            P("section", None, None, "heads"),
            P("section", None, None, "heads"),
            P("section", "heads", None),
            P("section", None, "heads"),
            P("section", "heads", None),
        ),
        check_vma=False,
    )
```

```python
import functools
import math

import jax
import jax.numpy as jnp
import numpy as np
from jax import lax
from jax.experimental import pallas as pl
from jax.experimental.pallas import tpu as pltpu
from jax.sharding import PartitionSpec as P

HEAD_DIM = 64
FREQ = 256
EPS = 1e-06
BF = jnp.bfloat16
F32 = jnp.float32
MIB = 1024 * 1024


def partner(value, axis, by):
    if by == 0:
        return value
    return lax.ppermute(value, axis, [(i, i ^ by) for i in range(lax.axis_size(axis))])


def order_of(count):
    return (3, 1, 2) if count == 4 else tuple(range(count - 1, 0, -1))


def gather(value, axis):
    count = lax.axis_size(axis)
    out = [value] * count
    for k in order_of(count):
        out[k] = partner(value, axis, k)
    return out


def exchange(chunks, axis):
    out = list(chunks)
    for k in order_of(len(chunks)):
        out[k] = partner(chunks[k], axis, k)
    return out


def swap(value):
    return lax.ppermute(value, "section", [(0, 1), (1, 0)])


def to_owner(value, layer):
    return lax.ppermute(value, "section", [(1 - layer, layer)])


def crossed(value, step):
    length = lax.axis_size("seq")
    last = length.bit_length() - 2
    pairs = []
    for c in range(2):
        by = 1 << (step if c == 0 else last - step)
        pairs += [(c * length + i, c * length + (i ^ by)) for i in range(length)]
    return lax.ppermute(value, ("section", "seq"), pairs)


def after(value, *done):
    value = lax.optimization_barrier((value, done))[0]
    return list(value) if isinstance(value, (list, tuple)) else value


def add_chunks(chunks):
    total = chunks[0].astype(F32)
    for chunk in chunks[1:]:
        total = total + chunk.astype(F32)
    return total.astype(BF)


def dot(left, right, contract=((1,), (0,))):
    return lax.dot_general(left, right, (contract, ((), ())), preferred_element_type=F32)


def split3(value):
    high = value.astype(BF)
    rest = value - high.astype(F32)
    middle = rest.astype(BF)
    low = (rest - middle.astype(F32)).astype(BF)
    return high, middle, low


def diagonal(rows, columns):
    row = lax.broadcasted_iota(jnp.int32, (rows, columns), 0)
    return (row == lax.broadcasted_iota(jnp.int32, (rows, columns), 1)).astype(BF)


def exact_dot(left, right, contract=((1,), (0,))):
    rows = left.shape[0]
    stacked = jnp.concatenate(split3(left), axis=0)
    out = dot(stacked, right, contract)
    return out[:rows] + (out[rows : 2 * rows] + out[2 * rows :])


def exact_outer(left, right):
    tall, wide = outer_parts(left, right)
    return dot(tall, wide, ((0,), (0,)))


def outer_parts(left, right):
    a, b = split3(left), split3(right)
    tall = jnp.concatenate([a[0], a[0], a[1]], axis=0)
    wide = jnp.concatenate([b[0], b[1], b[0]], axis=0)
    return tall, wide


def segments(sc, shape, axis, first):
    index = lax.broadcasted_iota(jnp.int32, shape, axis) + first
    return (index >= sc[3]).astype(jnp.int32) + (index >= sc[4]).astype(jnp.int32)


def spread(mod, layer, which, seg, columns=slice(None)):
    block = mod[layer * 6 + which, :, columns]
    rows = [block[u : u + 1] for u in range(3)]
    return jnp.where(seg == 0, rows[0], jnp.where(seg == 1, rows[1], rows[2]))


def utterance_sums(value, seg):
    rows = [
        jnp.sum(jnp.where(seg == u, value, 0.0), axis=0, keepdims=True) for u in range(3)
    ]
    return jnp.concatenate(rows + [jnp.zeros_like(rows[0])], axis=0)


def norm_of(value):
    mean = jnp.mean(value, axis=1, keepdims=True)
    centred = value - mean
    inv = lax.rsqrt(jnp.mean(centred * centred, axis=1, keepdims=True) + EPS)
    return centred * inv, inv


def norm_pull(grad, normed, inv):
    return inv * (
        grad
        - jnp.mean(grad, axis=1, keepdims=True)
        - normed * jnp.mean(grad * normed, axis=1, keepdims=True)
    )


def lanes_of(index, count, width):
    return pl.ds(pl.multiple_of(lax.rem(index, count) * width, width), width)


def place(buffer, chunks, own, width):
    for k, chunk in enumerate(chunks):
        at = pl.multiple_of(jnp.bitwise_xor(own, k) * width, width)
        buffer[:, pl.ds(at, width)] = chunk[...].astype(buffer.dtype)


def hand_out(outs, buffer, own, width):
    for k, out in enumerate(outs):
        at = pl.multiple_of(jnp.bitwise_xor(own, k) * width, width)
        out[...] = buffer[:, pl.ds(at, width)].astype(out.dtype)


class Fetch:
    def __init__(self, sc, layer, own, other, buffer, sem):
        self.copy = pltpu.make_async_copy(own, buffer, sem)
        other_copy = pltpu.make_async_copy(other, buffer, sem)

        @pl.when(sc[2] == layer)
        def _():
            self.copy.start()

        @pl.when(sc[2] != layer)
        def _():
            other_copy.start()

    def wait(self):
        self.copy.wait()


def turn(value, cosine, sine):
    width = value.shape[1]
    even = lax.broadcasted_iota(jnp.int32, value.shape, 1) % 2 == 0
    swapped = jnp.where(even, pltpu.roll(value, width - 1, 1), pltpu.roll(value, 1, 1))
    return value * cosine + swapped * sine


def widen_table(table, width):
    copies = width // table.shape[1]
    return jnp.concatenate([table] * copies, axis=1) if copies > 1 else table[:, :width]


VM = pl.BlockSpec(memory_space=pltpu.VMEM)
SM = pl.BlockSpec(memory_space=pltpu.SMEM)
HB = pl.BlockSpec(memory_space=pltpu.HBM)


def sds(shape, dtype):
    return jax.ShapeDtypeStruct(tuple(shape), dtype)


class Place:
    def __init__(self, lengths):
        self.lengths = lengths
        self.known = {}
        for index in range(5):
            self[index]

    def __getitem__(self, index):
        if index not in self.known:
            self.known[index] = self.find(index)
        return self.known[index]

    def find(self, index):
        if index < 3:
            return lax.axis_index(("heads", "seq", "section")[index])
        if index == 3:
            return self.lengths[self[2], 0]
        if index == 4:
            return self[3] + self.lengths[self[2], 1]
        low = index - 5
        high = lax.axis_size("seq").bit_length() - 2 - low
        return jnp.where(self[2] == 0, self[1] >> low, self[1] >> high) & 1


def call(body, ins, specs, outs, scratch=(), limit=12, name=None):
    return pl_call(body, ins, specs, outs, [VM] * len(outs), scratch, limit, name)


def pl_call(body, ins, specs, outs, out_specs, scratch, limit, name):
    def placed(lengths, *refs):
        body(Place(lengths), *refs)

    return pl.pallas_call(
        placed,
        out_shape=list(outs),
        in_specs=list(specs),
        out_specs=list(out_specs),
        scratch_shapes=list(scratch),
        compiler_params=pltpu.CompilerParams(vmem_limit_bytes=limit * MIB),
        cost_estimate=pl.CostEstimate(flops=1, bytes_accessed=1, transcendentals=0),
        name=name,
    )(*ins)


def start(sc, time_ids, time_in, time_out, mod_weight):
    width = time_in.shape[1]
    kinds, _, narrow = mod_weight.shape
    half = FREQ // 2

    def body(sc, ids, time_in, time_out, mod_weight, *refs):
        sinus_out, inner_out, outer_out, act_out, mine_out, theirs_out = refs[:6]
        w_in, w_out, w_mod, sems = refs[6:]
        copies = [
            pltpu.make_async_copy(time_in, w_in, sems.at[0]),
            pltpu.make_async_copy(time_out, w_out, sems.at[1]),
            pltpu.make_async_copy(mod_weight, w_mod, sems.at[2]),
        ]
        for copy in copies:
            copy.start()
        row = lax.broadcasted_iota(jnp.int32, (8, half), 0)
        lane = lax.broadcasted_iota(jnp.int32, (8, half), 1).astype(F32)
        stamp = jnp.zeros((8, half), F32)
        for m in range(2):
            for u in range(3):
                stamp = jnp.where(row == m * 4 + u, ids[m, u].astype(F32), stamp)
        angle_t = stamp * jnp.exp(lane * (-math.log(10000.0) / (half - 1)))
        sinus = jnp.concatenate([jnp.sin(angle_t), jnp.cos(angle_t)], axis=1)
        sinus_out[...] = sinus

        copies[0].wait()
        inner = exact_dot(sinus, w_in[...])
        inner_out[...] = inner
        hidden = inner / (1.0 + jnp.exp(-inner))
        copies[1].wait()
        outer = exact_dot(hidden, w_out[...])
        outer_out[...] = outer
        act = outer / (1.0 + jnp.exp(-outer))
        act_out[...] = act
        copies[2].wait()
        for which in range(kinds):
            modul = exact_dot(act, w_mod[which])
            mine_out[which] = jnp.where(sc[2] == 0, modul[:4], modul[4:])
            theirs_out[which] = jnp.where(sc[2] == 0, modul[4:], modul[:4])

    return call(
        body,
        [sc, time_ids, time_in, time_out, mod_weight],
        [SM, SM, HB, HB, HB],
        [sds((8, FREQ), F32)]
        + [sds((8, width), F32)] * 3
        + [sds((kinds, 4, narrow), F32)] * 2,
        [
            pltpu.VMEM(time_in.shape, BF),
            pltpu.VMEM(time_out.shape, BF),
            pltpu.VMEM(mod_weight.shape, BF),
            pltpu.SemaphoreType.DMA((3,)),
        ],
        limit=56,
        name="start",
    )


def tables(sc, rows):
    def body(sc, cosine, sine):
        index = lax.broadcasted_iota(jnp.int32, (rows, 2 * HEAD_DIM), 0) + sc[1] * rows
        begin = jnp.where(index >= sc[4], sc[4], jnp.where(index >= sc[3], sc[3], 0))
        lane = lax.broadcasted_iota(jnp.int32, (rows, 2 * HEAD_DIM), 1)
        pair = lax.broadcasted_iota(jnp.int32, (1, 2 * HEAD_DIM), 1)
        rate = jnp.exp(
            ((pair % HEAD_DIM) // 2).astype(F32) * (-2.0 * math.log(10000.0) / HEAD_DIM)
        )
        angle = (index - begin).astype(F32) * rate
        cosine[...] = jnp.cos(angle)
        sine[...] = jnp.sin(angle) * jnp.where(lane % 2 == 0, -1.0, 1.0)

    return call(body, [sc], [SM], [sds((rows, 2 * HEAD_DIM), F32)] * 2, name="tables")


def project(dims, layer, sc, pieces, mods, weights, cosine, sine):
    first = layer == 0
    rows, width, narrow, local = dims.rows, dims.width, dims.narrow, dims.local
    count = dims.n_heads
    n_in, n_mod = len(pieces), len(mods)

    def body(sc, *refs):
        pieces, mods = refs[:n_in], refs[n_in : n_in + n_mod]
        w_own, w_other, cosine, sine = refs[n_in + n_mod : n_in + n_mod + 4]
        outs = refs[n_in + n_mod + 4 :]
        x_out, narrow_out, xa_out, q_out, kv_out = outs[:5]
        if first:
            mod = outs[5]
        else:
            mod = mods[0]
        buffer, weight, sem = outs[-3:]
        fetch = Fetch(sc, layer, w_own, w_other, weight, sem)
        seg = segments(sc, (rows, 1), 0, sc[1] * rows)
        if first:
            for k in range(count):
                at = pl.multiple_of(jnp.bitwise_xor(sc[0], k) * narrow, narrow)
                block = mods[k][...]
                for l in range(2):
                    mod[l * 6 : l * 6 + 6, :, pl.ds(at, narrow)] = jnp.where(
                        sc[2] == l, block[:6], block[6:]
                    )
            place(buffer, pieces, sc[0], narrow)
            x = buffer[...]
            x_out[...] = x.astype(BF)
            narrow_out[...] = pieces[0][...]
        else:
            place(buffer, pieces[1:], sc[0], narrow)
            x = pieces[0][...] + spread(mod, 0, 5, seg) * buffer[...]
            low = x.astype(BF)
            x_out[...] = low
            x = low.astype(F32)
            buffer[...] = x
            at = pl.multiple_of(sc[0] * narrow, narrow)
            narrow_out[...] = buffer[:, pl.ds(at, narrow)].astype(BF)
        normed, _ = norm_of(x)
        xa = (normed * (1.0 + spread(mod, layer, 1, seg)) + spread(mod, layer, 0, seg)).astype(BF)
        xa_out[...] = xa
        cos = widen_table(cosine[...], local)
        sin = widen_table(sine[...], local)
        fetch.wait()
        q_out[...] = turn(dot(xa, weight[0]), cos, sin).astype(BF)
        kv_out[:, :local] = turn(dot(xa, weight[1]), cos, sin).astype(BF)
        kv_out[:, local:] = dot(xa, weight[2]).astype(BF)

    return call(
        body,
        [sc] + pieces + mods + [weights[0], weights[1], cosine, sine],
        [SM] + [VM] * (n_in + n_mod) + [HB, HB, VM, VM],
        [
            sds((rows, width), BF),
            sds((rows, narrow), BF),
            sds((rows, width), BF),
            sds((rows, local), BF),
            sds((rows, 2 * local), BF),
        ]
        + ([sds((12, 4, width), F32)] if first else []),
        [
            pltpu.VMEM((rows, width), F32),
            pltpu.VMEM(weights[0].shape, BF),
            pltpu.SemaphoreType.DMA,
        ],
        name=f"project_{layer}",
    )


def attend(dims, layer, sc, chunks, queries, xa, weights):
    rows, n_seq, frames = dims.rows, dims.n_seq, dims.frames
    width, narrow, local, count = dims.width, dims.narrow, dims.local, dims.n_heads
    heads = local // HEAD_DIM

    def body(sc, *refs):
        chunks = refs[:n_seq]
        queries, xa, w_own, w_other = refs[n_seq : n_seq + 4]
        kept, probs, for_grads, exact = refs[n_seq + 4 : n_seq + 8]
        outs = refs[n_seq + 8 : n_seq + 8 + count]
        weight, buffer, sem = refs[n_seq + 8 + count :]
        fetch = Fetch(sc, layer, w_own, w_other, weight, sem)
        for k in range(n_seq):
            at = pl.multiple_of(jnp.bitwise_xor(sc[1], k) * rows, rows)
            kept[pl.ds(at, rows), :] = chunks[k][...]
        same = segments(sc, (rows, 1), 0, sc[1] * rows) == segments(sc, (1, frames), 1, 0)
        for head in range(heads):
            cols = slice(head * HEAD_DIM, (head + 1) * HEAD_DIM)
            scores = dot(queries[:, cols], kept[:, cols], ((1,), (1,)))
            scores = jnp.where(same, scores * (1.0 / math.sqrt(HEAD_DIM)), -1e30)
            prob = jnp.exp(scores - jnp.max(scores, axis=1, keepdims=True))
            prob = prob * (1.0 / jnp.sum(prob, axis=1, keepdims=True))
            low = prob.astype(BF)
            probs[head] = low
            value = kept[:, local + head * HEAD_DIM : local + (head + 1) * HEAD_DIM]
            exact[:, cols] = dot(low, value)
        mixed = exact[...].astype(BF)
        for_grads[:, :local] = mixed
        for_grads[:, local:] = xa[...]
        fetch.wait()
        buffer[...] = dot(mixed, weight[...]).astype(BF)
        hand_out(outs, buffer, sc[0], narrow)

    return call(
        body,
        [sc] + chunks + [queries, xa, weights[0], weights[1]],
        [SM] + [VM] * (n_seq + 2) + [HB, HB],
        [
            sds((frames, 2 * local), BF),
            sds((heads, rows, frames), BF),
            sds((rows, local + width), BF),
            sds((rows, local), F32),
        ]
        + [sds((rows, narrow), BF)] * count,
        [
            pltpu.VMEM(weights[0].shape, BF),
            pltpu.VMEM((rows, width), BF),
            pltpu.SemaphoreType.DMA,
        ],
        name=f"attend_{layer}",
    )


def feed_forward(dims, layer, sc, x, branch, mod, up, down):
    rows, width, narrow, count, hidden = (
        dims.rows, dims.width, dims.narrow, dims.n_heads, dims.hidden,
    )

    def body(sc, x, *refs):
        branch = refs[:count]
        mod, up_own, up_other, down_own, down_other = refs[count : count + 5]
        x1_out, for_grads, slope_out = refs[count + 5 : count + 8]
        outs = refs[count + 8 : 2 * count + 8]
        up, down, buffer, low, sem_up, sem_down = refs[2 * count + 8 :]
        fetch_up = Fetch(sc, layer, up_own, up_other, up, sem_up)
        fetch_down = Fetch(sc, layer, down_own, down_other, down, sem_down)
        seg = segments(sc, (rows, 1), 0, sc[1] * rows)
        place(buffer, branch, sc[0], narrow)
        x1 = x[...].astype(F32) + spread(mod, layer, 2, seg) * buffer[...]
        x1_out[...] = x1
        normed, _ = norm_of(x1)
        xf = (normed * (1.0 + spread(mod, layer, 4, seg)) + spread(mod, layer, 3, seg)).astype(BF)
        for_grads[:, hidden:] = xf
        fetch_up.wait()
        a = dot(xf, up[...])
        c0 = math.sqrt(2.0 / math.pi)
        square = a * a
        t = jnp.tanh(c0 * (a + 0.044715 * (a * square)))
        h = (0.5 * a * (1.0 + t)).astype(BF)
        for_grads[:, :hidden] = h
        slope_out[...] = 0.5 * (1.0 + t) + 0.5 * a * (1.0 - t * t) * (
            c0 * (1.0 + 3.0 * 0.044715 * square)
        )
        fetch_down.wait()
        low[...] = dot(h, down[...]).astype(BF)
        hand_out(outs, low, sc[0], narrow)

    return call(
        body,
        [sc, x] + branch + [mod, up[0], up[1], down[0], down[1]],
        [SM, VM] + [VM] * count + [VM, HB, HB, HB, HB],
        [
            sds((rows, width), F32),
            sds((rows, hidden + width), BF),
            sds((rows, hidden), F32),
        ]
        + [sds((rows, narrow), BF)] * count,
        [
            pltpu.VMEM(up[0].shape, BF),
            pltpu.VMEM(down[0].shape, BF),
            pltpu.VMEM((rows, width), F32),
            pltpu.VMEM((rows, width), BF),
            pltpu.SemaphoreType.DMA,
            pltpu.SemaphoreType.DMA,
        ],
        name=f"feed_forward_{layer}",
    )


def feed_backward(dims, layer, sc, pieces, slope, mod, up, down):
    rows, width, narrow, count, hidden = (
        dims.rows, dims.width, dims.narrow, dims.n_heads, dims.hidden,
    )
    last = layer == 1
    n_in = len(pieces)
    n_extra = 0 if last else 2

    def body(sc, *refs):
        pieces = refs[:n_in]
        slope, mod, up_own, up_other, down_own, down_other = refs[n_in : n_in + 6]
        rest = refs[n_in + 6 :]
        g_out, for_grads = rest[:2]
        outs = rest[2 : 2 + count]
        extra = rest[2 + count : 2 + count + n_extra]
        up, down, buffer, low, other_buffer, sem_up, sem_down = rest[2 + count + n_extra :]
        fetch_down = Fetch(sc, layer, down_own, down_other, down, sem_down)
        fetch_up = Fetch(sc, layer, up_own, up_other, up, sem_up)
        seg = segments(sc, (rows, 1), 0, sc[1] * rows)
        place(buffer, pieces[:count], sc[0], narrow)
        if last:
            g = buffer[...]
            g_out[...] = g.astype(BF)
        else:
            x, d_mid = pieces[count:]
            grad_out, sums_out = extra
            dxa = buffer[...]
            normed, inv = norm_of(x[...].astype(F32))
            other_buffer[...] = dxa * normed
            mine = pl.ds(pl.multiple_of(sc[0] * narrow, narrow), narrow)
            sums_out[0] = utterance_sums(buffer[:, mine], seg)
            sums_out[1] = utterance_sums(other_buffer[:, mine], seg)
            dx = d_mid[...] + norm_pull(dxa * (1.0 + spread(mod, 1, 1, seg)), normed, inv)
            other_buffer[...] = dx
            grad_out[...] = other_buffer[:, mine]
            g = dx.astype(BF)
            g_out[...] = g
            g = g.astype(F32)
        dz = (g * spread(mod, layer, 5, seg)).astype(BF)
        for_grads[:, :width] = dz
        fetch_down.wait()
        da = (dot(dz, down[...], ((1,), (1,))) * slope[...]).astype(BF)
        for_grads[:, width:] = da
        fetch_up.wait()
        low[...] = dot(da, up[...], ((1,), (1,))).astype(BF)
        hand_out(outs, low, sc[0], narrow)

    extra = [] if last else [sds((rows, narrow), F32), sds((2, 4, narrow), F32)]
    return call(
        body,
        [sc] + pieces + [slope, mod, up[0], up[1], down[0], down[1]],
        [SM] + [VM] * n_in + [VM, VM, HB, HB, HB, HB],
        [sds((rows, width), BF), sds((rows, width + hidden), BF)]
        + [sds((rows, narrow), BF)] * count
        + extra,
        [
            pltpu.VMEM(up[0].shape, BF),
            pltpu.VMEM(down[0].shape, BF),
            pltpu.VMEM((rows, width), F32),
            pltpu.VMEM((rows, width), BF),
            pltpu.VMEM((rows, width), F32),
            pltpu.SemaphoreType.DMA,
            pltpu.SemaphoreType.DMA,
        ],
        name=f"feed_backward_{layer}",
    )


def middle_backward(
    dims, layer, sc, g, x1, sums, branch, mod, weights, queries, kept, probs, exact, cosine, sine
):
    rows, width, narrow, local, count = (
        dims.rows, dims.width, dims.narrow, dims.local, dims.n_heads,
    )
    n_seq, frames = dims.n_seq, dims.frames
    heads = local // HEAD_DIM
    scale = 1.0 / math.sqrt(HEAD_DIM)

    def body(sc, g, x1, *refs):
        sums = refs[:count]
        branch, mod, w_own, w_other, queries, kept, probs, exact, cosine, sine = refs[
            count : count + 10
        ]
        d_mid_out, dy_out, small, q_out = refs[count + 10 : count + 14]
        outs = refs[count + 14 : count + 14 + n_seq]
        weight, buffer, other, done, sem = refs[count + 14 + n_seq :]
        fetch = Fetch(sc, layer, w_own, w_other, weight, sem)
        seg = segments(sc, (rows, 1), 0, sc[1] * rows)
        mine = pl.ds(pl.multiple_of(sc[0] * narrow, narrow), narrow)
        place(buffer, sums, sc[0], narrow)
        dxf = buffer[...]
        normed, inv = norm_of(x1[...])
        other[...] = dxf * normed
        small[1] = utterance_sums(buffer[:, mine], seg)
        small[2] = utterance_sums(other[:, mine], seg)
        d_mid = g[...].astype(F32) + norm_pull(
            dxf * (1.0 + spread(mod, layer, 4, seg)), normed, inv
        )
        d_mid_out[...] = d_mid
        other[...] = d_mid
        small[0] = utterance_sums(other[:, mine] * branch[...].astype(F32), seg)
        dy = (d_mid * spread(mod, layer, 2, seg)).astype(BF)
        dy_out[...] = dy
        fetch.wait()
        d_att = dot(dy, weight[...], ((1,), (1,))).astype(BF)
        shared = d_att.astype(F32) * exact[...]
        d_keys, d_vals = [], []
        cos = cosine[:, :HEAD_DIM]
        sin = -sine[:, :HEAD_DIM]
        for head in range(heads):
            cols = slice(head * HEAD_DIM, (head + 1) * HEAD_DIM)
            vals = slice(local + head * HEAD_DIM, local + (head + 1) * HEAD_DIM)
            low = probs[head]
            prob = low.astype(F32)
            grad = d_att[:, cols]
            d_prob = dot(grad, kept[:, vals], ((1,), (1,)))
            delta = jnp.sum(shared[:, cols], axis=1, keepdims=True)
            d_score = (prob * (d_prob - delta)).astype(BF)
            dq = dot(d_score, kept[:, cols]) * scale
            q_out[:, cols] = turn(dq, cos, sin).astype(BF)
            d_keys.append((dot(queries[:, cols], d_score, ((0,), (0,))) * scale).astype(BF))
            d_vals.append(dot(grad, low, ((0,), (0,))).astype(BF))
        for first, parts in ((0, d_keys), (local, d_vals)):
            for head in range(0, heads, 2):
                at = first + head * HEAD_DIM
                both = jnp.concatenate(parts[head : head + 2], axis=0)
                done[:, at : at + 2 * HEAD_DIM] = both.T
        for k in range(n_seq):
            at = pl.multiple_of(jnp.bitwise_xor(sc[1], k) * rows, rows)
            outs[k][...] = done[pl.ds(at, rows), :]

    return call(
        body,
        [sc, g, x1]
        + sums
        + [branch, mod, weights[0], weights[1], queries, kept, probs, exact, cosine, sine],
        [SM, VM, VM] + [VM] * count + [VM, VM, HB, HB] + [VM] * 6,
        [
            sds((rows, width), F32),
            sds((rows, width), BF),
            sds((3, 4, narrow), F32),
            sds((rows, local), BF),
        ]
        + [sds((rows, 2 * local), BF)] * n_seq,
        [
            pltpu.VMEM(weights[0].shape, BF),
            pltpu.VMEM((rows, width), F32),
            pltpu.VMEM((rows, width), F32),
            pltpu.VMEM((frames, 2 * local), BF),
            pltpu.SemaphoreType.DMA,
        ],
        name=f"middle_backward_{layer}",
    )


def project_backward(dims, layer, sc, dy, d_query, chunks, weights, cosine, sine):
    rows, width, narrow, local, count = (
        dims.rows, dims.width, dims.narrow, dims.local, dims.n_heads,
    )
    n_in = len(chunks)

    def body(sc, dy, d_query, *refs):
        chunks = refs[:n_in]
        w_own, w_other, cosine, sine, d_out = refs[n_in : n_in + 5]
        outs = refs[n_in + 5 : n_in + 5 + count]
        weight, buffer, sem = refs[n_in + 5 + count :]
        fetch = Fetch(sc, layer, w_own, w_other, weight, sem)
        total = chunks[0][...].astype(F32)
        for chunk in chunks[1:]:
            total = total + chunk[...].astype(F32)
        cos = widen_table(cosine[...], local)
        sin = -widen_table(sine[...], local)
        dk = turn(total[:, :local], cos, sin).astype(BF)
        dv = total[:, local:].astype(BF)
        d_out[:, :width] = dy[...]
        for i, part in enumerate((d_query[...], dk, dv)):
            d_out[:, width + i * local : width + (i + 1) * local] = part
        fetch.wait()
        total = dot(d_query[...], weight[0], ((1,), (1,)))
        total = total + dot(dk, weight[1], ((1,), (1,)))
        total = total + dot(dv, weight[2], ((1,), (1,)))
        buffer[...] = total.astype(BF)
        hand_out(outs, buffer, sc[0], narrow)

    return call(
        body,
        [sc, dy, d_query] + chunks + [weights[0], weights[1], cosine, sine],
        [SM, VM, VM] + [VM] * n_in + [HB, HB, VM, VM],
        [sds((rows, width + 3 * local), BF)] + [sds((rows, narrow), BF)] * count,
        [
            pltpu.VMEM(weights[0].shape, BF),
            pltpu.VMEM((rows, width), BF),
            pltpu.SemaphoreType.DMA,
        ],
        name=f"project_backward_{layer}",
    )


def products(left, right, local, width):
    first = dot(left[:, :local], right[:, :width], ((0,), (0,))).astype(BF)
    rest = dot(left[:, local:], right[:, width:], ((0,), (0,))).astype(BF)
    out = [[(slice(None), first)]]
    for i in range(rest.shape[1] // local):
        columns = slice(i * local, (i + 1) * local)
        lines = [slice(group * local, (group + 1) * local) for group in range(width // local)]
        out.append([(line, rest[line, columns]) for line in lines])
    return out


def half_grads(sc, left, right, local, name):
    width = left.shape[1] - local
    count = (1 + (right.shape[1] - width) // local) // 2

    def body(sc, left, right, mine, theirs):
        grads = products(left[...], right[...], local, width)
        for section in range(2):

            @pl.when(sc[2] == section)
            def _(section=section):
                for out, first in ((mine, section * count), (theirs, (1 - section) * count)):
                    for i in range(count):
                        for columns, value in grads[first + i]:
                            out[i * local : (i + 1) * local, columns] = value

    return call(
        body,
        [sc, left, right],
        [SM, VM, VM],
        [sds((count * local, width), BF)] * 2,
        name=name,
    )


def whole_grads(sc, left, right, local, name):
    count = len(left)
    rows, wide = left[0].shape
    width = wide - local
    tensors = 1 + (right[0].shape[1] - width) // local

    def body(sc, *refs):
        left, right = refs[:count], refs[count : 2 * count]
        out, all_left, all_right = refs[2 * count :]
        for k in range(count):
            all_left[k * rows : (k + 1) * rows, :] = left[k][...]
            all_right[k * rows : (k + 1) * rows, :] = right[k][...]
        grads = products(all_left[...], all_right[...], local, width)
        for i, grad in enumerate(grads):
            for columns, value in grad:
                out[i * local : (i + 1) * local, columns] = value

    return call(
        body,
        [sc] + list(left) + list(right),
        [SM] + [VM] * (2 * count),
        [sds((tensors * local, width), BF)],
        [
            pltpu.VMEM((count * rows, wide), BF),
            pltpu.VMEM((count * rows, right[0].shape[1]), BF),
        ],
        limit=24,
        name=name,
    )[0]


def add_split(sc, left, right, step):
    rows, width = left.shape
    half = rows // 2

    def body(sc, left, right, keep, send):
        bit = sc[5 + step]
        mine = pl.ds(pl.multiple_of(bit * half, half), half)
        other = pl.ds(pl.multiple_of((1 - bit) * half, half), half)
        keep[...] = (left[mine, :].astype(F32) + right[mine, :].astype(F32)).astype(BF)
        send[...] = (left[other, :].astype(F32) + right[other, :].astype(F32)).astype(BF)

    return call(
        body, [sc, left, right], [SM, VM, VM], [sds((half, width), BF)] * 2, name="add_split"
    )


def join(sc, mine, other, step):
    half, width = mine.shape

    def body(sc, mine, other, out):
        bit = sc[5 + step]
        out[pl.ds(pl.multiple_of(bit * half, half), half), :] = mine[...]
        out[pl.ds(pl.multiple_of((1 - bit) * half, half), half), :] = other[...]

    return call(
        body, [sc, mine, other], [SM, VM, VM], [sds((2 * half, width), BF)], name="join"
    )[0]


class HalfSum:
    def __init__(self, sc, layer, left, right, local, name):
        self.sc, self.layer = sc, layer
        self.mine, self.ready = half_grads(sc, left, right, local, name)
        self.bits = lax.axis_size("seq").bit_length() - 1
        self.at = 0
        self.taken = True
        self.pieces = []

    def send(self, *begin):
        value, bits = after(self.ready, *begin), self.bits
        if self.at == 0:
            self.came = swap(value)
        elif self.at <= bits:
            self.came = crossed(value, self.at - 1)
        else:
            if self.at == 2 * bits and not self.pieces:
                self.hand_over(value)
            self.came = crossed(value, 2 * bits - self.at)
        self.at += 1
        self.taken = False
        return self.came

    def hand_over(self, value):
        self.pieces.append((value, to_owner(value, self.layer)))

    def take(self):
        sc, bits = self.sc, self.bits
        self.taken = True
        if self.at <= bits:
            self.mine, self.ready = add_split(sc, self.mine, self.came, self.at - 1)
        elif self.at == bits + 1:
            self.mine = self.ready = add_chunks([self.mine, self.came])
        else:
            self.mine = self.ready = join(sc, self.mine, self.came, 2 * bits + 1 - self.at)
        return self.ready

    def last(self, *begin):
        while self.at <= 2 * self.bits:
            if not self.taken:
                self.take()
            self.send()
        self.hand_over(after(self.came, *begin))
        (own_0, other_0), (own_1, other_1) = self.pieces
        return [own_0, own_1, other_0, other_1]


class Spread:
    def __init__(self, value):
        self.parts = [value]
        self.bits = lax.axis_size("seq").bit_length() - 1
        self.early = None

    def one(self, *begin):
        self.parts.append(crossed(after(self.parts[0], *begin), 0))
        return self.parts[1]

    def two(self, *begin):
        self.early = crossed(after(self.parts[0], *begin), 1)
        return self.early

    def rest(self, *begin):
        for bit in range(1, self.bits):
            more = [] if bit > 1 else [self.early]
            start = 0 if bit > 1 else 1
            for part in self.parts[start:]:
                more.append(crossed(after(part, *begin), bit))
            self.parts = self.parts + more
        return self.parts[3:]


class Assembly:
    SCRATCH = 5

    @staticmethod
    def scratch(added, local, outs):
        width = added[0].shape[1]
        return [
            pltpu.VMEM((local, width), F32),
            pltpu.VMEM((outs - 1, width, local), F32),
            pltpu.VMEM((2, outs * local, width), BF),
            pltpu.SemaphoreType.DMA((outs, 2)),
            pltpu.SemaphoreType.DMA((outs,)),
        ]

    def __init__(self, sc, added, pieces, outs, scratch):
        self.sc, self.added, self.pieces = sc, added, pieces
        self.first_out, self.rest_out = outs
        self.first, self.rest, self.held, self.sems, self.out_sems = scratch
        self.outs = 1 + self.rest.shape[0]
        self.local, self.width = self.first.shape
        self.size = pieces[0].shape[0]

    def fetches_added(self):
        copies = []
        for i in range(self.outs):
            at = pl.ds(i * self.local, self.local)
            for j in range(2):
                copies.append(
                    pltpu.make_async_copy(
                        self.added[j].at[at, :], self.held.at[j, at, :], self.sems.at[i, j]
                    )
                )
        return copies

    def fetches_pieces(self):
        return [
            pltpu.make_async_copy(
                self.pieces[p],
                self.held.at[0, pl.ds(p * self.size, self.size), :],
                self.sems.at[p // 2, p % 2],
            )
            for p in range(4)
        ]

    def start(self):
        @pl.when(self.sc[2] == 0)
        def _():
            for copy in self.fetches_added():
                copy.start()

        @pl.when(self.sc[2] == 1)
        def _():
            for copy in self.fetches_pieces():
                copy.start()

    def store(self, index):
        if index == 0:
            return pltpu.make_async_copy(self.first, self.first_out, self.out_sems.at[0])
        return pltpu.make_async_copy(
            self.rest.at[index - 1], self.rest_out.at[index - 1], self.out_sems.at[index]
        )

    def put(self, index, value, line):
        lines = value.shape[0]
        if index == 0:
            self.first[line : line + lines, :] = value
            return
        for group in range(self.width // self.local):
            columns = slice(group * self.local, (group + 1) * self.local)
            at = group * self.local + line
            self.rest[index - 1, at : at + lines, :] = value[:, columns]

    def run(self):
        sc, local, size, held = self.sc, self.local, self.size, self.held
        count = self.outs // 2

        @pl.when(sc[2] == 0)
        def _():
            copies = self.fetches_added()
            for i in range(self.outs):
                copies[2 * i].wait()
                copies[2 * i + 1].wait()
                at = slice(i * local, (i + 1) * local)
                self.put(i, held[0, at, :].astype(F32) + held[1, at, :].astype(F32), 0)
                self.store(i).start()

        bits = lax.axis_size("seq").bit_length() - 1
        low, high = sc[1] & 1, (sc[1] >> (bits - 1)) & 1

        @pl.when(sc[2] == 1)
        def _():
            for copy in self.fetches_pieces():
                copy.wait()
            for section, at, bit in ((1, 0, high), (0, 2, low)):
                for turn in range(2):

                    @pl.when(bit == turn)
                    def _(section=section, at=at, turn=turn):
                        for place in range(2):
                            base = (at + (place ^ turn)) * size
                            for i in range(count):
                                begin = max(i * local, place * size)
                                end = min((i + 1) * local, (place + 1) * size)
                                if begin < end:
                                    row = base + begin - place * size
                                    value = held[0, row : row + end - begin, :].astype(F32)
                                    self.put(section * count + i, value, begin - i * local)

            for i in range(self.outs):
                self.store(i).start()

    def wait(self):
        for i in range(self.outs):
            self.store(i).wait()


def by_section(sc, mine, theirs, layer_0, layer_1):
    mine[...] = jnp.where(sc[2] == 0, layer_0, layer_1)
    theirs[...] = jnp.where(sc[2] == 0, layer_1, layer_0)


def gate_sums(dims, layer, sc, g, x1, z, mod, passed):
    rows, narrow = dims.rows, dims.narrow

    def body(sc, g, x1, z, mod, passed, small, *shown):
        seg = segments(sc, (rows, 1), 0, sc[1] * rows)
        mine = pl.ds(pl.multiple_of(sc[0] * narrow, narrow), narrow)
        value = z[...].astype(F32)
        small[...] = utterance_sums(g[:, mine].astype(F32) * value, seg)
        if shown:
            gate = spread(mod, layer, 5, seg, mine)
            result = (x1[:, mine] + gate * value).astype(BF)
            by_section(sc, *shown, passed[...], result)

    outs = [sds((4, narrow), F32)]
    if layer == 1:
        outs += [sds((rows, narrow), BF)] * 2
    return call(
        body, [sc, g, x1, z, mod, passed], [SM] + [VM] * 5, outs, name=f"gate_sums_{layer}"
    )


def last_norm(dims, sc, terms, x, mod, small_0, small_1):
    rows, narrow, count = dims.rows, dims.narrow, dims.n_heads

    def body(sc, *refs):
        terms = refs[:count]
        x, mod, mid_0, gate_0, in_1, mid_1, gate_1 = refs[count : count + 7]
        total_out, normed_out, inv_out, mine_out, theirs_out, rows_out, buffer = refs[count + 7 :]
        seg = segments(sc, (rows, 1), 0, sc[1] * rows)
        mine = pl.ds(pl.multiple_of(sc[0] * narrow, narrow), narrow)
        total = terms[0][...].astype(F32)
        for term in terms[1:]:
            total = total + term[...].astype(F32)
        normed, inv = norm_of(x[...].astype(F32))
        buffer[...] = normed
        normed = buffer[:, mine]
        first = (
            [utterance_sums(total, seg), utterance_sums(total * normed, seg)]
            + [mid_0[i] for i in range(3)]
            + [gate_0[...]]
        )
        second = [in_1[0], in_1[1]] + [mid_1[i] for i in range(3)] + [gate_1[...]]
        for i in range(6):
            by_section(sc, mine_out.at[i], theirs_out.at[i], first[i], second[i])
        grad = total * (1.0 + spread(mod, 0, 1, seg, mine))
        total_out[...] = grad
        normed_out[...] = normed
        inv_out[...] = inv
        lane = lax.broadcasted_iota(jnp.int32, (rows, 128), 1)
        sums = jnp.where(lane == 0, jnp.sum(grad, axis=1, keepdims=True), 0.0)
        sums = jnp.where(lane == 1, jnp.sum(grad * normed, axis=1, keepdims=True), sums)
        pick = diagonal(8, 128)
        rows_out[...] = sum(dot(pick, part, ((1,), (1,))) for part in split3(sums))

    return call(
        body,
        [sc] + terms + [x, mod] + small_0 + small_1,
        [SM] + [VM] * (count + 7),
        [
            sds((rows, narrow), F32),
            sds((rows, narrow), F32),
            sds((rows, 1), F32),
            sds((6, 4, narrow), F32),
            sds((6, 4, narrow), F32),
            sds((8, rows), F32),
        ],
        [pltpu.VMEM((rows, dims.width), F32)],
        name="last_norm",
    )


def last_pull(dims, sc, d_mid, grad, normed, inv, sums, middle_grad):
    rows, narrow, count, width = dims.rows, dims.narrow, dims.n_heads, dims.width

    def body(sc, d_mid, grad, normed, inv, middle, *refs):
        sums, outs = refs[:count], refs[count:]
        total = sums[0][:8, :rows]
        for term in sums[1:]:
            total = total + term[:8, :rows]
        row = lax.broadcasted_iota(jnp.int32, (8, 128), 0)
        lane = lax.broadcasted_iota(jnp.int32, (8, 128), 1)
        pick = (row == 4 * lane + 3).astype(BF)
        total = sum(dot(part, pick, ((0,), (0,))) for part in split3(total * (1.0 / width)))
        mine = pl.ds(pl.multiple_of(sc[0] * narrow, narrow), narrow)
        first = d_mid[:, mine] + inv[...] * (
            grad[...] - total[:, 0:1] - normed[...] * total[:, 1:2]
        )
        by_section(sc, *outs, first, middle[...])

    return call(
        body,
        [sc, d_mid, grad, normed, inv, middle_grad] + sums,
        [SM] + [VM] * (5 + count),
        [sds((rows, narrow), F32)] * 2,
        name="last_pull",
    )


def modulation_part(sc, mod_weight, row_sums, own, n_seq):
    kinds, width, narrow = mod_weight.shape

    def body(sc, mod_weight, row_sums, *refs):
        own = refs[:n_seq]
        grads_out, part, box = refs[n_seq:]
        for k in range(n_seq):
            box[jnp.bitwise_xor(sc[1], k)] = own[k][...]
        total = box[0]
        for j in range(1, n_seq):
            total = total + box[j]
        result = jnp.zeros((8, width), F32)
        for which in range(kinds):
            mine, theirs = total[which], total[kinds + which]
            grad = jnp.concatenate(
                [jnp.where(sc[2] == 0, mine, theirs), jnp.where(sc[2] == 0, theirs, mine)],
                axis=0,
            )
            grads_out[which] = grad
            result = result + exact_dot(grad, mod_weight[which], ((1,), (1,)))
        part[...] = result
        for row in range(2):
            part[4 * row + 3 : 4 * row + 4, : row_sums.shape[1]] = row_sums[row : row + 1, :]

    return call(
        body,
        [sc, mod_weight, row_sums] + own,
        [SM, VM, VM] + [VM] * n_seq,
        [sds((kinds, 8, narrow), F32), sds((8, width), F32)],
        [pltpu.VMEM((n_seq, 2 * kinds, 4, narrow), F32)],
        name="modulation_part",
    )


def modulation_weight(sc, act, grads):
    kinds, rows, narrow = grads.shape
    width = act.shape[1]

    def body(sc, act, grads, out, held, sems):
        tall = outer_parts(act[...], act[...])[0].astype(F32).T.astype(BF)

        def store(which):
            return pltpu.make_async_copy(held.at[which], out.at[which], sems.at[which])

        for which in range(kinds):
            wide = outer_parts(grads[which], grads[which])[1]
            held[which] = dot(tall, wide)
            store(which).start()
        for which in range(kinds):
            store(which).wait()

    return pl_call(
        body,
        [sc, act, grads],
        [SM, VM, VM],
        [sds((kinds, width, narrow), F32)],
        [HB],
        [pltpu.VMEM((kinds, width, narrow), F32), pltpu.SemaphoreType.DMA((kinds,))],
        limit=16,
        name="modulation_weight",
    )[0]


def time_backward(sc, sinus, inner, outer, time_out, own):
    count = len(own)
    rows, width = inner.shape
    freq = sinus.shape[1]
    block = width // 4

    def body(sc, sinus, inner, outer, time_out, *refs):
        own = refs[:count]
        g_in, g_out, box, held_in, held_out, sems = refs[count:]
        for k in range(count):
            at = jnp.bitwise_xor(sc[0], k)
            box[at, sc[2]] = own[k][:rows]
            box[at, 1 - sc[2]] = own[k][rows:]
        total = jnp.zeros((rows, width), F32)
        for j in range(count):
            for c in range(2):
                total = total + box[j, c]
        row = lax.broadcasted_iota(jnp.int32, (rows, width), 0)
        total = jnp.where(row % 4 == 3, 0.0, total)

        def slope(value):
            gate = 1.0 / (1.0 + jnp.exp(-value))
            return gate * (1.0 + value * (1.0 - gate))

        pre = inner[...]
        hidden = pre / (1.0 + jnp.exp(-pre))
        d_outer = total * slope(outer[...])
        tall, wide = outer_parts(hidden, d_outer)
        tall = tall.astype(F32).T.astype(BF)
        copies = []
        for i in range(4):
            at = slice(i * block, (i + 1) * block)
            held_out[at, :] = dot(tall[at], wide)
            copies.append(
                pltpu.make_async_copy(held_out.at[at, :], g_out.at[at, :], sems.at[i])
            )
            copies[-1].start()
        d_inner = exact_dot(d_outer, time_out[...], ((1,), (1,))) * slope(pre)
        held_in[...] = exact_outer(sinus[...], d_inner)
        copies.append(pltpu.make_async_copy(held_in, g_in, sems.at[4]))
        copies[-1].start()
        for copy in copies:
            copy.wait()

    return pl_call(
        body,
        [sc, sinus, inner, outer, time_out] + list(own),
        [SM] + [VM] * (4 + count),
        [sds((freq, width), F32), sds((width, width), F32)],
        [HB, HB],
        [
            pltpu.VMEM((count, 2, rows, width), F32),
            pltpu.VMEM((freq, width), F32),
            pltpu.VMEM((width, width), F32),
            pltpu.SemaphoreType.DMA((5,)),
        ],
        limit=16,
        name="time_backward",
    )


def finish(dims, sc, feed, attention, acts, grads):
    n = Assembly.SCRATCH

    def body(sc, act_own, act_other, grad_own, grad_other, *refs):
        sources, outs, scratch = refs[:12], refs[12:18], refs[18:]
        feed = Assembly(sc, sources[:2], sources[2:6], outs[:2], scratch[:n])
        attention = Assembly(sc, sources[6:8], sources[8:], outs[2:4], scratch[n:])
        feed.start()
        attention.start()
        outs[4][sc[2]] = act_own[...]
        outs[4][1 - sc[2]] = act_other[...]
        outs[5][sc[2]] = grad_own[...]
        outs[5][1 - sc[2]] = grad_other[...]
        feed.run()
        attention.run()
        feed.wait()
        attention.wait()

    width = dims.width
    sources = list(feed[0]) + list(feed[1]) + list(attention[0]) + list(attention[1])
    return pl_call(
        body,
        [sc] + list(acts) + list(grads) + sources,
        [SM] + [VM] * 4 + [HB] * 12,
        [
            sds((dims.hidden, width), F32),
            sds((1, width, dims.hidden), F32),
            sds((dims.local, width), F32),
            sds((3, width, dims.local), F32),
            sds((2,) + acts[0].shape, BF),
            sds((2,) + grads[0].shape, F32),
        ],
        [HB] * 4 + [VM] * 2,
        Assembly.scratch(feed[0], dims.hidden, 2) + Assembly.scratch(attention[0], dims.local, 4),
        limit=24,
        name="finish",
    )


class Dims:
    pass


def local_program(
    frames,
    cotangent,
    utt_lengths,
    time_ids,
    w_time_in,
    w_time_out,
    w_mod,
    w_qkv,
    w_out,
    w_up,
    w_down,
):
    dims = Dims()
    dims.n_heads = lax.axis_size("heads")
    dims.n_seq = n_seq = lax.axis_size("seq")
    _, dims.rows, dims.narrow = frames.shape
    dims.width = dims.narrow * dims.n_heads
    dims.local = w_qkv.shape[3]
    dims.hidden = w_up.shape[2]
    dims.frames = dims.rows * n_seq
    section = lax.axis_index("section")

    def here(both):
        return lax.dynamic_index_in_dim(both, section, 0, keepdims=False)

    sc = utt_lengths
    qkv = jnp.transpose(w_qkv[0], (1, 0, 2))
    mod_weight = jnp.transpose(w_mod[0], (1, 0, 2))
    wide_frames = gather(here(frames), "heads")
    qkv_w = (qkv, swap(qkv))
    sinus, inner, outer, act, mod_mine, mod_theirs = start(
        sc, time_ids, w_time_in, w_time_out, mod_weight
    )
    mod_theirs = swap(after(mod_theirs, *wide_frames))
    mods = gather(jnp.concatenate([mod_mine, mod_theirs], axis=0), "heads")
    cosine, sine = tables(sc, dims.rows)
    mods = after(mods, cosine, sine)

    x_0, _, xa, q_0, kv, mod = project(dims, 0, sc, wide_frames, mods, qkv_w, cosine, sine)
    chunks = gather(kv, "seq")
    out_w = (w_out[0], swap(after(w_out[0], mods[0])))
    kept_0, probs_0, for_attention, exact_0, *terms = attend(
        dims, 0, sc, chunks, q_0, xa, out_w
    )
    fwd_a = Spread(for_attention)

    up_w, down_w = [(w[0], swap(after(w[0], terms[0]))) for w in (w_up, w_down)]
    total = after(add_chunks(exchange(terms, "heads")), up_w[1], down_w[1])

    branch_0 = gather(total, "heads")
    fwd_a.one(total)
    fwd_a.two(total)
    x1_0, for_feed, slope_0, *terms = feed_forward(
        dims, 0, sc, x_0, branch_0, mod, up_w, down_w
    )
    fwd_f = Spread(for_feed)

    total = after(add_chunks(exchange(terms, "heads")), fwd_a.parts[1], fwd_a.early)

    z_0 = gather(total, "heads")
    fwd_a.rest(total)
    fwd_f.one(total)

    x_2, passed, xa, q_1, kv = project(
        dims, 1, sc, [x1_0] + z_0, [mod], qkv_w, cosine, sine
    )
    kv = after(kv, fwd_f.parts[1], *fwd_a.parts[3:])
    chunks = gather(kv, "seq")
    wide_cotangent = gather(after(here(cotangent), chunks[1]), "heads")
    kept_1, probs_1, for_attention_1, exact_1, *terms = attend(
        dims, 1, sc, chunks, q_1, xa, out_w
    )

    terms[0] = after(terms[0], *wide_cotangent)
    total = add_chunks(exchange(terms, "heads"))
    fwd_f.two(terms[0])

    branch_1 = gather(total, "heads")
    x1_1, for_feed, slope_1, *z_terms = feed_forward(
        dims, 1, sc, x_2, branch_1, mod, up_w, down_w
    )
    g_1, late, *terms = feed_backward(
        dims, 1, sc, wide_cotangent, slope_1, mod, up_w, down_w
    )
    terms = after(terms, fwd_f.early)
    feed_1 = HalfSum(sc, 1, for_feed, late, dims.hidden, "feed_grads_1")
    feed_1.send()
    got = exchange(terms, "heads")
    total = after(add_chunks(got), feed_1.came, *fwd_f.rest(terms[0]))

    feed_1.take()
    feed_1.send(total)
    sums = after(gather(total, "heads"), feed_1.came)

    feed_1.take()
    feed_1.send(sums[0])
    d_mid_1, dy, small_f1, dq, *sent = middle_backward(
        dims, 1, sc, g_1, x1_1, after(sums, feed_1.ready), branch_1[0], mod, out_w,
        q_1, kept_1, probs_1, exact_1, cosine, sine,
    )
    sent = after(sent, feed_1.came)

    got = exchange(sent, "seq")
    feed_1.take()
    z_1 = add_chunks(exchange(after(z_terms, sent[0]), "heads"))
    gate_1, *acts = gate_sums(dims, 1, sc, g_1, x1_1, z_1, mod, passed)
    got = after(got, feed_1.ready, *acts)
    late, *terms = project_backward(dims, 1, sc, dy, dq, got, qkv_w, cosine, sine)

    got = exchange(terms, "heads")
    feed_1.send(terms[0])
    attention_1 = HalfSum(sc, 1, for_attention_1, late, dims.local, "attend_grads_1")
    acts = [acts[0], swap(after(acts[1], terms[0]))]
    total = after(
        add_chunks(got), feed_1.came, attention_1.mine, attention_1.ready, acts
    )

    feed_1.take()
    feed_1.send(total)
    attention_1.send(total)
    pieces = gather(total, "heads")

    g_0, late, *rest = feed_backward(
        dims, 0, sc, pieces + [x_2, d_mid_1], slope_0, mod, up_w, down_w
    )
    terms, (middle_grad, small_a1) = rest[: dims.n_heads], rest[dims.n_heads :]
    terms = after(terms, feed_1.came, attention_1.came)
    late_f = Spread(late)
    got = exchange(terms, "heads")
    attention_1.take()
    attention_1.send(terms[0])
    total = after(add_chunks(got), attention_1.came, late_f.one(terms[0]))

    attention_1.take()
    attention_1.send(total)
    late_f.two(total)
    sums = after(gather(total, "heads"), attention_1.came)

    attention_1.take()
    attention_1.send(sums[0])
    d_mid_0, dy, small_f0, dq, *sent = middle_backward(
        dims, 0, sc, g_0, x1_0, after(sums, attention_1.ready), branch_0[0], mod, out_w,
        q_0, kept_0, probs_0, exact_0, cosine, sine,
    )
    sent = after(sent, attention_1.came, late_f.early)

    got = exchange(sent, "seq")
    attention_1.take()
    if attention_1.at == 2 * attention_1.bits:
        attention_1.hand_over(after(attention_1.ready, got[0]))
    feed_1 = feed_1.last(sent[0])
    gate_0, *_ = gate_sums(dims, 0, sc, g_0, x1_0, z_0[0], mod, passed)
    got = after(got, attention_1.ready, gate_0, feed_1)
    late, *terms = project_backward(dims, 0, sc, dy, dq, got, qkv_w, cosine, sine)
    late_a = Spread(late)

    got = exchange(terms, "heads")
    late_a.one(terms[0])
    late_f.rest(terms[0])

    grad, normed, inv, mine, theirs, row_sums = last_norm(
        dims, sc, got, x_0, mod, [small_f0, gate_0], [small_a1, small_f1, gate_1]
    )
    late_a.two(row_sums)
    theirs = after(swap(theirs), late_a.parts[1], *late_f.parts[3:])
    both = jnp.concatenate([mine, theirs], axis=0)
    both = gather(both, "seq")
    feed_0 = whole_grads(
        sc, after(fwd_f.parts, theirs), late_f.parts, dims.hidden, "feed_grads_0"
    )
    both = after(both, feed_0, late_a.early)
    mod_grads, part = modulation_part(sc, mod_weight, row_sums, both, n_seq)

    late_a.rest(part)
    attention_1.send(part)
    feed_0 = [feed_0, to_owner(after(feed_0, both[0]), 0)]
    ends = jnp.concatenate([part, swap(part)], axis=0)
    ends = gather(after(ends, feed_0), "heads")
    g_mod = modulation_weight(sc, act, mod_grads)
    ends = after(ends, *late_a.parts[3:], g_mod, attention_1.came)

    attention_0 = whole_grads(
        sc, after(fwd_a.parts, *ends), late_a.parts, dims.local, "attend_grads_0"
    )
    attention_0 = [attention_0, to_owner(attention_0, 0)]
    attention_1 = attention_1.last(attention_0[0])
    grads = last_pull(
        dims, sc, d_mid_0, grad, normed, inv, after(ends, attention_0[0]), middle_grad
    )
    grads = [grads[0], swap(grads[1])]
    g_first, g_second = time_backward(
        sc, sinus, inner, outer, w_time_out, after(ends, attention_0[0])
    )
    g_reduce, g_expand, g_out, g_qkv, acts, grads = finish(
        dims, sc, (feed_0, feed_1), (after(attention_0, g_second), attention_1), acts, grads
    )

    return (
        acts[None],
        grads[None],
        g_first,
        g_second,
        jnp.transpose(g_mod, (1, 0, 2))[None],
        jnp.transpose(g_qkv, (1, 0, 2))[None],
        g_out[None],
        g_expand,
        g_reduce[None],
    )


def solution(mesh):
    placed = (
        P(None, "seq", "heads"),
        P(None, "seq", "heads"),
        P(),
        P(),
        P(),
        P(),
        P("section", None, None, "heads"),
        P("section", None, None, "heads"),
        P("section", "heads", None),
        P("section", None, "heads"),
        P("section", "heads", None),
    )
    return jax.shard_map(
        local_program,
        mesh=mesh,
        in_specs=placed,
        out_specs=(
            P("section", None, "seq", "heads"),
            P("section", None, "seq", "heads"),
            P(),
            P(),
            P("section", None, None, "heads"),
            P("section", None, None, "heads"),
            P("section", "heads", None),
            P("section", None, "heads"),
            P("section", "heads", None),
        ),
        check_vma=False,
    )
```

```python
import functools
import math

import jax
import jax.numpy as jnp
import numpy as np
from jax import lax
from jax.experimental import pallas as pl
from jax.experimental.pallas import tpu as pltpu
from jax.sharding import PartitionSpec as P

HEAD_DIM = 64
FREQ = 256
EPS = 1e-06
BF = jnp.bfloat16
F32 = jnp.float32
MIB = 1024 * 1024


def partner(value, axis, by):
    if by == 0:
        return value
    return lax.ppermute(value, axis, [(i, i ^ by) for i in range(lax.axis_size(axis))])


def order_of(count):
    return (3, 1, 2) if count == 4 else tuple(range(count - 1, 0, -1))


def gather(value, axis):
    count = lax.axis_size(axis)
    out = [value] * count
    for k in order_of(count):
        out[k] = partner(value, axis, k)
    return out


def exchange(chunks, axis):
    out = list(chunks)
    for k in order_of(len(chunks)):
        out[k] = partner(chunks[k], axis, k)
    return out


def swap(value):
    return lax.ppermute(value, "section", [(0, 1), (1, 0)])


def to_owner(value, layer):
    return lax.ppermute(value, "section", [(1 - layer, layer)])


def crossed(value, step):
    length = lax.axis_size("seq")
    last = length.bit_length() - 2
    pairs = []
    for c in range(2):
        by = 1 << (step if c == 0 else last - step)
        pairs += [(c * length + i, c * length + (i ^ by)) for i in range(length)]
    return lax.ppermute(value, ("section", "seq"), pairs)


def after(value, *done):
    value = lax.optimization_barrier((value, done))[0]
    return list(value) if isinstance(value, (list, tuple)) else value


def add_chunks(chunks):
    total = chunks[0].astype(F32)
    for chunk in chunks[1:]:
        total = total + chunk.astype(F32)
    return total.astype(BF)


def dot(left, right, contract=((1,), (0,))):
    return lax.dot_general(left, right, (contract, ((), ())), preferred_element_type=F32)


def split3(value):
    high = value.astype(BF)
    rest = value - high.astype(F32)
    middle = rest.astype(BF)
    low = (rest - middle.astype(F32)).astype(BF)
    return high, middle, low


def diagonal(rows, columns):
    row = lax.broadcasted_iota(jnp.int32, (rows, columns), 0)
    return (row == lax.broadcasted_iota(jnp.int32, (rows, columns), 1)).astype(BF)


def exact_dot(left, right, contract=((1,), (0,))):
    rows = left.shape[0]
    stacked = jnp.concatenate(split3(left), axis=0)
    out = dot(stacked, right, contract)
    return out[:rows] + (out[rows : 2 * rows] + out[2 * rows :])


def exact_outer(left, right):
    tall, wide = outer_parts(left, right)
    return dot(tall, wide, ((0,), (0,)))


def outer_parts(left, right):
    a, b = split3(left), split3(right)
    tall = jnp.concatenate([a[0], a[0], a[1]], axis=0)
    wide = jnp.concatenate([b[0], b[1], b[0]], axis=0)
    return tall, wide


def segments(sc, shape, axis, first):
    index = lax.broadcasted_iota(jnp.int32, shape, axis) + first
    return (index >= sc[3]).astype(jnp.int32) + (index >= sc[4]).astype(jnp.int32)


def spread(mod, layer, which, seg, columns=slice(None)):
    block = mod[layer * 6 + which, :, columns]
    rows = [block[u : u + 1] for u in range(3)]
    return jnp.where(seg == 0, rows[0], jnp.where(seg == 1, rows[1], rows[2]))


def utterance_sums(value, seg):
    rows = [
        jnp.sum(jnp.where(seg == u, value, 0.0), axis=0, keepdims=True) for u in range(3)
    ]
    return jnp.concatenate(rows + [jnp.zeros_like(rows[0])], axis=0)


def norm_of(value):
    mean = jnp.mean(value, axis=1, keepdims=True)
    centred = value - mean
    inv = lax.rsqrt(jnp.mean(centred * centred, axis=1, keepdims=True) + EPS)
    return centred * inv, inv


def norm_pull(grad, normed, inv):
    return inv * (
        grad
        - jnp.mean(grad, axis=1, keepdims=True)
        - normed * jnp.mean(grad * normed, axis=1, keepdims=True)
    )


def lanes_of(index, count, width):
    return pl.ds(pl.multiple_of(lax.rem(index, count) * width, width), width)


def place(buffer, chunks, own, width):
    for k, chunk in enumerate(chunks):
        at = pl.multiple_of(jnp.bitwise_xor(own, k) * width, width)
        buffer[:, pl.ds(at, width)] = chunk[...].astype(buffer.dtype)


def hand_out(outs, buffer, own, width):
    for k, out in enumerate(outs):
        at = pl.multiple_of(jnp.bitwise_xor(own, k) * width, width)
        out[...] = buffer[:, pl.ds(at, width)].astype(out.dtype)


class Fetch:
    def __init__(self, sc, layer, own, other, buffer, sem):
        self.copy = pltpu.make_async_copy(own, buffer, sem)
        other_copy = pltpu.make_async_copy(other, buffer, sem)

        @pl.when(sc[2] == layer)
        def _():
            self.copy.start()

        @pl.when(sc[2] != layer)
        def _():
            other_copy.start()

    def wait(self):
        self.copy.wait()


def turn(value, cosine, sine):
    width = value.shape[1]
    even = lax.broadcasted_iota(jnp.int32, value.shape, 1) % 2 == 0
    swapped = jnp.where(even, pltpu.roll(value, width - 1, 1), pltpu.roll(value, 1, 1))
    return value * cosine + swapped * sine


def widen_table(table, width):
    copies = width // table.shape[1]
    return jnp.concatenate([table] * copies, axis=1) if copies > 1 else table[:, :width]


VM = pl.BlockSpec(memory_space=pltpu.VMEM)
SM = pl.BlockSpec(memory_space=pltpu.SMEM)
HB = pl.BlockSpec(memory_space=pltpu.HBM)


def sds(shape, dtype):
    return jax.ShapeDtypeStruct(tuple(shape), dtype)


class Place:
    def __init__(self, lengths):
        self.lengths = lengths
        self.known = {}
        for index in range(5):
            self[index]

    def __getitem__(self, index):
        if index not in self.known:
            self.known[index] = self.find(index)
        return self.known[index]

    def find(self, index):
        if index < 3:
            return lax.axis_index(("heads", "seq", "section")[index])
        if index == 3:
            return self.lengths[self[2], 0]
        if index == 4:
            return self[3] + self.lengths[self[2], 1]
        low = index - 5
        high = lax.axis_size("seq").bit_length() - 2 - low
        return jnp.where(self[2] == 0, self[1] >> low, self[1] >> high) & 1


def call(body, ins, specs, outs, scratch=(), limit=12, name=None):
    return pl_call(body, ins, specs, outs, [VM] * len(outs), scratch, limit, name)


def pl_call(body, ins, specs, outs, out_specs, scratch, limit, name):
    def placed(lengths, *refs):
        body(Place(lengths), *refs)

    return pl.pallas_call(
        placed,
        out_shape=list(outs),
        in_specs=list(specs),
        out_specs=list(out_specs),
        scratch_shapes=list(scratch),
        compiler_params=pltpu.CompilerParams(vmem_limit_bytes=limit * MIB),
        cost_estimate=pl.CostEstimate(flops=1, bytes_accessed=1, transcendentals=0),
        name=name,
    )(*ins)


def start(sc, time_ids, time_in, time_out, mod_weight):
    width = time_in.shape[1]
    kinds, _, narrow = mod_weight.shape
    half = FREQ // 2

    def body(sc, ids, time_in, time_out, mod_weight, *refs):
        sinus_out, inner_out, outer_out, act_out, mine_out, theirs_out = refs[:6]
        w_in, w_out, w_mod, sems = refs[6:]
        copies = [
            pltpu.make_async_copy(time_in, w_in, sems.at[0]),
            pltpu.make_async_copy(time_out, w_out, sems.at[1]),
            pltpu.make_async_copy(mod_weight, w_mod, sems.at[2]),
        ]
        for copy in copies:
            copy.start()
        row = lax.broadcasted_iota(jnp.int32, (8, half), 0)
        lane = lax.broadcasted_iota(jnp.int32, (8, half), 1).astype(F32)
        stamp = jnp.zeros((8, half), F32)
        for m in range(2):
            for u in range(3):
                stamp = jnp.where(row == m * 4 + u, ids[m, u].astype(F32), stamp)
        angle_t = stamp * jnp.exp(lane * (-math.log(10000.0) / (half - 1)))
        sinus = jnp.concatenate([jnp.sin(angle_t), jnp.cos(angle_t)], axis=1)
        sinus_out[...] = sinus

        copies[0].wait()
        inner = exact_dot(sinus, w_in[...])
        inner_out[...] = inner
        hidden = inner / (1.0 + jnp.exp(-inner))
        copies[1].wait()
        outer = exact_dot(hidden, w_out[...])
        outer_out[...] = outer
        act = outer / (1.0 + jnp.exp(-outer))
        act_out[...] = act
        copies[2].wait()
        for which in range(kinds):
            modul = exact_dot(act, w_mod[which])
            mine_out[which] = jnp.where(sc[2] == 0, modul[:4], modul[4:])
            theirs_out[which] = jnp.where(sc[2] == 0, modul[4:], modul[:4])

    return call(
        body,
        [sc, time_ids, time_in, time_out, mod_weight],
        [SM, SM, HB, HB, HB],
        [sds((8, FREQ), F32)]
        + [sds((8, width), F32)] * 3
        + [sds((kinds, 4, narrow), F32)] * 2,
        [
            pltpu.VMEM(time_in.shape, BF),
            pltpu.VMEM(time_out.shape, BF),
            pltpu.VMEM(mod_weight.shape, BF),
            pltpu.SemaphoreType.DMA((3,)),
        ],
        limit=56,
        name="start",
    )


def tables(sc, rows):
    def body(sc, cosine, sine):
        index = lax.broadcasted_iota(jnp.int32, (rows, 2 * HEAD_DIM), 0) + sc[1] * rows
        begin = jnp.where(index >= sc[4], sc[4], jnp.where(index >= sc[3], sc[3], 0))
        lane = lax.broadcasted_iota(jnp.int32, (rows, 2 * HEAD_DIM), 1)
        pair = lax.broadcasted_iota(jnp.int32, (1, 2 * HEAD_DIM), 1)
        rate = jnp.exp(
            ((pair % HEAD_DIM) // 2).astype(F32) * (-2.0 * math.log(10000.0) / HEAD_DIM)
        )
        angle = (index - begin).astype(F32) * rate
        cosine[...] = jnp.cos(angle)
        sine[...] = jnp.sin(angle) * jnp.where(lane % 2 == 0, -1.0, 1.0)

    return call(body, [sc], [SM], [sds((rows, 2 * HEAD_DIM), F32)] * 2, name="tables")


def project(dims, layer, sc, pieces, mods, weights, cosine, sine):
    first = layer == 0
    rows, width, narrow, local = dims.rows, dims.width, dims.narrow, dims.local
    count = dims.n_heads
    n_in, n_mod = len(pieces), len(mods)

    def body(sc, *refs):
        pieces, mods = refs[:n_in], refs[n_in : n_in + n_mod]
        w_own, w_other, cosine, sine = refs[n_in + n_mod : n_in + n_mod + 4]
        outs = refs[n_in + n_mod + 4 :]
        x_out, narrow_out, xa_out, q_out, kv_out = outs[:5]
        if first:
            mod = outs[5]
        else:
            mod = mods[0]
        buffer, weight, sem = outs[-3:]
        fetch = Fetch(sc, layer, w_own, w_other, weight, sem)
        seg = segments(sc, (rows, 1), 0, sc[1] * rows)
        if first:
            for k in range(count):
                at = pl.multiple_of(jnp.bitwise_xor(sc[0], k) * narrow, narrow)
                block = mods[k][...]
                for l in range(2):
                    mod[l * 6 : l * 6 + 6, :, pl.ds(at, narrow)] = jnp.where(
                        sc[2] == l, block[:6], block[6:]
                    )
            place(buffer, pieces, sc[0], narrow)
            x = buffer[...]
            x_out[...] = x.astype(BF)
            narrow_out[...] = pieces[0][...]
        else:
            place(buffer, pieces[1:], sc[0], narrow)
            x = pieces[0][...] + spread(mod, 0, 5, seg) * buffer[...]
            low = x.astype(BF)
            x_out[...] = low
            x = low.astype(F32)
            buffer[...] = x
            at = pl.multiple_of(sc[0] * narrow, narrow)
            narrow_out[...] = buffer[:, pl.ds(at, narrow)].astype(BF)
        normed, _ = norm_of(x)
        xa = (normed * (1.0 + spread(mod, layer, 1, seg)) + spread(mod, layer, 0, seg)).astype(BF)
        xa_out[...] = xa
        cos = widen_table(cosine[...], local)
        sin = widen_table(sine[...], local)
        fetch.wait()
        q_out[...] = turn(dot(xa, weight[0]), cos, sin).astype(BF)
        kv_out[:, :local] = turn(dot(xa, weight[1]), cos, sin).astype(BF)
        kv_out[:, local:] = dot(xa, weight[2]).astype(BF)

    return call(
        body,
        [sc] + pieces + mods + [weights[0], weights[1], cosine, sine],
        [SM] + [VM] * (n_in + n_mod) + [HB, HB, VM, VM],
        [
            sds((rows, width), BF),
            sds((rows, narrow), BF),
            sds((rows, width), BF),
            sds((rows, local), BF),
            sds((rows, 2 * local), BF),
        ]
        + ([sds((12, 4, width), F32)] if first else []),
        [
            pltpu.VMEM((rows, width), F32),
            pltpu.VMEM(weights[0].shape, BF),
            pltpu.SemaphoreType.DMA,
        ],
        name=f"project_{layer}",
    )


def attend(dims, layer, sc, chunks, queries, xa, weights):
    rows, n_seq, frames = dims.rows, dims.n_seq, dims.frames
    width, narrow, local, count = dims.width, dims.narrow, dims.local, dims.n_heads
    heads = local // HEAD_DIM

    def body(sc, *refs):
        chunks = refs[:n_seq]
        queries, xa, w_own, w_other = refs[n_seq : n_seq + 4]
        kept, probs, for_grads, exact = refs[n_seq + 4 : n_seq + 8]
        outs = refs[n_seq + 8 : n_seq + 8 + count]
        weight, buffer, sem = refs[n_seq + 8 + count :]
        fetch = Fetch(sc, layer, w_own, w_other, weight, sem)
        for k in range(n_seq):
            at = pl.multiple_of(jnp.bitwise_xor(sc[1], k) * rows, rows)
            kept[pl.ds(at, rows), :] = chunks[k][...]
        same = segments(sc, (rows, 1), 0, sc[1] * rows) == segments(sc, (1, frames), 1, 0)
        for head in range(heads):
            cols = slice(head * HEAD_DIM, (head + 1) * HEAD_DIM)
            scores = dot(queries[:, cols], kept[:, cols], ((1,), (1,)))
            scores = jnp.where(same, scores * (1.0 / math.sqrt(HEAD_DIM)), -1e30)
            prob = jnp.exp(scores - jnp.max(scores, axis=1, keepdims=True))
            prob = prob * (1.0 / jnp.sum(prob, axis=1, keepdims=True))
            low = prob.astype(BF)
            probs[head] = low
            value = kept[:, local + head * HEAD_DIM : local + (head + 1) * HEAD_DIM]
            exact[:, cols] = dot(low, value)
        mixed = exact[...].astype(BF)
        for_grads[:, :local] = mixed
        for_grads[:, local:] = xa[...]
        fetch.wait()
        buffer[...] = dot(mixed, weight[...]).astype(BF)
        hand_out(outs, buffer, sc[0], narrow)

    return call(
        body,
        [sc] + chunks + [queries, xa, weights[0], weights[1]],
        [SM] + [VM] * (n_seq + 2) + [HB, HB],
        [
            sds((frames, 2 * local), BF),
            sds((heads, rows, frames), BF),
            sds((rows, local + width), BF),
            sds((rows, local), F32),
        ]
        + [sds((rows, narrow), BF)] * count,
        [
            pltpu.VMEM(weights[0].shape, BF),
            pltpu.VMEM((rows, width), BF),
            pltpu.SemaphoreType.DMA,
        ],
        name=f"attend_{layer}",
    )


def feed_forward(dims, layer, sc, x, branch, mod, up, down):
    rows, width, narrow, count, hidden = (
        dims.rows, dims.width, dims.narrow, dims.n_heads, dims.hidden,
    )

    def body(sc, x, *refs):
        branch = refs[:count]
        mod, up_own, up_other, down_own, down_other = refs[count : count + 5]
        x1_out, for_grads, slope_out = refs[count + 5 : count + 8]
        outs = refs[count + 8 : 2 * count + 8]
        up, down, buffer, low, sem_up, sem_down = refs[2 * count + 8 :]
        fetch_up = Fetch(sc, layer, up_own, up_other, up, sem_up)
        fetch_down = Fetch(sc, layer, down_own, down_other, down, sem_down)
        seg = segments(sc, (rows, 1), 0, sc[1] * rows)
        place(buffer, branch, sc[0], narrow)
        x1 = x[...].astype(F32) + spread(mod, layer, 2, seg) * buffer[...]
        x1_out[...] = x1
        normed, _ = norm_of(x1)
        xf = (normed * (1.0 + spread(mod, layer, 4, seg)) + spread(mod, layer, 3, seg)).astype(BF)
        for_grads[:, hidden:] = xf
        fetch_up.wait()
        a = dot(xf, up[...])
        c0 = math.sqrt(2.0 / math.pi)
        square = a * a
        t = jnp.tanh(c0 * (a + 0.044715 * (a * square)))
        h = (0.5 * a * (1.0 + t)).astype(BF)
        for_grads[:, :hidden] = h
        slope_out[...] = 0.5 * (1.0 + t) + 0.5 * a * (1.0 - t * t) * (
            c0 * (1.0 + 3.0 * 0.044715 * square)
        )
        fetch_down.wait()
        low[...] = dot(h, down[...]).astype(BF)
        hand_out(outs, low, sc[0], narrow)

    return call(
        body,
        [sc, x] + branch + [mod, up[0], up[1], down[0], down[1]],
        [SM, VM] + [VM] * count + [VM, HB, HB, HB, HB],
        [
            sds((rows, width), F32),
            sds((rows, hidden + width), BF),
            sds((rows, hidden), F32),
        ]
        + [sds((rows, narrow), BF)] * count,
        [
            pltpu.VMEM(up[0].shape, BF),
            pltpu.VMEM(down[0].shape, BF),
            pltpu.VMEM((rows, width), F32),
            pltpu.VMEM((rows, width), BF),
            pltpu.SemaphoreType.DMA,
            pltpu.SemaphoreType.DMA,
        ],
        name=f"feed_forward_{layer}",
    )


def feed_backward(dims, layer, sc, pieces, slope, mod, up, down):
    rows, width, narrow, count, hidden = (
        dims.rows, dims.width, dims.narrow, dims.n_heads, dims.hidden,
    )
    last = layer == 1
    n_in = len(pieces)
    n_extra = 0 if last else 2

    def body(sc, *refs):
        pieces = refs[:n_in]
        slope, mod, up_own, up_other, down_own, down_other = refs[n_in : n_in + 6]
        rest = refs[n_in + 6 :]
        g_out, for_grads = rest[:2]
        outs = rest[2 : 2 + count]
        extra = rest[2 + count : 2 + count + n_extra]
        up, down, buffer, low, other_buffer, sem_up, sem_down = rest[2 + count + n_extra :]
        fetch_down = Fetch(sc, layer, down_own, down_other, down, sem_down)
        fetch_up = Fetch(sc, layer, up_own, up_other, up, sem_up)
        seg = segments(sc, (rows, 1), 0, sc[1] * rows)
        place(buffer, pieces[:count], sc[0], narrow)
        if last:
            g = buffer[...]
            g_out[...] = g.astype(BF)
        else:
            x, d_mid = pieces[count:]
            grad_out, sums_out = extra
            dxa = buffer[...]
            normed, inv = norm_of(x[...].astype(F32))
            other_buffer[...] = dxa * normed
            mine = pl.ds(pl.multiple_of(sc[0] * narrow, narrow), narrow)
            sums_out[0] = utterance_sums(buffer[:, mine], seg)
            sums_out[1] = utterance_sums(other_buffer[:, mine], seg)
            dx = d_mid[...] + norm_pull(dxa * (1.0 + spread(mod, 1, 1, seg)), normed, inv)
            other_buffer[...] = dx
            grad_out[...] = other_buffer[:, mine]
            g = dx.astype(BF)
            g_out[...] = g
            g = g.astype(F32)
        dz = (g * spread(mod, layer, 5, seg)).astype(BF)
        for_grads[:, :width] = dz
        fetch_down.wait()
        da = (dot(dz, down[...], ((1,), (1,))) * slope[...]).astype(BF)
        for_grads[:, width:] = da
        fetch_up.wait()
        low[...] = dot(da, up[...], ((1,), (1,))).astype(BF)
        hand_out(outs, low, sc[0], narrow)

    extra = [] if last else [sds((rows, narrow), F32), sds((2, 4, narrow), F32)]
    return call(
        body,
        [sc] + pieces + [slope, mod, up[0], up[1], down[0], down[1]],
        [SM] + [VM] * n_in + [VM, VM, HB, HB, HB, HB],
        [sds((rows, width), BF), sds((rows, width + hidden), BF)]
        + [sds((rows, narrow), BF)] * count
        + extra,
        [
            pltpu.VMEM(up[0].shape, BF),
            pltpu.VMEM(down[0].shape, BF),
            pltpu.VMEM((rows, width), F32),
            pltpu.VMEM((rows, width), BF),
            pltpu.VMEM((rows, width), F32),
            pltpu.SemaphoreType.DMA,
            pltpu.SemaphoreType.DMA,
        ],
        name=f"feed_backward_{layer}",
    )


def middle_backward(
    dims, layer, sc, g, x1, sums, branch, mod, weights, queries, kept, probs, exact, cosine, sine
):
    rows, width, narrow, local, count = (
        dims.rows, dims.width, dims.narrow, dims.local, dims.n_heads,
    )
    n_seq, frames = dims.n_seq, dims.frames
    heads = local // HEAD_DIM
    scale = 1.0 / math.sqrt(HEAD_DIM)

    def body(sc, g, x1, *refs):
        sums = refs[:count]
        branch, mod, w_own, w_other, queries, kept, probs, exact, cosine, sine = refs[
            count : count + 10
        ]
        d_mid_out, dy_out, small, q_out = refs[count + 10 : count + 14]
        outs = refs[count + 14 : count + 14 + n_seq]
        weight, buffer, other, done, sem = refs[count + 14 + n_seq :]
        fetch = Fetch(sc, layer, w_own, w_other, weight, sem)
        seg = segments(sc, (rows, 1), 0, sc[1] * rows)
        mine = pl.ds(pl.multiple_of(sc[0] * narrow, narrow), narrow)
        place(buffer, sums, sc[0], narrow)
        dxf = buffer[...]
        normed, inv = norm_of(x1[...])
        other[...] = dxf * normed
        small[1] = utterance_sums(buffer[:, mine], seg)
        small[2] = utterance_sums(other[:, mine], seg)
        d_mid = g[...].astype(F32) + norm_pull(
            dxf * (1.0 + spread(mod, layer, 4, seg)), normed, inv
        )
        d_mid_out[...] = d_mid
        other[...] = d_mid
        small[0] = utterance_sums(other[:, mine] * branch[...].astype(F32), seg)
        dy = (d_mid * spread(mod, layer, 2, seg)).astype(BF)
        dy_out[...] = dy
        fetch.wait()
        d_att = dot(dy, weight[...], ((1,), (1,))).astype(BF)
        shared = d_att.astype(F32) * exact[...]
        d_keys, d_vals = [], []
        cos = cosine[:, :HEAD_DIM]
        sin = -sine[:, :HEAD_DIM]
        for head in range(heads):
            cols = slice(head * HEAD_DIM, (head + 1) * HEAD_DIM)
            vals = slice(local + head * HEAD_DIM, local + (head + 1) * HEAD_DIM)
            low = probs[head]
            prob = low.astype(F32)
            grad = d_att[:, cols]
            d_prob = dot(grad, kept[:, vals], ((1,), (1,)))
            delta = jnp.sum(shared[:, cols], axis=1, keepdims=True)
            d_score = (prob * (d_prob - delta)).astype(BF)
            dq = dot(d_score, kept[:, cols]) * scale
            q_out[:, cols] = turn(dq, cos, sin).astype(BF)
            d_keys.append((dot(queries[:, cols], d_score, ((0,), (0,))) * scale).astype(BF))
            d_vals.append(dot(grad, low, ((0,), (0,))).astype(BF))
        for first, parts in ((0, d_keys), (local, d_vals)):
            for head in range(0, heads, 2):
                at = first + head * HEAD_DIM
                both = jnp.concatenate(parts[head : head + 2], axis=0)
                done[:, at : at + 2 * HEAD_DIM] = both.T
        for k in range(n_seq):
            at = pl.multiple_of(jnp.bitwise_xor(sc[1], k) * rows, rows)
            outs[k][...] = done[pl.ds(at, rows), :]

    return call(
        body,
        [sc, g, x1]
        + sums
        + [branch, mod, weights[0], weights[1], queries, kept, probs, exact, cosine, sine],
        [SM, VM, VM] + [VM] * count + [VM, VM, HB, HB] + [VM] * 6,
        [
            sds((rows, width), F32),
            sds((rows, width), BF),
            sds((3, 4, narrow), F32),
            sds((rows, local), BF),
        ]
        + [sds((rows, 2 * local), BF)] * n_seq,
        [
            pltpu.VMEM(weights[0].shape, BF),
            pltpu.VMEM((rows, width), F32),
            pltpu.VMEM((rows, width), F32),
            pltpu.VMEM((frames, 2 * local), BF),
            pltpu.SemaphoreType.DMA,
        ],
        name=f"middle_backward_{layer}",
    )


def project_backward(dims, layer, sc, dy, d_query, chunks, weights, cosine, sine):
    rows, width, narrow, local, count = (
        dims.rows, dims.width, dims.narrow, dims.local, dims.n_heads,
    )
    n_in = len(chunks)

    def body(sc, dy, d_query, *refs):
        chunks = refs[:n_in]
        w_own, w_other, cosine, sine, d_out = refs[n_in : n_in + 5]
        outs = refs[n_in + 5 : n_in + 5 + count]
        weight, buffer, sem = refs[n_in + 5 + count :]
        fetch = Fetch(sc, layer, w_own, w_other, weight, sem)
        total = chunks[0][...].astype(F32)
        for chunk in chunks[1:]:
            total = total + chunk[...].astype(F32)
        cos = widen_table(cosine[...], local)
        sin = -widen_table(sine[...], local)
        dk = turn(total[:, :local], cos, sin).astype(BF)
        dv = total[:, local:].astype(BF)
        d_out[:, :width] = dy[...]
        for i, part in enumerate((d_query[...], dk, dv)):
            d_out[:, width + i * local : width + (i + 1) * local] = part
        fetch.wait()
        total = dot(d_query[...], weight[0], ((1,), (1,)))
        total = total + dot(dk, weight[1], ((1,), (1,)))
        total = total + dot(dv, weight[2], ((1,), (1,)))
        buffer[...] = total.astype(BF)
        hand_out(outs, buffer, sc[0], narrow)

    return call(
        body,
        [sc, dy, d_query] + chunks + [weights[0], weights[1], cosine, sine],
        [SM, VM, VM] + [VM] * n_in + [HB, HB, VM, VM],
        [sds((rows, width + 3 * local), BF)] + [sds((rows, narrow), BF)] * count,
        [
            pltpu.VMEM(weights[0].shape, BF),
            pltpu.VMEM((rows, width), BF),
            pltpu.SemaphoreType.DMA,
        ],
        name=f"project_backward_{layer}",
    )


def products(left, right, local, width):
    first = dot(left[:, :local], right[:, :width], ((0,), (0,))).astype(BF)
    rest = dot(left[:, local:], right[:, width:], ((0,), (0,))).astype(BF)
    out = [[(slice(None), first)]]
    for i in range(rest.shape[1] // local):
        columns = slice(i * local, (i + 1) * local)
        lines = [slice(group * local, (group + 1) * local) for group in range(width // local)]
        out.append([(line, rest[line, columns]) for line in lines])
    return out


def half_grads(sc, left, right, local, name):
    width = left.shape[1] - local
    count = (1 + (right.shape[1] - width) // local) // 2

    def body(sc, left, right, mine, theirs):
        grads = products(left[...], right[...], local, width)
        for section in range(2):

            @pl.when(sc[2] == section)
            def _(section=section):
                for out, first in ((mine, section * count), (theirs, (1 - section) * count)):
                    for i in range(count):
                        for columns, value in grads[first + i]:
                            out[i * local : (i + 1) * local, columns] = value

    return call(
        body,
        [sc, left, right],
        [SM, VM, VM],
        [sds((count * local, width), BF)] * 2,
        name=name,
    )


def whole_grads(sc, left, right, local, name):
    count = len(left)
    rows, wide = left[0].shape
    width = wide - local
    tensors = 1 + (right[0].shape[1] - width) // local

    def body(sc, *refs):
        left, right = refs[:count], refs[count : 2 * count]
        out, all_left, all_right = refs[2 * count :]
        last = count.bit_length() - 2
        for k in range(count):
            mirrored = sum(1 << (last - i) for i in range(last + 1) if k >> i & 1)
            owner = jnp.bitwise_xor(sc[1], jnp.where(sc[2] == 0, k, mirrored))
            at = pl.ds(pl.multiple_of(owner * rows, rows), rows)
            all_left[at, :] = left[k][...]
            all_right[at, :] = right[k][...]
        grads = products(all_left[...], all_right[...], local, width)
        for i, grad in enumerate(grads):
            for columns, value in grad:
                out[i * local : (i + 1) * local, columns] = value

    return call(
        body,
        [sc] + list(left) + list(right),
        [SM] + [VM] * (2 * count),
        [sds((tensors * local, width), BF)],
        [
            pltpu.VMEM((count * rows, wide), BF),
            pltpu.VMEM((count * rows, right[0].shape[1]), BF),
        ],
        limit=24,
        name=name,
    )[0]


def add_split(sc, left, right, step):
    rows, width = left.shape
    half = rows // 2

    def body(sc, left, right, keep, send):
        bit = sc[5 + step]
        mine = pl.ds(pl.multiple_of(bit * half, half), half)
        other = pl.ds(pl.multiple_of((1 - bit) * half, half), half)
        keep[...] = (left[mine, :].astype(F32) + right[mine, :].astype(F32)).astype(BF)
        send[...] = (left[other, :].astype(F32) + right[other, :].astype(F32)).astype(BF)

    return call(
        body, [sc, left, right], [SM, VM, VM], [sds((half, width), BF)] * 2, name="add_split"
    )


def join(sc, mine, other, step):
    half, width = mine.shape

    def body(sc, mine, other, out):
        bit = sc[5 + step]
        out[pl.ds(pl.multiple_of(bit * half, half), half), :] = mine[...]
        out[pl.ds(pl.multiple_of((1 - bit) * half, half), half), :] = other[...]

    return call(
        body, [sc, mine, other], [SM, VM, VM], [sds((2 * half, width), BF)], name="join"
    )[0]


class HalfSum:
    def __init__(self, sc, layer, left, right, local, name):
        self.sc, self.layer = sc, layer
        self.mine, self.ready = half_grads(sc, left, right, local, name)
        self.bits = lax.axis_size("seq").bit_length() - 1
        self.at = 0
        self.taken = True
        self.pieces = []

    def send(self, *begin):
        value, bits = after(self.ready, *begin), self.bits
        if self.at == 0:
            self.came = swap(value)
        elif self.at <= bits:
            self.came = crossed(value, self.at - 1)
        else:
            if self.at == 2 * bits and not self.pieces:
                self.hand_over(value)
            self.came = crossed(value, 2 * bits - self.at)
        self.at += 1
        self.taken = False
        return self.came

    def hand_over(self, value):
        self.pieces.append((value, to_owner(value, self.layer)))

    def take(self):
        sc, bits = self.sc, self.bits
        self.taken = True
        if self.at <= bits:
            self.mine, self.ready = add_split(sc, self.mine, self.came, self.at - 1)
        elif self.at == bits + 1:
            self.mine = self.ready = add_chunks([self.mine, self.came])
        else:
            self.mine = self.ready = join(sc, self.mine, self.came, 2 * bits + 1 - self.at)
        return self.ready

    def last(self, *begin):
        while self.at <= 2 * self.bits:
            if not self.taken:
                self.take()
            self.send()
        self.hand_over(after(self.came, *begin))
        (own_0, other_0), (own_1, other_1) = self.pieces
        return [own_0, own_1, other_0, other_1]


class Spread:
    def __init__(self, value):
        self.parts = [value]
        self.bits = lax.axis_size("seq").bit_length() - 1
        self.early = None

    def one(self, *begin):
        self.parts.append(crossed(after(self.parts[0], *begin), 0))
        return self.parts[1]

    def two(self, *begin):
        self.early = crossed(after(self.parts[0], *begin), 1)
        return self.early

    def rest(self, *begin):
        for bit in range(1, self.bits):
            more = [] if bit > 1 else [self.early]
            start = 0 if bit > 1 else 1
            for part in self.parts[start:]:
                more.append(crossed(after(part, *begin), bit))
            self.parts = self.parts + more
        return self.parts[3:]


class Assembly:
    SCRATCH = 5

    @staticmethod
    def scratch(added, local, outs):
        width = added[0].shape[1]
        return [
            pltpu.VMEM((local, width), F32),
            pltpu.VMEM((outs - 1, width, local), F32),
            pltpu.VMEM((2, outs * local, width), BF),
            pltpu.SemaphoreType.DMA((outs, 2)),
            pltpu.SemaphoreType.DMA((outs,)),
        ]

    def __init__(self, sc, added, pieces, outs, scratch):
        self.sc, self.added, self.pieces = sc, added, pieces
        self.first_out, self.rest_out = outs
        self.first, self.rest, self.held, self.sems, self.out_sems = scratch
        self.outs = 1 + self.rest.shape[0]
        self.local, self.width = self.first.shape
        self.size = pieces[0].shape[0]

    def fetches_added(self):
        copies = []
        for i in range(self.outs):
            at = pl.ds(i * self.local, self.local)
            for j in range(2):
                copies.append(
                    pltpu.make_async_copy(
                        self.added[j].at[at, :], self.held.at[j, at, :], self.sems.at[i, j]
                    )
                )
        return copies

    def fetches_pieces(self):
        return [
            pltpu.make_async_copy(
                self.pieces[p],
                self.held.at[0, pl.ds(p * self.size, self.size), :],
                self.sems.at[p // 2, p % 2],
            )
            for p in range(4)
        ]

    def start(self):
        @pl.when(self.sc[2] == 0)
        def _():
            for copy in self.fetches_added():
                copy.start()

        @pl.when(self.sc[2] == 1)
        def _():
            for copy in self.fetches_pieces():
                copy.start()

    def store(self, index):
        if index == 0:
            return pltpu.make_async_copy(self.first, self.first_out, self.out_sems.at[0])
        return pltpu.make_async_copy(
            self.rest.at[index - 1], self.rest_out.at[index - 1], self.out_sems.at[index]
        )

    def put(self, index, value, line):
        lines = value.shape[0]
        if index == 0:
            self.first[line : line + lines, :] = value
            return
        for group in range(self.width // self.local):
            columns = slice(group * self.local, (group + 1) * self.local)
            at = group * self.local + line
            self.rest[index - 1, at : at + lines, :] = value[:, columns]

    def run(self):
        sc, local, size, held = self.sc, self.local, self.size, self.held
        count = self.outs // 2

        @pl.when(sc[2] == 0)
        def _():
            copies = self.fetches_added()
            for i in range(self.outs):
                copies[2 * i].wait()
                copies[2 * i + 1].wait()
                at = slice(i * local, (i + 1) * local)
                self.put(i, held[0, at, :].astype(F32) + held[1, at, :].astype(F32), 0)
                self.store(i).start()

        bits = lax.axis_size("seq").bit_length() - 1
        low, high = sc[1] & 1, (sc[1] >> (bits - 1)) & 1

        @pl.when(sc[2] == 1)
        def _():
            for copy in self.fetches_pieces():
                copy.wait()
            for section, at, bit in ((1, 0, high), (0, 2, low)):
                for turn in range(2):

                    @pl.when(bit == turn)
                    def _(section=section, at=at, turn=turn):
                        for place in range(2):
                            base = (at + (place ^ turn)) * size
                            for i in range(count):
                                begin = max(i * local, place * size)
                                end = min((i + 1) * local, (place + 1) * size)
                                if begin < end:
                                    row = base + begin - place * size
                                    value = held[0, row : row + end - begin, :].astype(F32)
                                    self.put(section * count + i, value, begin - i * local)

            for i in range(self.outs):
                self.store(i).start()

    def wait(self):
        for i in range(self.outs):
            self.store(i).wait()


def by_section(sc, mine, theirs, layer_0, layer_1):
    mine[...] = jnp.where(sc[2] == 0, layer_0, layer_1)
    theirs[...] = jnp.where(sc[2] == 0, layer_1, layer_0)


def gate_sums(dims, layer, sc, g, x1, z, mod, passed):
    rows, narrow = dims.rows, dims.narrow

    def body(sc, g, x1, z, mod, passed, small, *shown):
        seg = segments(sc, (rows, 1), 0, sc[1] * rows)
        mine = pl.ds(pl.multiple_of(sc[0] * narrow, narrow), narrow)
        value = z[...].astype(F32)
        small[...] = utterance_sums(g[:, mine].astype(F32) * value, seg)
        if shown:
            gate = spread(mod, layer, 5, seg, mine)
            result = (x1[:, mine] + gate * value).astype(BF)
            by_section(sc, *shown, passed[...], result)

    outs = [sds((4, narrow), F32)]
    if layer == 1:
        outs += [sds((rows, narrow), BF)] * 2
    return call(
        body, [sc, g, x1, z, mod, passed], [SM] + [VM] * 5, outs, name=f"gate_sums_{layer}"
    )


def last_norm(dims, sc, terms, x, mod, small_0, small_1):
    rows, narrow, count = dims.rows, dims.narrow, dims.n_heads

    def body(sc, *refs):
        terms = refs[:count]
        x, mod, mid_0, gate_0, in_1, mid_1, gate_1 = refs[count : count + 7]
        total_out, normed_out, inv_out, mine_out, theirs_out, rows_out, buffer = refs[count + 7 :]
        seg = segments(sc, (rows, 1), 0, sc[1] * rows)
        mine = pl.ds(pl.multiple_of(sc[0] * narrow, narrow), narrow)
        total = terms[0][...].astype(F32)
        for term in terms[1:]:
            total = total + term[...].astype(F32)
        normed, inv = norm_of(x[...].astype(F32))
        buffer[...] = normed
        normed = buffer[:, mine]
        first = (
            [utterance_sums(total, seg), utterance_sums(total * normed, seg)]
            + [mid_0[i] for i in range(3)]
            + [gate_0[...]]
        )
        second = [in_1[0], in_1[1]] + [mid_1[i] for i in range(3)] + [gate_1[...]]
        for i in range(6):
            by_section(sc, mine_out.at[i], theirs_out.at[i], first[i], second[i])
        grad = total * (1.0 + spread(mod, 0, 1, seg, mine))
        total_out[...] = grad
        normed_out[...] = normed
        inv_out[...] = inv
        lane = lax.broadcasted_iota(jnp.int32, (rows, 128), 1)
        sums = jnp.where(lane == 0, jnp.sum(grad, axis=1, keepdims=True), 0.0)
        sums = jnp.where(lane == 1, jnp.sum(grad * normed, axis=1, keepdims=True), sums)
        pick = diagonal(8, 128)
        rows_out[...] = sum(dot(pick, part, ((1,), (1,))) for part in split3(sums))

    return call(
        body,
        [sc] + terms + [x, mod] + small_0 + small_1,
        [SM] + [VM] * (count + 7),
        [
            sds((rows, narrow), F32),
            sds((rows, narrow), F32),
            sds((rows, 1), F32),
            sds((6, 4, narrow), F32),
            sds((6, 4, narrow), F32),
            sds((8, rows), F32),
        ],
        [pltpu.VMEM((rows, dims.width), F32)],
        name="last_norm",
    )


def last_pull(dims, sc, d_mid, grad, normed, inv, sums, middle_grad):
    rows, narrow, count, width = dims.rows, dims.narrow, dims.n_heads, dims.width

    def body(sc, d_mid, grad, normed, inv, middle, *refs):
        sums, outs = refs[:count], refs[count:]
        total = sums[0][:8, :rows]
        for term in sums[1:]:
            total = total + term[:8, :rows]
        row = lax.broadcasted_iota(jnp.int32, (8, 128), 0)
        lane = lax.broadcasted_iota(jnp.int32, (8, 128), 1)
        pick = (row == 4 * lane + 3).astype(BF)
        total = sum(dot(part, pick, ((0,), (0,))) for part in split3(total * (1.0 / width)))
        mine = pl.ds(pl.multiple_of(sc[0] * narrow, narrow), narrow)
        first = d_mid[:, mine] + inv[...] * (
            grad[...] - total[:, 0:1] - normed[...] * total[:, 1:2]
        )
        by_section(sc, *outs, first, middle[...])

    return call(
        body,
        [sc, d_mid, grad, normed, inv, middle_grad] + sums,
        [SM] + [VM] * (5 + count),
        [sds((rows, narrow), F32)] * 2,
        name="last_pull",
    )


def modulation_part(sc, mod_weight, row_sums, own, n_seq):
    kinds, width, narrow = mod_weight.shape

    def body(sc, mod_weight, row_sums, *refs):
        own = refs[:n_seq]
        grads_out, part, box = refs[n_seq:]
        for k in range(n_seq):
            box[jnp.bitwise_xor(sc[1], k)] = own[k][...]
        total = box[0]
        for j in range(1, n_seq):
            total = total + box[j]
        result = jnp.zeros((8, width), F32)
        for which in range(kinds):
            mine, theirs = total[which], total[kinds + which]
            grad = jnp.concatenate(
                [jnp.where(sc[2] == 0, mine, theirs), jnp.where(sc[2] == 0, theirs, mine)],
                axis=0,
            )
            grads_out[which] = grad
            result = result + exact_dot(grad, mod_weight[which], ((1,), (1,)))
        part[...] = result
        for row in range(2):
            part[4 * row + 3 : 4 * row + 4, : row_sums.shape[1]] = row_sums[row : row + 1, :]

    return call(
        body,
        [sc, mod_weight, row_sums] + own,
        [SM, VM, VM] + [VM] * n_seq,
        [sds((kinds, 8, narrow), F32), sds((8, width), F32)],
        [pltpu.VMEM((n_seq, 2 * kinds, 4, narrow), F32)],
        name="modulation_part",
    )


def modulation_weight(sc, act, grads):
    kinds, rows, narrow = grads.shape
    width = act.shape[1]

    def body(sc, act, grads, out, held, sems):
        tall = outer_parts(act[...], act[...])[0].astype(F32).T.astype(BF)

        def store(which):
            return pltpu.make_async_copy(held.at[which], out.at[which], sems.at[which])

        for which in range(kinds):
            wide = outer_parts(grads[which], grads[which])[1]
            held[which] = dot(tall, wide)
            store(which).start()
        for which in range(kinds):
            store(which).wait()

    return pl_call(
        body,
        [sc, act, grads],
        [SM, VM, VM],
        [sds((kinds, width, narrow), F32)],
        [HB],
        [pltpu.VMEM((kinds, width, narrow), F32), pltpu.SemaphoreType.DMA((kinds,))],
        limit=16,
        name="modulation_weight",
    )[0]


def time_backward(sc, sinus, inner, outer, time_out, own):
    count = len(own)
    rows, width = inner.shape
    freq = sinus.shape[1]
    block = width // 4

    def body(sc, sinus, inner, outer, time_out, *refs):
        own = refs[:count]
        g_in, g_out, box, held_in, held_out, sems = refs[count:]
        for k in range(count):
            at = jnp.bitwise_xor(sc[0], k)
            box[at, sc[2]] = own[k][:rows]
            box[at, 1 - sc[2]] = own[k][rows:]
        total = jnp.zeros((rows, width), F32)
        for j in range(count):
            for c in range(2):
                total = total + box[j, c]
        row = lax.broadcasted_iota(jnp.int32, (rows, width), 0)
        total = jnp.where(row % 4 == 3, 0.0, total)

        def slope(value):
            gate = 1.0 / (1.0 + jnp.exp(-value))
            return gate * (1.0 + value * (1.0 - gate))

        pre = inner[...]
        hidden = pre / (1.0 + jnp.exp(-pre))
        d_outer = total * slope(outer[...])
        tall, wide = outer_parts(hidden, d_outer)
        tall = tall.astype(F32).T.astype(BF)
        copies = []
        for i in range(4):
            at = slice(i * block, (i + 1) * block)
            held_out[at, :] = dot(tall[at], wide)
            copies.append(
                pltpu.make_async_copy(held_out.at[at, :], g_out.at[at, :], sems.at[i])
            )
            copies[-1].start()
        d_inner = exact_dot(d_outer, time_out[...], ((1,), (1,))) * slope(pre)
        held_in[...] = exact_outer(sinus[...], d_inner)
        copies.append(pltpu.make_async_copy(held_in, g_in, sems.at[4]))
        copies[-1].start()
        for copy in copies:
            copy.wait()

    return pl_call(
        body,
        [sc, sinus, inner, outer, time_out] + list(own),
        [SM] + [VM] * (4 + count),
        [sds((freq, width), F32), sds((width, width), F32)],
        [HB, HB],
        [
            pltpu.VMEM((count, 2, rows, width), F32),
            pltpu.VMEM((freq, width), F32),
            pltpu.VMEM((width, width), F32),
            pltpu.SemaphoreType.DMA((5,)),
        ],
        limit=16,
        name="time_backward",
    )


def finish(dims, sc, feed, attention, acts, grads):
    n = Assembly.SCRATCH

    def body(sc, act_own, act_other, grad_own, grad_other, *refs):
        sources, outs, scratch = refs[:12], refs[12:18], refs[18:]
        feed = Assembly(sc, sources[:2], sources[2:6], outs[:2], scratch[:n])
        attention = Assembly(sc, sources[6:8], sources[8:], outs[2:4], scratch[n:])
        feed.start()
        attention.start()
        outs[4][sc[2]] = act_own[...]
        outs[4][1 - sc[2]] = act_other[...]
        outs[5][sc[2]] = grad_own[...]
        outs[5][1 - sc[2]] = grad_other[...]
        feed.run()
        attention.run()
        feed.wait()
        attention.wait()

    width = dims.width
    sources = list(feed[0]) + list(feed[1]) + list(attention[0]) + list(attention[1])
    return pl_call(
        body,
        [sc] + list(acts) + list(grads) + sources,
        [SM] + [VM] * 4 + [HB] * 12,
        [
            sds((dims.hidden, width), F32),
            sds((1, width, dims.hidden), F32),
            sds((dims.local, width), F32),
            sds((3, width, dims.local), F32),
            sds((2,) + acts[0].shape, BF),
            sds((2,) + grads[0].shape, F32),
        ],
        [HB] * 4 + [VM] * 2,
        Assembly.scratch(feed[0], dims.hidden, 2) + Assembly.scratch(attention[0], dims.local, 4),
        limit=24,
        name="finish",
    )


class Dims:
    pass


def local_program(
    frames,
    cotangent,
    utt_lengths,
    time_ids,
    w_time_in,
    w_time_out,
    w_mod,
    w_qkv,
    w_out,
    w_up,
    w_down,
):
    dims = Dims()
    dims.n_heads = lax.axis_size("heads")
    dims.n_seq = n_seq = lax.axis_size("seq")
    _, dims.rows, dims.narrow = frames.shape
    dims.width = dims.narrow * dims.n_heads
    dims.local = w_qkv.shape[3]
    dims.hidden = w_up.shape[2]
    dims.frames = dims.rows * n_seq
    section = lax.axis_index("section")

    def here(both):
        return lax.dynamic_index_in_dim(both, section, 0, keepdims=False)

    sc = utt_lengths
    qkv = jnp.transpose(w_qkv[0], (1, 0, 2))
    mod_weight = jnp.transpose(w_mod[0], (1, 0, 2))
    wide_frames = gather(here(frames), "heads")
    qkv_w = (qkv, swap(qkv))
    sinus, inner, outer, act, mod_mine, mod_theirs = start(
        sc, time_ids, w_time_in, w_time_out, mod_weight
    )
    mod_theirs = swap(after(mod_theirs, *wide_frames))
    mods = gather(jnp.concatenate([mod_mine, mod_theirs], axis=0), "heads")
    cosine, sine = tables(sc, dims.rows)
    mods = after(mods, cosine, sine)

    x_0, _, xa, q_0, kv, mod = project(dims, 0, sc, wide_frames, mods, qkv_w, cosine, sine)
    chunks = gather(kv, "seq")
    out_w = (w_out[0], swap(after(w_out[0], mods[0])))
    kept_0, probs_0, for_attention, exact_0, *terms = attend(
        dims, 0, sc, chunks, q_0, xa, out_w
    )
    fwd_a = Spread(for_attention)

    up_w, down_w = [(w[0], swap(after(w[0], terms[0]))) for w in (w_up, w_down)]
    total = after(add_chunks(exchange(terms, "heads")), up_w[1], down_w[1])

    branch_0 = gather(total, "heads")
    fwd_a.one(total)
    fwd_a.two(total)
    x1_0, for_feed, slope_0, *terms = feed_forward(
        dims, 0, sc, x_0, branch_0, mod, up_w, down_w
    )
    fwd_f = Spread(for_feed)

    total = after(add_chunks(exchange(terms, "heads")), fwd_a.parts[1], fwd_a.early)

    z_0 = gather(total, "heads")
    fwd_a.rest(total)
    fwd_f.one(total)

    x_2, passed, xa, q_1, kv = project(
        dims, 1, sc, [x1_0] + z_0, [mod], qkv_w, cosine, sine
    )
    kv = after(kv, fwd_f.parts[1], *fwd_a.parts[3:])
    chunks = gather(kv, "seq")
    wide_cotangent = gather(after(here(cotangent), chunks[1]), "heads")
    kept_1, probs_1, for_attention_1, exact_1, *terms = attend(
        dims, 1, sc, chunks, q_1, xa, out_w
    )

    terms[0] = after(terms[0], *wide_cotangent)
    total = add_chunks(exchange(terms, "heads"))
    fwd_f.two(terms[0])

    branch_1 = gather(total, "heads")
    x1_1, for_feed, slope_1, *z_terms = feed_forward(
        dims, 1, sc, x_2, branch_1, mod, up_w, down_w
    )
    g_1, late, *terms = feed_backward(
        dims, 1, sc, wide_cotangent, slope_1, mod, up_w, down_w
    )
    terms = after(terms, fwd_f.early)
    feed_1 = HalfSum(sc, 1, for_feed, late, dims.hidden, "feed_grads_1")
    feed_1.send()
    got = exchange(terms, "heads")
    total = after(add_chunks(got), feed_1.came, *fwd_f.rest(terms[0]))

    feed_1.take()
    feed_1.send(total)
    sums = after(gather(total, "heads"), feed_1.came)

    feed_1.take()
    feed_1.send(sums[0])
    d_mid_1, dy, small_f1, dq, *sent = middle_backward(
        dims, 1, sc, g_1, x1_1, after(sums, feed_1.ready), branch_1[0], mod, out_w,
        q_1, kept_1, probs_1, exact_1, cosine, sine,
    )
    sent = after(sent, feed_1.came)

    got = exchange(sent, "seq")
    feed_1.take()
    z_1 = add_chunks(exchange(after(z_terms, sent[0]), "heads"))
    gate_1, *acts = gate_sums(dims, 1, sc, g_1, x1_1, z_1, mod, passed)
    got = after(got, feed_1.ready, *acts)
    late, *terms = project_backward(dims, 1, sc, dy, dq, got, qkv_w, cosine, sine)

    got = exchange(terms, "heads")
    feed_1.send(terms[0])
    attention_1 = HalfSum(sc, 1, for_attention_1, late, dims.local, "attend_grads_1")
    acts = [acts[0], swap(after(acts[1], terms[0]))]
    total = after(
        add_chunks(got), feed_1.came, attention_1.mine, attention_1.ready, acts
    )

    feed_1.take()
    feed_1.send(total)
    attention_1.send(total)
    pieces = gather(total, "heads")

    g_0, late, *rest = feed_backward(
        dims, 0, sc, pieces + [x_2, d_mid_1], slope_0, mod, up_w, down_w
    )
    terms, (middle_grad, small_a1) = rest[: dims.n_heads], rest[dims.n_heads :]
    terms = after(terms, feed_1.came, attention_1.came)
    late_f = Spread(late)
    got = exchange(terms, "heads")
    attention_1.take()
    attention_1.send(terms[0])
    total = after(add_chunks(got), attention_1.came, late_f.one(terms[0]))

    attention_1.take()
    attention_1.send(total)
    late_f.two(total)
    sums = after(gather(total, "heads"), attention_1.came)

    attention_1.take()
    attention_1.send(sums[0])
    d_mid_0, dy, small_f0, dq, *sent = middle_backward(
        dims, 0, sc, g_0, x1_0, after(sums, attention_1.ready), branch_0[0], mod, out_w,
        q_0, kept_0, probs_0, exact_0, cosine, sine,
    )
    sent = after(sent, attention_1.came, late_f.early)

    got = exchange(sent, "seq")
    attention_1.take()
    if attention_1.at == 2 * attention_1.bits:
        attention_1.hand_over(after(attention_1.ready, got[0]))
    feed_1 = feed_1.last(sent[0])
    gate_0, *_ = gate_sums(dims, 0, sc, g_0, x1_0, z_0[0], mod, passed)
    got = after(got, attention_1.ready, gate_0, feed_1)
    late, *terms = project_backward(dims, 0, sc, dy, dq, got, qkv_w, cosine, sine)
    late_a = Spread(late)

    got = exchange(terms, "heads")
    late_a.one(terms[0])
    late_f.rest(terms[0])

    grad, normed, inv, mine, theirs, row_sums = last_norm(
        dims, sc, got, x_0, mod, [small_f0, gate_0], [small_a1, small_f1, gate_1]
    )
    late_a.two(row_sums)
    theirs = after(swap(theirs), late_a.parts[1], *late_f.parts[3:])
    both = jnp.concatenate([mine, theirs], axis=0)
    both = gather(both, "seq")
    feed_0 = whole_grads(
        sc, after(fwd_f.parts, theirs), late_f.parts, dims.hidden, "feed_grads_0"
    )
    both = after(both, feed_0, late_a.early)
    mod_grads, part = modulation_part(sc, mod_weight, row_sums, both, n_seq)

    late_a.rest(part)
    attention_1.send(part)
    feed_0 = [feed_0, to_owner(after(feed_0, both[0]), 0)]
    ends = jnp.concatenate([part, swap(part)], axis=0)
    ends = gather(after(ends, feed_0), "heads")
    g_mod = modulation_weight(sc, act, mod_grads)
    ends = after(ends, *late_a.parts[3:], g_mod)

    attention_0 = whole_grads(
        sc, after(fwd_a.parts, *ends), late_a.parts, dims.local, "attend_grads_0"
    )
    attention_0 = after(attention_0, attention_1.came)
    attention_0 = [attention_0, to_owner(attention_0, 0)]
    attention_1 = attention_1.last(attention_0[0])
    grads = last_pull(
        dims, sc, d_mid_0, grad, normed, inv, after(ends, attention_0[0]), middle_grad
    )
    grads = [grads[0], swap(grads[1])]
    g_first, g_second = time_backward(
        sc, sinus, inner, outer, w_time_out, after(ends, attention_0[0])
    )
    g_reduce, g_expand, g_out, g_qkv, acts, grads = finish(
        dims, sc, (feed_0, feed_1), (after(attention_0, g_second), attention_1), acts, grads
    )

    return (
        acts[None],
        grads[None],
        g_first,
        g_second,
        jnp.transpose(g_mod, (1, 0, 2))[None],
        jnp.transpose(g_qkv, (1, 0, 2))[None],
        g_out[None],
        g_expand,
        g_reduce[None],
    )


def solution(mesh):
    placed = (
        P(None, "seq", "heads"),
        P(None, "seq", "heads"),
        P(),
        P(),
        P(),
        P(),
        P("section", None, None, "heads"),
        P("section", None, None, "heads"),
        P("section", "heads", None),
        P("section", None, "heads"),
        P("section", "heads", None),
    )
    return jax.shard_map(
        local_program,
        mesh=mesh,
        in_specs=placed,
        out_specs=(
            P("section", None, "seq", "heads"),
            P("section", None, "seq", "heads"),
            P(),
            P(),
            P("section", None, None, "heads"),
            P("section", None, None, "heads"),
            P("section", "heads", None),
            P("section", None, "heads"),
            P("section", "heads", None),
        ),
        check_vma=False,
    )
```

```python
import functools
import math

import jax
import jax.numpy as jnp
import numpy as np
from jax import lax
from jax.experimental import pallas as pl
from jax.experimental.pallas import tpu as pltpu
from jax.sharding import PartitionSpec as P

HEAD_DIM = 64
FREQ = 256
EPS = 1e-06
BF = jnp.bfloat16
F32 = jnp.float32
MIB = 1024 * 1024


def partner(value, axis, by):
    if by == 0:
        return value
    return lax.ppermute(value, axis, [(i, i ^ by) for i in range(lax.axis_size(axis))])


def order_of(count):
    return (3, 1, 2) if count == 4 else tuple(range(count - 1, 0, -1))


def gather(value, axis):
    count = lax.axis_size(axis)
    out = [value] * count
    for k in order_of(count):
        out[k] = partner(value, axis, k)
    return out


def exchange(chunks, axis):
    out = list(chunks)
    for k in order_of(len(chunks)):
        out[k] = partner(chunks[k], axis, k)
    return out


def swap(value):
    return lax.ppermute(value, "section", [(0, 1), (1, 0)])


def to_owner(value, layer):
    return lax.ppermute(value, "section", [(1 - layer, layer)])


def crossed(value, step):
    length = lax.axis_size("seq")
    last = length.bit_length() - 2
    pairs = []
    for c in range(2):
        by = 1 << (step if c == 0 else last - step)
        pairs += [(c * length + i, c * length + (i ^ by)) for i in range(length)]
    return lax.ppermute(value, ("section", "seq"), pairs)


def after(value, *done):
    value = lax.optimization_barrier((value, done))[0]
    return list(value) if isinstance(value, (list, tuple)) else value


def add_chunks(chunks):
    total = chunks[0].astype(F32)
    for chunk in chunks[1:]:
        total = total + chunk.astype(F32)
    return total.astype(BF)


def dot(left, right, contract=((1,), (0,))):
    return lax.dot_general(left, right, (contract, ((), ())), preferred_element_type=F32)


def split3(value):
    high = value.astype(BF)
    rest = value - high.astype(F32)
    middle = rest.astype(BF)
    low = (rest - middle.astype(F32)).astype(BF)
    return high, middle, low


def diagonal(rows, columns):
    row = lax.broadcasted_iota(jnp.int32, (rows, columns), 0)
    return (row == lax.broadcasted_iota(jnp.int32, (rows, columns), 1)).astype(BF)


def exact_dot(left, right, contract=((1,), (0,))):
    rows = left.shape[0]
    stacked = jnp.concatenate(split3(left), axis=0)
    out = dot(stacked, right, contract)
    return out[:rows] + (out[rows : 2 * rows] + out[2 * rows :])


def exact_outer(left, right):
    tall, wide = outer_parts(left, right)
    return dot(tall, wide, ((0,), (0,)))


def outer_parts(left, right):
    a, b = split3(left), split3(right)
    tall = jnp.concatenate([a[0], a[0], a[1]], axis=0)
    wide = jnp.concatenate([b[0], b[1], b[0]], axis=0)
    return tall, wide


def segments(sc, shape, axis, first):
    index = lax.broadcasted_iota(jnp.int32, shape, axis) + first
    return (index >= sc[3]).astype(jnp.int32) + (index >= sc[4]).astype(jnp.int32)


def spread(mod, layer, which, seg, columns=slice(None)):
    block = mod[layer * 6 + which, :, columns]
    rows = [block[u : u + 1] for u in range(3)]
    return jnp.where(seg == 0, rows[0], jnp.where(seg == 1, rows[1], rows[2]))


def utterance_sums(value, seg):
    rows = [
        jnp.sum(jnp.where(seg == u, value, 0.0), axis=0, keepdims=True) for u in range(3)
    ]
    return jnp.concatenate(rows + [jnp.zeros_like(rows[0])], axis=0)


def norm_of(value):
    mean = jnp.mean(value, axis=1, keepdims=True)
    centred = value - mean
    inv = lax.rsqrt(jnp.mean(centred * centred, axis=1, keepdims=True) + EPS)
    return centred * inv, inv


def norm_pull(grad, normed, inv):
    return inv * (
        grad
        - jnp.mean(grad, axis=1, keepdims=True)
        - normed * jnp.mean(grad * normed, axis=1, keepdims=True)
    )


def lanes_of(index, count, width):
    return pl.ds(pl.multiple_of(lax.rem(index, count) * width, width), width)


def place(buffer, chunks, own, width):
    for k, chunk in enumerate(chunks):
        at = pl.multiple_of(jnp.bitwise_xor(own, k) * width, width)
        buffer[:, pl.ds(at, width)] = chunk[...].astype(buffer.dtype)


def hand_out(outs, buffer, own, width):
    for k, out in enumerate(outs):
        at = pl.multiple_of(jnp.bitwise_xor(own, k) * width, width)
        out[...] = buffer[:, pl.ds(at, width)].astype(out.dtype)


class Fetch:
    def __init__(self, sc, layer, own, other, buffer, sem):
        self.copy = pltpu.make_async_copy(own, buffer, sem)
        other_copy = pltpu.make_async_copy(other, buffer, sem)

        @pl.when(sc[2] == layer)
        def _():
            self.copy.start()

        @pl.when(sc[2] != layer)
        def _():
            other_copy.start()

    def wait(self):
        self.copy.wait()


def turn(value, cosine, sine):
    width = value.shape[1]
    even = lax.broadcasted_iota(jnp.int32, value.shape, 1) % 2 == 0
    swapped = jnp.where(even, pltpu.roll(value, width - 1, 1), pltpu.roll(value, 1, 1))
    return value * cosine + swapped * sine


def widen_table(table, width):
    copies = width // table.shape[1]
    return jnp.concatenate([table] * copies, axis=1) if copies > 1 else table[:, :width]


VM = pl.BlockSpec(memory_space=pltpu.VMEM)
SM = pl.BlockSpec(memory_space=pltpu.SMEM)
HB = pl.BlockSpec(memory_space=pltpu.HBM)


def sds(shape, dtype):
    return jax.ShapeDtypeStruct(tuple(shape), dtype)


class Place:
    def __init__(self, lengths):
        self.lengths = lengths
        self.known = {}
        for index in range(5):
            self[index]

    def __getitem__(self, index):
        if index not in self.known:
            self.known[index] = self.find(index)
        return self.known[index]

    def find(self, index):
        if index < 3:
            return lax.axis_index(("heads", "seq", "section")[index])
        if index == 3:
            return self.lengths[self[2], 0]
        if index == 4:
            return self[3] + self.lengths[self[2], 1]
        low = index - 5
        high = lax.axis_size("seq").bit_length() - 2 - low
        return jnp.where(self[2] == 0, self[1] >> low, self[1] >> high) & 1


def call(body, ins, specs, outs, scratch=(), limit=12, name=None):
    return pl_call(body, ins, specs, outs, [VM] * len(outs), scratch, limit, name)


def pl_call(body, ins, specs, outs, out_specs, scratch, limit, name):
    def placed(lengths, *refs):
        body(Place(lengths), *refs)

    return pl.pallas_call(
        placed,
        out_shape=list(outs),
        in_specs=list(specs),
        out_specs=list(out_specs),
        scratch_shapes=list(scratch),
        compiler_params=pltpu.CompilerParams(vmem_limit_bytes=limit * MIB),
        cost_estimate=pl.CostEstimate(flops=1, bytes_accessed=1, transcendentals=0),
        name=name,
    )(*ins)


def start(sc, time_ids, time_in, time_out, mod_weight):
    width = time_in.shape[1]
    kinds, _, narrow = mod_weight.shape
    half = FREQ // 2

    def body(sc, ids, time_in, time_out, mod_weight, *refs):
        sinus_out, inner_out, outer_out, act_out, mine_out, theirs_out = refs[:6]
        w_in, w_out, w_mod, sems = refs[6:]
        copies = [
            pltpu.make_async_copy(time_in, w_in, sems.at[0]),
            pltpu.make_async_copy(time_out, w_out, sems.at[1]),
            pltpu.make_async_copy(mod_weight, w_mod, sems.at[2]),
        ]
        for copy in copies:
            copy.start()
        row = lax.broadcasted_iota(jnp.int32, (8, half), 0)
        lane = lax.broadcasted_iota(jnp.int32, (8, half), 1).astype(F32)
        stamp = jnp.zeros((8, half), F32)
        for m in range(2):
            for u in range(3):
                stamp = jnp.where(row == m * 4 + u, ids[m, u].astype(F32), stamp)
        angle_t = stamp * jnp.exp(lane * (-math.log(10000.0) / (half - 1)))
        sinus = jnp.concatenate([jnp.sin(angle_t), jnp.cos(angle_t)], axis=1)
        sinus_out[...] = sinus

        copies[0].wait()
        inner = exact_dot(sinus, w_in[...])
        inner_out[...] = inner
        hidden = inner / (1.0 + jnp.exp(-inner))
        copies[1].wait()
        outer = exact_dot(hidden, w_out[...])
        outer_out[...] = outer
        act = outer / (1.0 + jnp.exp(-outer))
        act_out[...] = act
        copies[2].wait()
        for which in range(kinds):
            modul = exact_dot(act, w_mod[which])
            mine_out[which] = jnp.where(sc[2] == 0, modul[:4], modul[4:])
            theirs_out[which] = jnp.where(sc[2] == 0, modul[4:], modul[:4])

    return call(
        body,
        [sc, time_ids, time_in, time_out, mod_weight],
        [SM, SM, HB, HB, HB],
        [sds((8, FREQ), F32)]
        + [sds((8, width), F32)] * 3
        + [sds((kinds, 4, narrow), F32)] * 2,
        [
            pltpu.VMEM(time_in.shape, BF),
            pltpu.VMEM(time_out.shape, BF),
            pltpu.VMEM(mod_weight.shape, BF),
            pltpu.SemaphoreType.DMA((3,)),
        ],
        limit=56,
        name="start",
    )


def tables(sc, rows):
    def body(sc, cosine, sine):
        index = lax.broadcasted_iota(jnp.int32, (rows, 2 * HEAD_DIM), 0) + sc[1] * rows
        begin = jnp.where(index >= sc[4], sc[4], jnp.where(index >= sc[3], sc[3], 0))
        lane = lax.broadcasted_iota(jnp.int32, (rows, 2 * HEAD_DIM), 1)
        pair = lax.broadcasted_iota(jnp.int32, (1, 2 * HEAD_DIM), 1)
        rate = jnp.exp(
            ((pair % HEAD_DIM) // 2).astype(F32) * (-2.0 * math.log(10000.0) / HEAD_DIM)
        )
        angle = (index - begin).astype(F32) * rate
        cosine[...] = jnp.cos(angle)
        sine[...] = jnp.sin(angle) * jnp.where(lane % 2 == 0, -1.0, 1.0)

    return call(body, [sc], [SM], [sds((rows, 2 * HEAD_DIM), F32)] * 2, name="tables")


def project(dims, layer, sc, pieces, mods, weights, cosine, sine):
    first = layer == 0
    rows, width, narrow, local = dims.rows, dims.width, dims.narrow, dims.local
    count = dims.n_heads
    n_in, n_mod = len(pieces), len(mods)

    def body(sc, *refs):
        pieces, mods = refs[:n_in], refs[n_in : n_in + n_mod]
        w_own, w_other, cosine, sine = refs[n_in + n_mod : n_in + n_mod + 4]
        outs = refs[n_in + n_mod + 4 :]
        x_out, narrow_out, xa_out, q_out, kv_out = outs[:5]
        if first:
            mod = outs[5]
        else:
            mod = mods[0]
        buffer, weight, sem = outs[-3:]
        fetch = Fetch(sc, layer, w_own, w_other, weight, sem)
        seg = segments(sc, (rows, 1), 0, sc[1] * rows)
        if first:
            for k in range(count):
                at = pl.multiple_of(jnp.bitwise_xor(sc[0], k) * narrow, narrow)
                block = mods[k][...]
                for l in range(2):
                    mod[l * 6 : l * 6 + 6, :, pl.ds(at, narrow)] = jnp.where(
                        sc[2] == l, block[:6], block[6:]
                    )
            place(buffer, pieces, sc[0], narrow)
            x = buffer[...]
            x_out[...] = x.astype(BF)
            narrow_out[...] = pieces[0][...]
        else:
            place(buffer, pieces[1:], sc[0], narrow)
            x = pieces[0][...] + spread(mod, 0, 5, seg) * buffer[...]
            low = x.astype(BF)
            x_out[...] = low
            x = low.astype(F32)
            buffer[...] = x
            at = pl.multiple_of(sc[0] * narrow, narrow)
            narrow_out[...] = buffer[:, pl.ds(at, narrow)].astype(BF)
        normed, _ = norm_of(x)
        xa = (normed * (1.0 + spread(mod, layer, 1, seg)) + spread(mod, layer, 0, seg)).astype(BF)
        xa_out[...] = xa
        cos = widen_table(cosine[...], local)
        sin = widen_table(sine[...], local)
        fetch.wait()
        q_out[...] = turn(dot(xa, weight[0]), cos, sin).astype(BF)
        kv_out[:, :local] = turn(dot(xa, weight[1]), cos, sin).astype(BF)
        kv_out[:, local:] = dot(xa, weight[2]).astype(BF)

    return call(
        body,
        [sc] + pieces + mods + [weights[0], weights[1], cosine, sine],
        [SM] + [VM] * (n_in + n_mod) + [HB, HB, VM, VM],
        [
            sds((rows, width), BF),
            sds((rows, narrow), BF),
            sds((rows, width), BF),
            sds((rows, local), BF),
            sds((rows, 2 * local), BF),
        ]
        + ([sds((12, 4, width), F32)] if first else []),
        [
            pltpu.VMEM((rows, width), F32),
            pltpu.VMEM(weights[0].shape, BF),
            pltpu.SemaphoreType.DMA,
        ],
        name=f"project_{layer}",
    )


def attend(dims, layer, sc, chunks, queries, xa, weights):
    rows, n_seq, frames = dims.rows, dims.n_seq, dims.frames
    width, narrow, local, count = dims.width, dims.narrow, dims.local, dims.n_heads
    heads = local // HEAD_DIM

    def body(sc, *refs):
        chunks = refs[:n_seq]
        queries, xa, w_own, w_other = refs[n_seq : n_seq + 4]
        kept, probs, for_grads, exact = refs[n_seq + 4 : n_seq + 8]
        outs = refs[n_seq + 8 : n_seq + 8 + count]
        weight, buffer, sem = refs[n_seq + 8 + count :]
        fetch = Fetch(sc, layer, w_own, w_other, weight, sem)
        for k in range(n_seq):
            at = pl.multiple_of(jnp.bitwise_xor(sc[1], k) * rows, rows)
            kept[pl.ds(at, rows), :] = chunks[k][...]
        same = segments(sc, (rows, 1), 0, sc[1] * rows) == segments(sc, (1, frames), 1, 0)
        for head in range(heads):
            cols = slice(head * HEAD_DIM, (head + 1) * HEAD_DIM)
            scores = dot(queries[:, cols], kept[:, cols], ((1,), (1,)))
            scores = jnp.where(same, scores * (1.0 / math.sqrt(HEAD_DIM)), -1e30)
            prob = jnp.exp(scores - jnp.max(scores, axis=1, keepdims=True))
            prob = prob * (1.0 / jnp.sum(prob, axis=1, keepdims=True))
            low = prob.astype(BF)
            probs[head] = low
            value = kept[:, local + head * HEAD_DIM : local + (head + 1) * HEAD_DIM]
            exact[:, cols] = dot(low, value)
        mixed = exact[...].astype(BF)
        for_grads[:, :local] = mixed
        for_grads[:, local:] = xa[...]
        fetch.wait()
        buffer[...] = dot(mixed, weight[...]).astype(BF)
        hand_out(outs, buffer, sc[0], narrow)

    return call(
        body,
        [sc] + chunks + [queries, xa, weights[0], weights[1]],
        [SM] + [VM] * (n_seq + 2) + [HB, HB],
        [
            sds((frames, 2 * local), BF),
            sds((heads, rows, frames), BF),
            sds((rows, local + width), BF),
            sds((rows, local), F32),
        ]
        + [sds((rows, narrow), BF)] * count,
        [
            pltpu.VMEM(weights[0].shape, BF),
            pltpu.VMEM((rows, width), BF),
            pltpu.SemaphoreType.DMA,
        ],
        name=f"attend_{layer}",
    )


def feed_forward(dims, layer, sc, x, branch, mod, up, down):
    rows, width, narrow, count, hidden = (
        dims.rows, dims.width, dims.narrow, dims.n_heads, dims.hidden,
    )

    def body(sc, x, *refs):
        branch = refs[:count]
        mod, up_own, up_other, down_own, down_other = refs[count : count + 5]
        x1_out, for_grads, slope_out = refs[count + 5 : count + 8]
        outs = refs[count + 8 : 2 * count + 8]
        up, down, buffer, low, sem_up, sem_down = refs[2 * count + 8 :]
        fetch_up = Fetch(sc, layer, up_own, up_other, up, sem_up)
        fetch_down = Fetch(sc, layer, down_own, down_other, down, sem_down)
        seg = segments(sc, (rows, 1), 0, sc[1] * rows)
        place(buffer, branch, sc[0], narrow)
        x1 = x[...].astype(F32) + spread(mod, layer, 2, seg) * buffer[...]
        x1_out[...] = x1
        normed, _ = norm_of(x1)
        xf = (normed * (1.0 + spread(mod, layer, 4, seg)) + spread(mod, layer, 3, seg)).astype(BF)
        for_grads[:, hidden:] = xf
        fetch_up.wait()
        a = dot(xf, up[...])
        c0 = math.sqrt(2.0 / math.pi)
        square = a * a
        t = jnp.tanh(c0 * (a + 0.044715 * (a * square)))
        h = (0.5 * a * (1.0 + t)).astype(BF)
        for_grads[:, :hidden] = h
        slope_out[...] = 0.5 * (1.0 + t) + 0.5 * a * (1.0 - t * t) * (
            c0 * (1.0 + 3.0 * 0.044715 * square)
        )
        fetch_down.wait()
        low[...] = dot(h, down[...]).astype(BF)
        hand_out(outs, low, sc[0], narrow)

    return call(
        body,
        [sc, x] + branch + [mod, up[0], up[1], down[0], down[1]],
        [SM, VM] + [VM] * count + [VM, HB, HB, HB, HB],
        [
            sds((rows, width), F32),
            sds((rows, hidden + width), BF),
            sds((rows, hidden), F32),
        ]
        + [sds((rows, narrow), BF)] * count,
        [
            pltpu.VMEM(up[0].shape, BF),
            pltpu.VMEM(down[0].shape, BF),
            pltpu.VMEM((rows, width), F32),
            pltpu.VMEM((rows, width), BF),
            pltpu.SemaphoreType.DMA,
            pltpu.SemaphoreType.DMA,
        ],
        name=f"feed_forward_{layer}",
    )


def feed_backward(dims, layer, sc, pieces, slope, mod, up, down):
    rows, width, narrow, count, hidden = (
        dims.rows, dims.width, dims.narrow, dims.n_heads, dims.hidden,
    )
    last = layer == 1
    n_in = len(pieces)
    n_extra = 0 if last else 2

    def body(sc, *refs):
        pieces = refs[:n_in]
        slope, mod, up_own, up_other, down_own, down_other = refs[n_in : n_in + 6]
        rest = refs[n_in + 6 :]
        g_out, for_grads = rest[:2]
        outs = rest[2 : 2 + count]
        extra = rest[2 + count : 2 + count + n_extra]
        up, down, buffer, low, other_buffer, sem_up, sem_down = rest[2 + count + n_extra :]
        fetch_down = Fetch(sc, layer, down_own, down_other, down, sem_down)
        fetch_up = Fetch(sc, layer, up_own, up_other, up, sem_up)
        seg = segments(sc, (rows, 1), 0, sc[1] * rows)
        place(buffer, pieces[:count], sc[0], narrow)
        if last:
            g = buffer[...]
            g_out[...] = g.astype(BF)
        else:
            x, d_mid = pieces[count:]
            grad_out, sums_out = extra
            dxa = buffer[...]
            normed, inv = norm_of(x[...].astype(F32))
            other_buffer[...] = dxa * normed
            mine = pl.ds(pl.multiple_of(sc[0] * narrow, narrow), narrow)
            sums_out[0] = utterance_sums(buffer[:, mine], seg)
            sums_out[1] = utterance_sums(other_buffer[:, mine], seg)
            dx = d_mid[...] + norm_pull(dxa * (1.0 + spread(mod, 1, 1, seg)), normed, inv)
            other_buffer[...] = dx
            grad_out[...] = other_buffer[:, mine]
            g = dx.astype(BF)
            g_out[...] = g
            g = g.astype(F32)
        dz = (g * spread(mod, layer, 5, seg)).astype(BF)
        for_grads[:, :width] = dz
        fetch_down.wait()
        da = (dot(dz, down[...], ((1,), (1,))) * slope[...]).astype(BF)
        for_grads[:, width:] = da
        fetch_up.wait()
        low[...] = dot(da, up[...], ((1,), (1,))).astype(BF)
        hand_out(outs, low, sc[0], narrow)

    extra = [] if last else [sds((rows, narrow), F32), sds((2, 4, narrow), F32)]
    return call(
        body,
        [sc] + pieces + [slope, mod, up[0], up[1], down[0], down[1]],
        [SM] + [VM] * n_in + [VM, VM, HB, HB, HB, HB],
        [sds((rows, width), BF), sds((rows, width + hidden), BF)]
        + [sds((rows, narrow), BF)] * count
        + extra,
        [
            pltpu.VMEM(up[0].shape, BF),
            pltpu.VMEM(down[0].shape, BF),
            pltpu.VMEM((rows, width), F32),
            pltpu.VMEM((rows, width), BF),
            pltpu.VMEM((rows, width), F32),
            pltpu.SemaphoreType.DMA,
            pltpu.SemaphoreType.DMA,
        ],
        name=f"feed_backward_{layer}",
    )


def middle_backward(
    dims, layer, sc, g, x1, sums, branch, mod, weights, queries, kept, probs, exact, cosine, sine
):
    rows, width, narrow, local, count = (
        dims.rows, dims.width, dims.narrow, dims.local, dims.n_heads,
    )
    n_seq, frames = dims.n_seq, dims.frames
    heads = local // HEAD_DIM
    scale = 1.0 / math.sqrt(HEAD_DIM)

    def body(sc, g, x1, *refs):
        sums = refs[:count]
        branch, mod, w_own, w_other, queries, kept, probs, exact, cosine, sine = refs[
            count : count + 10
        ]
        d_mid_out, dy_out, small, q_out = refs[count + 10 : count + 14]
        outs = refs[count + 14 : count + 14 + n_seq]
        weight, buffer, other, done, sem = refs[count + 14 + n_seq :]
        fetch = Fetch(sc, layer, w_own, w_other, weight, sem)
        seg = segments(sc, (rows, 1), 0, sc[1] * rows)
        mine = pl.ds(pl.multiple_of(sc[0] * narrow, narrow), narrow)
        place(buffer, sums, sc[0], narrow)
        dxf = buffer[...]
        normed, inv = norm_of(x1[...])
        other[...] = dxf * normed
        small[1] = utterance_sums(buffer[:, mine], seg)
        small[2] = utterance_sums(other[:, mine], seg)
        d_mid = g[...].astype(F32) + norm_pull(
            dxf * (1.0 + spread(mod, layer, 4, seg)), normed, inv
        )
        d_mid_out[...] = d_mid
        other[...] = d_mid
        small[0] = utterance_sums(other[:, mine] * branch[...].astype(F32), seg)
        dy = (d_mid * spread(mod, layer, 2, seg)).astype(BF)
        dy_out[...] = dy
        fetch.wait()
        d_att = dot(dy, weight[...], ((1,), (1,))).astype(BF)
        shared = d_att.astype(F32) * exact[...]
        d_keys, d_vals = [], []
        cos = cosine[:, :HEAD_DIM]
        sin = -sine[:, :HEAD_DIM]
        for head in range(heads):
            cols = slice(head * HEAD_DIM, (head + 1) * HEAD_DIM)
            vals = slice(local + head * HEAD_DIM, local + (head + 1) * HEAD_DIM)
            low = probs[head]
            prob = low.astype(F32)
            grad = d_att[:, cols]
            d_prob = dot(grad, kept[:, vals], ((1,), (1,)))
            delta = jnp.sum(shared[:, cols], axis=1, keepdims=True)
            d_score = (prob * (d_prob - delta)).astype(BF)
            dq = dot(d_score, kept[:, cols]) * scale
            q_out[:, cols] = turn(dq, cos, sin).astype(BF)
            d_keys.append((dot(queries[:, cols], d_score, ((0,), (0,))) * scale).astype(BF))
            d_vals.append(dot(grad, low, ((0,), (0,))).astype(BF))
        for first, parts in ((0, d_keys), (local, d_vals)):
            for head in range(0, heads, 2):
                at = first + head * HEAD_DIM
                both = jnp.concatenate(parts[head : head + 2], axis=0)
                done[:, at : at + 2 * HEAD_DIM] = both.T
        for k in range(n_seq):
            at = pl.multiple_of(jnp.bitwise_xor(sc[1], k) * rows, rows)
            outs[k][...] = done[pl.ds(at, rows), :]

    return call(
        body,
        [sc, g, x1]
        + sums
        + [branch, mod, weights[0], weights[1], queries, kept, probs, exact, cosine, sine],
        [SM, VM, VM] + [VM] * count + [VM, VM, HB, HB] + [VM] * 6,
        [
            sds((rows, width), F32),
            sds((rows, width), BF),
            sds((3, 4, narrow), F32),
            sds((rows, local), BF),
        ]
        + [sds((rows, 2 * local), BF)] * n_seq,
        [
            pltpu.VMEM(weights[0].shape, BF),
            pltpu.VMEM((rows, width), F32),
            pltpu.VMEM((rows, width), F32),
            pltpu.VMEM((frames, 2 * local), BF),
            pltpu.SemaphoreType.DMA,
        ],
        name=f"middle_backward_{layer}",
    )


def project_backward(dims, layer, sc, dy, d_query, chunks, weights, cosine, sine):
    rows, width, narrow, local, count = (
        dims.rows, dims.width, dims.narrow, dims.local, dims.n_heads,
    )
    n_in = len(chunks)

    def body(sc, dy, d_query, *refs):
        chunks = refs[:n_in]
        w_own, w_other, cosine, sine, d_out = refs[n_in : n_in + 5]
        outs = refs[n_in + 5 : n_in + 5 + count]
        weight, buffer, sem = refs[n_in + 5 + count :]
        fetch = Fetch(sc, layer, w_own, w_other, weight, sem)
        total = chunks[0][...].astype(F32)
        for chunk in chunks[1:]:
            total = total + chunk[...].astype(F32)
        cos = widen_table(cosine[...], local)
        sin = -widen_table(sine[...], local)
        dk = turn(total[:, :local], cos, sin).astype(BF)
        dv = total[:, local:].astype(BF)
        d_out[:, :width] = dy[...]
        for i, part in enumerate((d_query[...], dk, dv)):
            d_out[:, width + i * local : width + (i + 1) * local] = part
        fetch.wait()
        total = dot(d_query[...], weight[0], ((1,), (1,)))
        total = total + dot(dk, weight[1], ((1,), (1,)))
        total = total + dot(dv, weight[2], ((1,), (1,)))
        buffer[...] = total.astype(BF)
        hand_out(outs, buffer, sc[0], narrow)

    return call(
        body,
        [sc, dy, d_query] + chunks + [weights[0], weights[1], cosine, sine],
        [SM, VM, VM] + [VM] * n_in + [HB, HB, VM, VM],
        [sds((rows, width + 3 * local), BF)] + [sds((rows, narrow), BF)] * count,
        [
            pltpu.VMEM(weights[0].shape, BF),
            pltpu.VMEM((rows, width), BF),
            pltpu.SemaphoreType.DMA,
        ],
        name=f"project_backward_{layer}",
    )


def products(left, right, local, width):
    first = dot(left[:, :local], right[:, :width], ((0,), (0,))).astype(BF)
    rest = dot(left[:, local:], right[:, width:], ((0,), (0,))).astype(BF)
    out = [[(slice(None), first)]]
    for i in range(rest.shape[1] // local):
        columns = slice(i * local, (i + 1) * local)
        lines = [slice(group * local, (group + 1) * local) for group in range(width // local)]
        out.append([(line, rest[line, columns]) for line in lines])
    return out


def half_grads(sc, left, right, local, name):
    width = left.shape[1] - local
    count = (1 + (right.shape[1] - width) // local) // 2

    def body(sc, left, right, mine, theirs):
        grads = products(left[...], right[...], local, width)
        for section in range(2):

            @pl.when(sc[2] == section)
            def _(section=section):
                for out, first in ((mine, section * count), (theirs, (1 - section) * count)):
                    for i in range(count):
                        for columns, value in grads[first + i]:
                            out[i * local : (i + 1) * local, columns] = value

    return call(
        body,
        [sc, left, right],
        [SM, VM, VM],
        [sds((count * local, width), BF)] * 2,
        name=name,
    )


def whole_grads(sc, left, right, local, name):
    count = len(left)
    rows, wide = left[0].shape
    width = wide - local
    tensors = 1 + (right[0].shape[1] - width) // local

    def body(sc, *refs):
        left, right = refs[:count], refs[count : 2 * count]
        out, all_left, all_right = refs[2 * count :]
        last = count.bit_length() - 2
        for k in range(count):
            mirrored = sum(1 << (last - i) for i in range(last + 1) if k >> i & 1)
            owner = jnp.bitwise_xor(sc[1], jnp.where(sc[2] == 0, k, mirrored))
            at = pl.ds(pl.multiple_of(owner * rows, rows), rows)
            all_left[at, :] = left[k][...]
            all_right[at, :] = right[k][...]
        grads = products(all_left[...], all_right[...], local, width)
        for i, grad in enumerate(grads):
            for columns, value in grad:
                out[i * local : (i + 1) * local, columns] = value

    return call(
        body,
        [sc] + list(left) + list(right),
        [SM] + [VM] * (2 * count),
        [sds((tensors * local, width), BF)],
        [
            pltpu.VMEM((count * rows, wide), BF),
            pltpu.VMEM((count * rows, right[0].shape[1]), BF),
        ],
        limit=24,
        name=name,
    )[0]


def add_split(sc, left, right, step):
    rows, width = left.shape
    half = rows // 2

    def body(sc, left, right, keep, send):
        bit = sc[5 + step]
        mine = pl.ds(pl.multiple_of(bit * half, half), half)
        other = pl.ds(pl.multiple_of((1 - bit) * half, half), half)
        keep[...] = (left[mine, :].astype(F32) + right[mine, :].astype(F32)).astype(BF)
        send[...] = (left[other, :].astype(F32) + right[other, :].astype(F32)).astype(BF)

    return call(
        body, [sc, left, right], [SM, VM, VM], [sds((half, width), BF)] * 2, name="add_split"
    )


def join(sc, mine, other, step):
    half, width = mine.shape

    def body(sc, mine, other, out):
        bit = sc[5 + step]
        out[pl.ds(pl.multiple_of(bit * half, half), half), :] = mine[...]
        out[pl.ds(pl.multiple_of((1 - bit) * half, half), half), :] = other[...]

    return call(
        body, [sc, mine, other], [SM, VM, VM], [sds((2 * half, width), BF)], name="join"
    )[0]


class HalfSum:
    def __init__(self, sc, layer, left, right, local, name):
        self.sc, self.layer = sc, layer
        self.mine, self.ready = half_grads(sc, left, right, local, name)
        self.bits = lax.axis_size("seq").bit_length() - 1
        self.at = 0
        self.taken = True
        self.pieces = []

    def send(self, *begin):
        value, bits = after(self.ready, *begin), self.bits
        if self.at == 0:
            self.came = swap(value)
        elif self.at <= bits:
            self.came = crossed(value, self.at - 1)
        else:
            if self.at == 2 * bits and not self.pieces:
                self.hand_over(value)
            self.came = crossed(value, 2 * bits - self.at)
        self.at += 1
        self.taken = False
        return self.came

    def hand_over(self, value):
        self.pieces.append((value, to_owner(value, self.layer)))

    def take(self):
        sc, bits = self.sc, self.bits
        self.taken = True
        if self.at <= bits:
            self.mine, self.ready = add_split(sc, self.mine, self.came, self.at - 1)
        elif self.at == bits + 1:
            self.mine = self.ready = add_chunks([self.mine, self.came])
        else:
            self.mine = self.ready = join(sc, self.mine, self.came, 2 * bits + 1 - self.at)
        return self.ready

    def last(self, *begin):
        while self.at <= 2 * self.bits:
            if not self.taken:
                self.take()
            self.send()
        self.hand_over(after(self.came, *begin))
        (own_0, other_0), (own_1, other_1) = self.pieces
        return [own_0, own_1, other_0, other_1]


class Spread:
    def __init__(self, value):
        self.parts = [value]
        self.bits = lax.axis_size("seq").bit_length() - 1
        self.early = None

    def one(self, *begin):
        self.parts.append(crossed(after(self.parts[0], *begin), 0))
        return self.parts[1]

    def two(self, *begin):
        self.early = crossed(after(self.parts[0], *begin), 1)
        return self.early

    def rest(self, *begin):
        for bit in range(1, self.bits):
            more = [] if bit > 1 else [self.early]
            start = 0 if bit > 1 else 1
            for part in self.parts[start:]:
                more.append(crossed(after(part, *begin), bit))
            self.parts = self.parts + more
        return self.parts[3:]


class Assembly:
    SCRATCH = 5

    @staticmethod
    def scratch(added, local, outs):
        width = added[0].shape[1]
        return [
            pltpu.VMEM((local, width), F32),
            pltpu.VMEM((outs - 1, width, local), F32),
            pltpu.VMEM((2, outs * local, width), BF),
            pltpu.SemaphoreType.DMA((outs, 2)),
            pltpu.SemaphoreType.DMA((outs,)),
        ]

    def __init__(self, sc, added, pieces, outs, scratch):
        self.sc, self.added, self.pieces = sc, added, pieces
        self.first_out, self.rest_out = outs
        self.first, self.rest, self.held, self.sems, self.out_sems = scratch
        self.outs = 1 + self.rest.shape[0]
        self.local, self.width = self.first.shape
        self.size = pieces[0].shape[0]

    def fetches_added(self):
        copies = []
        for i in range(self.outs):
            at = pl.ds(i * self.local, self.local)
            for j in range(2):
                copies.append(
                    pltpu.make_async_copy(
                        self.added[j].at[at, :], self.held.at[j, at, :], self.sems.at[i, j]
                    )
                )
        return copies

    def fetches_pieces(self):
        return [
            pltpu.make_async_copy(
                self.pieces[p],
                self.held.at[0, pl.ds(p * self.size, self.size), :],
                self.sems.at[p // 2, p % 2],
            )
            for p in range(4)
        ]

    def start(self):
        @pl.when(self.sc[2] == 0)
        def _():
            for copy in self.fetches_added():
                copy.start()

        @pl.when(self.sc[2] == 1)
        def _():
            for copy in self.fetches_pieces():
                copy.start()

    def store(self, index):
        if index == 0:
            return pltpu.make_async_copy(self.first, self.first_out, self.out_sems.at[0])
        return pltpu.make_async_copy(
            self.rest.at[index - 1], self.rest_out.at[index - 1], self.out_sems.at[index]
        )

    def put(self, index, value, line):
        lines = value.shape[0]
        if index == 0:
            self.first[line : line + lines, :] = value
            return
        for group in range(self.width // self.local):
            columns = slice(group * self.local, (group + 1) * self.local)
            at = group * self.local + line
            self.rest[index - 1, at : at + lines, :] = value[:, columns]

    def run(self):
        sc, local, size, held = self.sc, self.local, self.size, self.held
        count = self.outs // 2

        @pl.when(sc[2] == 0)
        def _():
            copies = self.fetches_added()
            for i in range(self.outs):
                copies[2 * i].wait()
                copies[2 * i + 1].wait()
                at = slice(i * local, (i + 1) * local)
                self.put(i, held[0, at, :].astype(F32) + held[1, at, :].astype(F32), 0)
                self.store(i).start()

        bits = lax.axis_size("seq").bit_length() - 1
        low, high = sc[1] & 1, (sc[1] >> (bits - 1)) & 1

        @pl.when(sc[2] == 1)
        def _():
            for copy in self.fetches_pieces():
                copy.wait()
            for section, at, bit in ((1, 0, high), (0, 2, low)):
                for turn in range(2):

                    @pl.when(bit == turn)
                    def _(section=section, at=at, turn=turn):
                        for place in range(2):
                            base = (at + (place ^ turn)) * size
                            for i in range(count):
                                begin = max(i * local, place * size)
                                end = min((i + 1) * local, (place + 1) * size)
                                if begin < end:
                                    row = base + begin - place * size
                                    value = held[0, row : row + end - begin, :].astype(F32)
                                    self.put(section * count + i, value, begin - i * local)

            for i in range(self.outs):
                self.store(i).start()

    def wait(self):
        for i in range(self.outs):
            self.store(i).wait()


def by_section(sc, mine, theirs, layer_0, layer_1):
    mine[...] = jnp.where(sc[2] == 0, layer_0, layer_1)
    theirs[...] = jnp.where(sc[2] == 0, layer_1, layer_0)


def gate_sums(dims, layer, sc, g, x1, z, mod, passed):
    rows, narrow = dims.rows, dims.narrow

    def body(sc, g, x1, z, mod, passed, small, *shown):
        seg = segments(sc, (rows, 1), 0, sc[1] * rows)
        mine = pl.ds(pl.multiple_of(sc[0] * narrow, narrow), narrow)
        value = z[...].astype(F32)
        small[...] = utterance_sums(g[:, mine].astype(F32) * value, seg)
        if shown:
            gate = spread(mod, layer, 5, seg, mine)
            result = (x1[:, mine] + gate * value).astype(BF)
            by_section(sc, *shown, passed[...], result)

    outs = [sds((4, narrow), F32)]
    if layer == 1:
        outs += [sds((rows, narrow), BF)] * 2
    return call(
        body, [sc, g, x1, z, mod, passed], [SM] + [VM] * 5, outs, name=f"gate_sums_{layer}"
    )


def last_norm(dims, sc, terms, x, mod, small_0, small_1):
    rows, narrow, count = dims.rows, dims.narrow, dims.n_heads

    def body(sc, *refs):
        terms = refs[:count]
        x, mod, mid_0, gate_0, in_1, mid_1, gate_1 = refs[count : count + 7]
        total_out, normed_out, inv_out, mine_out, theirs_out, rows_out, buffer = refs[count + 7 :]
        seg = segments(sc, (rows, 1), 0, sc[1] * rows)
        mine = pl.ds(pl.multiple_of(sc[0] * narrow, narrow), narrow)
        total = terms[0][...].astype(F32)
        for term in terms[1:]:
            total = total + term[...].astype(F32)
        normed, inv = norm_of(x[...].astype(F32))
        buffer[...] = normed
        normed = buffer[:, mine]
        first = (
            [utterance_sums(total, seg), utterance_sums(total * normed, seg)]
            + [mid_0[i] for i in range(3)]
            + [gate_0[...]]
        )
        second = [in_1[0], in_1[1]] + [mid_1[i] for i in range(3)] + [gate_1[...]]
        for i in range(6):
            by_section(sc, mine_out.at[i], theirs_out.at[i], first[i], second[i])
        grad = total * (1.0 + spread(mod, 0, 1, seg, mine))
        total_out[...] = grad
        normed_out[...] = normed
        inv_out[...] = inv
        lane = lax.broadcasted_iota(jnp.int32, (rows, 128), 1)
        sums = jnp.where(lane == 0, jnp.sum(grad, axis=1, keepdims=True), 0.0)
        sums = jnp.where(lane == 1, jnp.sum(grad * normed, axis=1, keepdims=True), sums)
        pick = diagonal(8, 128)
        rows_out[...] = sum(dot(pick, part, ((1,), (1,))) for part in split3(sums))

    return call(
        body,
        [sc] + terms + [x, mod] + small_0 + small_1,
        [SM] + [VM] * (count + 7),
        [
            sds((rows, narrow), F32),
            sds((rows, narrow), F32),
            sds((rows, 1), F32),
            sds((6, 4, narrow), F32),
            sds((6, 4, narrow), F32),
            sds((8, rows), F32),
        ],
        [pltpu.VMEM((rows, dims.width), F32)],
        name="last_norm",
    )


def last_pull(dims, sc, d_mid, grad, normed, inv, sums, middle_grad):
    rows, narrow, count, width = dims.rows, dims.narrow, dims.n_heads, dims.width

    def body(sc, d_mid, grad, normed, inv, middle, *refs):
        sums, outs = refs[:count], refs[count:]
        total = sums[0][:8, :rows]
        for term in sums[1:]:
            total = total + term[:8, :rows]
        row = lax.broadcasted_iota(jnp.int32, (8, 128), 0)
        lane = lax.broadcasted_iota(jnp.int32, (8, 128), 1)
        pick = (row == 4 * lane + 3).astype(BF)
        total = sum(dot(part, pick, ((0,), (0,))) for part in split3(total * (1.0 / width)))
        mine = pl.ds(pl.multiple_of(sc[0] * narrow, narrow), narrow)
        first = d_mid[:, mine] + inv[...] * (
            grad[...] - total[:, 0:1] - normed[...] * total[:, 1:2]
        )
        by_section(sc, *outs, first, middle[...])

    return call(
        body,
        [sc, d_mid, grad, normed, inv, middle_grad] + sums,
        [SM] + [VM] * (5 + count),
        [sds((rows, narrow), F32)] * 2,
        name="last_pull",
    )


def modulation_part(sc, mod_weight, row_sums, own, n_seq):
    kinds, width, narrow = mod_weight.shape

    def body(sc, mod_weight, row_sums, *refs):
        own = refs[:n_seq]
        grads_out, part, box = refs[n_seq:]
        for k in range(n_seq):
            box[jnp.bitwise_xor(sc[1], k)] = own[k][...]
        total = box[0]
        for j in range(1, n_seq):
            total = total + box[j]
        result = jnp.zeros((8, width), F32)
        for which in range(kinds):
            mine, theirs = total[which], total[kinds + which]
            grad = jnp.concatenate(
                [jnp.where(sc[2] == 0, mine, theirs), jnp.where(sc[2] == 0, theirs, mine)],
                axis=0,
            )
            grads_out[which] = grad
            result = result + exact_dot(grad, mod_weight[which], ((1,), (1,)))
        part[...] = result
        for row in range(2):
            part[4 * row + 3 : 4 * row + 4, : row_sums.shape[1]] = row_sums[row : row + 1, :]

    return call(
        body,
        [sc, mod_weight, row_sums] + own,
        [SM, VM, VM] + [VM] * n_seq,
        [sds((kinds, 8, narrow), F32), sds((8, width), F32)],
        [pltpu.VMEM((n_seq, 2 * kinds, 4, narrow), F32)],
        name="modulation_part",
    )


def modulation_weight(sc, act, grads):
    kinds, rows, narrow = grads.shape
    width = act.shape[1]

    def body(sc, act, grads, out, held, sems):
        tall = outer_parts(act[...], act[...])[0].astype(F32).T.astype(BF)

        def store(which):
            return pltpu.make_async_copy(held.at[which], out.at[which], sems.at[which])

        for which in range(kinds):
            wide = outer_parts(grads[which], grads[which])[1]
            held[which] = dot(tall, wide)
            store(which).start()
        for which in range(kinds):
            store(which).wait()

    return pl_call(
        body,
        [sc, act, grads],
        [SM, VM, VM],
        [sds((kinds, width, narrow), F32)],
        [HB],
        [pltpu.VMEM((kinds, width, narrow), F32), pltpu.SemaphoreType.DMA((kinds,))],
        limit=16,
        name="modulation_weight",
    )[0]


def time_backward(sc, sinus, inner, outer, time_out, own):
    count = len(own)
    rows, width = inner.shape
    freq = sinus.shape[1]
    block = width // 4

    def body(sc, sinus, inner, outer, time_out, *refs):
        own = refs[:count]
        g_in, g_out, box, held_in, held_out, sems = refs[count:]
        for k in range(count):
            at = jnp.bitwise_xor(sc[0], k)
            box[at, sc[2]] = own[k][:rows]
            box[at, 1 - sc[2]] = own[k][rows:]
        total = jnp.zeros((rows, width), F32)
        for j in range(count):
            for c in range(2):
                total = total + box[j, c]
        row = lax.broadcasted_iota(jnp.int32, (rows, width), 0)
        total = jnp.where(row % 4 == 3, 0.0, total)

        def slope(value):
            gate = 1.0 / (1.0 + jnp.exp(-value))
            return gate * (1.0 + value * (1.0 - gate))

        pre = inner[...]
        hidden = pre / (1.0 + jnp.exp(-pre))
        d_outer = total * slope(outer[...])
        tall, wide = outer_parts(hidden, d_outer)
        tall = tall.astype(F32).T.astype(BF)
        copies = []
        for i in range(4):
            at = slice(i * block, (i + 1) * block)
            held_out[at, :] = dot(tall[at], wide)
            copies.append(
                pltpu.make_async_copy(held_out.at[at, :], g_out.at[at, :], sems.at[i])
            )
            copies[-1].start()
        d_inner = exact_dot(d_outer, time_out[...], ((1,), (1,))) * slope(pre)
        held_in[...] = exact_outer(sinus[...], d_inner)
        copies.append(pltpu.make_async_copy(held_in, g_in, sems.at[4]))
        copies[-1].start()
        for copy in copies:
            copy.wait()

    return pl_call(
        body,
        [sc, sinus, inner, outer, time_out] + list(own),
        [SM] + [VM] * (4 + count),
        [sds((freq, width), F32), sds((width, width), F32)],
        [HB, HB],
        [
            pltpu.VMEM((count, 2, rows, width), F32),
            pltpu.VMEM((freq, width), F32),
            pltpu.VMEM((width, width), F32),
            pltpu.SemaphoreType.DMA((5,)),
        ],
        limit=16,
        name="time_backward",
    )


def finish(dims, sc, feed, attention, acts, grads):
    n = Assembly.SCRATCH

    def body(sc, act_own, act_other, grad_own, grad_other, *refs):
        sources, outs, scratch = refs[:12], refs[12:18], refs[18:]
        feed = Assembly(sc, sources[:2], sources[2:6], outs[:2], scratch[:n])
        attention = Assembly(sc, sources[6:8], sources[8:], outs[2:4], scratch[n:])
        feed.start()
        attention.start()
        outs[4][sc[2]] = act_own[...]
        outs[4][1 - sc[2]] = act_other[...]
        outs[5][sc[2]] = grad_own[...]
        outs[5][1 - sc[2]] = grad_other[...]
        feed.run()
        attention.run()
        feed.wait()
        attention.wait()

    width = dims.width
    sources = list(feed[0]) + list(feed[1]) + list(attention[0]) + list(attention[1])
    return pl_call(
        body,
        [sc] + list(acts) + list(grads) + sources,
        [SM] + [VM] * 4 + [HB] * 12,
        [
            sds((dims.hidden, width), F32),
            sds((1, width, dims.hidden), F32),
            sds((dims.local, width), F32),
            sds((3, width, dims.local), F32),
            sds((2,) + acts[0].shape, BF),
            sds((2,) + grads[0].shape, F32),
        ],
        [HB] * 4 + [VM] * 2,
        Assembly.scratch(feed[0], dims.hidden, 2) + Assembly.scratch(attention[0], dims.local, 4),
        limit=24,
        name="finish",
    )


class Dims:
    pass


def local_program(
    frames,
    cotangent,
    utt_lengths,
    time_ids,
    w_time_in,
    w_time_out,
    w_mod,
    w_qkv,
    w_out,
    w_up,
    w_down,
):
    dims = Dims()
    dims.n_heads = lax.axis_size("heads")
    dims.n_seq = n_seq = lax.axis_size("seq")
    _, dims.rows, dims.narrow = frames.shape
    dims.width = dims.narrow * dims.n_heads
    dims.local = w_qkv.shape[3]
    dims.hidden = w_up.shape[2]
    dims.frames = dims.rows * n_seq
    section = lax.axis_index("section")

    def here(both):
        return lax.dynamic_index_in_dim(both, section, 0, keepdims=False)

    sc = utt_lengths
    qkv = jnp.transpose(w_qkv[0], (1, 0, 2))
    mod_weight = jnp.transpose(w_mod[0], (1, 0, 2))
    wide_frames = gather(here(frames), "heads")
    qkv_w = (qkv, swap(qkv))
    sinus, inner, outer, act, mod_mine, mod_theirs = start(
        sc, time_ids, w_time_in, w_time_out, mod_weight
    )
    mod_theirs = swap(after(mod_theirs, *wide_frames))
    mods = gather(jnp.concatenate([mod_mine, mod_theirs], axis=0), "heads")
    cosine, sine = tables(sc, dims.rows)
    mods = after(mods, cosine, sine)

    x_0, _, xa, q_0, kv, mod = project(dims, 0, sc, wide_frames, mods, qkv_w, cosine, sine)
    chunks = gather(kv, "seq")
    out_w = (w_out[0], swap(after(w_out[0], mods[0])))
    kept_0, probs_0, for_attention, exact_0, *terms = attend(
        dims, 0, sc, chunks, q_0, xa, out_w
    )
    fwd_a = Spread(for_attention)

    up_w, down_w = [(w[0], swap(after(w[0], terms[0]))) for w in (w_up, w_down)]
    total = after(add_chunks(exchange(terms, "heads")), up_w[1], down_w[1])

    branch_0 = gather(total, "heads")
    fwd_a.one(total)
    fwd_a.two(total)
    x1_0, for_feed, slope_0, *terms = feed_forward(
        dims, 0, sc, x_0, branch_0, mod, up_w, down_w
    )
    fwd_f = Spread(for_feed)

    total = after(add_chunks(exchange(terms, "heads")), fwd_a.parts[1], fwd_a.early)

    z_0 = gather(total, "heads")
    fwd_a.rest(total)
    fwd_f.one(total)

    x_2, passed, xa, q_1, kv = project(
        dims, 1, sc, [x1_0] + z_0, [mod], qkv_w, cosine, sine
    )
    kv = after(kv, fwd_f.parts[1], *fwd_a.parts[3:])
    chunks = gather(kv, "seq")
    wide_cotangent = gather(after(here(cotangent), chunks[1]), "heads")
    kept_1, probs_1, for_attention_1, exact_1, *terms = attend(
        dims, 1, sc, chunks, q_1, xa, out_w
    )

    terms[0] = after(terms[0], *wide_cotangent)
    total = add_chunks(exchange(terms, "heads"))
    fwd_f.two(terms[0])

    branch_1 = gather(total, "heads")
    x1_1, for_feed, slope_1, *z_terms = feed_forward(
        dims, 1, sc, x_2, branch_1, mod, up_w, down_w
    )
    g_1, late, *terms = feed_backward(
        dims, 1, sc, wide_cotangent, slope_1, mod, up_w, down_w
    )
    terms = after(terms, fwd_f.early)
    feed_1 = HalfSum(sc, 1, for_feed, late, dims.hidden, "feed_grads_1")
    feed_1.send()
    got = exchange(terms, "heads")
    total = after(add_chunks(got), feed_1.came, *fwd_f.rest(terms[0]))

    feed_1.take()
    feed_1.send(total)
    sums = after(gather(total, "heads"), feed_1.came)

    feed_1.take()
    feed_1.send(sums[0])
    d_mid_1, dy, small_f1, dq, *sent = middle_backward(
        dims, 1, sc, g_1, x1_1, after(sums, feed_1.ready), branch_1[0], mod, out_w,
        q_1, kept_1, probs_1, exact_1, cosine, sine,
    )
    sent = after(sent, feed_1.came)

    got = exchange(sent, "seq")
    feed_1.take()
    z_1 = add_chunks(exchange(after(z_terms, sent[0]), "heads"))
    gate_1, *acts = gate_sums(dims, 1, sc, g_1, x1_1, z_1, mod, passed)
    got = after(got, feed_1.ready, *acts)
    late, *terms = project_backward(dims, 1, sc, dy, dq, got, qkv_w, cosine, sine)

    got = exchange(terms, "heads")
    feed_1.send(terms[0])
    attention_1 = HalfSum(sc, 1, for_attention_1, late, dims.local, "attend_grads_1")
    acts = [acts[0], swap(after(acts[1], terms[0]))]
    total = after(
        add_chunks(got), feed_1.came, attention_1.mine, attention_1.ready, acts
    )

    feed_1.take()
    feed_1.send(total)
    attention_1.send(total)
    pieces = gather(total, "heads")

    g_0, late, *rest = feed_backward(
        dims, 0, sc, pieces + [x_2, d_mid_1], slope_0, mod, up_w, down_w
    )
    terms, (middle_grad, small_a1) = rest[: dims.n_heads], rest[dims.n_heads :]
    terms = after(terms, feed_1.came, attention_1.came)
    late_f = Spread(late)
    got = exchange(terms, "heads")
    attention_1.take()
    attention_1.send(terms[0])
    late_f.one(terms[0])
    total = after(add_chunks(got), attention_1.came)

    attention_1.take()
    attention_1.send(total)
    late_f.two(total)
    sums = after(gather(total, "heads"), attention_1.came, late_f.parts[1])

    attention_1.take()
    attention_1.send(sums[0])
    d_mid_0, dy, small_f0, dq, *sent = middle_backward(
        dims, 0, sc, g_0, x1_0, after(sums, attention_1.ready), branch_0[0], mod, out_w,
        q_0, kept_0, probs_0, exact_0, cosine, sine,
    )
    sent = after(sent, attention_1.came, late_f.early)

    got = exchange(sent, "seq")
    attention_1.take()
    if attention_1.at == 2 * attention_1.bits:
        attention_1.hand_over(after(attention_1.ready, got[0]))
    feed_1 = feed_1.last(sent[0])
    gate_0, *_ = gate_sums(dims, 0, sc, g_0, x1_0, z_0[0], mod, passed)
    got = after(got, attention_1.ready, gate_0, feed_1)
    late, *terms = project_backward(dims, 0, sc, dy, dq, got, qkv_w, cosine, sine)
    late_a = Spread(late)

    got = exchange(terms, "heads")
    late_a.one(terms[0])
    late_f.rest(terms[0])

    grad, normed, inv, mine, theirs, row_sums = last_norm(
        dims, sc, got, x_0, mod, [small_f0, gate_0], [small_a1, small_f1, gate_1]
    )
    late_a.two(row_sums)
    theirs = after(swap(theirs), late_a.parts[1], *late_f.parts[3:])
    both = jnp.concatenate([mine, theirs], axis=0)
    both = gather(both, "seq")
    feed_0 = whole_grads(
        sc, after(fwd_f.parts, theirs), late_f.parts, dims.hidden, "feed_grads_0"
    )
    both = after(both, feed_0, late_a.early)
    mod_grads, part = modulation_part(sc, mod_weight, row_sums, both, n_seq)

    late_a.rest(part)
    attention_1.send(part)
    feed_0 = [feed_0, to_owner(after(feed_0, both[0]), 0)]
    ends = jnp.concatenate([part, swap(part)], axis=0)
    ends = gather(after(ends, feed_0), "heads")
    g_mod = modulation_weight(sc, act, mod_grads)
    ends = after(ends, *late_a.parts[3:], g_mod)

    attention_0 = whole_grads(
        sc, after(fwd_a.parts, *ends), late_a.parts, dims.local, "attend_grads_0"
    )
    attention_0 = after(attention_0, attention_1.came)
    attention_0 = [attention_0, to_owner(attention_0, 0)]
    attention_1 = attention_1.last(attention_0[0])
    grads = last_pull(
        dims, sc, d_mid_0, grad, normed, inv, after(ends, attention_0[0]), middle_grad
    )
    grads = [grads[0], swap(grads[1])]
    g_first, g_second = time_backward(
        sc, sinus, inner, outer, w_time_out, after(ends, attention_0[0])
    )
    g_reduce, g_expand, g_out, g_qkv, acts, grads = finish(
        dims, sc, (feed_0, feed_1), (after(attention_0, g_second), attention_1), acts, grads
    )

    return (
        acts[None],
        grads[None],
        g_first,
        g_second,
        jnp.transpose(g_mod, (1, 0, 2))[None],
        jnp.transpose(g_qkv, (1, 0, 2))[None],
        g_out[None],
        g_expand,
        g_reduce[None],
    )


def solution(mesh):
    placed = (
        P(None, "seq", "heads"),
        P(None, "seq", "heads"),
        P(),
        P(),
        P(),
        P(),
        P("section", None, None, "heads"),
        P("section", None, None, "heads"),
        P("section", "heads", None),
        P("section", None, "heads"),
        P("section", "heads", None),
    )
    return jax.shard_map(
        local_program,
        mesh=mesh,
        in_specs=placed,
        out_specs=(
            P("section", None, "seq", "heads"),
            P("section", None, "seq", "heads"),
            P(),
            P(),
            P("section", None, None, "heads"),
            P("section", None, None, "heads"),
            P("section", "heads", None),
            P("section", None, "heads"),
            P("section", "heads", None),
        ),
        check_vma=False,
    )
```

```python
import functools
import math

import jax
import jax.numpy as jnp
import numpy as np
from jax import lax
from jax.experimental import pallas as pl
from jax.experimental.pallas import tpu as pltpu
from jax.sharding import PartitionSpec as P

HEAD_DIM = 64
FREQ = 256
EPS = 1e-06
BF = jnp.bfloat16
F32 = jnp.float32
MIB = 1024 * 1024


def partner(value, axis, by):
    if by == 0:
        return value
    return lax.ppermute(value, axis, [(i, i ^ by) for i in range(lax.axis_size(axis))])


def order_of(count):
    return (3, 1, 2) if count == 4 else tuple(range(count - 1, 0, -1))


def gather(value, axis):
    count = lax.axis_size(axis)
    out = [value] * count
    for k in order_of(count):
        out[k] = partner(value, axis, k)
    return out


def exchange(chunks, axis):
    out = list(chunks)
    for k in order_of(len(chunks)):
        out[k] = partner(chunks[k], axis, k)
    return out


def swap(value):
    return lax.ppermute(value, "section", [(0, 1), (1, 0)])


def to_owner(value, layer):
    return lax.ppermute(value, "section", [(1 - layer, layer)])


def crossed(value, step):
    length = lax.axis_size("seq")
    last = length.bit_length() - 2
    pairs = []
    for c in range(2):
        by = 1 << (step if c == 0 else last - step)
        pairs += [(c * length + i, c * length + (i ^ by)) for i in range(length)]
    return lax.ppermute(value, ("section", "seq"), pairs)


def after(value, *done):
    value = lax.optimization_barrier((value, done))[0]
    return list(value) if isinstance(value, (list, tuple)) else value


def add_chunks(chunks):
    total = chunks[0].astype(F32)
    for chunk in chunks[1:]:
        total = total + chunk.astype(F32)
    return total.astype(BF)


def dot(left, right, contract=((1,), (0,))):
    return lax.dot_general(left, right, (contract, ((), ())), preferred_element_type=F32)


def split3(value):
    high = value.astype(BF)
    rest = value - high.astype(F32)
    middle = rest.astype(BF)
    low = (rest - middle.astype(F32)).astype(BF)
    return high, middle, low


def diagonal(rows, columns):
    row = lax.broadcasted_iota(jnp.int32, (rows, columns), 0)
    return (row == lax.broadcasted_iota(jnp.int32, (rows, columns), 1)).astype(BF)


def exact_dot(left, right, contract=((1,), (0,))):
    rows = left.shape[0]
    stacked = jnp.concatenate(split3(left), axis=0)
    out = dot(stacked, right, contract)
    return out[:rows] + (out[rows : 2 * rows] + out[2 * rows :])


def exact_outer(left, right):
    tall, wide = outer_parts(left, right)
    return dot(tall, wide, ((0,), (0,)))


def outer_parts(left, right):
    a, b = split3(left), split3(right)
    tall = jnp.concatenate([a[0], a[0], a[1]], axis=0)
    wide = jnp.concatenate([b[0], b[1], b[0]], axis=0)
    return tall, wide


def segments(sc, shape, axis, first):
    index = lax.broadcasted_iota(jnp.int32, shape, axis) + first
    return (index >= sc[3]).astype(jnp.int32) + (index >= sc[4]).astype(jnp.int32)


def spread(mod, layer, which, seg, columns=slice(None)):
    block = mod[layer * 6 + which, :, columns]
    rows = [block[u : u + 1] for u in range(3)]
    return jnp.where(seg == 0, rows[0], jnp.where(seg == 1, rows[1], rows[2]))


def utterance_sums(value, seg):
    rows = [
        jnp.sum(jnp.where(seg == u, value, 0.0), axis=0, keepdims=True) for u in range(3)
    ]
    return jnp.concatenate(rows + [jnp.zeros_like(rows[0])], axis=0)


def norm_of(value):
    mean = jnp.mean(value, axis=1, keepdims=True)
    centred = value - mean
    inv = lax.rsqrt(jnp.mean(centred * centred, axis=1, keepdims=True) + EPS)
    return centred * inv, inv


def norm_pull(grad, normed, inv):
    return inv * (
        grad
        - jnp.mean(grad, axis=1, keepdims=True)
        - normed * jnp.mean(grad * normed, axis=1, keepdims=True)
    )


def lanes_of(index, count, width):
    return pl.ds(pl.multiple_of(lax.rem(index, count) * width, width), width)


def place(buffer, chunks, own, width):
    for k, chunk in enumerate(chunks):
        at = pl.multiple_of(jnp.bitwise_xor(own, k) * width, width)
        buffer[:, pl.ds(at, width)] = chunk[...].astype(buffer.dtype)


def hand_out(outs, buffer, own, width):
    for k, out in enumerate(outs):
        at = pl.multiple_of(jnp.bitwise_xor(own, k) * width, width)
        out[...] = buffer[:, pl.ds(at, width)].astype(out.dtype)


class Fetch:
    def __init__(self, sc, layer, own, other, buffer, sem):
        self.copy = pltpu.make_async_copy(own, buffer, sem)
        other_copy = pltpu.make_async_copy(other, buffer, sem)

        @pl.when(sc[2] == layer)
        def _():
            self.copy.start()

        @pl.when(sc[2] != layer)
        def _():
            other_copy.start()

    def wait(self):
        self.copy.wait()


def turn(value, cosine, sine):
    width = value.shape[1]
    even = lax.broadcasted_iota(jnp.int32, value.shape, 1) % 2 == 0
    swapped = jnp.where(even, pltpu.roll(value, width - 1, 1), pltpu.roll(value, 1, 1))
    return value * cosine + swapped * sine


def widen_table(table, width):
    copies = width // table.shape[1]
    return jnp.concatenate([table] * copies, axis=1) if copies > 1 else table[:, :width]


VM = pl.BlockSpec(memory_space=pltpu.VMEM)
SM = pl.BlockSpec(memory_space=pltpu.SMEM)
HB = pl.BlockSpec(memory_space=pltpu.HBM)


def sds(shape, dtype):
    return jax.ShapeDtypeStruct(tuple(shape), dtype)


class Place:
    def __init__(self, lengths):
        self.lengths = lengths
        self.known = {}
        for index in range(5):
            self[index]

    def __getitem__(self, index):
        if index not in self.known:
            self.known[index] = self.find(index)
        return self.known[index]

    def find(self, index):
        if index < 3:
            return lax.axis_index(("heads", "seq", "section")[index])
        if index == 3:
            return self.lengths[self[2], 0]
        if index == 4:
            return self[3] + self.lengths[self[2], 1]
        low = index - 5
        high = lax.axis_size("seq").bit_length() - 2 - low
        return jnp.where(self[2] == 0, self[1] >> low, self[1] >> high) & 1


def call(body, ins, specs, outs, scratch=(), limit=12, name=None):
    return pl_call(body, ins, specs, outs, [VM] * len(outs), scratch, limit, name)


def pl_call(body, ins, specs, outs, out_specs, scratch, limit, name):
    def placed(lengths, *refs):
        body(Place(lengths), *refs)

    return pl.pallas_call(
        placed,
        out_shape=list(outs),
        in_specs=list(specs),
        out_specs=list(out_specs),
        scratch_shapes=list(scratch),
        compiler_params=pltpu.CompilerParams(vmem_limit_bytes=limit * MIB),
        cost_estimate=pl.CostEstimate(flops=1, bytes_accessed=1, transcendentals=0),
        name=name,
    )(*ins)


def start(sc, time_ids, time_in, time_out, mod_weight):
    width = time_in.shape[1]
    kinds, _, narrow = mod_weight.shape
    half = FREQ // 2

    def body(sc, ids, time_in, time_out, mod_weight, *refs):
        sinus_out, inner_out, outer_out, act_out, mine_out, theirs_out = refs[:6]
        w_in, w_out, w_mod, sems = refs[6:]
        copies = [
            pltpu.make_async_copy(time_in, w_in, sems.at[0]),
            pltpu.make_async_copy(time_out, w_out, sems.at[1]),
            pltpu.make_async_copy(mod_weight, w_mod, sems.at[2]),
        ]
        for copy in copies:
            copy.start()
        row = lax.broadcasted_iota(jnp.int32, (8, half), 0)
        lane = lax.broadcasted_iota(jnp.int32, (8, half), 1).astype(F32)
        stamp = jnp.zeros((8, half), F32)
        for m in range(2):
            for u in range(3):
                stamp = jnp.where(row == m * 4 + u, ids[m, u].astype(F32), stamp)
        angle_t = stamp * jnp.exp(lane * (-math.log(10000.0) / (half - 1)))
        sinus = jnp.concatenate([jnp.sin(angle_t), jnp.cos(angle_t)], axis=1)
        sinus_out[...] = sinus

        copies[0].wait()
        inner = exact_dot(sinus, w_in[...])
        inner_out[...] = inner
        hidden = inner / (1.0 + jnp.exp(-inner))
        copies[1].wait()
        outer = exact_dot(hidden, w_out[...])
        outer_out[...] = outer
        act = outer / (1.0 + jnp.exp(-outer))
        act_out[...] = act
        copies[2].wait()
        for which in range(kinds):
            modul = exact_dot(act, w_mod[which])
            mine_out[which] = jnp.where(sc[2] == 0, modul[:4], modul[4:])
            theirs_out[which] = jnp.where(sc[2] == 0, modul[4:], modul[:4])

    return call(
        body,
        [sc, time_ids, time_in, time_out, mod_weight],
        [SM, SM, HB, HB, HB],
        [sds((8, FREQ), F32)]
        + [sds((8, width), F32)] * 3
        + [sds((kinds, 4, narrow), F32)] * 2,
        [
            pltpu.VMEM(time_in.shape, BF),
            pltpu.VMEM(time_out.shape, BF),
            pltpu.VMEM(mod_weight.shape, BF),
            pltpu.SemaphoreType.DMA((3,)),
        ],
        limit=56,
        name="start",
    )


def tables(sc, rows):
    def body(sc, cosine, sine):
        index = lax.broadcasted_iota(jnp.int32, (rows, 2 * HEAD_DIM), 0) + sc[1] * rows
        begin = jnp.where(index >= sc[4], sc[4], jnp.where(index >= sc[3], sc[3], 0))
        lane = lax.broadcasted_iota(jnp.int32, (rows, 2 * HEAD_DIM), 1)
        pair = lax.broadcasted_iota(jnp.int32, (1, 2 * HEAD_DIM), 1)
        rate = jnp.exp(
            ((pair % HEAD_DIM) // 2).astype(F32) * (-2.0 * math.log(10000.0) / HEAD_DIM)
        )
        angle = (index - begin).astype(F32) * rate
        cosine[...] = jnp.cos(angle)
        sine[...] = jnp.sin(angle) * jnp.where(lane % 2 == 0, -1.0, 1.0)

    return call(body, [sc], [SM], [sds((rows, 2 * HEAD_DIM), F32)] * 2, name="tables")


def project(dims, layer, sc, pieces, mods, weights, cosine, sine):
    first = layer == 0
    rows, width, narrow, local = dims.rows, dims.width, dims.narrow, dims.local
    count = dims.n_heads
    n_in, n_mod = len(pieces), len(mods)

    def body(sc, *refs):
        pieces, mods = refs[:n_in], refs[n_in : n_in + n_mod]
        w_own, w_other, cosine, sine = refs[n_in + n_mod : n_in + n_mod + 4]
        outs = refs[n_in + n_mod + 4 :]
        x_out, narrow_out, xa_out, q_out, kv_out = outs[:5]
        if first:
            mod = outs[5]
        else:
            mod = mods[0]
        buffer, weight, sem = outs[-3:]
        fetch = Fetch(sc, layer, w_own, w_other, weight, sem)
        seg = segments(sc, (rows, 1), 0, sc[1] * rows)
        if first:
            for k in range(count):
                at = pl.multiple_of(jnp.bitwise_xor(sc[0], k) * narrow, narrow)
                block = mods[k][...]
                for l in range(2):
                    mod[l * 6 : l * 6 + 6, :, pl.ds(at, narrow)] = jnp.where(
                        sc[2] == l, block[:6], block[6:]
                    )
            place(buffer, pieces, sc[0], narrow)
            x = buffer[...]
            x_out[...] = x.astype(BF)
            narrow_out[...] = pieces[0][...]
        else:
            place(buffer, pieces[1:], sc[0], narrow)
            x = pieces[0][...] + spread(mod, 0, 5, seg) * buffer[...]
            low = x.astype(BF)
            x_out[...] = low
            x = low.astype(F32)
            buffer[...] = x
            at = pl.multiple_of(sc[0] * narrow, narrow)
            narrow_out[...] = buffer[:, pl.ds(at, narrow)].astype(BF)
        normed, _ = norm_of(x)
        xa = (normed * (1.0 + spread(mod, layer, 1, seg)) + spread(mod, layer, 0, seg)).astype(BF)
        xa_out[...] = xa
        cos = widen_table(cosine[...], local)
        sin = widen_table(sine[...], local)
        fetch.wait()
        q_out[...] = turn(dot(xa, weight[0]), cos, sin).astype(BF)
        kv_out[:, :local] = turn(dot(xa, weight[1]), cos, sin).astype(BF)
        kv_out[:, local:] = dot(xa, weight[2]).astype(BF)

    return call(
        body,
        [sc] + pieces + mods + [weights[0], weights[1], cosine, sine],
        [SM] + [VM] * (n_in + n_mod) + [HB, HB, VM, VM],
        [
            sds((rows, width), BF),
            sds((rows, narrow), BF),
            sds((rows, width), BF),
            sds((rows, local), BF),
            sds((rows, 2 * local), BF),
        ]
        + ([sds((12, 4, width), F32)] if first else []),
        [
            pltpu.VMEM((rows, width), F32),
            pltpu.VMEM(weights[0].shape, BF),
            pltpu.SemaphoreType.DMA,
        ],
        name=f"project_{layer}",
    )


def attend(dims, layer, sc, chunks, queries, xa, weights):
    rows, n_seq, frames = dims.rows, dims.n_seq, dims.frames
    width, narrow, local, count = dims.width, dims.narrow, dims.local, dims.n_heads
    heads = local // HEAD_DIM

    def body(sc, *refs):
        chunks = refs[:n_seq]
        queries, xa, w_own, w_other = refs[n_seq : n_seq + 4]
        kept, probs, for_grads, exact = refs[n_seq + 4 : n_seq + 8]
        outs = refs[n_seq + 8 : n_seq + 8 + count]
        weight, buffer, sem = refs[n_seq + 8 + count :]
        fetch = Fetch(sc, layer, w_own, w_other, weight, sem)
        for k in range(n_seq):
            at = pl.multiple_of(jnp.bitwise_xor(sc[1], k) * rows, rows)
            kept[pl.ds(at, rows), :] = chunks[k][...]
        same = segments(sc, (rows, 1), 0, sc[1] * rows) == segments(sc, (1, frames), 1, 0)
        for head in range(heads):
            cols = slice(head * HEAD_DIM, (head + 1) * HEAD_DIM)
            scores = dot(queries[:, cols], kept[:, cols], ((1,), (1,)))
            scores = jnp.where(same, scores * (1.0 / math.sqrt(HEAD_DIM)), -1e30)
            prob = jnp.exp(scores - jnp.max(scores, axis=1, keepdims=True))
            prob = prob * (1.0 / jnp.sum(prob, axis=1, keepdims=True))
            low = prob.astype(BF)
            probs[head] = low
            value = kept[:, local + head * HEAD_DIM : local + (head + 1) * HEAD_DIM]
            exact[:, cols] = dot(low, value)
        mixed = exact[...].astype(BF)
        for_grads[:, :local] = mixed
        for_grads[:, local:] = xa[...]
        fetch.wait()
        buffer[...] = dot(mixed, weight[...]).astype(BF)
        hand_out(outs, buffer, sc[0], narrow)

    return call(
        body,
        [sc] + chunks + [queries, xa, weights[0], weights[1]],
        [SM] + [VM] * (n_seq + 2) + [HB, HB],
        [
            sds((frames, 2 * local), BF),
            sds((heads, rows, frames), BF),
            sds((rows, local + width), BF),
            sds((rows, local), F32),
        ]
        + [sds((rows, narrow), BF)] * count,
        [
            pltpu.VMEM(weights[0].shape, BF),
            pltpu.VMEM((rows, width), BF),
            pltpu.SemaphoreType.DMA,
        ],
        name=f"attend_{layer}",
    )


def feed_forward(dims, layer, sc, x, branch, mod, up, down):
    rows, width, narrow, count, hidden = (
        dims.rows, dims.width, dims.narrow, dims.n_heads, dims.hidden,
    )

    def body(sc, x, *refs):
        branch = refs[:count]
        mod, up_own, up_other, down_own, down_other = refs[count : count + 5]
        x1_out, for_grads, slope_out = refs[count + 5 : count + 8]
        outs = refs[count + 8 : 2 * count + 8]
        up, down, buffer, low, sem_up, sem_down = refs[2 * count + 8 :]
        fetch_up = Fetch(sc, layer, up_own, up_other, up, sem_up)
        fetch_down = Fetch(sc, layer, down_own, down_other, down, sem_down)
        seg = segments(sc, (rows, 1), 0, sc[1] * rows)
        place(buffer, branch, sc[0], narrow)
        x1 = x[...].astype(F32) + spread(mod, layer, 2, seg) * buffer[...]
        x1_out[...] = x1
        normed, _ = norm_of(x1)
        xf = (normed * (1.0 + spread(mod, layer, 4, seg)) + spread(mod, layer, 3, seg)).astype(BF)
        for_grads[:, hidden:] = xf
        fetch_up.wait()
        a = dot(xf, up[...])
        c0 = math.sqrt(2.0 / math.pi)
        square = a * a
        t = jnp.tanh(c0 * (a + 0.044715 * (a * square)))
        h = (0.5 * a * (1.0 + t)).astype(BF)
        for_grads[:, :hidden] = h
        slope_out[...] = 0.5 * (1.0 + t) + 0.5 * a * (1.0 - t * t) * (
            c0 * (1.0 + 3.0 * 0.044715 * square)
        )
        fetch_down.wait()
        low[...] = dot(h, down[...]).astype(BF)
        hand_out(outs, low, sc[0], narrow)

    return call(
        body,
        [sc, x] + branch + [mod, up[0], up[1], down[0], down[1]],
        [SM, VM] + [VM] * count + [VM, HB, HB, HB, HB],
        [
            sds((rows, width), F32),
            sds((rows, hidden + width), BF),
            sds((rows, hidden), F32),
        ]
        + [sds((rows, narrow), BF)] * count,
        [
            pltpu.VMEM(up[0].shape, BF),
            pltpu.VMEM(down[0].shape, BF),
            pltpu.VMEM((rows, width), F32),
            pltpu.VMEM((rows, width), BF),
            pltpu.SemaphoreType.DMA,
            pltpu.SemaphoreType.DMA,
        ],
        name=f"feed_forward_{layer}",
    )


def feed_backward(dims, layer, sc, pieces, slope, mod, up, down):
    rows, width, narrow, count, hidden = (
        dims.rows, dims.width, dims.narrow, dims.n_heads, dims.hidden,
    )
    last = layer == 1
    n_in = len(pieces)
    n_extra = 0 if last else 2

    def body(sc, *refs):
        pieces = refs[:n_in]
        slope, mod, up_own, up_other, down_own, down_other = refs[n_in : n_in + 6]
        rest = refs[n_in + 6 :]
        g_out, for_grads = rest[:2]
        outs = rest[2 : 2 + count]
        extra = rest[2 + count : 2 + count + n_extra]
        up, down, buffer, low, other_buffer, sem_up, sem_down = rest[2 + count + n_extra :]
        fetch_down = Fetch(sc, layer, down_own, down_other, down, sem_down)
        fetch_up = Fetch(sc, layer, up_own, up_other, up, sem_up)
        seg = segments(sc, (rows, 1), 0, sc[1] * rows)
        place(buffer, pieces[:count], sc[0], narrow)
        if last:
            g = buffer[...]
            g_out[...] = g.astype(BF)
        else:
            x, d_mid = pieces[count:]
            grad_out, sums_out = extra
            dxa = buffer[...]
            normed, inv = norm_of(x[...].astype(F32))
            other_buffer[...] = dxa * normed
            mine = pl.ds(pl.multiple_of(sc[0] * narrow, narrow), narrow)
            sums_out[0] = utterance_sums(buffer[:, mine], seg)
            sums_out[1] = utterance_sums(other_buffer[:, mine], seg)
            dx = d_mid[...] + norm_pull(dxa * (1.0 + spread(mod, 1, 1, seg)), normed, inv)
            other_buffer[...] = dx
            grad_out[...] = other_buffer[:, mine]
            g = dx.astype(BF)
            g_out[...] = g
            g = g.astype(F32)
        dz = (g * spread(mod, layer, 5, seg)).astype(BF)
        for_grads[:, :width] = dz
        fetch_down.wait()
        da = (dot(dz, down[...], ((1,), (1,))) * slope[...]).astype(BF)
        for_grads[:, width:] = da
        fetch_up.wait()
        low[...] = dot(da, up[...], ((1,), (1,))).astype(BF)
        hand_out(outs, low, sc[0], narrow)

    extra = [] if last else [sds((rows, narrow), F32), sds((2, 4, narrow), F32)]
    return call(
        body,
        [sc] + pieces + [slope, mod, up[0], up[1], down[0], down[1]],
        [SM] + [VM] * n_in + [VM, VM, HB, HB, HB, HB],
        [sds((rows, width), BF), sds((rows, width + hidden), BF)]
        + [sds((rows, narrow), BF)] * count
        + extra,
        [
            pltpu.VMEM(up[0].shape, BF),
            pltpu.VMEM(down[0].shape, BF),
            pltpu.VMEM((rows, width), F32),
            pltpu.VMEM((rows, width), BF),
            pltpu.VMEM((rows, width), F32),
            pltpu.SemaphoreType.DMA,
            pltpu.SemaphoreType.DMA,
        ],
        name=f"feed_backward_{layer}",
    )


def middle_backward(
    dims, layer, sc, g, x1, sums, branch, mod, weights, queries, kept, probs, exact, cosine, sine
):
    rows, width, narrow, local, count = (
        dims.rows, dims.width, dims.narrow, dims.local, dims.n_heads,
    )
    n_seq, frames = dims.n_seq, dims.frames
    heads = local // HEAD_DIM
    scale = 1.0 / math.sqrt(HEAD_DIM)

    def body(sc, g, x1, *refs):
        sums = refs[:count]
        branch, mod, w_own, w_other, queries, kept, probs, exact, cosine, sine = refs[
            count : count + 10
        ]
        d_mid_out, dy_out, small, q_out = refs[count + 10 : count + 14]
        outs = refs[count + 14 : count + 14 + n_seq]
        weight, buffer, other, done, sem = refs[count + 14 + n_seq :]
        fetch = Fetch(sc, layer, w_own, w_other, weight, sem)
        seg = segments(sc, (rows, 1), 0, sc[1] * rows)
        mine = pl.ds(pl.multiple_of(sc[0] * narrow, narrow), narrow)
        place(buffer, sums, sc[0], narrow)
        dxf = buffer[...]
        normed, inv = norm_of(x1[...])
        other[...] = dxf * normed
        small[1] = utterance_sums(buffer[:, mine], seg)
        small[2] = utterance_sums(other[:, mine], seg)
        d_mid = g[...].astype(F32) + norm_pull(
            dxf * (1.0 + spread(mod, layer, 4, seg)), normed, inv
        )
        d_mid_out[...] = d_mid
        other[...] = d_mid
        small[0] = utterance_sums(other[:, mine] * branch[...].astype(F32), seg)
        dy = (d_mid * spread(mod, layer, 2, seg)).astype(BF)
        dy_out[...] = dy
        fetch.wait()
        d_att = dot(dy, weight[...], ((1,), (1,))).astype(BF)
        shared = d_att.astype(F32) * exact[...]
        d_keys, d_vals = [], []
        cos = cosine[:, :HEAD_DIM]
        sin = -sine[:, :HEAD_DIM]
        for head in range(heads):
            cols = slice(head * HEAD_DIM, (head + 1) * HEAD_DIM)
            vals = slice(local + head * HEAD_DIM, local + (head + 1) * HEAD_DIM)
            low = probs[head]
            prob = low.astype(F32)
            grad = d_att[:, cols]
            d_prob = dot(grad, kept[:, vals], ((1,), (1,)))
            delta = jnp.sum(shared[:, cols], axis=1, keepdims=True)
            d_score = (prob * (d_prob - delta)).astype(BF)
            dq = dot(d_score, kept[:, cols]) * scale
            q_out[:, cols] = turn(dq, cos, sin).astype(BF)
            d_keys.append((dot(queries[:, cols], d_score, ((0,), (0,))) * scale).astype(BF))
            d_vals.append(dot(grad, low, ((0,), (0,))).astype(BF))
        for first, parts in ((0, d_keys), (local, d_vals)):
            for head in range(0, heads, 2):
                at = first + head * HEAD_DIM
                both = jnp.concatenate(parts[head : head + 2], axis=0)
                done[:, at : at + 2 * HEAD_DIM] = both.T
        for k in range(n_seq):
            at = pl.multiple_of(jnp.bitwise_xor(sc[1], k) * rows, rows)
            outs[k][...] = done[pl.ds(at, rows), :]

    return call(
        body,
        [sc, g, x1]
        + sums
        + [branch, mod, weights[0], weights[1], queries, kept, probs, exact, cosine, sine],
        [SM, VM, VM] + [VM] * count + [VM, VM, HB, HB] + [VM] * 6,
        [
            sds((rows, width), F32),
            sds((rows, width), BF),
            sds((3, 4, narrow), F32),
            sds((rows, local), BF),
        ]
        + [sds((rows, 2 * local), BF)] * n_seq,
        [
            pltpu.VMEM(weights[0].shape, BF),
            pltpu.VMEM((rows, width), F32),
            pltpu.VMEM((rows, width), F32),
            pltpu.VMEM((frames, 2 * local), BF),
            pltpu.SemaphoreType.DMA,
        ],
        name=f"middle_backward_{layer}",
    )


def project_backward(dims, layer, sc, dy, d_query, chunks, weights, cosine, sine):
    rows, width, narrow, local, count = (
        dims.rows, dims.width, dims.narrow, dims.local, dims.n_heads,
    )
    n_in = len(chunks)

    def body(sc, dy, d_query, *refs):
        chunks = refs[:n_in]
        w_own, w_other, cosine, sine, d_out = refs[n_in : n_in + 5]
        outs = refs[n_in + 5 : n_in + 5 + count]
        weight, buffer, sem = refs[n_in + 5 + count :]
        fetch = Fetch(sc, layer, w_own, w_other, weight, sem)
        total = chunks[0][...].astype(F32)
        for chunk in chunks[1:]:
            total = total + chunk[...].astype(F32)
        cos = widen_table(cosine[...], local)
        sin = -widen_table(sine[...], local)
        dk = turn(total[:, :local], cos, sin).astype(BF)
        dv = total[:, local:].astype(BF)
        d_out[:, :width] = dy[...]
        for i, part in enumerate((d_query[...], dk, dv)):
            d_out[:, width + i * local : width + (i + 1) * local] = part
        fetch.wait()
        total = dot(d_query[...], weight[0], ((1,), (1,)))
        total = total + dot(dk, weight[1], ((1,), (1,)))
        total = total + dot(dv, weight[2], ((1,), (1,)))
        buffer[...] = total.astype(BF)
        hand_out(outs, buffer, sc[0], narrow)

    return call(
        body,
        [sc, dy, d_query] + chunks + [weights[0], weights[1], cosine, sine],
        [SM, VM, VM] + [VM] * n_in + [HB, HB, VM, VM],
        [sds((rows, width + 3 * local), BF)] + [sds((rows, narrow), BF)] * count,
        [
            pltpu.VMEM(weights[0].shape, BF),
            pltpu.VMEM((rows, width), BF),
            pltpu.SemaphoreType.DMA,
        ],
        name=f"project_backward_{layer}",
    )


def products(left, right, local, width):
    first = dot(left[:, :local], right[:, :width], ((0,), (0,))).astype(BF)
    rest = dot(left[:, local:], right[:, width:], ((0,), (0,))).astype(BF)
    out = [[(slice(None), first)]]
    for i in range(rest.shape[1] // local):
        columns = slice(i * local, (i + 1) * local)
        lines = [slice(group * local, (group + 1) * local) for group in range(width // local)]
        out.append([(line, rest[line, columns]) for line in lines])
    return out


def half_grads(sc, left, right, local, name):
    width = left.shape[1] - local
    count = (1 + (right.shape[1] - width) // local) // 2

    def body(sc, left, right, mine, theirs):
        grads = products(left[...], right[...], local, width)
        for section in range(2):

            @pl.when(sc[2] == section)
            def _(section=section):
                for out, first in ((mine, section * count), (theirs, (1 - section) * count)):
                    for i in range(count):
                        for columns, value in grads[first + i]:
                            out[i * local : (i + 1) * local, columns] = value

    return call(
        body,
        [sc, left, right],
        [SM, VM, VM],
        [sds((count * local, width), BF)] * 2,
        name=name,
    )


def whole_grads(sc, left, right, local, name):
    count = len(left)
    rows, wide = left[0].shape
    width = wide - local
    tensors = 1 + (right[0].shape[1] - width) // local

    def body(sc, *refs):
        left, right = refs[:count], refs[count : 2 * count]
        out, all_left, all_right = refs[2 * count :]
        last = count.bit_length() - 2
        for k in range(count):
            mirrored = sum(1 << (last - i) for i in range(last + 1) if k >> i & 1)
            owner = jnp.bitwise_xor(sc[1], jnp.where(sc[2] == 0, k, mirrored))
            at = pl.ds(pl.multiple_of(owner * rows, rows), rows)
            all_left[at, :] = left[k][...]
            all_right[at, :] = right[k][...]
        grads = products(all_left[...], all_right[...], local, width)
        for i, grad in enumerate(grads):
            for columns, value in grad:
                out[i * local : (i + 1) * local, columns] = value

    return call(
        body,
        [sc] + list(left) + list(right),
        [SM] + [VM] * (2 * count),
        [sds((tensors * local, width), BF)],
        [
            pltpu.VMEM((count * rows, wide), BF),
            pltpu.VMEM((count * rows, right[0].shape[1]), BF),
        ],
        limit=24,
        name=name,
    )[0]


def add_split(sc, left, right, step):
    rows, width = left.shape
    half = rows // 2

    def body(sc, left, right, keep, send):
        bit = sc[5 + step]
        mine = pl.ds(pl.multiple_of(bit * half, half), half)
        other = pl.ds(pl.multiple_of((1 - bit) * half, half), half)
        keep[...] = (left[mine, :].astype(F32) + right[mine, :].astype(F32)).astype(BF)
        send[...] = (left[other, :].astype(F32) + right[other, :].astype(F32)).astype(BF)

    return call(
        body, [sc, left, right], [SM, VM, VM], [sds((half, width), BF)] * 2, name="add_split"
    )


def join(sc, mine, other, step):
    half, width = mine.shape

    def body(sc, mine, other, out):
        bit = sc[5 + step]
        out[pl.ds(pl.multiple_of(bit * half, half), half), :] = mine[...]
        out[pl.ds(pl.multiple_of((1 - bit) * half, half), half), :] = other[...]

    return call(
        body, [sc, mine, other], [SM, VM, VM], [sds((2 * half, width), BF)], name="join"
    )[0]


class HalfSum:
    def __init__(self, sc, layer, left, right, local, name):
        self.sc, self.layer = sc, layer
        self.mine, self.ready = half_grads(sc, left, right, local, name)
        self.bits = lax.axis_size("seq").bit_length() - 1
        self.at = 0
        self.taken = True
        self.pieces = []

    def send(self, *begin):
        value, bits = after(self.ready, *begin), self.bits
        if self.at == 0:
            self.came = swap(value)
        elif self.at <= bits:
            self.came = crossed(value, self.at - 1)
        else:
            if self.at == 2 * bits and not self.pieces:
                self.hand_over(value)
            self.came = crossed(value, 2 * bits - self.at)
        self.at += 1
        self.taken = False
        return self.came

    def hand_over(self, value):
        self.pieces.append((value, to_owner(value, self.layer)))

    def take(self):
        sc, bits = self.sc, self.bits
        self.taken = True
        if self.at <= bits:
            self.mine, self.ready = add_split(sc, self.mine, self.came, self.at - 1)
        elif self.at == bits + 1:
            self.mine = self.ready = add_chunks([self.mine, self.came])
        else:
            self.mine = self.ready = join(sc, self.mine, self.came, 2 * bits + 1 - self.at)
        return self.ready

    def last(self, *begin):
        while self.at <= 2 * self.bits:
            if not self.taken:
                self.take()
            self.send()
        self.hand_over(after(self.came, *begin))
        (own_0, other_0), (own_1, other_1) = self.pieces
        return [own_0, own_1, other_0, other_1]


class Spread:
    def __init__(self, value):
        self.parts = [value]
        self.bits = lax.axis_size("seq").bit_length() - 1
        self.early = None

    def one(self, *begin):
        self.parts.append(crossed(after(self.parts[0], *begin), 0))
        return self.parts[1]

    def two(self, *begin):
        self.early = crossed(after(self.parts[0], *begin), 1)
        return self.early

    def rest(self, *begin):
        for bit in range(1, self.bits):
            more = [] if bit > 1 else [self.early]
            start = 0 if bit > 1 else 1
            for part in self.parts[start:]:
                more.append(crossed(after(part, *begin), bit))
            self.parts = self.parts + more
        return self.parts[3:]


class Assembly:
    SCRATCH = 5

    @staticmethod
    def scratch(added, local, outs):
        width = added[0].shape[1]
        return [
            pltpu.VMEM((local, width), F32),
            pltpu.VMEM((outs - 1, width, local), F32),
            pltpu.VMEM((2, outs * local, width), BF),
            pltpu.SemaphoreType.DMA((outs, 2)),
            pltpu.SemaphoreType.DMA((outs,)),
        ]

    def __init__(self, sc, added, pieces, outs, scratch):
        self.sc, self.added, self.pieces = sc, added, pieces
        self.first_out, self.rest_out = outs
        self.first, self.rest, self.held, self.sems, self.out_sems = scratch
        self.outs = 1 + self.rest.shape[0]
        self.local, self.width = self.first.shape
        self.size = pieces[0].shape[0]

    def fetches_added(self):
        copies = []
        for i in range(self.outs):
            at = pl.ds(i * self.local, self.local)
            for j in range(2):
                copies.append(
                    pltpu.make_async_copy(
                        self.added[j].at[at, :], self.held.at[j, at, :], self.sems.at[i, j]
                    )
                )
        return copies

    def fetches_pieces(self):
        return [
            pltpu.make_async_copy(
                self.pieces[p],
                self.held.at[0, pl.ds(p * self.size, self.size), :],
                self.sems.at[p // 2, p % 2],
            )
            for p in range(4)
        ]

    def start(self):
        @pl.when(self.sc[2] == 0)
        def _():
            for copy in self.fetches_added():
                copy.start()

        @pl.when(self.sc[2] == 1)
        def _():
            for copy in self.fetches_pieces():
                copy.start()

    def store(self, index):
        if index == 0:
            return pltpu.make_async_copy(self.first, self.first_out, self.out_sems.at[0])
        return pltpu.make_async_copy(
            self.rest.at[index - 1], self.rest_out.at[index - 1], self.out_sems.at[index]
        )

    def put(self, index, value, line):
        lines = value.shape[0]
        if index == 0:
            self.first[line : line + lines, :] = value
            return
        for group in range(self.width // self.local):
            columns = slice(group * self.local, (group + 1) * self.local)
            at = group * self.local + line
            self.rest[index - 1, at : at + lines, :] = value[:, columns]

    def run(self):
        sc, local, size, held = self.sc, self.local, self.size, self.held
        count = self.outs // 2

        @pl.when(sc[2] == 0)
        def _():
            copies = self.fetches_added()
            for i in range(self.outs):
                copies[2 * i].wait()
                copies[2 * i + 1].wait()
                at = slice(i * local, (i + 1) * local)
                self.put(i, held[0, at, :].astype(F32) + held[1, at, :].astype(F32), 0)
                self.store(i).start()

        bits = lax.axis_size("seq").bit_length() - 1
        low, high = sc[1] & 1, (sc[1] >> (bits - 1)) & 1

        @pl.when(sc[2] == 1)
        def _():
            for copy in self.fetches_pieces():
                copy.wait()
            for section, at, bit in ((1, 0, high), (0, 2, low)):
                for turn in range(2):

                    @pl.when(bit == turn)
                    def _(section=section, at=at, turn=turn):
                        for place in range(2):
                            base = (at + (place ^ turn)) * size
                            for i in range(count):
                                begin = max(i * local, place * size)
                                end = min((i + 1) * local, (place + 1) * size)
                                if begin < end:
                                    row = base + begin - place * size
                                    value = held[0, row : row + end - begin, :].astype(F32)
                                    self.put(section * count + i, value, begin - i * local)

            for i in range(self.outs):
                self.store(i).start()

    def wait(self):
        for i in range(self.outs):
            self.store(i).wait()


def by_section(sc, mine, theirs, layer_0, layer_1):
    mine[...] = jnp.where(sc[2] == 0, layer_0, layer_1)
    theirs[...] = jnp.where(sc[2] == 0, layer_1, layer_0)


def gate_sums(dims, layer, sc, g, x1, z, mod, passed):
    rows, narrow = dims.rows, dims.narrow

    def body(sc, g, x1, z, mod, passed, small, *shown):
        seg = segments(sc, (rows, 1), 0, sc[1] * rows)
        mine = pl.ds(pl.multiple_of(sc[0] * narrow, narrow), narrow)
        value = z[...].astype(F32)
        small[...] = utterance_sums(g[:, mine].astype(F32) * value, seg)
        if shown:
            gate = spread(mod, layer, 5, seg, mine)
            result = (x1[:, mine] + gate * value).astype(BF)
            by_section(sc, *shown, passed[...], result)

    outs = [sds((4, narrow), F32)]
    if layer == 1:
        outs += [sds((rows, narrow), BF)] * 2
    return call(
        body, [sc, g, x1, z, mod, passed], [SM] + [VM] * 5, outs, name=f"gate_sums_{layer}"
    )


def last_norm(dims, sc, terms, x, mod, small_0, small_1):
    rows, narrow, count = dims.rows, dims.narrow, dims.n_heads

    def body(sc, *refs):
        terms = refs[:count]
        x, mod, mid_0, gate_0, in_1, mid_1, gate_1 = refs[count : count + 7]
        total_out, normed_out, inv_out, mine_out, theirs_out, rows_out, buffer = refs[count + 7 :]
        seg = segments(sc, (rows, 1), 0, sc[1] * rows)
        mine = pl.ds(pl.multiple_of(sc[0] * narrow, narrow), narrow)
        total = terms[0][...].astype(F32)
        for term in terms[1:]:
            total = total + term[...].astype(F32)
        normed, inv = norm_of(x[...].astype(F32))
        buffer[...] = normed
        normed = buffer[:, mine]
        first = (
            [utterance_sums(total, seg), utterance_sums(total * normed, seg)]
            + [mid_0[i] for i in range(3)]
            + [gate_0[...]]
        )
        second = [in_1[0], in_1[1]] + [mid_1[i] for i in range(3)] + [gate_1[...]]
        for i in range(6):
            by_section(sc, mine_out.at[i], theirs_out.at[i], first[i], second[i])
        grad = total * (1.0 + spread(mod, 0, 1, seg, mine))
        total_out[...] = grad
        normed_out[...] = normed
        inv_out[...] = inv
        lane = lax.broadcasted_iota(jnp.int32, (rows, 128), 1)
        sums = jnp.where(lane == 0, jnp.sum(grad, axis=1, keepdims=True), 0.0)
        sums = jnp.where(lane == 1, jnp.sum(grad * normed, axis=1, keepdims=True), sums)
        pick = diagonal(8, 128)
        rows_out[...] = sum(dot(pick, part, ((1,), (1,))) for part in split3(sums))

    return call(
        body,
        [sc] + terms + [x, mod] + small_0 + small_1,
        [SM] + [VM] * (count + 7),
        [
            sds((rows, narrow), F32),
            sds((rows, narrow), F32),
            sds((rows, 1), F32),
            sds((6, 4, narrow), F32),
            sds((6, 4, narrow), F32),
            sds((8, rows), F32),
        ],
        [pltpu.VMEM((rows, dims.width), F32)],
        name="last_norm",
    )


def last_pull(dims, sc, d_mid, grad, normed, inv, sums, middle_grad):
    rows, narrow, count, width = dims.rows, dims.narrow, dims.n_heads, dims.width

    def body(sc, d_mid, grad, normed, inv, middle, *refs):
        sums, outs = refs[:count], refs[count:]
        total = sums[0][:8, :rows]
        for term in sums[1:]:
            total = total + term[:8, :rows]
        row = lax.broadcasted_iota(jnp.int32, (8, 128), 0)
        lane = lax.broadcasted_iota(jnp.int32, (8, 128), 1)
        pick = (row == 4 * lane + 3).astype(BF)
        total = sum(dot(part, pick, ((0,), (0,))) for part in split3(total * (1.0 / width)))
        mine = pl.ds(pl.multiple_of(sc[0] * narrow, narrow), narrow)
        first = d_mid[:, mine] + inv[...] * (
            grad[...] - total[:, 0:1] - normed[...] * total[:, 1:2]
        )
        by_section(sc, *outs, first, middle[...])

    return call(
        body,
        [sc, d_mid, grad, normed, inv, middle_grad] + sums,
        [SM] + [VM] * (5 + count),
        [sds((rows, narrow), F32)] * 2,
        name="last_pull",
    )


def modulation_part(sc, mod_weight, row_sums, own, n_seq):
    kinds, width, narrow = mod_weight.shape

    def body(sc, mod_weight, row_sums, *refs):
        own = refs[:n_seq]
        grads_out, part, box = refs[n_seq:]
        for k in range(n_seq):
            box[jnp.bitwise_xor(sc[1], k)] = own[k][...]
        total = box[0]
        for j in range(1, n_seq):
            total = total + box[j]
        result = jnp.zeros((8, width), F32)
        for which in range(kinds):
            mine, theirs = total[which], total[kinds + which]
            grad = jnp.concatenate(
                [jnp.where(sc[2] == 0, mine, theirs), jnp.where(sc[2] == 0, theirs, mine)],
                axis=0,
            )
            grads_out[which] = grad
            result = result + exact_dot(grad, mod_weight[which], ((1,), (1,)))
        part[...] = result
        for row in range(2):
            part[4 * row + 3 : 4 * row + 4, : row_sums.shape[1]] = row_sums[row : row + 1, :]

    return call(
        body,
        [sc, mod_weight, row_sums] + own,
        [SM, VM, VM] + [VM] * n_seq,
        [sds((kinds, 8, narrow), F32), sds((8, width), F32)],
        [pltpu.VMEM((n_seq, 2 * kinds, 4, narrow), F32)],
        name="modulation_part",
    )


def modulation_weight(sc, act, grads):
    kinds, rows, narrow = grads.shape
    width = act.shape[1]

    def body(sc, act, grads, out, held, sems):
        tall = outer_parts(act[...], act[...])[0].astype(F32).T.astype(BF)

        def store(which):
            return pltpu.make_async_copy(held.at[which], out.at[which], sems.at[which])

        for which in range(kinds):
            wide = outer_parts(grads[which], grads[which])[1]
            held[which] = dot(tall, wide)
            store(which).start()
        for which in range(kinds):
            store(which).wait()

    return pl_call(
        body,
        [sc, act, grads],
        [SM, VM, VM],
        [sds((kinds, width, narrow), F32)],
        [HB],
        [pltpu.VMEM((kinds, width, narrow), F32), pltpu.SemaphoreType.DMA((kinds,))],
        limit=16,
        name="modulation_weight",
    )[0]


def time_backward(sc, sinus, inner, outer, time_out, own):
    count = len(own)
    rows, width = inner.shape
    freq = sinus.shape[1]
    block = width // 4

    def body(sc, sinus, inner, outer, time_out, *refs):
        own = refs[:count]
        g_in, g_out, box, held_in, held_out, sems = refs[count:]
        for k in range(count):
            at = jnp.bitwise_xor(sc[0], k)
            box[at, sc[2]] = own[k][:rows]
            box[at, 1 - sc[2]] = own[k][rows:]
        total = jnp.zeros((rows, width), F32)
        for j in range(count):
            for c in range(2):
                total = total + box[j, c]
        row = lax.broadcasted_iota(jnp.int32, (rows, width), 0)
        total = jnp.where(row % 4 == 3, 0.0, total)

        def slope(value):
            gate = 1.0 / (1.0 + jnp.exp(-value))
            return gate * (1.0 + value * (1.0 - gate))

        pre = inner[...]
        hidden = pre / (1.0 + jnp.exp(-pre))
        d_outer = total * slope(outer[...])
        tall, wide = outer_parts(hidden, d_outer)
        tall = tall.astype(F32).T.astype(BF)
        copies = []
        for i in range(4):
            at = slice(i * block, (i + 1) * block)
            held_out[at, :] = dot(tall[at], wide)
            copies.append(
                pltpu.make_async_copy(held_out.at[at, :], g_out.at[at, :], sems.at[i])
            )
            copies[-1].start()
        d_inner = exact_dot(d_outer, time_out[...], ((1,), (1,))) * slope(pre)
        held_in[...] = exact_outer(sinus[...], d_inner)
        copies.append(pltpu.make_async_copy(held_in, g_in, sems.at[4]))
        copies[-1].start()
        for copy in copies:
            copy.wait()

    return pl_call(
        body,
        [sc, sinus, inner, outer, time_out] + list(own),
        [SM] + [VM] * (4 + count),
        [sds((freq, width), F32), sds((width, width), F32)],
        [HB, HB],
        [
            pltpu.VMEM((count, 2, rows, width), F32),
            pltpu.VMEM((freq, width), F32),
            pltpu.VMEM((width, width), F32),
            pltpu.SemaphoreType.DMA((5,)),
        ],
        limit=16,
        name="time_backward",
    )


def finish(dims, sc, feed, attention, acts, grads):
    n = Assembly.SCRATCH

    def body(sc, act_own, act_other, grad_own, grad_other, *refs):
        sources, outs, scratch = refs[:12], refs[12:18], refs[18:]
        feed = Assembly(sc, sources[:2], sources[2:6], outs[:2], scratch[:n])
        attention = Assembly(sc, sources[6:8], sources[8:], outs[2:4], scratch[n:])
        feed.start()
        attention.start()
        outs[4][sc[2]] = act_own[...]
        outs[4][1 - sc[2]] = act_other[...]
        outs[5][sc[2]] = grad_own[...]
        outs[5][1 - sc[2]] = grad_other[...]
        feed.run()
        attention.run()
        feed.wait()
        attention.wait()

    width = dims.width
    sources = list(feed[0]) + list(feed[1]) + list(attention[0]) + list(attention[1])
    return pl_call(
        body,
        [sc] + list(acts) + list(grads) + sources,
        [SM] + [VM] * 4 + [HB] * 12,
        [
            sds((dims.hidden, width), F32),
            sds((1, width, dims.hidden), F32),
            sds((dims.local, width), F32),
            sds((3, width, dims.local), F32),
            sds((2,) + acts[0].shape, BF),
            sds((2,) + grads[0].shape, F32),
        ],
        [HB] * 4 + [VM] * 2,
        Assembly.scratch(feed[0], dims.hidden, 2) + Assembly.scratch(attention[0], dims.local, 4),
        limit=24,
        name="finish",
    )


class Dims:
    pass


def local_program(
    frames,
    cotangent,
    utt_lengths,
    time_ids,
    w_time_in,
    w_time_out,
    w_mod,
    w_qkv,
    w_out,
    w_up,
    w_down,
):
    dims = Dims()
    dims.n_heads = lax.axis_size("heads")
    dims.n_seq = n_seq = lax.axis_size("seq")
    _, dims.rows, dims.narrow = frames.shape
    dims.width = dims.narrow * dims.n_heads
    dims.local = w_qkv.shape[3]
    dims.hidden = w_up.shape[2]
    dims.frames = dims.rows * n_seq
    section = lax.axis_index("section")

    def here(both):
        return lax.dynamic_index_in_dim(both, section, 0, keepdims=False)

    sc = utt_lengths
    qkv = jnp.transpose(w_qkv[0], (1, 0, 2))
    mod_weight = jnp.transpose(w_mod[0], (1, 0, 2))
    wide_frames = gather(here(frames), "heads")
    qkv_w = (qkv, swap(qkv))
    sinus, inner, outer, act, mod_mine, mod_theirs = start(
        sc, time_ids, w_time_in, w_time_out, mod_weight
    )
    mod_theirs = swap(after(mod_theirs, *wide_frames))
    mods = gather(jnp.concatenate([mod_mine, mod_theirs], axis=0), "heads")
    cosine, sine = tables(sc, dims.rows)
    mods = after(mods, cosine, sine)

    x_0, _, xa, q_0, kv, mod = project(dims, 0, sc, wide_frames, mods, qkv_w, cosine, sine)
    chunks = gather(kv, "seq")
    out_w = (w_out[0], swap(after(w_out[0], mods[0])))
    kept_0, probs_0, for_attention, exact_0, *terms = attend(
        dims, 0, sc, chunks, q_0, xa, out_w
    )
    fwd_a = Spread(for_attention)

    up_w, down_w = [(w[0], swap(after(w[0], terms[0]))) for w in (w_up, w_down)]
    total = after(add_chunks(exchange(terms, "heads")), up_w[1], down_w[1])

    branch_0 = gather(total, "heads")
    fwd_a.one(total)
    fwd_a.two(total)
    x1_0, for_feed, slope_0, *terms = feed_forward(
        dims, 0, sc, x_0, branch_0, mod, up_w, down_w
    )
    fwd_f = Spread(for_feed)

    total = after(add_chunks(exchange(terms, "heads")), fwd_a.parts[1], fwd_a.early)

    z_0 = gather(total, "heads")
    fwd_a.rest(total)
    fwd_f.one(total)

    x_2, passed, xa, q_1, kv = project(
        dims, 1, sc, [x1_0] + z_0, [mod], qkv_w, cosine, sine
    )
    kv = after(kv, fwd_f.parts[1], *fwd_a.parts[3:])
    chunks = gather(kv, "seq")
    wide_cotangent = gather(after(here(cotangent), chunks[1]), "heads")
    kept_1, probs_1, for_attention_1, exact_1, *terms = attend(
        dims, 1, sc, chunks, q_1, xa, out_w
    )

    terms[0] = after(terms[0], *wide_cotangent)
    total = add_chunks(exchange(terms, "heads"))
    fwd_f.two(terms[0])

    branch_1 = gather(total, "heads")
    x1_1, for_feed, slope_1, *z_terms = feed_forward(
        dims, 1, sc, x_2, branch_1, mod, up_w, down_w
    )
    g_1, late, *terms = feed_backward(
        dims, 1, sc, wide_cotangent, slope_1, mod, up_w, down_w
    )
    terms = after(terms, fwd_f.early)
    feed_1 = HalfSum(sc, 1, for_feed, late, dims.hidden, "feed_grads_1")
    feed_1.send()
    got = exchange(terms, "heads")
    total = after(add_chunks(got), feed_1.came, *fwd_f.rest(terms[0]))

    feed_1.take()
    feed_1.send(total)
    sums = after(gather(total, "heads"), feed_1.came)

    feed_1.take()
    feed_1.send(sums[0])
    d_mid_1, dy, small_f1, dq, *sent = middle_backward(
        dims, 1, sc, g_1, x1_1, after(sums, feed_1.ready), branch_1[0], mod, out_w,
        q_1, kept_1, probs_1, exact_1, cosine, sine,
    )
    sent = after(sent, feed_1.came)

    got = exchange(sent, "seq")
    feed_1.take()
    z_1 = add_chunks(exchange(after(z_terms, sent[0]), "heads"))
    gate_1, *acts = gate_sums(dims, 1, sc, g_1, x1_1, z_1, mod, passed)
    got = after(got, feed_1.ready, *acts)
    late, *terms = project_backward(dims, 1, sc, dy, dq, got, qkv_w, cosine, sine)

    got = exchange(terms, "heads")
    feed_1.send(terms[0])
    attention_1 = HalfSum(sc, 1, for_attention_1, late, dims.local, "attend_grads_1")
    acts = [acts[0], swap(after(acts[1], terms[0]))]
    total = after(
        add_chunks(got), feed_1.came, attention_1.mine, attention_1.ready
    )

    feed_1.take()
    feed_1.send(total)
    attention_1.send(total)
    pieces = gather(total, "heads")

    g_0, late, *rest = feed_backward(
        dims, 0, sc, pieces + [x_2, d_mid_1], slope_0, mod, up_w, down_w
    )
    terms, (middle_grad, small_a1) = rest[: dims.n_heads], rest[dims.n_heads :]
    terms = after(terms, feed_1.came, attention_1.came, acts)
    late_f = Spread(late)
    got = exchange(terms, "heads")
    attention_1.take()
    attention_1.send(terms[0])
    late_f.one(terms[0])
    total = after(add_chunks(got), attention_1.came)

    attention_1.take()
    attention_1.send(total)
    late_f.two(total)
    sums = after(gather(total, "heads"), attention_1.came, late_f.parts[1])

    attention_1.take()
    attention_1.send(sums[0])
    d_mid_0, dy, small_f0, dq, *sent = middle_backward(
        dims, 0, sc, g_0, x1_0, after(sums, attention_1.ready), branch_0[0], mod, out_w,
        q_0, kept_0, probs_0, exact_0, cosine, sine,
    )
    sent = after(sent, attention_1.came, late_f.early)

    got = exchange(sent, "seq")
    attention_1.take()
    if attention_1.at == 2 * attention_1.bits:
        attention_1.hand_over(after(attention_1.ready, got[0]))
    feed_1 = feed_1.last(sent[0])
    gate_0, *_ = gate_sums(dims, 0, sc, g_0, x1_0, z_0[0], mod, passed)
    got = after(got, attention_1.ready, gate_0, feed_1)
    late, *terms = project_backward(dims, 0, sc, dy, dq, got, qkv_w, cosine, sine)
    late_a = Spread(late)

    got = exchange(terms, "heads")
    late_a.one(terms[0])
    late_f.rest(terms[0])

    grad, normed, inv, mine, theirs, row_sums = last_norm(
        dims, sc, got, x_0, mod, [small_f0, gate_0], [small_a1, small_f1, gate_1]
    )
    late_a.two(row_sums)
    theirs = after(swap(theirs), late_a.parts[1], *late_f.parts[3:])
    both = jnp.concatenate([mine, theirs], axis=0)
    both = gather(both, "seq")
    feed_0 = whole_grads(
        sc, after(fwd_f.parts, theirs), late_f.parts, dims.hidden, "feed_grads_0"
    )
    both = after(both, feed_0, late_a.early)
    mod_grads, part = modulation_part(sc, mod_weight, row_sums, both, n_seq)

    late_a.rest(part)
    attention_1.send(part)
    feed_0 = [feed_0, to_owner(after(feed_0, both[0]), 0)]
    ends = jnp.concatenate([part, swap(part)], axis=0)
    ends = gather(after(ends, feed_0), "heads")
    g_mod = modulation_weight(sc, act, mod_grads)
    ends = after(ends, *late_a.parts[3:], g_mod)

    attention_0 = whole_grads(
        sc, after(fwd_a.parts, *ends), late_a.parts, dims.local, "attend_grads_0"
    )
    attention_0 = after(attention_0, attention_1.came)
    attention_0 = [attention_0, to_owner(attention_0, 0)]
    attention_1 = attention_1.last(attention_0[0])
    grads = last_pull(
        dims, sc, d_mid_0, grad, normed, inv, after(ends, attention_0[0]), middle_grad
    )
    grads = [grads[0], swap(grads[1])]
    g_first, g_second = time_backward(
        sc, sinus, inner, outer, w_time_out, after(ends, attention_0[0])
    )
    g_reduce, g_expand, g_out, g_qkv, acts, grads = finish(
        dims, sc, (feed_0, feed_1), (after(attention_0, g_second), attention_1), acts, grads
    )

    return (
        acts[None],
        grads[None],
        g_first,
        g_second,
        jnp.transpose(g_mod, (1, 0, 2))[None],
        jnp.transpose(g_qkv, (1, 0, 2))[None],
        g_out[None],
        g_expand,
        g_reduce[None],
    )


def solution(mesh):
    placed = (
        P(None, "seq", "heads"),
        P(None, "seq", "heads"),
        P(),
        P(),
        P(),
        P(),
        P("section", None, None, "heads"),
        P("section", None, None, "heads"),
        P("section", "heads", None),
        P("section", None, "heads"),
        P("section", "heads", None),
    )
    return jax.shard_map(
        local_program,
        mesh=mesh,
        in_specs=placed,
        out_specs=(
            P("section", None, "seq", "heads"),
            P("section", None, "seq", "heads"),
            P(),
            P(),
            P("section", None, None, "heads"),
            P("section", None, None, "heads"),
            P("section", "heads", None),
            P("section", None, "heads"),
            P("section", "heads", None),
        ),
        check_vma=False,
    )
```
